32 devices in a mesh: loop: 4 (over x, core), rep: 8 (over z, y).
Axes of the slice: x: 2, y: 2, z: 4, core: 2. Of those that a mesh axis runs over, the one named last changes fastest.
Arguments:
- features: bfloat16 [768, 8, 1152], P('loop', 'rep'), may hold values from -6 to 6
- text: bfloat16 [768, 8, 1152], P('loop', 'rep'), may hold values from -6 to 6
- proj: bfloat16 [1152, 1152], replicated, may hold values from -0.1875 to 0.1875
- gain: float32 [1152], replicated, may hold values from 0.5 to 1.5
- scale: float32 [1], replicated, may hold values from 8 to 32
- bias: float32 [1], replicated, may hold values from -4 to 0
Outputs:
- feature_grad: bfloat16 [768, 8, 1152], P('loop', 'rep')
- text_grad: bfloat16 [768, 8, 1152], P('loop', 'rep')
- proj_grad: float32 [1152, 1152], P('rep')
- gain_gradient: float32 [1152], replicated
The draws below stay inside these ranges and needn't reach their ends.
All inputs are finite; a program needn't handle non-finite values.
Results may differ from the reference program's by a relative error of at most 0.024.
Values may be sent and summed in bfloat16 or wider, within the bound.
No kernel may reach another device: no remote copies, remote signals or barrier semaphores. Data moves between devices by JAX's collectives and lax.ppermute only.
A program may use at most 64 MiB of HBM per device.

```python
import math
import jax
import jax.numpy as jnp
from jax import lax

W = 1152
E = 1152
ROWS_DEV = 192
PAIRS_PER_GROUP = 768
GROUPS = 8
N_LOOP = 4


def with_spikes(entries, rng, source, target, shards_of, factor):
    def block_of(dim):
        return (jnp.arange(entries.shape[dim]) // (entries.shape[dim] // shards_of)).reshape((-1,) + (1,) * (entries.ndim - 1 - dim))

    first = jax.random.permutation(rng, shards_of)[block_of(target)]
    other_side = (block_of(target) + shards_of // 2) % shards_of
    return jnp.where((block_of(source) == first) | (block_of(source) == other_side), factor * entries, entries)


def block_levels(own_key, extent, cuts, low, high):
    loudness = 1.0
    for axis_at, blocks in cuts:
        draws = jax.random.uniform(jax.random.fold_in(jax.random.fold_in(own_key, 6), axis_at), (blocks,), jnp.float32, low / len(cuts), high / len(cuts))
        loudness = loudness * jnp.repeat(jnp.exp(draws), extent[axis_at] // blocks).reshape((-1,) + (1,) * (len(extent) - 1 - axis_at))
    return loudness


def centred(stream_key, extent, spread, limit, shards=(), kind=jnp.bfloat16):
    factor_of = block_levels(stream_key, extent, shards, -0.22, 0.18) if shards else 1.0
    array = jax.random.normal(stream_key, extent, jnp.float32) * spread * factor_of
    return jnp.minimum(jnp.maximum(array, -limit), limit).astype(kind)


def gaussian_with(rng, dims, scale, most, shards, heavy, kind=jnp.bfloat16):
    values = scale * jax.random.normal(rng, dims, jnp.float32)
    if shards:
        values = values * block_levels(rng, dims, shards, -0.22, 0.18)
    return jnp.clip(with_spikes(values, jax.random.fold_in(rng, 3), *heavy), -most, most).astype(kind)


def setup_inputs(seed: int = 0) -> dict:
    keys = jax.random.split(jax.random.key(seed), 7)
    return {
        "features": gaussian_with(keys[0], (PAIRS_PER_GROUP, GROUPS, W), 1.0, 6.0, ((0, 4), (1, 8)), (1, 2, 8, 2.0)),
        "text": centred(keys[1], (PAIRS_PER_GROUP, GROUPS, E), 1.0, 6.0, ((0, 4), (1, 8))),
        "proj": centred(keys[2], (W, E), W ** -0.5, 0.1875),
        "gain": jnp.clip(1.0 + 0.1 * jax.random.normal(keys[3], (W,), jnp.float32), 0.5, 1.5),
        "scale": jnp.clip(jnp.exp(jax.random.uniform(keys[4], (1,), jnp.float32, math.log(8.0), math.log(32.0))), 8.0, 32.0),
        "bias": jnp.clip(jax.random.uniform(keys[5], (1,), jnp.float32, -4.0, 0.0), -4.0, 0.0),
    }


def unit_rows(values):
    inverse = lax.rsqrt(lax.optimization_barrier(jnp.sum(values * values, axis=-1, keepdims=True)) + 1e-06)
    return (values * inverse, inverse)

def reference(features, text, proj, gain, scale, bias):
    logit_scale = scale[0]
    logit_bias = bias[0]
    diag_mask = jnp.eye(PAIRS_PER_GROUP, dtype=jnp.float32)

    def group_pass(carry, inputs):
        proj_sum, gain_total = carry
        image_rows, text_rows = inputs
        xvalues = image_rows.astype(jnp.float32)
        row_mean = lax.optimization_barrier(jnp.mean(xvalues, axis=-1, keepdims=True))
        mean_removed = xvalues - row_mean
        row_inverse_deviation = lax.rsqrt(lax.optimization_barrier(jnp.mean(mean_removed * mean_removed, axis=-1, keepdims=True)) + 1e-06)
        standardized_input = mean_removed * row_inverse_deviation
        normalized_rows = (standardized_input * gain).astype(jnp.bfloat16)
        projected = jnp.dot(normalized_rows, proj, preferred_element_type=jnp.float32)
        img_dir, img_inv = unit_rows(projected)
        img_unit = img_dir.astype(jnp.bfloat16)
        txt_dir, txt_inv = unit_rows(text_rows.astype(jnp.float32))
        txt_unit = txt_dir.astype(jnp.bfloat16)
        logits = logit_scale * jnp.dot(img_unit, txt_unit.T, preferred_element_type=jnp.float32) + logit_bias
        pair_weight = (jax.nn.sigmoid(logits) - diag_mask).astype(jnp.bfloat16)
        img_back = logit_scale * jnp.dot(pair_weight, txt_unit, preferred_element_type=jnp.float32)
        txt_back = logit_scale * jnp.dot(pair_weight.T, img_unit, preferred_element_type=jnp.float32)
        proj_back = ((img_back - img_dir * lax.optimization_barrier(jnp.sum(img_dir * img_back, axis=-1, keepdims=True))) * img_inv).astype(jnp.bfloat16)
        text_out = ((txt_back - txt_dir * lax.optimization_barrier(jnp.sum(txt_dir * txt_back, axis=-1, keepdims=True))) * txt_inv).astype(jnp.bfloat16)
        norm_backward = jnp.dot(proj_back, proj.T, preferred_element_type=jnp.float32)
        scaled_backward = norm_backward * gain
        feature_result = (row_inverse_deviation * (scaled_backward - lax.optimization_barrier(jnp.mean(scaled_backward, axis=-1, keepdims=True)) - standardized_input * lax.optimization_barrier(jnp.mean(scaled_backward * standardized_input, axis=-1, keepdims=True)))).astype(jnp.bfloat16)
        normed_blocks = normalized_rows.astype(jnp.float32).reshape(N_LOOP, ROWS_DEV, W)
        back_blocks = proj_back.astype(jnp.float32).reshape(N_LOOP, ROWS_DEV, E)
        partials = jnp.einsum('lrw,lre->lwe', normed_blocks, back_blocks, precision=lax.Precision.HIGHEST) / PAIRS_PER_GROUP
        partials = lax.optimization_barrier(partials.astype(jnp.bfloat16))
        proj_sum = proj_sum + lax.optimization_barrier(jnp.sum(partials.astype(jnp.float32), axis=0))
        gain_total = gain_total + lax.optimization_barrier(jnp.sum(norm_backward * standardized_input, axis=0)) / PAIRS_PER_GROUP
        return ((proj_sum, gain_total), (feature_result, text_out))
    start = (jnp.zeros((W, E), jnp.float32), jnp.zeros((W,), jnp.float32))
    (proj_grad, gain_gradient), (feature_all, text_all) = lax.scan(group_pass, start, (jnp.transpose(features, (1, 0, 2)), jnp.transpose(text, (1, 0, 2))))
    feature_grad = jnp.transpose(feature_all, (1, 0, 2))
    text_grad = jnp.transpose(text_all, (1, 0, 2))
    return (feature_grad, text_grad, proj_grad, gain_gradient)
```

```python
import jax
import jax.numpy as jnp
from jax import lax
from jax.sharding import PartitionSpec as P

F32 = jnp.float32
BF16 = jnp.bfloat16
LAST = (((1,), (1,)), ((), ()))
FIRST = (((0,), (0,)), ((), ()))


def dot(a, b, dims=(((1,), (0,)), ((), ()))):
    return lax.dot_general(a, b, dims, preferred_element_type=F32)


def unit_rows(values):
    inverse = lax.rsqrt(jnp.sum(values * values, axis=-1, keepdims=True) + 1e-06)
    return values * inverse, inverse


def standardize(rows):
    values = rows.astype(F32)
    centred = values - jnp.mean(values, axis=-1, keepdims=True)
    inverse = lax.rsqrt(jnp.mean(centred * centred, axis=-1, keepdims=True) + 1e-06)
    return centred * inverse, inverse


def send(value, axis, target):
    count = lax.axis_size(axis)
    return lax.ppermute(value, axis, [(p, target(p)) for p in range(count)])


def gather_group(value, count):
    mine = [value]
    for step in range(1, count // 2):
        mine.append(send(value, "loop", lambda p: (p + 2 * step) % count))
    mates = [send(block, "loop", lambda p: p ^ 1) for block in mine]
    return mine + mates


def local(features, text, proj, gain, scale, bias):
    n = lax.axis_size("loop")
    m = lax.axis_size("rep")
    me = lax.axis_index("loop")
    half = n // 2
    rows, width = features.shape[0], features.shape[2]
    columns = proj.shape[1] // n
    group_rows = rows * n
    logit_scale, logit_bias = scale[0], bias[0]

    own_features = features[:, 0, :]
    own_text = text[:, 0, :]
    text_blocks = gather_group(own_text, n)
    feature_blocks = gather_group(own_features, n)

    xhat, deviation = standardize(own_features)
    normed = (xhat * gain).astype(BF16)
    img_dir, img_inv = unit_rows(dot(normed, proj))
    img_unit = img_dir.astype(BF16)

    txt_dir, txt_inv = unit_rows(own_text.astype(F32))
    own_txt_unit = txt_dir.astype(BF16)
    txt_unit = jnp.concatenate(
        [own_txt_unit] + [unit_rows(block.astype(F32))[0].astype(BF16) for block in text_blocks[1:]]
    )
    row_ids = lax.broadcasted_iota(jnp.int32, (rows, group_rows), 0)
    column_ids = lax.broadcasted_iota(jnp.int32, (rows, group_rows), 1)
    diagonal = (row_ids == column_ids).astype(F32)

    def weights(left, right):
        logits = logit_scale * dot(left, right, LAST) + logit_bias
        return (jax.nn.sigmoid(logits) - diagonal).astype(BF16)

    img_back = logit_scale * dot(weights(img_unit, txt_unit), txt_unit)
    proj_back = (
        (img_back - img_dir * jnp.sum(img_dir * img_back, axis=-1, keepdims=True)) * img_inv
    ).astype(BF16)

    blocks = jnp.transpose(proj_back.reshape(rows, n, columns), (1, 0, 2))
    blocks = lax.all_to_all(blocks, "loop", 0, 0, tiled=True)
    back_columns = blocks.reshape(group_rows, columns)

    norm_back = dot(proj_back, proj, LAST)
    scaled = norm_back * gain
    feature_grad = (
        deviation
        * (
            scaled
            - jnp.mean(scaled, axis=-1, keepdims=True)
            - xhat * jnp.mean(scaled * xhat, axis=-1, keepdims=True)
        )
    ).astype(BF16)
    gain_term = jnp.sum(norm_back * xhat, axis=0) * (1.0 / group_rows)

    other_normed = [(standardize(block)[0] * gain).astype(BF16) for block in feature_blocks[1:]]
    relative = jnp.stack([normed] + other_normed)
    member = jnp.arange(n)
    same_core = (member % 2) == (me % 2)
    chips_back = ((me // 2 - member // 2) % half)
    position = jnp.where(same_core, chips_back, half + chips_back)
    group_normed = relative[position].reshape(group_rows, width)

    partial = (dot(group_normed, back_columns, FIRST) * (1.0 / group_rows)).astype(BF16)
    pieces = lax.all_to_all(partial.reshape(m, width // m, columns), "rep", 0, 0, tiled=True)
    reduced = jnp.sum(pieces.astype(F32), axis=0).astype(BF16)
    gains = lax.all_gather(gain_term, "rep")
    gain_sum = jnp.sum(gains, axis=0)
    proj_rows = lax.all_gather(reduced, "loop")
    proj_grad = jnp.transpose(proj_rows, (1, 0, 2)).reshape(width // m, n * columns).astype(F32)
    gain_gradient = jnp.sum(lax.all_gather(gain_sum, "loop"), axis=0)

    group_unit = jnp.concatenate(
        [img_unit] + [unit_rows(dot(block, proj))[0].astype(BF16) for block in other_normed]
    )
    text_weights = weights(own_txt_unit, group_unit)
    txt_back = logit_scale * dot(text_weights, group_unit)
    text_grad = (
        (txt_back - txt_dir * jnp.sum(txt_dir * txt_back, axis=-1, keepdims=True)) * txt_inv
    ).astype(BF16)
    return feature_grad[:, None, :], text_grad[:, None, :], proj_grad, gain_gradient


def solution(mesh):
    return jax.shard_map(
        local,
        mesh=mesh,
        in_specs=(P("loop", "rep", None), P("loop", "rep", None), P(), P(), P(), P()),
        out_specs=(P("loop", "rep", None), P("loop", "rep", None), P("rep", None), P()),
        check_vma=False,
    )
```

```python
import functools

import jax
import jax.numpy as jnp
from jax import lax
from jax.experimental import pallas as pl
from jax.experimental.pallas import tpu as pltpu
from jax.sharding import PartitionSpec as P

F32 = jnp.float32
BF16 = jnp.bfloat16
LAST = (((1,), (1,)), ((), ()))
FIRST = (((0,), (0,)), ((), ()))


def dot(a, b, dims=(((1,), (0,)), ((), ()))):
    return lax.dot_general(a, b, dims, preferred_element_type=F32)


def unit_rows(values):
    inverse = lax.rsqrt(jnp.sum(values * values, axis=-1, keepdims=True) + 1e-06)
    return values * inverse, inverse


def standardize(rows):
    values = rows.astype(F32)
    centred = values - jnp.mean(values, axis=-1, keepdims=True)
    inverse = lax.rsqrt(jnp.mean(centred * centred, axis=-1, keepdims=True) + 1e-06)
    return centred * inverse, inverse


def send(value, axis, target):
    count = lax.axis_size(axis)
    return lax.ppermute(value, axis, [(p, target(p)) for p in range(count)])


def gather_group(value, count):
    mine = [value]
    for step in range(1, count // 2):
        mine.append(send(value, "loop", lambda p: (p + 2 * step) % count))
    mates = [send(block, "loop", lambda p: p ^ 1) for block in mine]
    return mine + mates


def local_any_size(features, text, proj, gain, scale, bias):
    n = lax.axis_size("loop")
    m = lax.axis_size("rep")
    me = lax.axis_index("loop")
    half = n // 2
    rows, width = features.shape[0], features.shape[2]
    columns = proj.shape[1] // n
    group_rows = rows * n
    logit_scale, logit_bias = scale[0], bias[0]

    own_features = features[:, 0, :]
    own_text = text[:, 0, :]
    text_blocks = gather_group(own_text, n)
    feature_blocks = gather_group(own_features, n)

    xhat, deviation = standardize(own_features)
    normed = (xhat * gain).astype(BF16)
    img_dir, img_inv = unit_rows(dot(normed, proj))
    img_unit = img_dir.astype(BF16)

    txt_dir, txt_inv = unit_rows(own_text.astype(F32))
    own_txt_unit = txt_dir.astype(BF16)
    txt_unit = jnp.concatenate(
        [own_txt_unit] + [unit_rows(block.astype(F32))[0].astype(BF16) for block in text_blocks[1:]]
    )
    row_ids = lax.broadcasted_iota(jnp.int32, (rows, group_rows), 0)
    column_ids = lax.broadcasted_iota(jnp.int32, (rows, group_rows), 1)
    diagonal = (row_ids == column_ids).astype(F32)

    def weights(left, right):
        logits = logit_scale * dot(left, right, LAST) + logit_bias
        return (jax.nn.sigmoid(logits) - diagonal).astype(BF16)

    img_back = logit_scale * dot(weights(img_unit, txt_unit), txt_unit)
    proj_back = (
        (img_back - img_dir * jnp.sum(img_dir * img_back, axis=-1, keepdims=True)) * img_inv
    ).astype(BF16)

    blocks = jnp.transpose(proj_back.reshape(rows, n, columns), (1, 0, 2))
    blocks = lax.all_to_all(blocks, "loop", 0, 0, tiled=True)
    back_columns = blocks.reshape(group_rows, columns)

    norm_back = dot(proj_back, proj, LAST)
    scaled = norm_back * gain
    feature_grad = (
        deviation
        * (
            scaled
            - jnp.mean(scaled, axis=-1, keepdims=True)
            - xhat * jnp.mean(scaled * xhat, axis=-1, keepdims=True)
        )
    ).astype(BF16)
    gain_term = jnp.sum(norm_back * xhat, axis=0) * (1.0 / group_rows)

    other_normed = [(standardize(block)[0] * gain).astype(BF16) for block in feature_blocks[1:]]
    relative = jnp.stack([normed] + other_normed)
    member = jnp.arange(n)
    same_core = (member % 2) == (me % 2)
    chips_back = ((me // 2 - member // 2) % half)
    position = jnp.where(same_core, chips_back, half + chips_back)
    group_normed = relative[position].reshape(group_rows, width)

    partial = (dot(group_normed, back_columns, FIRST) * (1.0 / group_rows)).astype(BF16)
    pieces = lax.all_to_all(partial.reshape(m, width // m, columns), "rep", 0, 0, tiled=True)
    reduced = jnp.sum(pieces.astype(F32), axis=0).astype(BF16)
    gains = lax.all_gather(gain_term, "rep")
    gain_sum = jnp.sum(gains, axis=0)
    proj_rows = lax.all_gather(reduced, "loop")
    proj_grad = jnp.transpose(proj_rows, (1, 0, 2)).reshape(width // m, n * columns).astype(F32)
    gain_gradient = jnp.sum(lax.all_gather(gain_sum, "loop"), axis=0)

    group_unit = jnp.concatenate(
        [img_unit] + [unit_rows(dot(block, proj))[0].astype(BF16) for block in other_normed]
    )
    text_weights = weights(own_txt_unit, group_unit)
    txt_back = logit_scale * dot(text_weights, group_unit)
    text_grad = (
        (txt_back - txt_dir * jnp.sum(txt_dir * txt_back, axis=-1, keepdims=True)) * txt_inv
    ).astype(BF16)
    return feature_grad[:, None, :], text_grad[:, None, :], proj_grad, gain_gradient


VMEM = pl.BlockSpec(memory_space=pltpu.VMEM)
SMEM = pl.BlockSpec(memory_space=pltpu.SMEM)
LANES = 128
BAND = 16


def call(body, outs, scratch=(), smem=0, flops=0, moved=0):
    def run(*operands):
        specs = [SMEM] * smem + [VMEM] * (len(operands) - smem)
        return pl.pallas_call(
            body,
            out_shape=[jax.ShapeDtypeStruct(shape, kind) for shape, kind in outs],
            in_specs=specs,
            out_specs=[VMEM] * len(outs),
            scratch_shapes=list(scratch),
            compiler_params=pltpu.CompilerParams(vmem_limit_bytes=36 * 2**20),
            cost_estimate=pl.CostEstimate(flops=flops, bytes_accessed=moved, transcendentals=0),
        )(*operands)

    return run


def over_rows(count, step, body):
    def turn(index, _):
        body(pl.ds(pl.multiple_of(index * step, step), step))
        return 0

    lax.fori_loop(0, count // step, turn, 0, unroll=2)


def sums(values):
    return jnp.sum(values, axis=-1, keepdims=True)


def normalize_into(source, gain, target, at):
    rows, width = source.shape

    def chunk(where):
        values = source[where, :].astype(F32)
        centred = values - sums(values) * (1.0 / width)
        inverse = lax.rsqrt(sums(centred * centred) * (1.0 / width) + 1e-06)
        target[pl.ds(at + where.start, where.size), :] = (centred * inverse * gain[...]).astype(BF16)

    over_rows(rows, 32, chunk)


def unit_into(source, target, at, inverses=None):
    rows = source.shape[0]

    def chunk(where):
        values = source[where, :].astype(F32)
        inverse = lax.rsqrt(sums(values * values) + 1e-06)
        place = pl.ds(at + where.start, where.size)
        target[place, :] = (values * inverse).astype(BF16)
        if inverses is not None:
            inverses[place, :] = inverse

    over_rows(rows, 32, chunk)


def weigh(dots, scale, bias, first_column, weights, columns_at, totals, add_to):
    rows, columns = dots.shape

    def chunk(where):
        product = dots[where, :]
        logits = scale * product + bias
        weight = 1.0 / (1.0 + jnp.exp(-logits))
        row = where.start + lax.broadcasted_iota(jnp.int32, product.shape, 0)
        column = first_column + lax.broadcasted_iota(jnp.int32, product.shape, 1)
        weight = jnp.where(row == column, weight - 1.0, weight).astype(BF16)
        weights[where, columns_at : columns_at + columns] = weight
        total = sums(weight.astype(F32) * product)
        totals[where, :] = total if add_to is None else add_to[where, :] + total

    over_rows(rows, 64, chunk)


def near_body(f0, f1, t0, t1, proj, gain, normed, unit, inverse, text_unit, projected):
    rows = f0.shape[0]
    for k, source in enumerate((f0, f1)):
        normalize_into(source, gain, normed, k * rows)
    for k, source in enumerate((t0, t1)):
        unit_into(source, text_unit, k * rows)
    projected[...] = dot(normed[...], proj[...])
    unit_into(projected, unit, 0, inverse)


def far_body(
    scalars, f2, f3, proj, gain, normed_near, unit_near, inverse_near, text_near,
    normed, unit, inverse, weights, totals, projected, dots,
):
    rows = f2.shape[0]
    near = 2 * rows
    normed[:near, :] = normed_near[...]
    unit[:near, :] = unit_near[...]
    inverse[:near, :] = inverse_near[...]
    for k, source in enumerate((f2, f3)):
        normalize_into(source, gain, normed, near + k * rows)
    projected[...] = dot(normed[near:, :], proj[...])
    unit_into(projected, unit, near, inverse)
    dots[...] = dot(unit[...], text_near[...], LAST)
    weigh(dots, scalars[0], scalars[1], 0, weights, 0, totals, None)


def pack_into(target, block, full):
    rows, columns = block.shape
    rest = columns - full
    target[:rows, :] = block[:, :full].astype(BF16)
    per_band = full // rest
    tail = block[:, full:]
    chunks = [tail[at : at + BAND, :] for at in range(0, rows, BAND)]
    for band in range(0, len(chunks), per_band):
        part = chunks[band : band + per_band]
        if len(part) < per_band:
            part.append(jnp.zeros((BAND, full - rest * len(part)), block.dtype))
        at = rows + (band // per_band) * BAND
        target[at : at + BAND, :] = jnp.concatenate(part, axis=1).astype(BF16)


def partial_body(
    members, groups, scalars, place, t2, t3, text_near, unit, inverse, normed, weights_near, totals_near,
    *refs,
):
    packets, (text_far, weights_own), scratch = refs[:groups], refs[groups : groups + 2], refs[groups + 2 :]
    weights, totals, dots, text_columns, unit_columns, back, packed = scratch
    rows = t2.shape[0]
    near = 2 * rows
    every = members * rows
    width = unit.shape[1]
    columns = width // members
    full = packed.shape[2]
    scale, bias = scalars[0], scalars[1]
    for k, source in enumerate((t2, t3)):
        unit_into(source, text_far, k * rows)
    dots[...] = dot(unit[...], text_far[...], LAST)
    weights[:, :near] = weights_near[...]
    weigh(dots, scale, bias, near, weights, near, totals, totals_near)
    weights_own[...] = weights[:rows, :]
    for member in range(members):

        @pl.when(place[0] == member)
        def _():
            where = slice(member * columns, (member + 1) * columns)
            text_columns[:near, :] = text_near[:, where]
            text_columns[near:, :] = text_far[:, where]
            unit_columns[...] = unit[:, where]

    image_back = dot(weights[...], text_columns[...])
    back[...] = (
        (image_back - unit_columns[...].astype(F32) * totals[...]) * (inverse[...] * scale)
    ).astype(BF16)
    each = width // groups
    product = dot(normed[...], back[...], FIRST) * (1.0 / every)
    for group in range(groups):
        pack_into(packed.at[group], product[group * each : (group + 1) * each, :], full)
    for step in range(groups):
        packets[step][...] = packed[place[1] ^ step]


def own_body(
    scalars, features, text, proj, gain, text_near, text_far, weights_own, weights_near, unit, inverse,
    feature_grad, text_grad, gain_term, back, norm_back,
):
    rows, width = features.shape
    near = 2 * rows
    scale = scalars[0]
    image_back = dot(weights_own[:, :near], text_near[...]) + dot(weights_own[:, near:], text_far[...])
    norm_back[...] = image_back

    def image_chunk(where):
        values = norm_back[where, :] * scale
        direction = unit[where, :].astype(F32)
        back[where, :] = (
            (values - direction * sums(direction * values)) * inverse[where, :]
        ).astype(BF16)

    over_rows(rows, 32, image_chunk)
    norm_back[...] = dot(back[...], proj[...], LAST)
    gain_term[...] = jnp.zeros_like(gain_term)

    def feature_chunk(index, total):
        where = pl.ds(pl.multiple_of(index * 32, 32), 32)
        values = features[where, :].astype(F32)
        centred = values - sums(values) * (1.0 / width)
        deviation = lax.rsqrt(sums(centred * centred) * (1.0 / width) + 1e-06)
        xhat = centred * deviation
        upstream = norm_back[where, :]
        scaled = upstream * gain[...]
        feature_grad[where, :] = (
            deviation
            * (scaled - sums(scaled) * (1.0 / width) - xhat * (sums(scaled * xhat) * (1.0 / width)))
        ).astype(BF16)
        return total + jnp.sum((upstream * xhat).reshape(4, 8, width), axis=0)

    total = lax.fori_loop(0, rows // 32, feature_chunk, jnp.zeros((8, width), F32))
    total = jnp.sum(total, axis=0, keepdims=True) * (1.0 / unit.shape[0])
    for at in range(width // LANES):
        gain_term[at : at + 1, :] = total[:, at * LANES : (at + 1) * LANES]

    norm_back[...] = dot(weights_near[:, :rows], unit[...], FIRST)

    def text_chunk(where):
        values = norm_back[where, :] * scale
        own = text[where, :].astype(F32)
        own_inverse = lax.rsqrt(sums(own * own) + 1e-06)
        direction = own * own_inverse
        text_grad[where, :] = (
            (values - direction * sums(direction * values)) * own_inverse
        ).astype(BF16)

    over_rows(rows, 32, text_chunk)


def reduce_body(groups, each, place, *refs):
    packets, terms = refs[:groups], refs[groups : 2 * groups]
    total, ordered = refs[2 * groups :]
    count, full = total.shape

    def chunk(where):
        value = packets[0][where, :].astype(F32)
        for packet in packets[1:]:
            value = value + packet[where, :].astype(F32)
        total[where, :] = value.astype(BF16)

    over_rows(count, BAND, chunk)
    for step in range(groups):
        ordered[place[1] ^ step] = terms[step][...]
    value = ordered[0]
    for group in range(1, groups):
        value = value + ordered[group]
    total[count - BAND :, full - LANES :] = value.astype(BF16)


def finish_body(members, place, *refs):
    packets, (proj_grad, gain_gradient, ordered) = refs[:members], refs[members:]
    count, full = packets[0].shape
    rows, width = proj_grad.shape
    columns = width // members
    rest = columns - full
    per_band = full // rest
    for own in range(members):

        @pl.when(place[0] == own)
        def _():
            for k in range(members):
                base = (own ^ k) * columns
                packet = packets[k]
                main = packet[:rows, :].astype(F32)
                tails = []
                for index in range(rows // BAND):
                    at = rows + (index // per_band) * BAND
                    lane = (index % per_band) * rest
                    tails.append(packet[at : at + BAND, lane : lane + rest].astype(F32))
                proj_grad[:, base : base + full] = main
                proj_grad[:, base + full : base + columns] = jnp.concatenate(tails, axis=0)

    for k in range(members):
        ordered[place[0] ^ k] = packets[k][count - BAND :, full - LANES :].astype(F32)
    value = ordered[0]
    for member in range(1, members):
        value = value + ordered[member]
    for at in range(width // LANES):
        gain_gradient[:, at * LANES : (at + 1) * LANES] = value[at : at + 1, :]


def local_four(features, text, proj, gain, scale, bias):
    members = lax.axis_size("loop")
    groups = lax.axis_size("rep")
    place = jnp.stack([lax.axis_index("loop"), lax.axis_index("rep")]).astype(jnp.int32)
    scalars = jnp.concatenate([scale, bias])
    rows, width = features.shape[0], features.shape[2]
    near, every = 2 * rows, 4 * rows
    columns = width // members
    full = columns // LANES * LANES
    each = width // groups
    bands = -(-(each // BAND) // (full // (columns - full)))
    packet = (each + bands * BAND, full)
    gain_row = gain.reshape(1, width)

    f0, t0 = features[:, 0, :], text[:, 0, :]
    f1 = send(f0, "loop", lambda p: p ^ 1)
    t1 = send(t0, "loop", lambda p: p ^ 1)
    f2 = send(f0, "loop", lambda p: p ^ 2)
    t_after, f2 = lax.optimization_barrier((t0, f2))
    t2 = send(t_after, "loop", lambda p: p ^ 2)
    f3 = send(f2, "loop", lambda p: p ^ 1)
    t3 = send(t2, "loop", lambda p: p ^ 1)

    normed_near, unit_near, inverse_near, text_near = call(
        near_body,
        [((near, width), BF16), ((near, width), BF16), ((near, 1), F32), ((near, width), BF16)],
        [pltpu.VMEM((near, width), F32)],
        flops=2 * near * width * width,
        moved=8 * near * width,
    )(f0, f1, t0, t1, proj, gain_row)

    normed, unit, inverse, weights_near, totals_near = call(
        far_body,
        [((every, width), BF16), ((every, width), BF16), ((every, 1), F32), ((every, near), BF16), ((every, 1), F32)],
        [pltpu.VMEM((near, width), F32), pltpu.VMEM((every, near), F32)],
        smem=1,
        flops=4 * near * width * width,
        moved=16 * near * width,
    )(scalars, f2, f3, proj, gain_row, normed_near, unit_near, inverse_near, text_near)

    outs = call(
        functools.partial(partial_body, members, groups),
        [(packet, BF16)] * groups + [((near, width), BF16), ((rows, every), BF16)],
        [
            pltpu.VMEM((every, every), BF16),
            pltpu.VMEM((every, 1), F32),
            pltpu.VMEM((every, near), F32),
            pltpu.VMEM((every, columns), BF16),
            pltpu.VMEM((every, columns), BF16),
            pltpu.VMEM((every, columns), BF16),
            pltpu.VMEM((groups,) + packet, BF16),
        ],
        smem=2,
        flops=6 * near * width * width,
        moved=16 * near * width,
    )(scalars, place, t2, t3, text_near, unit, inverse, normed, weights_near, totals_near)
    packets, (text_far, weights_own) = outs[:groups], outs[groups:]
    arrived = [packets[0]] + [
        send(packets[step], "rep", lambda p: p ^ step) for step in range(1, groups)
    ]

    feature_grad, text_grad, gain_term = call(
        own_body,
        [((rows, width), BF16), ((rows, width), BF16), ((BAND, LANES), F32)],
        [pltpu.VMEM((rows, width), BF16), pltpu.VMEM((rows, width), F32)],
        smem=1,
        flops=6 * near * width * width,
        moved=16 * near * width,
    )(scalars, f0, t0, proj, gain_row, text_near, text_far, weights_own, weights_near, unit, inverse)
    terms = [gain_term] + [send(gain_term, "rep", lambda p: p ^ step) for step in range(1, groups)]

    (reduced,) = call(
        functools.partial(reduce_body, groups, each),
        [(packet, BF16)],
        [pltpu.VMEM((groups, BAND, LANES), F32)],
        smem=1,
        moved=4 * each * width,
    )(place, *arrived, *terms)
    blocks = [reduced] + [send(reduced, "loop", lambda p: p ^ k) for k in range(1, members)]

    proj_grad, gain_gradient = call(
        functools.partial(finish_body, members),
        [((each, width), F32), ((1, width), F32)],
        [pltpu.VMEM((members, BAND, LANES), F32)],
        smem=1,
        moved=8 * each * width,
    )(place, *blocks)
    return feature_grad[:, None, :], text_grad[:, None, :], proj_grad, gain_gradient.reshape(width)


def four_fits(mesh, rows_shape):
    members, groups = mesh.shape["loop"], mesh.shape["rep"]
    rows, width = rows_shape[0] // members, rows_shape[2]
    if members != 4 or groups & (groups - 1) or width % (members * groups) or width % LANES:
        return False
    columns, each = width // members, width // groups
    full = columns // LANES * LANES
    rest = columns - full
    if rest == 0 or full < LANES or full % rest or each % BAND or rows % 64 or width // LANES > BAND:
        return False
    chunks = each // BAND
    used = (chunks - 1) % (full // rest) + 1
    return used * rest <= full - LANES


def solution(mesh):
    def run(features, text, proj, gain, scale, bias):
        body = local_four if four_fits(mesh, features.shape) else local_any_size
        return jax.shard_map(
            body,
            mesh=mesh,
            in_specs=(P("loop", "rep", None), P("loop", "rep", None), P(), P(), P(), P()),
            out_specs=(P("loop", "rep", None), P("loop", "rep", None), P("rep", None), P()),
            check_vma=False,
        )(features, text, proj, gain, scale, bias)

    return run
```

```python
import functools

import jax
import jax.numpy as jnp
from jax import lax
from jax.experimental import pallas as pl
from jax.experimental.pallas import tpu as pltpu
from jax.sharding import PartitionSpec as P

F32 = jnp.float32
BF16 = jnp.bfloat16
LAST = (((1,), (1,)), ((), ()))
FIRST = (((0,), (0,)), ((), ()))


def dot(a, b, dims=(((1,), (0,)), ((), ()))):
    return lax.dot_general(a, b, dims, preferred_element_type=F32)


def unit_rows(values):
    inverse = lax.rsqrt(jnp.sum(values * values, axis=-1, keepdims=True) + 1e-06)
    return values * inverse, inverse


def standardize(rows):
    values = rows.astype(F32)
    centred = values - jnp.mean(values, axis=-1, keepdims=True)
    inverse = lax.rsqrt(jnp.mean(centred * centred, axis=-1, keepdims=True) + 1e-06)
    return centred * inverse, inverse


def send(value, axis, target):
    count = lax.axis_size(axis)
    return lax.ppermute(value, axis, [(p, target(p)) for p in range(count)])


def gather_group(value, count):
    mine = [value]
    for step in range(1, count // 2):
        mine.append(send(value, "loop", lambda p: (p + 2 * step) % count))
    mates = [send(block, "loop", lambda p: p ^ 1) for block in mine]
    return mine + mates


def local_any_size(features, text, proj, gain, scale, bias):
    n = lax.axis_size("loop")
    m = lax.axis_size("rep")
    me = lax.axis_index("loop")
    half = n // 2
    rows, width = features.shape[0], features.shape[2]
    columns = proj.shape[1] // n
    group_rows = rows * n
    logit_scale, logit_bias = scale[0], bias[0]

    own_features = features[:, 0, :]
    own_text = text[:, 0, :]
    text_blocks = gather_group(own_text, n)
    feature_blocks = gather_group(own_features, n)

    xhat, deviation = standardize(own_features)
    normed = (xhat * gain).astype(BF16)
    img_dir, img_inv = unit_rows(dot(normed, proj))
    img_unit = img_dir.astype(BF16)

    txt_dir, txt_inv = unit_rows(own_text.astype(F32))
    own_txt_unit = txt_dir.astype(BF16)
    txt_unit = jnp.concatenate(
        [own_txt_unit] + [unit_rows(block.astype(F32))[0].astype(BF16) for block in text_blocks[1:]]
    )
    row_ids = lax.broadcasted_iota(jnp.int32, (rows, group_rows), 0)
    column_ids = lax.broadcasted_iota(jnp.int32, (rows, group_rows), 1)
    diagonal = (row_ids == column_ids).astype(F32)

    def weights(left, right):
        logits = logit_scale * dot(left, right, LAST) + logit_bias
        return (jax.nn.sigmoid(logits) - diagonal).astype(BF16)

    img_back = logit_scale * dot(weights(img_unit, txt_unit), txt_unit)
    proj_back = (
        (img_back - img_dir * jnp.sum(img_dir * img_back, axis=-1, keepdims=True)) * img_inv
    ).astype(BF16)

    blocks = jnp.transpose(proj_back.reshape(rows, n, columns), (1, 0, 2))
    blocks = lax.all_to_all(blocks, "loop", 0, 0, tiled=True)
    back_columns = blocks.reshape(group_rows, columns)

    norm_back = dot(proj_back, proj, LAST)
    scaled = norm_back * gain
    feature_grad = (
        deviation
        * (
            scaled
            - jnp.mean(scaled, axis=-1, keepdims=True)
            - xhat * jnp.mean(scaled * xhat, axis=-1, keepdims=True)
        )
    ).astype(BF16)
    gain_term = jnp.sum(norm_back * xhat, axis=0) * (1.0 / group_rows)

    other_normed = [(standardize(block)[0] * gain).astype(BF16) for block in feature_blocks[1:]]
    relative = jnp.stack([normed] + other_normed)
    member = jnp.arange(n)
    same_core = (member % 2) == (me % 2)
    chips_back = ((me // 2 - member // 2) % half)
    position = jnp.where(same_core, chips_back, half + chips_back)
    group_normed = relative[position].reshape(group_rows, width)

    partial = (dot(group_normed, back_columns, FIRST) * (1.0 / group_rows)).astype(BF16)
    pieces = lax.all_to_all(partial.reshape(m, width // m, columns), "rep", 0, 0, tiled=True)
    reduced = jnp.sum(pieces.astype(F32), axis=0).astype(BF16)
    gains = lax.all_gather(gain_term, "rep")
    gain_sum = jnp.sum(gains, axis=0)
    proj_rows = lax.all_gather(reduced, "loop")
    proj_grad = jnp.transpose(proj_rows, (1, 0, 2)).reshape(width // m, n * columns).astype(F32)
    gain_gradient = jnp.sum(lax.all_gather(gain_sum, "loop"), axis=0)

    group_unit = jnp.concatenate(
        [img_unit] + [unit_rows(dot(block, proj))[0].astype(BF16) for block in other_normed]
    )
    text_weights = weights(own_txt_unit, group_unit)
    txt_back = logit_scale * dot(text_weights, group_unit)
    text_grad = (
        (txt_back - txt_dir * jnp.sum(txt_dir * txt_back, axis=-1, keepdims=True)) * txt_inv
    ).astype(BF16)
    return feature_grad[:, None, :], text_grad[:, None, :], proj_grad, gain_gradient


VMEM = pl.BlockSpec(memory_space=pltpu.VMEM)
SMEM = pl.BlockSpec(memory_space=pltpu.SMEM)
LANES = 128
BAND = 16


def call(body, outs, scratch=(), smem=0, flops=0, moved=0):
    def run(*operands):
        specs = [SMEM] * smem + [VMEM] * (len(operands) - smem)
        return pl.pallas_call(
            body,
            out_shape=[jax.ShapeDtypeStruct(shape, kind) for shape, kind in outs],
            in_specs=specs,
            out_specs=[VMEM] * len(outs),
            scratch_shapes=list(scratch),
            compiler_params=pltpu.CompilerParams(vmem_limit_bytes=36 * 2**20),
            cost_estimate=pl.CostEstimate(flops=flops, bytes_accessed=moved, transcendentals=0),
        )(*operands)

    return run


def over_rows(count, step, body):
    def turn(index, _):
        body(pl.ds(pl.multiple_of(index * step, step), step))
        return 0

    lax.fori_loop(0, count // step, turn, 0, unroll=2)


def sums(values):
    return jnp.sum(values, axis=-1, keepdims=True)


def normalize_into(source, gain, target, at):
    rows, width = source.shape

    def chunk(where):
        values = source[where, :].astype(F32)
        centred = values - sums(values) * (1.0 / width)
        inverse = lax.rsqrt(sums(centred * centred) * (1.0 / width) + 1e-06)
        target[pl.ds(at + where.start, where.size), :] = (centred * inverse * gain[...]).astype(BF16)

    over_rows(rows, 32, chunk)


def unit_into(source, target, at, inverses=None):
    rows = source.shape[0]

    def chunk(where):
        values = source[where, :].astype(F32)
        inverse = lax.rsqrt(sums(values * values) + 1e-06)
        place = pl.ds(at + where.start, where.size)
        target[place, :] = (values * inverse).astype(BF16)
        if inverses is not None:
            inverses[place, :] = inverse

    over_rows(rows, 32, chunk)


def weigh(dots, scale, bias, first_column, weights, columns_at, totals, add_to):
    rows, columns = dots.shape

    def chunk(where):
        product = dots[where, :]
        logits = scale * product + bias
        weight = 1.0 / (1.0 + jnp.exp(-logits))
        row = where.start + lax.broadcasted_iota(jnp.int32, product.shape, 0)
        column = first_column + lax.broadcasted_iota(jnp.int32, product.shape, 1)
        weight = jnp.where(row == column, weight - 1.0, weight).astype(BF16)
        weights[where, columns_at : columns_at + columns] = weight
        total = sums(weight.astype(F32) * product)
        totals[where, :] = total if add_to is None else add_to[where, :] + total

    over_rows(rows, 64, chunk)


def near_body(f0, f1, t0, t1, proj, gain, normed, unit, inverse, text_unit, projected):
    rows = f0.shape[0]
    for k, source in enumerate((f0, f1)):
        normalize_into(source, gain, normed, k * rows)
    for k, source in enumerate((t0, t1)):
        unit_into(source, text_unit, k * rows)
    projected[...] = dot(normed[...], proj[...])
    unit_into(projected, unit, 0, inverse)


def far_body(
    scalars, place, f2, f3, proj, gain, normed_near, unit_near, inverse_near, text_near,
    normed, unit, inverse, weights, totals, proj_columns, projected, dots,
):
    rows = f2.shape[0]
    near = 2 * rows
    members, columns = proj.shape[1] // proj_columns.shape[1], proj_columns.shape[1]
    for member in range(members):

        @pl.when(place[0] == member)
        def _():
            proj_columns[...] = proj[:, member * columns : (member + 1) * columns]

    normed[:near, :] = normed_near[...]
    unit[:near, :] = unit_near[...]
    inverse[:near, :] = inverse_near[...]
    for k, source in enumerate((f2, f3)):
        normalize_into(source, gain, normed, near + k * rows)
    projected[...] = dot(normed[near:, :], proj[...])
    unit_into(projected, unit, near, inverse)
    dots[...] = dot(unit[...], text_near[...], LAST)
    weigh(dots, scalars[0], scalars[1], 0, weights, 0, totals, None)


def pack_into(target, block, full):
    rows, columns = block.shape
    rest = columns - full
    target[:rows, :] = block[:, :full].astype(BF16)
    per_band = full // rest
    tail = block[:, full:]
    chunks = [tail[at : at + BAND, :] for at in range(0, rows, BAND)]
    for band in range(0, len(chunks), per_band):
        part = chunks[band : band + per_band]
        if len(part) < per_band:
            part.append(jnp.zeros((BAND, full - rest * len(part)), block.dtype))
        at = rows + (band // per_band) * BAND
        target[at : at + BAND, :] = jnp.concatenate(part, axis=1).astype(BF16)


def partial_body(
    members, groups, lead, scalars, place, t2, t3, text_near, unit, inverse, normed, weights_near, totals_near,
    proj_columns, gain, *refs,
):
    across, keep_lead, keep_tail, *refs = refs
    along, refs = refs[: groups // 2 - 1], refs[groups // 2 - 1 :]
    text_far, weights_own, weights, totals, dots, text_columns, unit_columns, back, packed = refs
    rows = t2.shape[0]
    near = 2 * rows
    every = members * rows
    width = unit.shape[1]
    columns = width // members
    count, full = packed.shape[1:]
    scale, bias = scalars[0], scalars[1]
    for k, source in enumerate((t2, t3)):
        unit_into(source, text_far, k * rows)
    dots[...] = dot(unit[...], text_far[...], LAST)
    weights[:, :near] = weights_near[...]
    weigh(dots, scale, bias, near, weights, near, totals, totals_near)
    weights_own[...] = weights[:rows, :]
    for member in range(members):

        @pl.when(place[0] == member)
        def _():
            where = slice(member * columns, (member + 1) * columns)
            text_columns[:near, :] = text_near[:, where]
            text_columns[near:, :] = text_far[:, where]
            unit_columns[...] = unit[:, where]

    image_back = dot(weights[...], text_columns[...])
    back[...] = (
        (image_back - unit_columns[...].astype(F32) * totals[...]) * (inverse[...] * scale)
    ).astype(BF16)
    each = width // groups
    product = dot(normed[...], back[...], FIRST) * (1.0 / every)
    for group in range(groups):
        pack_into(packed.at[group], product[group * each : (group + 1) * each, :], full)

    terms = product * proj_columns[...].astype(F32)
    folded = jnp.concatenate([terms[:, full:], jnp.zeros((width, full + LANES - columns), F32)], axis=1)
    for at in range(0, full, LANES):
        folded = folded + terms[:, at : at + LANES]
    high = folded.astype(BF16)
    low = (folded - high.astype(F32)).astype(BF16)
    ones = jnp.ones((BAND, 2 * LANES), BF16)
    gain_row = dot(ones, jnp.concatenate([high, low], axis=1), LAST)[:1, :] / gain[...]
    pieces = [gain_row[:, at : at + LANES] for at in range(0, width, LANES)]
    pieces.append(jnp.zeros((BAND - len(pieces), LANES), F32))
    gain_tile = jnp.concatenate(pieces, axis=0).astype(BF16)
    for group in range(groups):
        packed[group, count - BAND :, full - LANES :] = gain_tile

    own = place[1]
    for step in range(groups // 2):
        across[step] = packed[own ^ 1 ^ (2 * step), :lead, :]
        keep_lead[step] = packed[own ^ (2 * step), :lead, :]
    for other in range(2):
        keep_tail[other] = packed[own ^ other, lead:, :]
        for step in range(1, groups // 2):
            along[step - 1][other] = packed[own ^ (2 * step) ^ other, lead:, :]


def image_body(
    scalars, features, proj, gain, text_near, text_far, weights_own, unit, inverse,
    feature_grad, back, product,
):
    rows, width = features.shape
    near = 2 * rows
    scale = scalars[0]
    product[...] = dot(weights_own[:, :near], text_near[...]) + dot(weights_own[:, near:], text_far[...])

    def image_chunk(where):
        values = product[where, :] * scale
        direction = unit[where, :].astype(F32)
        back[where, :] = (
            (values - direction * sums(direction * values)) * inverse[where, :]
        ).astype(BF16)

    over_rows(rows, 32, image_chunk)
    product[...] = dot(back[...], proj[...], LAST)

    def feature_chunk(where):
        values = features[where, :].astype(F32)
        centred = values - sums(values) * (1.0 / width)
        deviation = lax.rsqrt(sums(centred * centred) * (1.0 / width) + 1e-06)
        xhat = centred * deviation
        scaled = product[where, :] * gain[...]
        feature_grad[where, :] = (
            deviation
            * (scaled - sums(scaled) * (1.0 / width) - xhat * (sums(scaled * xhat) * (1.0 / width)))
        ).astype(BF16)

    over_rows(rows, 32, feature_chunk)


def text_body(scalars, text, weights_near, unit, text_grad, product):
    rows = text.shape[0]
    scale = scalars[0]
    product[...] = dot(weights_near[:, :rows], unit[...], FIRST)

    def text_chunk(where):
        values = product[where, :] * scale
        own = text[where, :].astype(F32)
        own_inverse = lax.rsqrt(sums(own * own) + 1e-06)
        direction = own * own_inverse
        text_grad[where, :] = (
            (values - direction * sums(direction * values)) * own_inverse
        ).astype(BF16)

    over_rows(rows, 32, text_chunk)


def first_sum_body(place, keep_lead, across, keep_tail, *refs):
    steps = keep_lead.shape[0]
    along, refs = refs[: steps - 1], refs[steps - 1 :]
    leads, (tail, tail_across, ordered) = refs[:steps], refs[steps:]
    for step in range(steps):
        leads[step][...] = (keep_lead[step].astype(F32) + across[step].astype(F32)).astype(BF16)
    own = place[1] // 2
    ordered[own] = keep_tail[...]
    for step in range(1, steps):
        ordered[own ^ step] = along[step - 1][...]
    value = ordered[0].astype(F32)
    for step in range(1, steps):
        value = value + ordered[step].astype(F32)
    tail[...] = value[0].astype(BF16)
    tail_across[...] = value[1].astype(BF16)


def last_sum_body(tail, tail_across, *refs):
    leads, total = refs[:-1], refs[-1]
    split = leads[0].shape[0]
    value = leads[0][...].astype(F32)
    for lead in leads[1:]:
        value = value + lead[...].astype(F32)
    total[:split, :] = value.astype(BF16)
    total[split:, :] = (tail[...].astype(F32) + tail_across[...].astype(F32)).astype(BF16)


def finish_body(members, place, *refs):
    packets, (proj_grad, gain_gradient, ordered) = refs[:members], refs[members:]
    count, full = packets[0].shape
    rows, width = proj_grad.shape
    columns = width // members
    rest = columns - full
    per_band = full // rest
    for own in range(members):

        @pl.when(place[0] == own)
        def _():
            for k in range(members):
                base = (own ^ k) * columns
                packet = packets[k]
                main = packet[:rows, :].astype(F32)
                tails = []
                for index in range(rows // BAND):
                    at = rows + (index // per_band) * BAND
                    lane = (index % per_band) * rest
                    tails.append(packet[at : at + BAND, lane : lane + rest].astype(F32))
                proj_grad[:, base : base + full] = main
                proj_grad[:, base + full : base + columns] = jnp.concatenate(tails, axis=0)

    for k in range(members):
        ordered[place[0] ^ k] = packets[k][count - BAND :, full - LANES :].astype(F32)
    value = ordered[0]
    for member in range(1, members):
        value = value + ordered[member]
    for at in range(width // LANES):
        gain_gradient[:, at * LANES : (at + 1) * LANES] = value[at : at + 1, :]


def local_four(features, text, proj, gain, scale, bias):
    members = lax.axis_size("loop")
    groups = lax.axis_size("rep")
    place = jnp.stack([lax.axis_index("loop"), lax.axis_index("rep")]).astype(jnp.int32)
    scalars = jnp.concatenate([scale, bias])
    rows, width = features.shape[0], features.shape[2]
    near, every = 2 * rows, 4 * rows
    columns = width // members
    full = columns // LANES * LANES
    each = width // groups
    bands = -(-(each // BAND) // (full // (columns - full)))
    packet = (each + bands * BAND, full)
    gain_row = gain.reshape(1, width)

    lead = (2 * packet[0] // BAND // 3) * BAND
    tail = packet[0] - lead
    steps = groups // 2

    f0, t0 = features[:, 0, :], text[:, 0, :]
    f2 = send(f0, "loop", lambda p: p ^ 2)
    f1 = send(f0, "loop", lambda p: p ^ 1)
    t1 = send(t0, "loop", lambda p: p ^ 1)

    normed_near, unit_near, inverse_near, text_near = call(
        near_body,
        [((near, width), BF16), ((near, width), BF16), ((near, 1), F32), ((near, width), BF16)],
        [pltpu.VMEM((near, width), F32)],
        flops=2 * near * width * width,
        moved=8 * near * width,
    )(f0, f1, t0, t1, proj, gain_row)

    t_after, f2, normed_near, unit_near, inverse_near, text_near = lax.optimization_barrier(
        (t0, f2, normed_near, unit_near, inverse_near, text_near)
    )
    t2 = send(t_after, "loop", lambda p: p ^ 2)
    f3 = send(f2, "loop", lambda p: p ^ 1)

    normed, unit, inverse, weights_near, totals_near, proj_columns = call(
        far_body,
        [
            ((every, width), BF16), ((every, width), BF16), ((every, 1), F32),
            ((every, near), BF16), ((every, 1), F32), ((width, columns), BF16),
        ],
        [pltpu.VMEM((near, width), F32), pltpu.VMEM((every, near), F32)],
        smem=2,
        flops=4 * near * width * width,
        moved=16 * near * width,
    )(scalars, place, f2, f3, proj, gain_row, normed_near, unit_near, inverse_near, text_near)

    t2, normed, unit, inverse, weights_near, totals_near, proj_columns = lax.optimization_barrier(
        (t2, normed, unit, inverse, weights_near, totals_near, proj_columns)
    )
    t3 = send(t2, "loop", lambda p: p ^ 1)

    outs = call(
        functools.partial(partial_body, members, groups, lead),
        [((steps, lead, full), BF16), ((steps, lead, full), BF16), ((2, tail, full), BF16)]
        + [((2, tail, full), BF16)] * (steps - 1)
        + [((near, width), BF16), ((rows, every), BF16)],
        [
            pltpu.VMEM((every, every), BF16),
            pltpu.VMEM((every, 1), F32),
            pltpu.VMEM((every, near), F32),
            pltpu.VMEM((every, columns), BF16),
            pltpu.VMEM((every, columns), BF16),
            pltpu.VMEM((every, columns), BF16),
            pltpu.VMEM((groups,) + packet, BF16),
        ],
        smem=2,
        flops=6 * near * width * width,
        moved=16 * near * width,
    )(
        scalars, place, t2, t3, text_near, unit, inverse, normed, weights_near, totals_near,
        proj_columns, gain_row,
    )
    across, keep_lead, keep_tail = outs[:3]
    along, (text_far, weights_own) = outs[3 : 2 + steps], outs[2 + steps :]

    along = [send(along[step - 1], "rep", lambda p: p ^ (2 * step)) for step in range(1, steps)]
    across = send(across, "rep", lambda p: p ^ 1)

    (feature_grad,) = call(
        image_body,
        [((rows, width), BF16)],
        [pltpu.VMEM((rows, width), BF16), pltpu.VMEM((rows, width), F32)],
        smem=1,
        flops=4 * near * width * width,
        moved=12 * near * width,
    )(scalars, f0, proj, gain_row, text_near, text_far, weights_own, unit, inverse)
    feature_grad, across = lax.optimization_barrier((feature_grad, across))

    outs = call(
        first_sum_body,
        [((lead, full), BF16)] * steps + [((tail, full), BF16)] * 2,
        [pltpu.VMEM((steps, 2, tail, full), BF16)],
        smem=1,
        moved=4 * each * width,
    )(place, keep_lead, across, keep_tail, *along)
    leads = [outs[0]] + [send(outs[step], "rep", lambda p: p ^ (2 * step)) for step in range(1, steps)]
    tail_across = send(outs[steps + 1], "rep", lambda p: p ^ 1)

    (text_grad,) = call(
        text_body,
        [((rows, width), BF16)],
        [pltpu.VMEM((rows, width), F32)],
        smem=1,
        flops=2 * near * width * width,
        moved=6 * near * width,
    )(scalars, t0, weights_near, unit)
    text_grad, tail_across = lax.optimization_barrier((text_grad, tail_across))

    (reduced,) = call(
        last_sum_body,
        [(packet, BF16)],
        moved=4 * each * width,
    )(outs[steps], tail_across, *leads)
    blocks = [reduced] + [send(reduced, "loop", lambda p: p ^ k) for k in range(1, members)]

    proj_grad, gain_gradient = call(
        functools.partial(finish_body, members),
        [((each, width), F32), ((1, width), F32)],
        [pltpu.VMEM((members, BAND, LANES), F32)],
        smem=1,
        moved=8 * each * width,
    )(place, *blocks)
    return feature_grad[:, None, :], text_grad[:, None, :], proj_grad, gain_gradient.reshape(width)


def four_fits(mesh, rows_shape):
    members, groups = mesh.shape["loop"], mesh.shape["rep"]
    rows, width = rows_shape[0] // members, rows_shape[2]
    if members != 4 or groups & (groups - 1) or width % (members * groups) or width % LANES:
        return False
    columns, each = width // members, width // groups
    full = columns // LANES * LANES
    rest = columns - full
    if rest == 0 or full < LANES or full % rest or each % BAND or rows % 64 or width // LANES > BAND:
        return False
    chunks = each // BAND
    used = (chunks - 1) % (full // rest) + 1
    return used * rest <= full - LANES


def solution(mesh):
    def run(features, text, proj, gain, scale, bias):
        body = local_four if four_fits(mesh, features.shape) else local_any_size
        return jax.shard_map(
            body,
            mesh=mesh,
            in_specs=(P("loop", "rep", None), P("loop", "rep", None), P(), P(), P(), P()),
            out_specs=(P("loop", "rep", None), P("loop", "rep", None), P("rep", None), P()),
            check_vma=False,
        )(features, text, proj, gain, scale, bias)

    return run
```

```python
import functools

import jax
import jax.numpy as jnp
from jax import lax
from jax.experimental import pallas as pl
from jax.experimental.pallas import tpu as pltpu
from jax.sharding import PartitionSpec as P

F32 = jnp.float32
BF16 = jnp.bfloat16
LAST = (((1,), (1,)), ((), ()))
FIRST = (((0,), (0,)), ((), ()))


def dot(a, b, dims=(((1,), (0,)), ((), ()))):
    return lax.dot_general(a, b, dims, preferred_element_type=F32)


def unit_rows(values):
    inverse = lax.rsqrt(jnp.sum(values * values, axis=-1, keepdims=True) + 1e-06)
    return values * inverse, inverse


def standardize(rows):
    values = rows.astype(F32)
    centred = values - jnp.mean(values, axis=-1, keepdims=True)
    inverse = lax.rsqrt(jnp.mean(centred * centred, axis=-1, keepdims=True) + 1e-06)
    return centred * inverse, inverse


def send(value, axis, target):
    count = lax.axis_size(axis)
    return lax.ppermute(value, axis, [(p, target(p)) for p in range(count)])


def gather_group(value, count):
    mine = [value]
    for step in range(1, count // 2):
        mine.append(send(value, "loop", lambda p: (p + 2 * step) % count))
    mates = [send(block, "loop", lambda p: p ^ 1) for block in mine]
    return mine + mates


def local_any_size(features, text, proj, gain, scale, bias):
    n = lax.axis_size("loop")
    m = lax.axis_size("rep")
    me = lax.axis_index("loop")
    half = n // 2
    rows, width = features.shape[0], features.shape[2]
    columns = proj.shape[1] // n
    group_rows = rows * n
    logit_scale, logit_bias = scale[0], bias[0]

    own_features = features[:, 0, :]
    own_text = text[:, 0, :]
    text_blocks = gather_group(own_text, n)
    feature_blocks = gather_group(own_features, n)

    xhat, deviation = standardize(own_features)
    normed = (xhat * gain).astype(BF16)
    img_dir, img_inv = unit_rows(dot(normed, proj))
    img_unit = img_dir.astype(BF16)

    txt_dir, txt_inv = unit_rows(own_text.astype(F32))
    own_txt_unit = txt_dir.astype(BF16)
    txt_unit = jnp.concatenate(
        [own_txt_unit] + [unit_rows(block.astype(F32))[0].astype(BF16) for block in text_blocks[1:]]
    )
    row_ids = lax.broadcasted_iota(jnp.int32, (rows, group_rows), 0)
    column_ids = lax.broadcasted_iota(jnp.int32, (rows, group_rows), 1)
    diagonal = (row_ids == column_ids).astype(F32)

    def weights(left, right):
        logits = logit_scale * dot(left, right, LAST) + logit_bias
        return (jax.nn.sigmoid(logits) - diagonal).astype(BF16)

    img_back = logit_scale * dot(weights(img_unit, txt_unit), txt_unit)
    proj_back = (
        (img_back - img_dir * jnp.sum(img_dir * img_back, axis=-1, keepdims=True)) * img_inv
    ).astype(BF16)

    blocks = jnp.transpose(proj_back.reshape(rows, n, columns), (1, 0, 2))
    blocks = lax.all_to_all(blocks, "loop", 0, 0, tiled=True)
    back_columns = blocks.reshape(group_rows, columns)

    norm_back = dot(proj_back, proj, LAST)
    scaled = norm_back * gain
    feature_grad = (
        deviation
        * (
            scaled
            - jnp.mean(scaled, axis=-1, keepdims=True)
            - xhat * jnp.mean(scaled * xhat, axis=-1, keepdims=True)
        )
    ).astype(BF16)
    gain_term = jnp.sum(norm_back * xhat, axis=0) * (1.0 / group_rows)

    other_normed = [(standardize(block)[0] * gain).astype(BF16) for block in feature_blocks[1:]]
    relative = jnp.stack([normed] + other_normed)
    member = jnp.arange(n)
    same_core = (member % 2) == (me % 2)
    chips_back = ((me // 2 - member // 2) % half)
    position = jnp.where(same_core, chips_back, half + chips_back)
    group_normed = relative[position].reshape(group_rows, width)

    partial = (dot(group_normed, back_columns, FIRST) * (1.0 / group_rows)).astype(BF16)
    pieces = lax.all_to_all(partial.reshape(m, width // m, columns), "rep", 0, 0, tiled=True)
    reduced = jnp.sum(pieces.astype(F32), axis=0).astype(BF16)
    gains = lax.all_gather(gain_term, "rep")
    gain_sum = jnp.sum(gains, axis=0)
    proj_rows = lax.all_gather(reduced, "loop")
    proj_grad = jnp.transpose(proj_rows, (1, 0, 2)).reshape(width // m, n * columns).astype(F32)
    gain_gradient = jnp.sum(lax.all_gather(gain_sum, "loop"), axis=0)

    group_unit = jnp.concatenate(
        [img_unit] + [unit_rows(dot(block, proj))[0].astype(BF16) for block in other_normed]
    )
    text_weights = weights(own_txt_unit, group_unit)
    txt_back = logit_scale * dot(text_weights, group_unit)
    text_grad = (
        (txt_back - txt_dir * jnp.sum(txt_dir * txt_back, axis=-1, keepdims=True)) * txt_inv
    ).astype(BF16)
    return feature_grad[:, None, :], text_grad[:, None, :], proj_grad, gain_gradient


VMEM = pl.BlockSpec(memory_space=pltpu.VMEM)
SMEM = pl.BlockSpec(memory_space=pltpu.SMEM)
ANYWHERE = pl.BlockSpec(memory_space=pl.ANY)
LANES = 128
BAND = 16


def call(body, outs, scratch=(), smem=0, flops=0, moved=0):
    def run(*operands):
        specs = [SMEM] * smem + [VMEM] * (len(operands) - smem)
        return pl.pallas_call(
            body,
            out_shape=[jax.ShapeDtypeStruct(shape, kind) for shape, kind in outs],
            in_specs=specs,
            out_specs=[VMEM] * len(outs),
            scratch_shapes=list(scratch),
            compiler_params=pltpu.CompilerParams(vmem_limit_bytes=24 * 2**20),
            cost_estimate=pl.CostEstimate(flops=flops, bytes_accessed=moved, transcendentals=0),
        )(*operands)

    return run


def call_moving(body, outs, scratch, copies, smem=0, flops=0, moved=0):
    def run(*operands):
        specs = [SMEM] * smem + [ANYWHERE] * (len(operands) - smem)
        return pl.pallas_call(
            body,
            out_shape=[jax.ShapeDtypeStruct(shape, kind) for shape, kind in outs],
            in_specs=specs,
            out_specs=[ANYWHERE] * len(outs),
            scratch_shapes=list(scratch) + [pltpu.SemaphoreType.DMA((copies,))],
            compiler_params=pltpu.CompilerParams(vmem_limit_bytes=56 * 2**20),
            cost_estimate=pl.CostEstimate(flops=flops, bytes_accessed=moved, transcendentals=0),
        )(*operands)

    return run


class Mover:
    def __init__(self, semaphores):
        self.semaphores, self.used = semaphores, 0

    def __call__(self, source, target):
        copy = pltpu.make_async_copy(source, target, self.semaphores.at[self.used])
        self.used += 1
        copy.start()
        return copy


def wait_all(*copies):
    for copy in copies:
        copy.wait()


def over_rows(count, step, body):
    def turn(index, _):
        body(pl.ds(pl.multiple_of(index * step, step), step))
        return 0

    lax.fori_loop(0, count // step, turn, 0, unroll=min(4, count // step))


def sums(values):
    return jnp.sum(values, axis=-1, keepdims=True)


def normalize_into(source, gain, target, at):
    rows, width = source.shape

    def chunk(where):
        values = source[where, :].astype(F32)
        centred = values - sums(values) * (1.0 / width)
        inverse = lax.rsqrt(sums(centred * centred) * (1.0 / width) + 1e-06)
        target[pl.ds(at + where.start, where.size), :] = (centred * inverse * gain[...]).astype(BF16)

    over_rows(rows, 32, chunk)


def unit_into(source, target, at, inverses=None):
    rows = source.shape[0]

    def chunk(where):
        values = source[where, :].astype(F32)
        inverse = lax.rsqrt(sums(values * values) + 1e-06)
        place = pl.ds(at + where.start, where.size)
        target[place, :] = (values * inverse).astype(BF16)
        if inverses is not None:
            inverses[place, :] = inverse

    over_rows(rows, 32, chunk)


def weigh(dots, scale, bias, diagonal, weights, totals, add_to=None):
    def chunk(where):
        product = dots[where, :]
        weight = 1.0 / (1.0 + jnp.exp(-(scale * product + bias)))
        if diagonal is not None:
            row = where.start + lax.broadcasted_iota(jnp.int32, product.shape, 0)
            column = diagonal + lax.broadcasted_iota(jnp.int32, product.shape, 1)
            weight = jnp.where(row == column, weight - 1.0, weight)
        weight = weight.astype(BF16)
        weights[where, :] = weight
        total = sums(weight.astype(F32) * product)
        totals[where, :] = total if add_to is None else add_to[where, :] + total

    over_rows(dots.shape[0], 64, chunk)


def take_columns(place, source, target):
    columns = target.shape[1]
    for member in range(source.shape[1] // columns):

        @pl.when(place[0] == member)
        def _():
            target[...] = source[:, member * columns : (member + 1) * columns]


def near_body(
    scalars, place, f0, f1, t0, t1, proj, gain,
    normed, normed_turned, unit, unit_columns, inverse, text_unit, text_columns, weights, totals, proj_columns,
    f0_v, f1_v, t0_v, t1_v, proj_v, gain_v, normed_v, turned_v, unit_v, unit_columns_v, inverse_v, text_v,
    text_columns_v, weights_v, totals_v, proj_columns_v, projected, dots, semaphores,
):
    move = Mover(semaphores)
    rows = f0.shape[0]
    gain_in, f0_in, f1_in = move(gain, gain_v), move(f0, f0_v), move(f1, f1_v)
    proj_in, t0_in, t1_in = move(proj, proj_v), move(t0, t0_v), move(t1, t1_v)
    wait_all(gain_in, f0_in)
    normalize_into(f0_v, gain_v, normed_v, 0)
    f1_in.wait()
    normalize_into(f1_v, gain_v, normed_v, rows)
    out = [move(normed_v, normed)]
    proj_in.wait()
    projected[...] = dot(normed_v[...], proj_v[...])
    t0_in.wait()
    unit_into(t0_v, text_v, 0)
    t1_in.wait()
    unit_into(t1_v, text_v, rows)
    out.append(move(text_v, text_unit))
    unit_into(projected, unit_v, 0, inverse_v)
    out += [move(unit_v, unit), move(inverse_v, inverse)]
    dots[...] = dot(unit_v[...], text_v[...], LAST)
    weigh(dots, scalars[0], scalars[1], 0, weights_v, totals_v)
    out += [move(weights_v, weights), move(totals_v, totals)]
    take_columns(place, unit_v, unit_columns_v)
    take_columns(place, text_v, text_columns_v)
    take_columns(place, proj_v, proj_columns_v)
    out += [move(unit_columns_v, unit_columns), move(text_columns_v, text_columns)]
    out += [move(proj_columns_v, proj_columns)]
    turned_v[...] = normed_v[...].T
    out.append(move(turned_v, normed_turned))
    wait_all(*out)


def far_body(
    scalars, place, f2, f3, proj, gain, text_near,
    normed_turned, unit, unit_columns, inverse, weights, totals,
    f2_v, f3_v, proj_v, gain_v, text_v, normed_v, turned_v, unit_v, unit_columns_v, inverse_v, weights_v, totals_v,
    projected, dots, semaphores,
):
    move = Mover(semaphores)
    rows = f2.shape[0]
    gain_in, f2_in, f3_in = move(gain, gain_v), move(f2, f2_v), move(f3, f3_v)
    proj_in, text_in = move(proj, proj_v), move(text_near, text_v)
    wait_all(gain_in, f2_in)
    normalize_into(f2_v, gain_v, normed_v, 0)
    f3_in.wait()
    normalize_into(f3_v, gain_v, normed_v, rows)
    proj_in.wait()
    projected[...] = dot(normed_v[...], proj_v[...])
    unit_into(projected, unit_v, 0, inverse_v)
    out = [move(unit_v, unit), move(inverse_v, inverse)]
    text_in.wait()
    dots[...] = dot(unit_v[...], text_v[...], LAST)
    weigh(dots, scalars[0], scalars[1], None, weights_v, totals_v)
    out += [move(weights_v, weights), move(totals_v, totals)]
    take_columns(place, unit_v, unit_columns_v)
    out.append(move(unit_columns_v, unit_columns))
    turned_v[...] = normed_v[...].T
    out.append(move(turned_v, normed_turned))
    wait_all(*out)


def third_body(
    scalars, place, t2, unit_near, unit_far, weights_near, weights_far, totals_near, totals_far, text_columns_near,
    text_unit, weights_own, image_back, totals,
    t2_v, unit_v, weights_near_v, totals_v, text_columns_v, text_v, weights_v, back_v, dots, semaphores,
):
    move = Mover(semaphores)
    rows = t2.shape[0]
    near = 2 * rows
    t2_in = move(t2, t2_v)
    unit_in = [move(unit_near, unit_v.at[:near]), move(unit_far, unit_v.at[near:])]
    totals_in = [move(totals_near, totals_v.at[:near]), move(totals_far, totals_v.at[near:])]
    rest_in = [
        move(weights_near, weights_near_v.at[:near]),
        move(weights_far, weights_near_v.at[near:]),
        move(text_columns_near, text_columns_v.at[:near]),
    ]
    t2_in.wait()
    unit_into(t2_v, text_v, 0)
    out = [move(text_v, text_unit)]
    take_columns(place, text_v, text_columns_v.at[near : near + rows])
    wait_all(*unit_in)
    dots[...] = dot(unit_v[...], text_v[...], LAST)
    wait_all(*totals_in)
    weigh(dots, scalars[0], scalars[1], near, weights_v, totals_v, totals_v)
    out += [move(totals_v, totals), move(weights_v.at[:rows], weights_own)]
    wait_all(*rest_in)
    back_v[...] = dot(weights_near_v[...], text_columns_v[:near, :]) + dot(weights_v[...], text_columns_v[near:, :])
    out.append(move(back_v, image_back))
    wait_all(*out)


def pack_into(target, block, full):
    rows, columns = block.shape
    rest = columns - full
    target[:rows, :] = block[:, :full].astype(BF16)
    per_band = full // rest
    tail = block[:, full:]
    chunks = [tail[at : at + BAND, :] for at in range(0, rows, BAND)]
    for band in range(0, len(chunks), per_band):
        part = chunks[band : band + per_band]
        if len(part) < per_band:
            part.append(jnp.zeros((BAND, full - rest * len(part)), block.dtype))
        at = rows + (band // per_band) * BAND
        target[at : at + BAND, :] = jnp.concatenate(part, axis=1).astype(BF16)


def partial_body(
    members, groups, lead, scalars, place, t3, unit_near, unit_far, totals, image_back, unit_columns_near,
    unit_columns_far, inverse_near, inverse_far, turned_near, turned_far, proj_columns, gain, *refs,
):
    (across, keep_lead, keep_tail), refs = refs[:3], refs[3:]
    along, refs = refs[: groups // 2 - 1], refs[groups // 2 - 1 :]
    text_unit, weights_own, *refs = refs
    outs = [across, keep_lead, keep_tail, *along]
    outs_v, refs = refs[: len(outs)], refs[len(outs) :]
    (
        t3_v, unit_v, totals_v, back_v, unit_columns_v, inverse_v, turned_v, proj_columns_v, gain_v,
        text_v, text_columns, weights, dots, back, packed, semaphores,
    ) = refs
    across, keep_lead, keep_tail, *along = outs_v
    move = Mover(semaphores)
    rows = t3.shape[0]
    near = 2 * rows
    every = members * rows
    width = unit_near.shape[1]
    columns = width // members
    count, full = packed.shape[1:]
    scale, bias = scalars[0], scalars[1]
    t3_in = move(t3, t3_v)
    unit_in = [move(unit_near, unit_v.at[:near]), move(unit_far, unit_v.at[near:])]
    totals_in = move(totals, totals_v)
    back_in = [
        move(image_back, back_v),
        move(unit_columns_near, unit_columns_v.at[:near]),
        move(unit_columns_far, unit_columns_v.at[near:]),
        move(inverse_near, inverse_v.at[:near]),
        move(inverse_far, inverse_v.at[near:]),
    ]
    turned_in = [move(turned_near, turned_v.at[:, :near]), move(turned_far, turned_v.at[:, near:])]
    gain_in = [move(proj_columns, proj_columns_v), move(gain, gain_v)]
    t3_in.wait()
    unit_into(t3_v, text_v, 0)
    moved_out = [move(text_v, text_unit)]
    take_columns(place, text_v, text_columns)
    wait_all(*unit_in)
    dots[...] = dot(unit_v[...], text_v[...], LAST)
    totals_in.wait()
    weigh(dots, scale, bias, near + rows, weights, totals_v, totals_v)
    moved_out.append(move(weights.at[:rows], weights_own))
    wait_all(*back_in)
    image_back = back_v[...] + dot(weights[...], text_columns[...])
    back[...] = (
        (image_back - unit_columns_v[...].astype(F32) * totals_v[...]) * (inverse_v[...] * scale)
    ).astype(BF16)
    wait_all(*turned_in)
    each = width // groups
    product = dot(turned_v[...], back[...]) * (1.0 / every)
    for group in range(groups):
        pack_into(packed.at[group], product[group * each : (group + 1) * each, :], full)

    wait_all(*gain_in)
    terms = product * proj_columns_v[...].astype(F32)
    folded = jnp.concatenate([terms[:, full:], jnp.zeros((width, full + LANES - columns), F32)], axis=1)
    for at in range(0, full, LANES):
        folded = folded + terms[:, at : at + LANES]
    high = folded.astype(BF16)
    low = (folded - high.astype(F32)).astype(BF16)
    ones = jnp.ones((BAND, 2 * LANES), BF16)
    gain_row = dot(ones, jnp.concatenate([high, low], axis=1), LAST)[:1, :] / gain_v[...]
    pieces = [gain_row[:, at : at + LANES] for at in range(0, width, LANES)]
    pieces.append(jnp.zeros((BAND - len(pieces), LANES), F32))
    gain_tile = jnp.concatenate(pieces, axis=0).astype(BF16)
    for group in range(groups):
        packed[group, count - BAND :, full - LANES :] = gain_tile

    own = place[1]
    for step in range(groups // 2):
        across[step] = packed[own ^ 1 ^ (2 * step), :lead, :]
        keep_lead[step] = packed[own ^ (2 * step), :lead, :]
    for other in range(2):
        keep_tail[other] = packed[own ^ other, lead:, :]
        for step in range(1, groups // 2):
            along[step - 1][other] = packed[own ^ (2 * step) ^ other, lead:, :]
    moved_out += [move(source, target) for source, target in zip(outs_v, outs)]
    wait_all(*moved_out)


def image_body(
    scalars, features, proj, gain, text_near, text_third, text_fourth, weights_near, weights_third, weights_fourth,
    unit, inverse, feature_grad,
    features_v, proj_v, gain_v, text_v, weights_near_v, weights_third_v, weights_fourth_v, unit_v, inverse_v,
    grad_v, back, product, semaphores,
):
    move = Mover(semaphores)
    rows, width = features.shape
    near = 2 * rows
    scale = scalars[0]
    weights_in = [
        move(weights_near.at[:rows], weights_near_v),
        move(weights_third, weights_third_v),
        move(weights_fourth, weights_fourth_v),
    ]
    text_in = [
        move(text_near, text_v.at[:near]),
        move(text_third, text_v.at[near : near + rows]),
        move(text_fourth, text_v.at[near + rows :]),
    ]
    unit_in = [move(unit.at[:rows], unit_v), move(inverse.at[:rows], inverse_v)]
    proj_in = move(proj, proj_v)
    rest_in = [move(features, features_v), move(gain, gain_v)]
    wait_all(*weights_in, *text_in)
    product[...] = (
        dot(weights_near_v[...], text_v[:near, :])
        + dot(weights_third_v[...], text_v[near : near + rows, :])
        + dot(weights_fourth_v[...], text_v[near + rows :, :])
    )
    wait_all(*unit_in)

    def image_chunk(where):
        values = product[where, :] * scale
        direction = unit_v[where, :].astype(F32)
        back[where, :] = (
            (values - direction * sums(direction * values)) * inverse_v[where, :]
        ).astype(BF16)

    over_rows(rows, 32, image_chunk)
    proj_in.wait()
    product[...] = dot(back[...], proj_v[...], LAST)
    wait_all(*rest_in)

    def feature_chunk(where):
        values = features_v[where, :].astype(F32)
        centred = values - sums(values) * (1.0 / width)
        deviation = lax.rsqrt(sums(centred * centred) * (1.0 / width) + 1e-06)
        xhat = centred * deviation
        scaled = product[where, :] * gain_v[...]
        grad_v[where, :] = (
            deviation
            * (scaled - sums(scaled) * (1.0 / width) - xhat * (sums(scaled * xhat) * (1.0 / width)))
        ).astype(BF16)

    over_rows(rows, 32, feature_chunk)
    move(grad_v, feature_grad).wait()


def text_body(
    scalars, text, weights_near, weights_far, unit_near, unit_far, text_grad,
    text_v, weights_near_v, weights_far_v, unit_near_v, unit_far_v, grad_v, product, semaphores,
):
    move = Mover(semaphores)
    rows = text.shape[0]
    scale = scalars[0]
    copies = [
        move(weights_near, weights_near_v),
        move(unit_near, unit_near_v),
        move(weights_far, weights_far_v),
        move(unit_far, unit_far_v),
        move(text, text_v),
    ]
    wait_all(*copies)
    product[...] = dot(weights_near_v[:, :rows], unit_near_v[...], FIRST) + dot(
        weights_far_v[:, :rows], unit_far_v[...], FIRST
    )

    def text_chunk(where):
        values = product[where, :] * scale
        own = text_v[where, :].astype(F32)
        own_inverse = lax.rsqrt(sums(own * own) + 1e-06)
        direction = own * own_inverse
        grad_v[where, :] = (
            (values - direction * sums(direction * values)) * own_inverse
        ).astype(BF16)

    over_rows(rows, 32, text_chunk)
    move(grad_v, text_grad).wait()


def first_sum_body(place, keep_lead, across, keep_tail, *refs):
    steps = keep_lead.shape[0]
    along, refs = refs[: steps - 1], refs[steps - 1 :]
    leads, (tail, tail_across, ordered) = refs[:steps], refs[steps:]
    for step in range(steps):
        leads[step][...] = (keep_lead[step].astype(F32) + across[step].astype(F32)).astype(BF16)
    own = place[1] // 2
    ordered[own] = keep_tail[...]
    for step in range(1, steps):
        ordered[own ^ step] = along[step - 1][...]
    value = ordered[0].astype(F32)
    for step in range(1, steps):
        value = value + ordered[step].astype(F32)
    tail[...] = value[0].astype(BF16)
    tail_across[...] = value[1].astype(BF16)


def last_sum_body(tail, tail_across, *refs):
    leads, total = refs[:-1], refs[-1]
    split = leads[0].shape[0]
    value = leads[0][...].astype(F32)
    for lead in leads[1:]:
        value = value + lead[...].astype(F32)
    total[:split, :] = value.astype(BF16)
    total[split:, :] = (tail[...].astype(F32) + tail_across[...].astype(F32)).astype(BF16)


def finish_body(members, place, *refs):
    packets, (proj_grad, gain_gradient, ordered) = refs[:members], refs[members:]
    count, full = packets[0].shape
    rows, width = proj_grad.shape
    columns = width // members
    rest = columns - full
    per_band = full // rest
    for own in range(members):

        @pl.when(place[0] == own)
        def _():
            for k in range(members):
                base = (own ^ k) * columns
                packet = packets[k]
                main = packet[:rows, :].astype(F32)
                tails = []
                for index in range(rows // BAND):
                    at = rows + (index // per_band) * BAND
                    lane = (index % per_band) * rest
                    tails.append(packet[at : at + BAND, lane : lane + rest].astype(F32))
                proj_grad[:, base : base + full] = main
                proj_grad[:, base + full : base + columns] = jnp.concatenate(tails, axis=0)

    for k in range(members):
        ordered[place[0] ^ k] = packets[k][count - BAND :, full - LANES :].astype(F32)
    value = ordered[0]
    for member in range(1, members):
        value = value + ordered[member]
    for at in range(width // LANES):
        gain_gradient[:, at * LANES : (at + 1) * LANES] = value[at : at + 1, :]


def local_four(features, text, proj, gain, scale, bias):
    members = lax.axis_size("loop")
    groups = lax.axis_size("rep")
    place = jnp.stack([lax.axis_index("loop"), lax.axis_index("rep")]).astype(jnp.int32)
    scalars = jnp.concatenate([scale, bias])
    rows, width = features.shape[0], features.shape[2]
    near, every = 2 * rows, 4 * rows
    columns = width // members
    full = columns // LANES * LANES
    each = width // groups
    bands = -(-(each // BAND) // (full // (columns - full)))
    packet = (each + bands * BAND, full)
    gain_row = gain.reshape(1, width)

    lead = (2 * packet[0] // BAND // 3) * BAND
    tail = packet[0] - lead
    steps = groups // 2

    f0, t0 = features[:, 0, :], text[:, 0, :]
    f2 = send(f0, "loop", lambda p: p ^ 2)
    f1 = send(f0, "loop", lambda p: p ^ 1)
    t1 = send(t0, "loop", lambda p: p ^ 1)

    wide, half, one = ((near, width), BF16), ((rows, width), BF16), ((near, 1), F32)
    square, part, turned = ((near, near), BF16), ((near, columns), BF16), ((width, near), BF16)
    proj_kind, gain_kind = ((width, width), BF16), ((1, width), F32)

    def room(*kinds):
        return [pltpu.VMEM(shape, kind) for shape, kind in kinds]

    outs = [wide, turned, wide, part, one, wide, part, square, one, ((width, columns), BF16)]
    (
        normed_near, turned_near, unit_near, unit_columns_near, inverse_near, text_near, text_columns_near,
        weights_near, totals_near, proj_columns,
    ) = call_moving(
        near_body,
        outs,
        room(half, half, half, half, proj_kind, gain_kind, *outs, ((near, width), F32), ((near, near), F32)),
        16,
        smem=2,
        flops=3 * near * width * width,
        moved=8 * near * width,
    )(scalars, place, f0, f1, t0, t1, proj, gain_row)

    t_after, f2, text_near = lax.optimization_barrier((t0, f2, text_near))
    t2 = send(t_after, "loop", lambda p: p ^ 2)
    f3 = send(f2, "loop", lambda p: p ^ 1)

    outs = [turned, wide, part, one, square, one]
    turned_far, unit_far, unit_columns_far, inverse_far, weights_far, totals_far = call_moving(
        far_body,
        outs,
        room(half, half, proj_kind, gain_kind, wide, wide, *outs, ((near, width), F32), ((near, near), F32)),
        11,
        smem=2,
        flops=3 * near * width * width,
        moved=8 * near * width,
    )(scalars, place, f2, f3, proj, gain_row, text_near)

    t2, weights_far = lax.optimization_barrier((t2, weights_far))
    t3 = send(t2, "loop", lambda p: p ^ 1)

    narrow = ((every, rows), BF16)
    outs = [half, ((rows, rows), BF16), ((every, columns), F32), ((every, 1), F32)]
    text_third, weights_third, image_back, totals = call_moving(
        third_body,
        outs,
        room(
            half, ((every, width), BF16), ((every, near), BF16), ((every, 1), F32), ((near + rows, columns), BF16),
            half, narrow, ((every, columns), F32), ((every, rows), F32),
        ),
        12,
        smem=2,
        flops=2 * near * width * width,
        moved=8 * near * width,
    )(
        scalars, place, t2, unit_near, unit_far, weights_near, weights_far, totals_near, totals_far,
        text_columns_near,
    )
    t3, totals = lax.optimization_barrier((t3, totals))

    shared = [((steps, lead, full), BF16), ((steps, lead, full), BF16)] + [((2, tail, full), BF16)] * steps
    outs = call_moving(
        functools.partial(partial_body, members, groups, lead),
        shared + [half, ((rows, rows), BF16)],
        room(
            *shared,
            half, ((every, width), BF16), ((every, 1), F32), ((every, columns), F32), ((every, columns), BF16),
            ((every, 1), F32), ((width, every), BF16), ((width, columns), BF16), gain_kind,
            half, ((rows, columns), BF16), narrow, ((every, rows), F32), ((every, columns), BF16),
            ((groups,) + packet, BF16),
        ),
        15 + len(shared),
        smem=2,
        flops=4 * near * width * width,
        moved=16 * near * width,
    )(
        scalars, place, t3, unit_near, unit_far, totals, image_back, unit_columns_near, unit_columns_far,
        inverse_near, inverse_far, turned_near, turned_far, proj_columns, gain_row,
    )
    across, keep_lead, keep_tail = outs[:3]
    along, (text_fourth, weights_fourth) = outs[3 : 2 + steps], outs[2 + steps :]

    along = [send(along[step - 1], "rep", lambda p: p ^ (2 * step)) for step in range(1, steps)]
    across = send(across, "rep", lambda p: p ^ 1)

    (feature_grad,) = call_moving(
        image_body,
        [half],
        room(
            half, proj_kind, gain_kind, ((every, width), BF16), ((rows, near), BF16), ((rows, rows), BF16),
            ((rows, rows), BF16), half, ((rows, 1), F32), half, half, ((rows, width), F32),
        ),
        12,
        smem=1,
        flops=4 * near * width * width,
        moved=12 * near * width,
    )(
        scalars, f0, proj, gain_row, text_near, text_third, text_fourth, weights_near, weights_third,
        weights_fourth, unit_near, inverse_near,
    )
    feature_grad, across = lax.optimization_barrier((feature_grad, across))

    outs = call(
        first_sum_body,
        [((lead, full), BF16)] * steps + [((tail, full), BF16)] * 2,
        [pltpu.VMEM((steps, 2, tail, full), BF16)],
        smem=1,
        moved=4 * each * width,
    )(place, keep_lead, across, keep_tail, *along)
    leads = [outs[0]] + [send(outs[step], "rep", lambda p: p ^ (2 * step)) for step in range(1, steps)]
    tail_across = send(outs[steps + 1], "rep", lambda p: p ^ 1)

    (reduced,) = call(
        last_sum_body,
        [(packet, BF16)],
        moved=4 * each * width,
    )(outs[steps], tail_across, *leads)
    blocks = [reduced] + [send(reduced, "loop", lambda p: p ^ k) for k in range(1, members)]
    t0, _ = lax.optimization_barrier((t0, reduced))
    (text_grad,) = call_moving(
        text_body,
        [half],
        room(half, square, square, wide, wide, half, ((rows, width), F32)),
        6,
        smem=1,
        flops=2 * near * width * width,
        moved=6 * near * width,
    )(scalars, t0, weights_near, weights_far, unit_near, unit_far)
    text_grad, *blocks[1:] = lax.optimization_barrier((text_grad, *blocks[1:]))

    proj_grad, gain_gradient = call(
        functools.partial(finish_body, members),
        [((each, width), F32), ((1, width), F32)],
        [pltpu.VMEM((members, BAND, LANES), F32)],
        smem=1,
        moved=8 * each * width,
    )(place, *blocks)
    return feature_grad[:, None, :], text_grad[:, None, :], proj_grad, gain_gradient.reshape(width)


def four_fits(mesh, rows_shape):
    members, groups = mesh.shape["loop"], mesh.shape["rep"]
    rows, width = rows_shape[0] // members, rows_shape[2]
    if members != 4 or groups & (groups - 1) or width % (members * groups) or width % LANES:
        return False
    columns, each = width // members, width // groups
    full = columns // LANES * LANES
    rest = columns - full
    if rest == 0 or full < LANES or full % rest or each % BAND or rows % 64 or width // LANES > BAND:
        return False
    chunks = each // BAND
    used = (chunks - 1) % (full // rest) + 1
    return used * rest <= full - LANES


def solution(mesh):
    def run(features, text, proj, gain, scale, bias):
        body = local_four if four_fits(mesh, features.shape) else local_any_size
        return jax.shard_map(
            body,
            mesh=mesh,
            in_specs=(P("loop", "rep", None), P("loop", "rep", None), P(), P(), P(), P()),
            out_specs=(P("loop", "rep", None), P("loop", "rep", None), P("rep", None), P()),
            check_vma=False,
        )(features, text, proj, gain, scale, bias)

    return run
```

```python
import functools

import jax
import jax.numpy as jnp
from jax import lax
from jax.experimental import pallas as pl
from jax.experimental.pallas import tpu as pltpu
from jax.sharding import PartitionSpec as P

F32 = jnp.float32
BF16 = jnp.bfloat16
LAST = (((1,), (1,)), ((), ()))
FIRST = (((0,), (0,)), ((), ()))


def dot(a, b, dims=(((1,), (0,)), ((), ()))):
    return lax.dot_general(a, b, dims, preferred_element_type=F32)


def unit_rows(values):
    inverse = lax.rsqrt(jnp.sum(values * values, axis=-1, keepdims=True) + 1e-06)
    return values * inverse, inverse


def standardize(rows):
    values = rows.astype(F32)
    centred = values - jnp.mean(values, axis=-1, keepdims=True)
    inverse = lax.rsqrt(jnp.mean(centred * centred, axis=-1, keepdims=True) + 1e-06)
    return centred * inverse, inverse


def send(value, axis, target):
    count = lax.axis_size(axis)
    return lax.ppermute(value, axis, [(p, target(p)) for p in range(count)])


def gather_group(value, count):
    mine = [value]
    for step in range(1, count // 2):
        mine.append(send(value, "loop", lambda p: (p + 2 * step) % count))
    mates = [send(block, "loop", lambda p: p ^ 1) for block in mine]
    return mine + mates


def local_any_size(features, text, proj, gain, scale, bias):
    n = lax.axis_size("loop")
    m = lax.axis_size("rep")
    me = lax.axis_index("loop")
    half = n // 2
    rows, width = features.shape[0], features.shape[2]
    columns = proj.shape[1] // n
    group_rows = rows * n
    logit_scale, logit_bias = scale[0], bias[0]

    own_features = features[:, 0, :]
    own_text = text[:, 0, :]
    text_blocks = gather_group(own_text, n)
    feature_blocks = gather_group(own_features, n)

    xhat, deviation = standardize(own_features)
    normed = (xhat * gain).astype(BF16)
    img_dir, img_inv = unit_rows(dot(normed, proj))
    img_unit = img_dir.astype(BF16)

    txt_dir, txt_inv = unit_rows(own_text.astype(F32))
    own_txt_unit = txt_dir.astype(BF16)
    txt_unit = jnp.concatenate(
        [own_txt_unit] + [unit_rows(block.astype(F32))[0].astype(BF16) for block in text_blocks[1:]]
    )
    row_ids = lax.broadcasted_iota(jnp.int32, (rows, group_rows), 0)
    column_ids = lax.broadcasted_iota(jnp.int32, (rows, group_rows), 1)
    diagonal = (row_ids == column_ids).astype(F32)

    def weights(left, right):
        logits = logit_scale * dot(left, right, LAST) + logit_bias
        return (jax.nn.sigmoid(logits) - diagonal).astype(BF16)

    img_back = logit_scale * dot(weights(img_unit, txt_unit), txt_unit)
    proj_back = (
        (img_back - img_dir * jnp.sum(img_dir * img_back, axis=-1, keepdims=True)) * img_inv
    ).astype(BF16)

    blocks = jnp.transpose(proj_back.reshape(rows, n, columns), (1, 0, 2))
    blocks = lax.all_to_all(blocks, "loop", 0, 0, tiled=True)
    back_columns = blocks.reshape(group_rows, columns)

    norm_back = dot(proj_back, proj, LAST)
    scaled = norm_back * gain
    feature_grad = (
        deviation
        * (
            scaled
            - jnp.mean(scaled, axis=-1, keepdims=True)
            - xhat * jnp.mean(scaled * xhat, axis=-1, keepdims=True)
        )
    ).astype(BF16)
    gain_term = jnp.sum(norm_back * xhat, axis=0) * (1.0 / group_rows)

    other_normed = [(standardize(block)[0] * gain).astype(BF16) for block in feature_blocks[1:]]
    relative = jnp.stack([normed] + other_normed)
    member = jnp.arange(n)
    same_core = (member % 2) == (me % 2)
    chips_back = ((me // 2 - member // 2) % half)
    position = jnp.where(same_core, chips_back, half + chips_back)
    group_normed = relative[position].reshape(group_rows, width)

    partial = (dot(group_normed, back_columns, FIRST) * (1.0 / group_rows)).astype(BF16)
    pieces = lax.all_to_all(partial.reshape(m, width // m, columns), "rep", 0, 0, tiled=True)
    reduced = jnp.sum(pieces.astype(F32), axis=0).astype(BF16)
    gains = lax.all_gather(gain_term, "rep")
    gain_sum = jnp.sum(gains, axis=0)
    proj_rows = lax.all_gather(reduced, "loop")
    proj_grad = jnp.transpose(proj_rows, (1, 0, 2)).reshape(width // m, n * columns).astype(F32)
    gain_gradient = jnp.sum(lax.all_gather(gain_sum, "loop"), axis=0)

    group_unit = jnp.concatenate(
        [img_unit] + [unit_rows(dot(block, proj))[0].astype(BF16) for block in other_normed]
    )
    text_weights = weights(own_txt_unit, group_unit)
    txt_back = logit_scale * dot(text_weights, group_unit)
    text_grad = (
        (txt_back - txt_dir * jnp.sum(txt_dir * txt_back, axis=-1, keepdims=True)) * txt_inv
    ).astype(BF16)
    return feature_grad[:, None, :], text_grad[:, None, :], proj_grad, gain_gradient


VMEM = pl.BlockSpec(memory_space=pltpu.VMEM)
SMEM = pl.BlockSpec(memory_space=pltpu.SMEM)
LANES = 128
BAND = 16
TOKEN = ((8, LANES), F32)


def call(body, outs, scratch=(), smem=0, flops=0, moved=0):
    def run(*operands):
        specs = [SMEM] * smem + [VMEM] * (len(operands) - smem)
        return pl.pallas_call(
            body,
            out_shape=[jax.ShapeDtypeStruct(shape, kind) for shape, kind in outs],
            in_specs=specs,
            out_specs=[VMEM] * len(outs),
            scratch_shapes=[pltpu.VMEM(shape, kind) for shape, kind in scratch],
            compiler_params=pltpu.CompilerParams(vmem_limit_bytes=24 * 2**20),
            cost_estimate=pl.CostEstimate(flops=flops, bytes_accessed=moved, transcendentals=0),
        )(*operands)

    return run


def over_rows(count, step, body):
    def turn(index, _):
        body(pl.ds(pl.multiple_of(index * step, step), step))
        return 0

    lax.fori_loop(0, count // step, turn, 0, unroll=min(4, count // step))


def sums(values):
    return jnp.sum(values, axis=-1, keepdims=True)


def normalize_into(source, gain, target, at):
    rows, width = source.shape

    def chunk(where):
        values = source[where, :].astype(F32)
        centred = values - sums(values) * (1.0 / width)
        inverse = lax.rsqrt(sums(centred * centred) * (1.0 / width) + 1e-06)
        target[pl.ds(at + where.start, where.size), :] = (centred * inverse * gain[...]).astype(BF16)

    over_rows(rows, 32, chunk)


def unit_into(source, target, at, inverses=None):
    rows = source.shape[0]

    def chunk(where):
        values = source[where, :].astype(F32)
        inverse = lax.rsqrt(sums(values * values) + 1e-06)
        place = pl.ds(at + where.start, where.size)
        target[place, :] = (values * inverse).astype(BF16)
        if inverses is not None:
            inverses[place, :] = inverse

    over_rows(rows, 32, chunk)


def weigh(dots, scale, bias, diagonal, weights, totals, add_to=None):
    rows, columns = dots.shape

    def part(first, count, with_pairs):
        def chunk(where):
            where = pl.ds(first + where.start, where.size)
            product = dots[where, :]
            weight = jnp.tanh((0.5 * scale) * product + 0.5 * bias)
            offset = 0.5
            if with_pairs:
                row = where.start - diagonal + lax.broadcasted_iota(jnp.int32, product.shape, 0)
                column = lax.broadcasted_iota(jnp.int32, product.shape, 1)
                offset = jnp.where(row == column, -0.5, 0.5)
            weight = (0.5 * weight + offset).astype(BF16)
            weights[where, :] = weight
            total = sums(weight.astype(F32) * product)
            totals[where, :] = total if add_to is None else add_to[where, :] + total

        over_rows(count, 32, chunk)

    if diagonal is None:
        part(0, rows, False)
        return
    if diagonal:
        part(0, diagonal, False)
    part(diagonal, columns, True)
    if diagonal + columns < rows:
        part(diagonal + columns, rows - diagonal - columns, False)


def take_columns(place, source, target):
    columns = target.shape[1]
    for member in range(source.shape[1] // columns):

        @pl.when(place[0] == member)
        def _():
            target[...] = source[:, member * columns : (member + 1) * columns]


def near_body(
    scalars, place, f0, f1, t0, t1, proj, gain,
    normed_turned, unit, unit_columns, inverse, text_unit, text_columns, weights, totals, proj_columns, token,
    normed, projected, dots,
):
    rows = f0.shape[0]
    normalize_into(f0, gain, normed, 0)
    normalize_into(f1, gain, normed, rows)
    projected[...] = dot(normed[...], proj[...])
    unit_into(t0, text_unit, 0)
    unit_into(t1, text_unit, rows)
    unit_into(projected, unit, 0, inverse)
    dots[...] = dot(unit[...], text_unit[...], LAST)
    weigh(dots, scalars[0], scalars[1], 0, weights, totals)
    take_columns(place, unit, unit_columns)
    take_columns(place, text_unit, text_columns)
    take_columns(place, proj, proj_columns)
    normed_turned[...] = normed[...].T
    token[...] = jnp.zeros_like(token)


def far_body(
    scalars, place, f2, f3, proj, gain, text_near, before,
    normed_turned, unit, unit_columns, inverse, weights, totals, token,
    normed, projected, dots,
):
    rows = f2.shape[0]
    normalize_into(f2, gain, normed, 0)
    normalize_into(f3, gain, normed, rows)
    projected[...] = dot(normed[...], proj[...])
    unit_into(projected, unit, 0, inverse)
    dots[...] = dot(unit[...], text_near[...], LAST)
    weigh(dots, scalars[0], scalars[1], None, weights, totals)
    take_columns(place, unit, unit_columns)
    normed_turned[...] = normed[...].T
    token[...] = jnp.zeros_like(token)


def third_body(
    scalars, place, t2, unit_near, unit_far, weights_near, weights_far, totals_near, totals_far, text_columns_near, before,
    text_unit, weights_own, image_back, totals,
    text_columns, weights, dots,
):
    rows = t2.shape[0]
    near = 2 * rows
    unit_into(t2, text_unit, 0)
    take_columns(place, text_unit, text_columns)
    dots[:near, :] = dot(unit_near[...], text_unit[...], LAST)
    dots[near:, :] = dot(unit_far[...], text_unit[...], LAST)
    totals[:near, :] = totals_near[...]
    totals[near:, :] = totals_far[...]
    weigh(dots, scalars[0], scalars[1], near, weights, totals, totals)
    weights_own[...] = weights[:rows, :]
    for at, earlier in ((0, weights_near), (near, weights_far)):
        image_back[at : at + near, :] = dot(earlier[...], text_columns_near[...]) + dot(
            weights[at : at + near, :], text_columns[...]
        )


def pack_into(target, block, full):
    rows, columns = block.shape
    rest = columns - full
    target[:rows, :] = block[:, :full].astype(BF16)
    per_band = full // rest
    tail = block[:, full:]
    chunks = [tail[at : at + BAND, :] for at in range(0, rows, BAND)]
    for band in range(0, len(chunks), per_band):
        part = chunks[band : band + per_band]
        if len(part) < per_band:
            part.append(jnp.zeros((BAND, full - rest * len(part)), block.dtype))
        at = rows + (band // per_band) * BAND
        target[at : at + BAND, :] = jnp.concatenate(part, axis=1).astype(BF16)


def partial_body(
    members, groups, lead, scalars, place, t3, unit_near, unit_far, totals, image_back, unit_columns_near,
    unit_columns_far, inverse_near, inverse_far, turned_near, turned_far, proj_columns, gain, *refs,
):
    (across, keep_lead, keep_tail), refs = refs[:3], refs[3:]
    along, refs = refs[: groups // 2 - 1], refs[groups // 2 - 1 :]
    text_unit, weights_own, text_columns, weights, dots, all_totals, back, packed = refs
    rows = t3.shape[0]
    near = 2 * rows
    every = members * rows
    width = unit_near.shape[1]
    columns = width // members
    count, full = packed.shape[1:]
    scale, bias = scalars[0], scalars[1]
    unit_into(t3, text_unit, 0)
    take_columns(place, text_unit, text_columns)
    dots[:near, :] = dot(unit_near[...], text_unit[...], LAST)
    dots[near:, :] = dot(unit_far[...], text_unit[...], LAST)
    weigh(dots, scale, bias, near + rows, weights, all_totals, totals)
    weights_own[...] = weights[:rows, :]
    for at, unit_columns, inverse in ((0, unit_columns_near, inverse_near), (near, unit_columns_far, inverse_far)):
        where = slice(at, at + near)
        whole = image_back[where, :] + dot(weights[where, :], text_columns[...])
        back[where, :] = (
            (whole - unit_columns[...].astype(F32) * all_totals[where, :]) * (inverse[...] * scale)
        ).astype(BF16)
    each = width // groups
    product = (dot(turned_near[...], back[:near, :]) + dot(turned_far[...], back[near:, :])) * (1.0 / every)
    for group in range(groups):
        pack_into(packed.at[group], product[group * each : (group + 1) * each, :], full)

    terms = product * proj_columns[...].astype(F32)
    folded = jnp.concatenate([terms[:, full:], jnp.zeros((width, full + LANES - columns), F32)], axis=1)
    for at in range(0, full, LANES):
        folded = folded + terms[:, at : at + LANES]
    high = folded.astype(BF16)
    low = (folded - high.astype(F32)).astype(BF16)
    ones = jnp.ones((BAND, 2 * LANES), BF16)
    gain_row = dot(ones, jnp.concatenate([high, low], axis=1), LAST)[:1, :] / gain[...]
    pieces = [gain_row[:, at : at + LANES] for at in range(0, width, LANES)]
    pieces.append(jnp.zeros((BAND - len(pieces), LANES), F32))
    gain_tile = jnp.concatenate(pieces, axis=0).astype(BF16)
    for group in range(groups):
        packed[group, count - BAND :, full - LANES :] = gain_tile

    own = place[1]
    for step in range(groups // 2):
        across[step] = packed[own ^ 1 ^ (2 * step), :lead, :]
        keep_lead[step] = packed[own ^ (2 * step), :lead, :]
    for other in range(2):
        keep_tail[other] = packed[own ^ other, lead:, :]
        for step in range(1, groups // 2):
            along[step - 1][other] = packed[own ^ (2 * step) ^ other, lead:, :]


def image_body(
    scalars, features, proj, gain, text_near, text_third, text_fourth, weights_near, weights_third, weights_fourth,
    unit, inverse, feature_grad, token, back, product,
):
    rows, width = features.shape
    scale = scalars[0]
    product[...] = (
        dot(weights_near[:rows, :], text_near[...])
        + dot(weights_third[...], text_third[...])
        + dot(weights_fourth[...], text_fourth[...])
    )

    def image_chunk(where):
        values = product[where, :] * scale
        direction = unit[where, :].astype(F32)
        back[where, :] = (
            (values - direction * sums(direction * values)) * inverse[where, :]
        ).astype(BF16)

    over_rows(rows, 32, image_chunk)
    product[...] = dot(back[...], proj[...], LAST)

    def feature_chunk(where):
        values = features[where, :].astype(F32)
        centred = values - sums(values) * (1.0 / width)
        deviation = lax.rsqrt(sums(centred * centred) * (1.0 / width) + 1e-06)
        xhat = centred * deviation
        scaled = product[where, :] * gain[...]
        feature_grad[where, :] = (
            deviation
            * (scaled - sums(scaled) * (1.0 / width) - xhat * (sums(scaled * xhat) * (1.0 / width)))
        ).astype(BF16)

    over_rows(rows, 32, feature_chunk)
    token[...] = jnp.zeros_like(token)


def text_body(scalars, text, weights_near, weights_far, unit_near, unit_far, after, text_grad, token, product):
    rows = text.shape[0]
    scale = scalars[0]
    product[...] = dot(weights_near[:, :rows], unit_near[...], FIRST) + dot(
        weights_far[:, :rows], unit_far[...], FIRST
    )

    def text_chunk(where):
        values = product[where, :] * scale
        own = text[where, :].astype(F32)
        own_inverse = lax.rsqrt(sums(own * own) + 1e-06)
        direction = own * own_inverse
        text_grad[where, :] = (
            (values - direction * sums(direction * values)) * own_inverse
        ).astype(BF16)

    over_rows(rows, 32, text_chunk)
    token[...] = after[:8, :LANES].astype(F32) * 0.0


def first_sum_body(place, token, keep_lead, across, keep_tail, *refs):
    steps = keep_lead.shape[0]
    along, refs = refs[: steps - 1], refs[steps - 1 :]
    leads, (tail, tail_across, ordered) = refs[:steps], refs[steps:]
    for step in range(steps):
        leads[step][...] = (keep_lead[step].astype(F32) + across[step].astype(F32)).astype(BF16)
    own = place[1] // 2
    ordered[own] = keep_tail[...]
    for step in range(1, steps):
        ordered[own ^ step] = along[step - 1][...]
    value = ordered[0].astype(F32)
    for step in range(1, steps):
        value = value + ordered[step].astype(F32)
    tail[...] = value[0].astype(BF16)
    tail_across[...] = value[1].astype(BF16)


def last_sum_body(tail, tail_across, *refs):
    leads, total = refs[:-1], refs[-1]
    split = leads[0].shape[0]
    value = leads[0][...].astype(F32)
    for lead in leads[1:]:
        value = value + lead[...].astype(F32)
    total[:split, :] = value.astype(BF16)
    total[split:, :] = (tail[...].astype(F32) + tail_across[...].astype(F32)).astype(BF16)


def finish_body(members, place, token, *refs):
    packets, (proj_grad, gain_gradient, ordered) = refs[:members], refs[members:]
    count, full = packets[0].shape
    rows, width = proj_grad.shape
    columns = width // members
    rest = columns - full
    per_band = full // rest
    for own in range(members):

        @pl.when(place[0] == own)
        def _():
            for k in range(members):
                base = (own ^ k) * columns
                packet = packets[k]
                main = packet[:rows, :].astype(F32)
                tails = []
                for index in range(rows // BAND):
                    at = rows + (index // per_band) * BAND
                    lane = (index % per_band) * rest
                    tails.append(packet[at : at + BAND, lane : lane + rest].astype(F32))
                proj_grad[:, base : base + full] = main
                proj_grad[:, base + full : base + columns] = jnp.concatenate(tails, axis=0)

    for k in range(members):
        ordered[place[0] ^ k] = packets[k][count - BAND :, full - LANES :].astype(F32)
    value = ordered[0]
    for member in range(1, members):
        value = value + ordered[member]
    for at in range(width // LANES):
        gain_gradient[:, at * LANES : (at + 1) * LANES] = value[at : at + 1, :]


def local_four(features, text, proj, gain, scale, bias):
    members = lax.axis_size("loop")
    groups = lax.axis_size("rep")
    place = jnp.stack([lax.axis_index("loop"), lax.axis_index("rep")]).astype(jnp.int32)
    scalars = jnp.concatenate([scale, bias])
    rows, width = features.shape[0], features.shape[2]
    near, every = 2 * rows, 4 * rows
    columns = width // members
    full = columns // LANES * LANES
    each = width // groups
    bands = -(-(each // BAND) // (full // (columns - full)))
    packet = (each + bands * BAND, full)
    gain_row = gain.reshape(1, width)

    lead = (2 * packet[0] // BAND // 3) * BAND
    tail = packet[0] - lead
    steps = groups // 2

    f0, t0 = features[:, 0, :], text[:, 0, :]
    f2 = send(f0, "loop", lambda p: p ^ 2)
    f1 = send(f0, "loop", lambda p: p ^ 1)
    t1 = send(t0, "loop", lambda p: p ^ 1)

    wide, half, one = ((near, width), BF16), ((rows, width), BF16), ((near, 1), F32)
    square, part, turned = ((near, near), BF16), ((near, columns), BF16), ((width, near), BF16)

    outs = [turned, wide, part, one, wide, part, square, one, ((width, columns), BF16), TOKEN]
    (
        turned_near, unit_near, unit_columns_near, inverse_near, text_near, text_columns_near,
        weights_near, totals_near, proj_columns, token,
    ) = call(
        near_body,
        outs,
        [wide, ((near, width), F32), ((near, near), F32)],
        smem=2,
        flops=3 * near * width * width,
        moved=8 * near * width,
    )(scalars, place, f0, f1, t0, t1, proj, gain_row)

    t_after, f2_after, token = lax.optimization_barrier((t0, f2, token))
    t2 = send(t_after, "loop", lambda p: p ^ 2)
    f3 = send(f2_after, "loop", lambda p: p ^ 1)

    turned_far, unit_far, unit_columns_far, inverse_far, weights_far, totals_far, token = call(
        far_body,
        [turned, wide, part, one, square, one, TOKEN],
        [wide, ((near, width), F32), ((near, near), F32)],
        smem=2,
        flops=3 * near * width * width,
        moved=8 * near * width,
    )(scalars, place, f2, f3, proj, gain_row, text_near, token)

    t2_after, token = lax.optimization_barrier((t2, token))
    t3 = send(t2_after, "loop", lambda p: p ^ 1)

    narrow = ((every, rows), BF16)
    text_third, weights_third, image_back, totals = call(
        third_body,
        [half, ((rows, rows), BF16), ((every, columns), F32), ((every, 1), F32)],
        [((rows, columns), BF16), narrow, ((every, rows), F32)],
        smem=2,
        flops=2 * near * width * width,
        moved=8 * near * width,
    )(
        scalars, place, t2, unit_near, unit_far, weights_near, weights_far, totals_near, totals_far,
        text_columns_near, token,
    )

    outs = call(
        functools.partial(partial_body, members, groups, lead),
        [((steps, lead, full), BF16), ((steps, lead, full), BF16)]
        + [((2, tail, full), BF16)] * steps
        + [half, ((rows, rows), BF16)],
        [
            ((rows, columns), BF16), narrow, ((every, rows), F32), ((every, 1), F32), ((every, columns), BF16),
            ((groups,) + packet, BF16),
        ],
        smem=2,
        flops=4 * near * width * width,
        moved=16 * near * width,
    )(
        scalars, place, t3, unit_near, unit_far, totals, image_back, unit_columns_near, unit_columns_far,
        inverse_near, inverse_far, turned_near, turned_far, proj_columns, gain_row,
    )
    across, keep_lead, keep_tail = outs[:3]
    along, (text_fourth, weights_fourth) = outs[3 : 2 + steps], outs[2 + steps :]

    along = [send(along[step - 1], "rep", lambda p: p ^ (2 * step)) for step in range(1, steps)]
    across = send(across, "rep", lambda p: p ^ 1)

    feature_grad, token = call(
        image_body,
        [half, TOKEN],
        [half, ((rows, width), F32)],
        smem=1,
        flops=4 * near * width * width,
        moved=12 * near * width,
    )(
        scalars, f0, proj, gain_row, text_near, text_third, text_fourth, weights_near, weights_third,
        weights_fourth, unit_near, inverse_near,
    )

    outs = call(
        first_sum_body,
        [((lead, full), BF16)] * steps + [((tail, full), BF16)] * 2,
        [((steps, 2, tail, full), BF16)],
        smem=1,
        moved=4 * each * width,
    )(place, token, keep_lead, across, keep_tail, *along)
    leads = [outs[0]] + [send(outs[step], "rep", lambda p: p ^ (2 * step)) for step in range(1, steps)]
    tail_across = send(outs[steps + 1], "rep", lambda p: p ^ 1)

    (reduced,) = call(
        last_sum_body,
        [(packet, BF16)],
        moved=4 * each * width,
    )(outs[steps], tail_across, *leads)
    blocks = [reduced] + [send(reduced, "loop", lambda p: p ^ k) for k in range(1, members)]
    text_grad, token = call(
        text_body,
        [half, TOKEN],
        [((rows, width), F32)],
        smem=1,
        flops=2 * near * width * width,
        moved=6 * near * width,
    )(scalars, t0, weights_near, weights_far, unit_near, unit_far, reduced)

    proj_grad, gain_gradient = call(
        functools.partial(finish_body, members),
        [((each, width), F32), ((1, width), F32)],
        [((members, BAND, LANES), F32)],
        smem=1,
        moved=8 * each * width,
    )(place, token, *blocks)
    return feature_grad[:, None, :], text_grad[:, None, :], proj_grad, gain_gradient.reshape(width)


def four_fits(mesh, rows_shape):
    members, groups = mesh.shape["loop"], mesh.shape["rep"]
    rows, width = rows_shape[0] // members, rows_shape[2]
    if members != 4 or groups & (groups - 1) or width % (members * groups) or width % LANES:
        return False
    columns, each = width // members, width // groups
    full = columns // LANES * LANES
    rest = columns - full
    if rest == 0 or full < LANES or full % rest or each % BAND or rows % 64 or width // LANES > BAND:
        return False
    chunks = each // BAND
    used = (chunks - 1) % (full // rest) + 1
    return used * rest <= full - LANES


def solution(mesh):
    def run(features, text, proj, gain, scale, bias):
        body = local_four if four_fits(mesh, features.shape) else local_any_size
        return jax.shard_map(
            body,
            mesh=mesh,
            in_specs=(P("loop", "rep", None), P("loop", "rep", None), P(), P(), P(), P()),
            out_specs=(P("loop", "rep", None), P("loop", "rep", None), P("rep", None), P()),
            check_vma=False,
        )(features, text, proj, gain, scale, bias)

    return run
```

```python
import functools

import jax
import jax.numpy as jnp
from jax import lax
from jax.experimental import pallas as pl
from jax.experimental.pallas import tpu as pltpu
from jax.sharding import PartitionSpec as P

F32 = jnp.float32
BF16 = jnp.bfloat16
LAST = (((1,), (1,)), ((), ()))
FIRST = (((0,), (0,)), ((), ()))


def dot(a, b, dims=(((1,), (0,)), ((), ()))):
    return lax.dot_general(a, b, dims, preferred_element_type=F32)


def unit_rows(values):
    inverse = lax.rsqrt(jnp.sum(values * values, axis=-1, keepdims=True) + 1e-06)
    return values * inverse, inverse


def standardize(rows):
    values = rows.astype(F32)
    centred = values - jnp.mean(values, axis=-1, keepdims=True)
    inverse = lax.rsqrt(jnp.mean(centred * centred, axis=-1, keepdims=True) + 1e-06)
    return centred * inverse, inverse


def send(value, axis, target):
    count = lax.axis_size(axis)
    return lax.ppermute(value, axis, [(p, target(p)) for p in range(count)])


def gather_group(value, count):
    mine = [value]
    for step in range(1, count // 2):
        mine.append(send(value, "loop", lambda p: (p + 2 * step) % count))
    mates = [send(block, "loop", lambda p: p ^ 1) for block in mine]
    return mine + mates


def local_any_size(features, text, proj, gain, scale, bias):
    n = lax.axis_size("loop")
    m = lax.axis_size("rep")
    me = lax.axis_index("loop")
    half = n // 2
    rows, width = features.shape[0], features.shape[2]
    columns = proj.shape[1] // n
    group_rows = rows * n
    logit_scale, logit_bias = scale[0], bias[0]

    own_features = features[:, 0, :]
    own_text = text[:, 0, :]
    text_blocks = gather_group(own_text, n)
    feature_blocks = gather_group(own_features, n)

    xhat, deviation = standardize(own_features)
    normed = (xhat * gain).astype(BF16)
    img_dir, img_inv = unit_rows(dot(normed, proj))
    img_unit = img_dir.astype(BF16)

    txt_dir, txt_inv = unit_rows(own_text.astype(F32))
    own_txt_unit = txt_dir.astype(BF16)
    txt_unit = jnp.concatenate(
        [own_txt_unit] + [unit_rows(block.astype(F32))[0].astype(BF16) for block in text_blocks[1:]]
    )
    row_ids = lax.broadcasted_iota(jnp.int32, (rows, group_rows), 0)
    column_ids = lax.broadcasted_iota(jnp.int32, (rows, group_rows), 1)
    diagonal = (row_ids == column_ids).astype(F32)

    def weights(left, right):
        logits = logit_scale * dot(left, right, LAST) + logit_bias
        return (jax.nn.sigmoid(logits) - diagonal).astype(BF16)

    img_back = logit_scale * dot(weights(img_unit, txt_unit), txt_unit)
    proj_back = (
        (img_back - img_dir * jnp.sum(img_dir * img_back, axis=-1, keepdims=True)) * img_inv
    ).astype(BF16)

    blocks = jnp.transpose(proj_back.reshape(rows, n, columns), (1, 0, 2))
    blocks = lax.all_to_all(blocks, "loop", 0, 0, tiled=True)
    back_columns = blocks.reshape(group_rows, columns)

    norm_back = dot(proj_back, proj, LAST)
    scaled = norm_back * gain
    feature_grad = (
        deviation
        * (
            scaled
            - jnp.mean(scaled, axis=-1, keepdims=True)
            - xhat * jnp.mean(scaled * xhat, axis=-1, keepdims=True)
        )
    ).astype(BF16)
    gain_term = jnp.sum(norm_back * xhat, axis=0) * (1.0 / group_rows)

    other_normed = [(standardize(block)[0] * gain).astype(BF16) for block in feature_blocks[1:]]
    relative = jnp.stack([normed] + other_normed)
    member = jnp.arange(n)
    same_core = (member % 2) == (me % 2)
    chips_back = ((me // 2 - member // 2) % half)
    position = jnp.where(same_core, chips_back, half + chips_back)
    group_normed = relative[position].reshape(group_rows, width)

    partial = (dot(group_normed, back_columns, FIRST) * (1.0 / group_rows)).astype(BF16)
    pieces = lax.all_to_all(partial.reshape(m, width // m, columns), "rep", 0, 0, tiled=True)
    reduced = jnp.sum(pieces.astype(F32), axis=0).astype(BF16)
    gains = lax.all_gather(gain_term, "rep")
    gain_sum = jnp.sum(gains, axis=0)
    proj_rows = lax.all_gather(reduced, "loop")
    proj_grad = jnp.transpose(proj_rows, (1, 0, 2)).reshape(width // m, n * columns).astype(F32)
    gain_gradient = jnp.sum(lax.all_gather(gain_sum, "loop"), axis=0)

    group_unit = jnp.concatenate(
        [img_unit] + [unit_rows(dot(block, proj))[0].astype(BF16) for block in other_normed]
    )
    text_weights = weights(own_txt_unit, group_unit)
    txt_back = logit_scale * dot(text_weights, group_unit)
    text_grad = (
        (txt_back - txt_dir * jnp.sum(txt_dir * txt_back, axis=-1, keepdims=True)) * txt_inv
    ).astype(BF16)
    return feature_grad[:, None, :], text_grad[:, None, :], proj_grad, gain_gradient


VMEM = pl.BlockSpec(memory_space=pltpu.VMEM)
SMEM = pl.BlockSpec(memory_space=pltpu.SMEM)
HBM = pl.BlockSpec(memory_space=pltpu.HBM)
LANES = 128
BAND = 16
TOKEN = ((8, LANES), F32)


def call(body, outs, scratch=(), smem=0, hbm=0, limit=24, flops=0, moved=0):
    def run(*operands):
        specs = [SMEM] * smem + [HBM] * hbm + [VMEM] * (len(operands) - smem - hbm)
        return pl.pallas_call(
            body,
            out_shape=[jax.ShapeDtypeStruct(shape, kind) for shape, kind in outs],
            in_specs=specs,
            out_specs=[VMEM] * len(outs),
            scratch_shapes=[pltpu.VMEM(shape, kind) for shape, kind in scratch]
            + [pltpu.SemaphoreType.DMA((hbm,))] * bool(hbm),
            compiler_params=pltpu.CompilerParams(vmem_limit_bytes=limit * 2**20),
            cost_estimate=pl.CostEstimate(flops=flops, bytes_accessed=moved, transcendentals=0),
        )(*operands)

    return run


def over_rows(count, step, body):
    def turn(index, _):
        body(pl.ds(pl.multiple_of(index * step, step), step))
        return 0

    lax.fori_loop(0, count // step, turn, 0, unroll=min(4, count // step))


def sums(values):
    return jnp.sum(values, axis=-1, keepdims=True)


def normalize_into(source, gain, target, at):
    rows, width = source.shape

    def chunk(where):
        values = source[where, :].astype(F32)
        centred = values - sums(values) * (1.0 / width)
        inverse = lax.rsqrt(sums(centred * centred) * (1.0 / width) + 1e-06)
        target[pl.ds(at + where.start, where.size), :] = (centred * inverse * gain[...]).astype(BF16)

    over_rows(rows, 32, chunk)


def unit_into(source, target, at, inverses=None):
    rows = source.shape[0]

    def chunk(where):
        values = source[where, :].astype(F32)
        inverse = lax.rsqrt(sums(values * values) + 1e-06)
        place = pl.ds(at + where.start, where.size)
        target[place, :] = (values * inverse).astype(BF16)
        if inverses is not None:
            inverses[place, :] = inverse

    over_rows(rows, 32, chunk)


def weigh(dots, scale, bias, diagonal, weights, totals, add_to=None):
    rows, columns = dots.shape

    def part(first, count, with_pairs):
        def chunk(where):
            where = pl.ds(first + where.start, where.size)
            product = dots[where, :]
            weight = jnp.tanh((0.5 * scale) * product + 0.5 * bias)
            offset = 0.5
            if with_pairs:
                row = where.start - diagonal + lax.broadcasted_iota(jnp.int32, product.shape, 0)
                column = lax.broadcasted_iota(jnp.int32, product.shape, 1)
                offset = jnp.where(row == column, -0.5, 0.5)
            weight = (0.5 * weight + offset).astype(BF16)
            weights[where, :] = weight
            total = sums(weight.astype(F32) * product)
            totals[where, :] = total if add_to is None else add_to[where, :] + total

        over_rows(count, 32, chunk)

    if diagonal is None:
        part(0, rows, False)
        return
    if diagonal:
        part(0, diagonal, False)
    part(diagonal, columns, True)
    if diagonal + columns < rows:
        part(diagonal + columns, rows - diagonal - columns, False)


def take_columns(place, source, target):
    columns = target.shape[1]
    for member in range(source.shape[1] // columns):

        @pl.when(place[0] == member)
        def _():
            target[...] = source[:, member * columns : (member + 1) * columns]


def near_body(
    scale, bias, place, f0_far, proj_far, t0_far, f1, t1, gain,
    normed_turned, unit, unit_columns, inverse, text_unit, text_columns, weights, totals, proj_columns, token,
    normed, projected, dots, f0, proj, t0, semaphores,
):
    rows = f0.shape[0]
    copies = [
        pltpu.make_async_copy(source, target, semaphores.at[at])
        for at, (source, target) in enumerate(((f0_far, f0), (proj_far, proj), (t0_far, t0)))
    ]
    for copy in copies:
        copy.start()
    normalize_into(f1, gain, normed, rows)
    unit_into(t1, text_unit, rows)
    copies[0].wait()
    normalize_into(f0, gain, normed, 0)
    copies[1].wait()
    projected[...] = dot(normed[...], proj[...])
    copies[2].wait()
    unit_into(t0, text_unit, 0)
    unit_into(projected, unit, 0, inverse)
    dots[...] = dot(unit[...], text_unit[...], LAST)
    weigh(dots, scale[0], bias[0], 0, weights, totals)
    take_columns(place, unit, unit_columns)
    take_columns(place, text_unit, text_columns)
    take_columns(place, proj, proj_columns)
    normed_turned[...] = normed[...].T
    token[...] = jnp.zeros_like(token)


def far_body(
    scale, bias, place, f2, f3, proj, gain, text_near, before,
    normed_turned, unit, unit_columns, inverse, weights, totals, token,
    normed, projected, dots,
):
    rows = f2.shape[0]
    normalize_into(f2, gain, normed, 0)
    normalize_into(f3, gain, normed, rows)
    projected[...] = dot(normed[...], proj[...])
    unit_into(projected, unit, 0, inverse)
    dots[...] = dot(unit[...], text_near[...], LAST)
    weigh(dots, scale[0], bias[0], None, weights, totals)
    take_columns(place, unit, unit_columns)
    normed_turned[...] = normed[...].T
    token[...] = jnp.zeros_like(token)


def third_body(
    scale, bias, place, t2, unit_near, unit_far, weights_near, weights_far, totals_near, totals_far, text_columns_near, before,
    text_unit, weights_own, image_back, totals,
    text_columns, weights, dots,
):
    rows = t2.shape[0]
    near = 2 * rows
    unit_into(t2, text_unit, 0)
    take_columns(place, text_unit, text_columns)
    dots[:near, :] = dot(unit_near[...], text_unit[...], LAST)
    dots[near:, :] = dot(unit_far[...], text_unit[...], LAST)
    totals[:near, :] = totals_near[...]
    totals[near:, :] = totals_far[...]
    weigh(dots, scale[0], bias[0], near, weights, totals, totals)
    weights_own[...] = weights[:rows, :]
    for at, earlier in ((0, weights_near), (near, weights_far)):
        image_back[at : at + near, :] = dot(earlier[...], text_columns_near[...]) + dot(
            weights[at : at + near, :], text_columns[...]
        )


def pack_into(target, block, full):
    rows, columns = block.shape
    rest = columns - full
    target[:rows, :] = block[:, :full].astype(BF16)
    per_band = full // rest
    tail = block[:, full:]
    chunks = [tail[at : at + BAND, :] for at in range(0, rows, BAND)]
    for band in range(0, len(chunks), per_band):
        part = chunks[band : band + per_band]
        if len(part) < per_band:
            part.append(jnp.zeros((BAND, full - rest * len(part)), block.dtype))
        at = rows + (band // per_band) * BAND
        target[at : at + BAND, :] = jnp.concatenate(part, axis=1).astype(BF16)


def partial_body(
    members, groups, lead, scale, bias, place, t3, unit_near, unit_far, totals, image_back, unit_columns_near,
    unit_columns_far, inverse_near, inverse_far, turned_near, turned_far, proj_columns, gain, *refs,
):
    (across, keep_lead, keep_tail), refs = refs[:3], refs[3:]
    along, refs = refs[: groups // 2 - 1], refs[groups // 2 - 1 :]
    text_unit, weights_own, text_columns, weights, dots, all_totals, back, packed = refs
    rows = t3.shape[0]
    near = 2 * rows
    every = members * rows
    width = unit_near.shape[1]
    columns = width // members
    count, full = packed.shape[1:]
    scale, bias = scale[0], bias[0]
    unit_into(t3, text_unit, 0)
    take_columns(place, text_unit, text_columns)
    dots[:near, :] = dot(unit_near[...], text_unit[...], LAST)
    dots[near:, :] = dot(unit_far[...], text_unit[...], LAST)
    weigh(dots, scale, bias, near + rows, weights, all_totals, totals)
    weights_own[...] = weights[:rows, :]
    for at, unit_columns, inverse in ((0, unit_columns_near, inverse_near), (near, unit_columns_far, inverse_far)):
        where = slice(at, at + near)
        whole = image_back[where, :] + dot(weights[where, :], text_columns[...])
        back[where, :] = (
            (whole - unit_columns[...].astype(F32) * all_totals[where, :]) * (inverse[...] * scale)
        ).astype(BF16)
    each = width // groups
    product = (dot(turned_near[...], back[:near, :]) + dot(turned_far[...], back[near:, :])) * (1.0 / every)
    for group in range(groups):
        pack_into(packed.at[group], product[group * each : (group + 1) * each, :], full)

    terms = product * proj_columns[...].astype(F32)
    folded = jnp.concatenate([terms[:, full:], jnp.zeros((width, full + LANES - columns), F32)], axis=1)
    for at in range(0, full, LANES):
        folded = folded + terms[:, at : at + LANES]
    high = folded.astype(BF16)
    low = (folded - high.astype(F32)).astype(BF16)
    ones = jnp.ones((BAND, 2 * LANES), BF16)
    gain_row = dot(ones, jnp.concatenate([high, low], axis=1), LAST)[:1, :] / gain[...]
    pieces = [gain_row[:, at : at + LANES] for at in range(0, width, LANES)]
    pieces.append(jnp.zeros((BAND - len(pieces), LANES), F32))
    gain_tile = jnp.concatenate(pieces, axis=0).astype(BF16)
    for group in range(groups):
        packed[group, count - BAND :, full - LANES :] = gain_tile

    own = place[1]
    for step in range(groups // 2):
        across[step] = packed[own ^ 1 ^ (2 * step), :lead, :]
        keep_lead[step] = packed[own ^ (2 * step), :lead, :]
    for other in range(2):
        keep_tail[other] = packed[own ^ other, lead:, :]
        for step in range(1, groups // 2):
            along[step - 1][other] = packed[own ^ (2 * step) ^ other, lead:, :]


def image_body(
    scale, features, proj, gain, text_near, text_third, text_fourth, weights_near, weights_third, weights_fourth,
    unit, inverse, feature_grad, token, back, product,
):
    rows, width = features.shape
    scale = scale[0]
    product[...] = (
        dot(weights_near[:rows, :], text_near[...])
        + dot(weights_third[...], text_third[...])
        + dot(weights_fourth[...], text_fourth[...])
    )

    def image_chunk(where):
        values = product[where, :] * scale
        direction = unit[where, :].astype(F32)
        back[where, :] = (
            (values - direction * sums(direction * values)) * inverse[where, :]
        ).astype(BF16)

    over_rows(rows, 32, image_chunk)
    product[...] = dot(back[...], proj[...], LAST)

    def feature_chunk(where):
        values = features[where, :].astype(F32)
        centred = values - sums(values) * (1.0 / width)
        deviation = lax.rsqrt(sums(centred * centred) * (1.0 / width) + 1e-06)
        xhat = centred * deviation
        scaled = product[where, :] * gain[...]
        feature_grad[where, :] = (
            deviation
            * (scaled - sums(scaled) * (1.0 / width) - xhat * (sums(scaled * xhat) * (1.0 / width)))
        ).astype(BF16)

    over_rows(rows, 32, feature_chunk)
    token[...] = jnp.zeros_like(token)


def text_body(scale, text, weights_near, weights_far, unit_near, unit_far, text_grad, token, product):
    rows = text.shape[0]
    scale = scale[0]
    product[...] = dot(weights_near[:, :rows], unit_near[...], FIRST) + dot(
        weights_far[:, :rows], unit_far[...], FIRST
    )

    def text_chunk(where):
        values = product[where, :] * scale
        own = text[where, :].astype(F32)
        own_inverse = lax.rsqrt(sums(own * own) + 1e-06)
        direction = own * own_inverse
        text_grad[where, :] = (
            (values - direction * sums(direction * values)) * own_inverse
        ).astype(BF16)

    over_rows(rows, 32, text_chunk)
    token[...] = jnp.zeros_like(token)


def first_sum_body(place, token, keep_lead, across, keep_tail, *refs):
    steps = keep_lead.shape[0]
    along, refs = refs[: steps - 1], refs[steps - 1 :]
    leads, (tail, tail_across, ordered) = refs[:steps], refs[steps:]
    for step in range(steps):
        leads[step][...] = (keep_lead[step].astype(F32) + across[step].astype(F32)).astype(BF16)
    own = place[1] // 2
    ordered[own] = keep_tail[...]
    for step in range(1, steps):
        ordered[own ^ step] = along[steps - 1 - step][...]
    value = ordered[0].astype(F32)
    for step in range(1, steps):
        value = value + ordered[step].astype(F32)
    tail[...] = value[0].astype(BF16)
    tail_across[...] = value[1].astype(BF16)


def last_sum_body(tail, tail_across, *refs):
    leads, total = refs[:-1], refs[-1]
    split = leads[0].shape[0]
    value = leads[0][...].astype(F32)
    for lead in leads[1:]:
        value = value + lead[...].astype(F32)
    total[:split, :] = value.astype(BF16)
    total[split:, :] = (tail[...].astype(F32) + tail_across[...].astype(F32)).astype(BF16)


def finish_body(members, place, *refs):
    packets, (proj_grad, gain_gradient, ordered) = refs[:members], refs[members:]
    count, full = packets[0].shape
    rows, width = proj_grad.shape
    columns = width // members
    rest = columns - full
    per_band = full // rest
    for own in range(members):

        @pl.when(place[0] == own)
        def _():
            for k in range(members):
                base = (own ^ k) * columns
                packet = packets[k]
                main = packet[:rows, :].astype(F32)
                tails = []
                for index in range(rows // BAND):
                    at = rows + (index // per_band) * BAND
                    lane = (index % per_band) * rest
                    tails.append(packet[at : at + BAND, lane : lane + rest].astype(F32))
                proj_grad[:, base : base + full] = main
                proj_grad[:, base + full : base + columns] = jnp.concatenate(tails, axis=0)

    for k in range(members):
        ordered[place[0] ^ k] = packets[k][count - BAND :, full - LANES :].astype(F32)
    value = ordered[0]
    for member in range(1, members):
        value = value + ordered[member]
    for at in range(width // LANES):
        gain_gradient[at * LANES : (at + 1) * LANES] = value[at]


def local_four(features, text, proj, gain, scale, bias):
    members = lax.axis_size("loop")
    groups = lax.axis_size("rep")
    place = jnp.stack([lax.axis_index("loop"), lax.axis_index("rep")]).astype(jnp.int32)
    rows, width = features.shape[0], features.shape[2]
    near, every = 2 * rows, 4 * rows
    columns = width // members
    full = columns // LANES * LANES
    each = width // groups
    bands = -(-(each // BAND) // (full // (columns - full)))
    packet = (each + bands * BAND, full)
    gain_row = gain.reshape(1, width)

    lead = (2 * packet[0] // BAND // 3) * BAND
    tail = packet[0] - lead
    steps = groups // 2

    f0, t0 = features[:, 0, :], text[:, 0, :]
    f2 = send(f0, "loop", lambda p: p ^ 2)
    f1 = send(f0, "loop", lambda p: p ^ 1)
    t1 = send(t0, "loop", lambda p: p ^ 1)

    wide, half, one = ((near, width), BF16), ((rows, width), BF16), ((near, 1), F32)
    square, part, turned = ((near, near), BF16), ((near, columns), BF16), ((width, near), BF16)

    outs = [turned, wide, part, one, wide, part, square, one, ((width, columns), BF16), TOKEN]
    (
        turned_near, unit_near, unit_columns_near, inverse_near, text_near, text_columns_near,
        weights_near, totals_near, proj_columns, token,
    ) = call(
        near_body,
        outs,
        [wide, ((near, width), F32), ((near, near), F32), half, ((width, width), BF16), half],
        smem=3,
        hbm=3,
        limit=43,
        flops=3 * near * width * width,
        moved=8 * near * width,
    )(scale, bias, place, f0, proj, t0, f1, t1, gain_row)

    t_after, f2_after, token = lax.optimization_barrier((t0, f2, token))
    t2 = send(t_after, "loop", lambda p: p ^ 2)
    f3 = send(f2_after, "loop", lambda p: p ^ 1)

    turned_far, unit_far, unit_columns_far, inverse_far, weights_far, totals_far, token = call(
        far_body,
        [turned, wide, part, one, square, one, TOKEN],
        [wide, ((near, width), F32), ((near, near), F32)],
        smem=3,
        flops=3 * near * width * width,
        moved=8 * near * width,
    )(scale, bias, place, f2, f3, proj, gain_row, text_near, token)

    text_grad, token = call(
        text_body,
        [half, TOKEN],
        [((rows, width), F32)],
        smem=1,
        flops=2 * near * width * width,
        moved=6 * near * width,
    )(scale, t0, weights_near, weights_far, unit_near, unit_far)

    t2_after, token = lax.optimization_barrier((t2, token))
    t3 = send(t2_after, "loop", lambda p: p ^ 1)

    narrow = ((every, rows), BF16)
    text_third, weights_third, image_back, totals = call(
        third_body,
        [half, ((rows, rows), BF16), ((every, columns), F32), ((every, 1), F32)],
        [((rows, columns), BF16), narrow, ((every, rows), F32)],
        smem=3,
        flops=2 * near * width * width,
        moved=8 * near * width,
    )(
        scale, bias, place, t2, unit_near, unit_far, weights_near, weights_far, totals_near, totals_far,
        text_columns_near, token,
    )

    outs = call(
        functools.partial(partial_body, members, groups, lead),
        [((steps, lead, full), BF16), ((steps, lead, full), BF16)]
        + [((2, tail, full), BF16)] * steps
        + [half, ((rows, rows), BF16)],
        [
            ((rows, columns), BF16), narrow, ((every, rows), F32), ((every, 1), F32), ((every, columns), BF16),
            ((groups,) + packet, BF16),
        ],
        smem=3,
        flops=4 * near * width * width,
        moved=16 * near * width,
    )(
        scale, bias, place, t3, unit_near, unit_far, totals, image_back, unit_columns_near, unit_columns_far,
        inverse_near, inverse_far, turned_near, turned_far, proj_columns, gain_row,
    )
    across, keep_lead, keep_tail = outs[:3]
    along, (text_fourth, weights_fourth) = outs[3 : 2 + steps], outs[2 + steps :]

    across = send(across, "rep", lambda p: p ^ 1)
    along = [send(along[step - 1], "rep", lambda p: p ^ (2 * step)) for step in reversed(range(1, steps))]

    feature_grad, token = call(
        image_body,
        [half, TOKEN],
        [half, ((rows, width), F32)],
        smem=1,
        flops=4 * near * width * width,
        moved=12 * near * width,
    )(
        scale, f0, proj, gain_row, text_near, text_third, text_fourth, weights_near, weights_third,
        weights_fourth, unit_near, inverse_near,
    )

    outs = call(
        first_sum_body,
        [((lead, full), BF16)] * steps + [((tail, full), BF16)] * 2,
        [((steps, 2, tail, full), BF16)],
        smem=1,
        moved=4 * each * width,
    )(place, token, keep_lead, across, keep_tail, *along)
    leads = [outs[0]] + [send(outs[step], "rep", lambda p: p ^ (2 * step)) for step in reversed(range(1, steps))]
    tail_across = send(outs[steps + 1], "rep", lambda p: p ^ 1)

    (reduced,) = call(
        last_sum_body,
        [(packet, BF16)],
        moved=4 * each * width,
    )(outs[steps], tail_across, *leads)
    far_block = send(reduced, "loop", lambda p: p ^ 2)
    near_block = send(reduced, "loop", lambda p: p ^ 1)
    blocks = [reduced, near_block, far_block, send(far_block, "loop", lambda p: p ^ 1)]

    proj_grad, gain_gradient = call(
        functools.partial(finish_body, members),
        [((each, width), F32), ((width,), F32)],
        [((members, BAND, LANES), F32)],
        smem=1,
        moved=8 * each * width,
    )(place, *blocks)
    return feature_grad[:, None, :], text_grad[:, None, :], proj_grad, gain_gradient


def four_fits(mesh, rows_shape):
    members, groups = mesh.shape["loop"], mesh.shape["rep"]
    rows, width = rows_shape[0] // members, rows_shape[2]
    if members != 4 or groups & (groups - 1) or width % (members * groups) or width % LANES:
        return False
    columns, each = width // members, width // groups
    full = columns // LANES * LANES
    rest = columns - full
    if rest == 0 or full < LANES or full % rest or each % BAND or rows % 64 or width // LANES > BAND:
        return False
    chunks = each // BAND
    used = (chunks - 1) % (full // rest) + 1
    return used * rest <= full - LANES


def solution(mesh):
    def run(features, text, proj, gain, scale, bias):
        body = local_four if four_fits(mesh, features.shape) else local_any_size
        return jax.shard_map(
            body,
            mesh=mesh,
            in_specs=(P("loop", "rep", None), P("loop", "rep", None), P(), P(), P(), P()),
            out_specs=(P("loop", "rep", None), P("loop", "rep", None), P("rep", None), P()),
            check_vma=False,
        )(features, text, proj, gain, scale, bias)

    return run
```

```python
import functools

import jax
import jax.numpy as jnp
from jax import lax
from jax.experimental import pallas as pl
from jax.experimental.pallas import tpu as pltpu
from jax.sharding import PartitionSpec as P

F32 = jnp.float32
BF16 = jnp.bfloat16
LAST = (((1,), (1,)), ((), ()))
FIRST = (((0,), (0,)), ((), ()))


def dot(a, b, dims=(((1,), (0,)), ((), ()))):
    return lax.dot_general(a, b, dims, preferred_element_type=F32)


def unit_rows(values):
    inverse = lax.rsqrt(jnp.sum(values * values, axis=-1, keepdims=True) + 1e-06)
    return values * inverse, inverse


def standardize(rows):
    values = rows.astype(F32)
    centred = values - jnp.mean(values, axis=-1, keepdims=True)
    inverse = lax.rsqrt(jnp.mean(centred * centred, axis=-1, keepdims=True) + 1e-06)
    return centred * inverse, inverse


def send(value, axis, target):
    count = lax.axis_size(axis)
    return lax.ppermute(value, axis, [(p, target(p)) for p in range(count)])


def gather_group(value, count):
    mine = [value]
    for step in range(1, count // 2):
        mine.append(send(value, "loop", lambda p: (p + 2 * step) % count))
    mates = [send(block, "loop", lambda p: p ^ 1) for block in mine]
    return mine + mates


def local_any_size(features, text, proj, gain, scale, bias):
    n = lax.axis_size("loop")
    m = lax.axis_size("rep")
    me = lax.axis_index("loop")
    half = n // 2
    rows, width = features.shape[0], features.shape[2]
    columns = proj.shape[1] // n
    group_rows = rows * n
    logit_scale, logit_bias = scale[0], bias[0]

    own_features = features[:, 0, :]
    own_text = text[:, 0, :]
    text_blocks = gather_group(own_text, n)
    feature_blocks = gather_group(own_features, n)

    xhat, deviation = standardize(own_features)
    normed = (xhat * gain).astype(BF16)
    img_dir, img_inv = unit_rows(dot(normed, proj))
    img_unit = img_dir.astype(BF16)

    txt_dir, txt_inv = unit_rows(own_text.astype(F32))
    own_txt_unit = txt_dir.astype(BF16)
    txt_unit = jnp.concatenate(
        [own_txt_unit] + [unit_rows(block.astype(F32))[0].astype(BF16) for block in text_blocks[1:]]
    )
    row_ids = lax.broadcasted_iota(jnp.int32, (rows, group_rows), 0)
    column_ids = lax.broadcasted_iota(jnp.int32, (rows, group_rows), 1)
    diagonal = (row_ids == column_ids).astype(F32)

    def weights(left, right):
        logits = logit_scale * dot(left, right, LAST) + logit_bias
        return (jax.nn.sigmoid(logits) - diagonal).astype(BF16)

    img_back = logit_scale * dot(weights(img_unit, txt_unit), txt_unit)
    proj_back = (
        (img_back - img_dir * jnp.sum(img_dir * img_back, axis=-1, keepdims=True)) * img_inv
    ).astype(BF16)

    blocks = jnp.transpose(proj_back.reshape(rows, n, columns), (1, 0, 2))
    blocks = lax.all_to_all(blocks, "loop", 0, 0, tiled=True)
    back_columns = blocks.reshape(group_rows, columns)

    norm_back = dot(proj_back, proj, LAST)
    scaled = norm_back * gain
    feature_grad = (
        deviation
        * (
            scaled
            - jnp.mean(scaled, axis=-1, keepdims=True)
            - xhat * jnp.mean(scaled * xhat, axis=-1, keepdims=True)
        )
    ).astype(BF16)
    gain_term = jnp.sum(norm_back * xhat, axis=0) * (1.0 / group_rows)

    other_normed = [(standardize(block)[0] * gain).astype(BF16) for block in feature_blocks[1:]]
    relative = jnp.stack([normed] + other_normed)
    member = jnp.arange(n)
    same_core = (member % 2) == (me % 2)
    chips_back = ((me // 2 - member // 2) % half)
    position = jnp.where(same_core, chips_back, half + chips_back)
    group_normed = relative[position].reshape(group_rows, width)

    partial = (dot(group_normed, back_columns, FIRST) * (1.0 / group_rows)).astype(BF16)
    pieces = lax.all_to_all(partial.reshape(m, width // m, columns), "rep", 0, 0, tiled=True)
    reduced = jnp.sum(pieces.astype(F32), axis=0).astype(BF16)
    gains = lax.all_gather(gain_term, "rep")
    gain_sum = jnp.sum(gains, axis=0)
    proj_rows = lax.all_gather(reduced, "loop")
    proj_grad = jnp.transpose(proj_rows, (1, 0, 2)).reshape(width // m, n * columns).astype(F32)
    gain_gradient = jnp.sum(lax.all_gather(gain_sum, "loop"), axis=0)

    group_unit = jnp.concatenate(
        [img_unit] + [unit_rows(dot(block, proj))[0].astype(BF16) for block in other_normed]
    )
    text_weights = weights(own_txt_unit, group_unit)
    txt_back = logit_scale * dot(text_weights, group_unit)
    text_grad = (
        (txt_back - txt_dir * jnp.sum(txt_dir * txt_back, axis=-1, keepdims=True)) * txt_inv
    ).astype(BF16)
    return feature_grad[:, None, :], text_grad[:, None, :], proj_grad, gain_gradient


VMEM = pl.BlockSpec(memory_space=pltpu.VMEM)
SMEM = pl.BlockSpec(memory_space=pltpu.SMEM)
HBM = pl.BlockSpec(memory_space=pltpu.HBM)
LANES = 128
BAND = 16
TOKEN = ((8, LANES), F32)


def call(body, outs, scratch=(), smem=0, hbm=0, limit=24, flops=0, moved=0):
    def run(*operands):
        specs = [SMEM] * smem + [HBM] * hbm + [VMEM] * (len(operands) - smem - hbm)
        return pl.pallas_call(
            body,
            out_shape=[jax.ShapeDtypeStruct(shape, kind) for shape, kind in outs],
            in_specs=specs,
            out_specs=[VMEM] * len(outs),
            scratch_shapes=[pltpu.VMEM(shape, kind) for shape, kind in scratch]
            + [pltpu.SemaphoreType.DMA((hbm,))] * bool(hbm),
            compiler_params=pltpu.CompilerParams(vmem_limit_bytes=limit * 2**20),
            cost_estimate=pl.CostEstimate(flops=flops, bytes_accessed=moved, transcendentals=0),
        )(*operands)

    return run


def over_rows(count, step, body):
    def turn(index, _):
        body(pl.ds(pl.multiple_of(index * step, step), step))
        return 0

    lax.fori_loop(0, count // step, turn, 0, unroll=min(4, count // step))


def sums(values):
    return jnp.sum(values, axis=-1, keepdims=True)


def normalize_into(source, gain, target, at):
    rows, width = source.shape

    def chunk(where):
        values = source[where, :].astype(F32)
        centred = values - sums(values) * (1.0 / width)
        inverse = lax.rsqrt(sums(centred * centred) * (1.0 / width) + 1e-06)
        target[pl.ds(at + where.start, where.size), :] = (centred * inverse * gain[...]).astype(BF16)

    over_rows(rows, 32, chunk)


def unit_into(source, target, at, inverses=None):
    rows = source.shape[0]

    def chunk(where):
        values = source[where, :].astype(F32)
        inverse = lax.rsqrt(sums(values * values) + 1e-06)
        place = pl.ds(at + where.start, where.size)
        target[place, :] = (values * inverse).astype(BF16)
        if inverses is not None:
            inverses[place, :] = jnp.broadcast_to(inverse, (where.size, LANES))

    over_rows(rows, 32, chunk)


def weigh(dots, scale, bias, diagonal, weights):
    texts, images = dots.shape

    def chunk(index, total):
        where = pl.ds(pl.multiple_of(index * BAND, BAND), BAND)
        product = dots[where, :]
        weight = jnp.tanh((0.5 * scale) * product + 0.5 * bias)
        offset = 0.5
        if diagonal is not None:
            text = index * BAND + diagonal + lax.broadcasted_iota(jnp.int32, product.shape, 0)
            image = lax.broadcasted_iota(jnp.int32, product.shape, 1)
            offset = jnp.where(text == image, -0.5, 0.5)
        weight = (0.5 * weight + offset).astype(BF16)
        weights[where, :] = weight
        both = weight.astype(F32) * product
        return total + both[:8, :] + both[8:, :]

    total = lax.fori_loop(0, texts // BAND, chunk, jnp.zeros((8, images), F32), unroll=4)
    return jnp.sum(total, axis=0, keepdims=True)


def take_columns(place, source, target):
    columns = target.shape[1]
    for member in range(source.shape[1] // columns):

        @pl.when(place[0] == member)
        def _():
            target[...] = source[:, member * columns : (member + 1) * columns]


def near_body(
    f0_far, proj_far, t0_far, f1, t1, gain,
    f0, proj, t0, normed, unit, factors, text_unit, token, projected, semaphores,
):
    rows = f0.shape[0]
    copies = [
        pltpu.make_async_copy(source, target, semaphores.at[at])
        for at, (source, target) in enumerate(((f0_far, f0), (proj_far, proj), (t0_far, t0)))
    ]
    for copy in copies:
        copy.start()
    normalize_into(f1, gain, normed, rows)
    unit_into(t1, text_unit, rows)
    copies[0].wait()
    normalize_into(f0, gain, normed, 0)
    copies[1].wait()
    projected[...] = dot(normed[...], proj[...])
    copies[2].wait()
    unit_into(t0, text_unit, 0)
    unit_into(projected, unit, 0, factors)
    token[...] = jnp.zeros_like(token)


def near_pairs_body(
    scale, bias, place, normed, unit, factors, text_unit, proj, before,
    normed_turned, unit_turned, inverse, text_columns, weights, totals, proj_columns, dots, turned,
):
    dots[...] = dot(text_unit[...], unit[...], LAST)
    totals[...] = weigh(dots, scale[0], bias[0], 0, weights)
    take_columns(place, text_unit, text_columns)
    take_columns(place, proj, proj_columns)
    turn_own(place, unit, factors, turned, unit_turned, inverse)
    normed_turned[...] = normed[...].T


def turn_own(place, unit, factors, turned, unit_turned, inverse):
    columns = unit_turned.shape[0]
    turned[...] = unit[...].T
    unit_turned[...] = turned[pl.ds(pl.multiple_of(place[0] * columns, BAND), columns), :]
    inverse[...] = factors[...].T[:1, :]


def far_body(
    scale, bias, place, f2, f3, proj, gain, text_near, before,
    normed_turned, unit, unit_turned, inverse, weights, totals, token,
    normed, projected, dots, turned, factors,
):
    rows = f2.shape[0]
    normalize_into(f2, gain, normed, 0)
    normalize_into(f3, gain, normed, rows)
    projected[...] = dot(normed[...], proj[...])
    unit_into(projected, unit, 0, factors)
    dots[...] = dot(text_near[...], unit[...], LAST)
    totals[...] = weigh(dots, scale[0], bias[0], None, weights)
    turn_own(place, unit, factors, turned, unit_turned, inverse)
    normed_turned[...] = normed[...].T
    token[...] = jnp.zeros_like(token)


def third_body(
    scale, bias, place, t2, unit_near, unit_far, weights_near, weights_far, totals_near, totals_far, text_columns_near,
    before, text_unit, weights, back_near, back_far, totals,
    text_columns, dots,
):
    rows = t2.shape[0]
    near = 2 * rows
    unit_into(t2, text_unit, 0)
    take_columns(place, text_unit, text_columns)
    dots[:, :near] = dot(text_unit[...], unit_near[...], LAST)
    dots[:, near:] = dot(text_unit[...], unit_far[...], LAST)
    added = weigh(dots, scale[0], bias[0], near, weights)
    totals[:, :near] = totals_near[...] + added[:, :near]
    totals[:, near:] = totals_far[...] + added[:, near:]
    back_near[...] = dot(text_columns_near[...], weights_near[...], FIRST) + dot(
        text_columns[...], weights[:, :near], FIRST
    )
    back_far[...] = dot(text_columns_near[...], weights_far[...], FIRST) + dot(
        text_columns[...], weights[:, near:], FIRST
    )


def pack_into(target, block, full):
    rows, columns = block.shape
    rest = columns - full
    target[:rows, :] = block[:, :full].astype(BF16)
    per_band = full // rest
    tail = block[:, full:]
    chunks = [tail[at : at + BAND, :] for at in range(0, rows, BAND)]
    for band in range(0, len(chunks), per_band):
        part = chunks[band : band + per_band]
        if len(part) < per_band:
            part.append(jnp.zeros((BAND, full - rest * len(part)), block.dtype))
        at = rows + (band // per_band) * BAND
        target[at : at + BAND, :] = jnp.concatenate(part, axis=1).astype(BF16)


def partial_body(
    members, groups, lead, scale, bias, place, t3, unit_near, unit_far, totals, back_near, back_far, unit_turned_near,
    unit_turned_far, inverse_near, inverse_far, turned_near, turned_far, proj_columns, gain, *refs,
):
    (across, keep_lead, keep_tail), refs = refs[:3], refs[3:]
    along, refs = refs[: groups // 2 - 1], refs[groups // 2 - 1 :]
    text_unit, weights, text_columns, dots, packed = refs
    rows = t3.shape[0]
    near = 2 * rows
    every = members * rows
    width = unit_near.shape[1]
    columns = width // members
    count, full = packed.shape[1:]
    scale, bias = scale[0], bias[0]
    unit_into(t3, text_unit, 0)
    take_columns(place, text_unit, text_columns)
    dots[:, :near] = dot(text_unit[...], unit_near[...], LAST)
    dots[:, near:] = dot(text_unit[...], unit_far[...], LAST)
    total = totals[...] + weigh(dots, scale, bias, near + rows, weights)
    product = None
    for where, earlier, unit_turned, inverse, turned in (
        (slice(0, near), back_near, unit_turned_near, inverse_near, turned_near),
        (slice(near, every), back_far, unit_turned_far, inverse_far, turned_far),
    ):
        whole = earlier[...] + dot(text_columns[...], weights[:, where], FIRST)
        back = (whole - unit_turned[...].astype(F32) * total[:, where]) * (inverse[...] * scale)
        part = dot(turned[...], back.astype(BF16), LAST)
        product = part if product is None else product + part
    each = width // groups
    product = product * (1.0 / every)
    for group in range(groups):
        pack_into(packed.at[group], product[group * each : (group + 1) * each, :], full)

    terms = product * proj_columns[...].astype(F32)
    folded = jnp.concatenate([terms[:, full:], jnp.zeros((width, full + LANES - columns), F32)], axis=1)
    for at in range(0, full, LANES):
        folded = folded + terms[:, at : at + LANES]
    high = folded.astype(BF16)
    low = (folded - high.astype(F32)).astype(BF16)
    ones = jnp.ones((BAND, 2 * LANES), BF16)
    gain_row = dot(ones, jnp.concatenate([high, low], axis=1), LAST)[:1, :] / gain[...]
    pieces = [gain_row[:, at : at + LANES] for at in range(0, width, LANES)]
    pieces.append(jnp.zeros((BAND - len(pieces), LANES), F32))
    gain_tile = jnp.concatenate(pieces, axis=0).astype(BF16)
    for group in range(groups):
        packed[group, count - BAND :, full - LANES :] = gain_tile

    own = place[1]
    for step in range(groups // 2):
        across[step] = packed[own ^ 1 ^ (2 * step), :lead, :]
        keep_lead[step] = packed[own ^ (2 * step), :lead, :]
    for other in range(2):
        keep_tail[other] = packed[own ^ other, lead:, :]
        for step in range(1, groups // 2):
            along[step - 1][other] = packed[own ^ (2 * step) ^ other, lead:, :]


def image_body(
    scale, features, proj, gain, text_near, text_third, text_fourth, weights_near, weights_third, weights_fourth,
    unit, factors, feature_grad, token, back, product,
):
    rows, width = features.shape
    scale = scale[0]
    product[...] = (
        dot(weights_near[:, :rows], text_near[...], FIRST)
        + dot(weights_third[:, :rows], text_third[...], FIRST)
        + dot(weights_fourth[:, :rows], text_fourth[...], FIRST)
    )

    def image_chunk(where):
        values = product[where, :] * scale
        direction = unit[where, :].astype(F32)
        back[where, :] = (
            (values - direction * sums(direction * values)) * factors[where, :1]
        ).astype(BF16)

    over_rows(rows, 32, image_chunk)
    product[...] = dot(back[...], proj[...], LAST)

    def feature_chunk(where):
        values = features[where, :].astype(F32)
        centred = values - sums(values) * (1.0 / width)
        deviation = lax.rsqrt(sums(centred * centred) * (1.0 / width) + 1e-06)
        xhat = centred * deviation
        scaled = product[where, :] * gain[...]
        feature_grad[where, :] = (
            deviation
            * (scaled - sums(scaled) * (1.0 / width) - xhat * (sums(scaled * xhat) * (1.0 / width)))
        ).astype(BF16)

    over_rows(rows, 32, feature_chunk)
    token[...] = jnp.zeros_like(token)


def text_body(scale, text, weights_near, weights_far, unit_near, unit_far, text_grad, token, product):
    rows = text.shape[0]
    scale = scale[0]
    product[...] = dot(weights_near[:rows, :], unit_near[...]) + dot(weights_far[:rows, :], unit_far[...])

    def text_chunk(where):
        values = product[where, :] * scale
        own = text[where, :].astype(F32)
        own_inverse = lax.rsqrt(sums(own * own) + 1e-06)
        direction = own * own_inverse
        text_grad[where, :] = (
            (values - direction * sums(direction * values)) * own_inverse
        ).astype(BF16)

    over_rows(rows, 32, text_chunk)
    token[...] = jnp.zeros_like(token)


def first_sum_body(place, token, keep_lead, across, keep_tail, *refs):
    steps = keep_lead.shape[0]
    along, refs = refs[: steps - 1], refs[steps - 1 :]
    leads, (tail, tail_across, ordered) = refs[:steps], refs[steps:]
    for step in range(steps):
        leads[step][...] = (keep_lead[step].astype(F32) + across[step].astype(F32)).astype(BF16)
    own = place[1] // 2
    ordered[own] = keep_tail[...]
    for step in range(1, steps):
        ordered[own ^ step] = along[steps - 1 - step][...]
    value = ordered[0].astype(F32)
    for step in range(1, steps):
        value = value + ordered[step].astype(F32)
    tail[...] = value[0].astype(BF16)
    tail_across[...] = value[1].astype(BF16)


def last_sum_body(tail, tail_across, *refs):
    leads, total = refs[:-1], refs[-1]
    split = leads[0].shape[0]
    value = leads[0][...].astype(F32)
    for lead in leads[1:]:
        value = value + lead[...].astype(F32)
    total[:split, :] = value.astype(BF16)
    total[split:, :] = (tail[...].astype(F32) + tail_across[...].astype(F32)).astype(BF16)


def finish_body(members, place, *refs):
    packets, (proj_grad, gain_gradient, ordered) = refs[:members], refs[members:]
    count, full = packets[0].shape
    rows, width = proj_grad.shape
    columns = width // members
    rest = columns - full
    per_band = full // rest
    for own in range(members):

        @pl.when(place[0] == own)
        def _():
            for k in range(members):
                base = (own ^ k) * columns
                packet = packets[k]
                main = packet[:rows, :].astype(F32)
                tails = []
                for index in range(rows // BAND):
                    at = rows + (index // per_band) * BAND
                    lane = (index % per_band) * rest
                    tails.append(packet[at : at + BAND, lane : lane + rest].astype(F32))
                proj_grad[:, base : base + full] = main
                proj_grad[:, base + full : base + columns] = jnp.concatenate(tails, axis=0)

    for k in range(members):
        ordered[place[0] ^ k] = packets[k][count - BAND :, full - LANES :].astype(F32)
    value = ordered[0]
    for member in range(1, members):
        value = value + ordered[member]
    for at in range(width // LANES):
        gain_gradient[at * LANES : (at + 1) * LANES] = value[at]


def local_four(features, text, proj, gain, scale, bias):
    members = lax.axis_size("loop")
    groups = lax.axis_size("rep")
    place = jnp.stack([lax.axis_index("loop"), lax.axis_index("rep")]).astype(jnp.int32)
    rows, width = features.shape[0], features.shape[2]
    near, every = 2 * rows, 4 * rows
    columns = width // members
    full = columns // LANES * LANES
    each = width // groups
    bands = -(-(each // BAND) // (full // (columns - full)))
    packet = (each + bands * BAND, full)
    gain_row = gain.reshape(1, width)

    lead = (3 * packet[0] // BAND // 4) * BAND
    tail = packet[0] - lead
    steps = groups // 2

    f0, t0 = features[:, 0, :], text[:, 0, :]
    f2 = send(f0, "loop", lambda p: p ^ 2)
    f1 = send(f0, "loop", lambda p: p ^ 1)
    t1 = send(t0, "loop", lambda p: p ^ 1)

    wide, half = ((near, width), BF16), ((rows, width), BF16)
    square, part, turned = ((near, near), BF16), ((near, columns), BF16), ((width, near), BF16)

    line, mine = ((1, near), F32), ((columns, near), BF16)
    kept = ((width, width), BF16)
    f0_kept, proj_kept, t0_kept, normed_near, unit_near, factors, text_near, token = call(
        near_body,
        [half, kept, half, wide, wide, ((near, LANES), F32), wide, TOKEN],
        [((near, width), F32)],
        hbm=3,
        limit=46,
        flops=2 * near * width * width,
        moved=8 * near * width,
    )(f0, proj, t0, f1, t1, gain_row)

    t_after, f2_after, token = lax.optimization_barrier((t0, f2, token))
    t2 = send(t_after, "loop", lambda p: p ^ 2)
    f3 = send(f2_after, "loop", lambda p: p ^ 1)

    (
        turned_near, unit_turned_near, inverse_near, text_columns_near, weights_near, totals_near, proj_columns,
    ) = call(
        near_pairs_body,
        [turned, mine, line, part, square, line, ((width, columns), BF16)],
        [((near, near), F32), turned],
        smem=3,
        flops=near * width * width,
        moved=8 * near * width,
    )(scale, bias, place, normed_near, unit_near, factors, text_near, proj_kept, token)

    turned_far, unit_far, unit_turned_far, inverse_far, weights_far, totals_far, token = call(
        far_body,
        [turned, wide, mine, line, square, line, TOKEN],
        [wide, ((near, width), F32), ((near, near), F32), turned, ((near, LANES), F32)],
        smem=3,
        flops=3 * near * width * width,
        moved=8 * near * width,
    )(scale, bias, place, f2, f3, proj_kept, gain_row, text_near, totals_near)

    text_grad, token = call(
        text_body,
        [half, TOKEN],
        [((rows, width), F32)],
        smem=1,
        flops=2 * near * width * width,
        moved=6 * near * width,
    )(scale, t0_kept, weights_near, weights_far, unit_near, unit_far)

    t2_after, token = lax.optimization_barrier((t2, token))
    t3 = send(t2_after, "loop", lambda p: p ^ 1)

    narrow, back_kind = ((rows, every), BF16), ((columns, near), F32)
    text_third, weights_third, back_near, back_far, totals = call(
        third_body,
        [half, narrow, back_kind, back_kind, ((1, every), F32)],
        [((rows, columns), BF16), ((rows, every), F32)],
        smem=3,
        flops=2 * near * width * width,
        moved=8 * near * width,
    )(
        scale, bias, place, t2, unit_near, unit_far, weights_near, weights_far, totals_near, totals_far,
        text_columns_near, token,
    )

    outs = call(
        functools.partial(partial_body, members, groups, lead),
        [((steps, lead, full), BF16), ((steps, lead, full), BF16)] + [((2, tail, full), BF16)] * steps + [half, narrow],
        [((rows, columns), BF16), ((rows, every), F32), ((groups,) + packet, BF16)],
        smem=3,
        flops=4 * near * width * width,
        moved=16 * near * width,
    )(
        scale, bias, place, t3, unit_near, unit_far, totals, back_near, back_far, unit_turned_near, unit_turned_far,
        inverse_near, inverse_far, turned_near, turned_far, proj_columns, gain_row,
    )
    across, keep_lead, keep_tail = outs[:3]
    along, (text_fourth, weights_fourth) = outs[3 : 2 + steps], outs[2 + steps :]

    across = send(across, "rep", lambda p: p ^ 1)
    along = [send(along[step - 1], "rep", lambda p: p ^ (2 * step)) for step in reversed(range(1, steps))]

    feature_grad, token = call(
        image_body,
        [half, TOKEN],
        [half, ((rows, width), F32)],
        smem=1,
        flops=4 * near * width * width,
        moved=12 * near * width,
    )(
        scale, f0_kept, proj_kept, gain_row, text_near, text_third, text_fourth, weights_near, weights_third,
        weights_fourth, unit_near, factors,
    )

    outs = call(
        first_sum_body,
        [((lead, full), BF16)] * steps + [((tail, full), BF16)] * 2,
        [((steps, 2, tail, full), BF16)],
        smem=1,
        moved=4 * each * width,
    )(place, token, keep_lead, across, keep_tail, *along)
    leads = [outs[0]] + [send(outs[step], "rep", lambda p: p ^ (2 * step)) for step in reversed(range(1, steps))]
    tail_across = send(outs[steps + 1], "rep", lambda p: p ^ 1)

    (reduced,) = call(
        last_sum_body,
        [(packet, BF16)],
        moved=4 * each * width,
    )(outs[steps], tail_across, *leads)
    far_block = send(reduced, "loop", lambda p: p ^ 2)
    near_block = send(reduced, "loop", lambda p: p ^ 1)
    blocks = [reduced, near_block, far_block, send(far_block, "loop", lambda p: p ^ 1)]

    proj_grad, gain_gradient = call(
        functools.partial(finish_body, members),
        [((each, width), F32), ((width,), F32)],
        [((members, BAND, LANES), F32)],
        smem=1,
        moved=8 * each * width,
    )(place, *blocks)
    return feature_grad[:, None, :], text_grad[:, None, :], proj_grad, gain_gradient


def four_fits(mesh, rows_shape):
    members, groups = mesh.shape["loop"], mesh.shape["rep"]
    rows, width = rows_shape[0] // members, rows_shape[2]
    if members != 4 or groups & (groups - 1) or width % (members * groups) or width % LANES:
        return False
    columns, each = width // members, width // groups
    full = columns // LANES * LANES
    rest = columns - full
    if rest == 0 or full < LANES or full % rest or each % BAND or rows % 64 or width // LANES > BAND:
        return False
    chunks = each // BAND
    used = (chunks - 1) % (full // rest) + 1
    return used * rest <= full - LANES


def solution(mesh):
    def run(features, text, proj, gain, scale, bias):
        body = local_four if four_fits(mesh, features.shape) else local_any_size
        return jax.shard_map(
            body,
            mesh=mesh,
            in_specs=(P("loop", "rep", None), P("loop", "rep", None), P(), P(), P(), P()),
            out_specs=(P("loop", "rep", None), P("loop", "rep", None), P("rep", None), P()),
            check_vma=False,
        )(features, text, proj, gain, scale, bias)

    return run
```

```python
import functools

import jax
import jax.numpy as jnp
from jax import lax
from jax.experimental import pallas as pl
from jax.experimental.pallas import tpu as pltpu
from jax.sharding import PartitionSpec as P

F32 = jnp.float32
BF16 = jnp.bfloat16
LAST = (((1,), (1,)), ((), ()))
FIRST = (((0,), (0,)), ((), ()))


def dot(a, b, dims=(((1,), (0,)), ((), ()))):
    return lax.dot_general(a, b, dims, preferred_element_type=F32)


def unit_rows(values):
    inverse = lax.rsqrt(jnp.sum(values * values, axis=-1, keepdims=True) + 1e-06)
    return values * inverse, inverse


def standardize(rows):
    values = rows.astype(F32)
    centred = values - jnp.mean(values, axis=-1, keepdims=True)
    inverse = lax.rsqrt(jnp.mean(centred * centred, axis=-1, keepdims=True) + 1e-06)
    return centred * inverse, inverse


def send(value, axis, target):
    count = lax.axis_size(axis)
    return lax.ppermute(value, axis, [(p, target(p)) for p in range(count)])


def gather_group(value, count):
    mine = [value]
    for step in range(1, count // 2):
        mine.append(send(value, "loop", lambda p: (p + 2 * step) % count))
    mates = [send(block, "loop", lambda p: p ^ 1) for block in mine]
    return mine + mates


def local_any_size(features, text, proj, gain, scale, bias):
    n = lax.axis_size("loop")
    m = lax.axis_size("rep")
    me = lax.axis_index("loop")
    half = n // 2
    rows, width = features.shape[0], features.shape[2]
    columns = proj.shape[1] // n
    group_rows = rows * n
    logit_scale, logit_bias = scale[0], bias[0]

    own_features = features[:, 0, :]
    own_text = text[:, 0, :]
    text_blocks = gather_group(own_text, n)
    feature_blocks = gather_group(own_features, n)

    xhat, deviation = standardize(own_features)
    normed = (xhat * gain).astype(BF16)
    img_dir, img_inv = unit_rows(dot(normed, proj))
    img_unit = img_dir.astype(BF16)

    txt_dir, txt_inv = unit_rows(own_text.astype(F32))
    own_txt_unit = txt_dir.astype(BF16)
    txt_unit = jnp.concatenate(
        [own_txt_unit] + [unit_rows(block.astype(F32))[0].astype(BF16) for block in text_blocks[1:]]
    )
    row_ids = lax.broadcasted_iota(jnp.int32, (rows, group_rows), 0)
    column_ids = lax.broadcasted_iota(jnp.int32, (rows, group_rows), 1)
    diagonal = (row_ids == column_ids).astype(F32)

    def weights(left, right):
        logits = logit_scale * dot(left, right, LAST) + logit_bias
        return (jax.nn.sigmoid(logits) - diagonal).astype(BF16)

    img_back = logit_scale * dot(weights(img_unit, txt_unit), txt_unit)
    proj_back = (
        (img_back - img_dir * jnp.sum(img_dir * img_back, axis=-1, keepdims=True)) * img_inv
    ).astype(BF16)

    blocks = jnp.transpose(proj_back.reshape(rows, n, columns), (1, 0, 2))
    blocks = lax.all_to_all(blocks, "loop", 0, 0, tiled=True)
    back_columns = blocks.reshape(group_rows, columns)

    norm_back = dot(proj_back, proj, LAST)
    scaled = norm_back * gain
    feature_grad = (
        deviation
        * (
            scaled
            - jnp.mean(scaled, axis=-1, keepdims=True)
            - xhat * jnp.mean(scaled * xhat, axis=-1, keepdims=True)
        )
    ).astype(BF16)
    gain_term = jnp.sum(norm_back * xhat, axis=0) * (1.0 / group_rows)

    other_normed = [(standardize(block)[0] * gain).astype(BF16) for block in feature_blocks[1:]]
    relative = jnp.stack([normed] + other_normed)
    member = jnp.arange(n)
    same_core = (member % 2) == (me % 2)
    chips_back = ((me // 2 - member // 2) % half)
    position = jnp.where(same_core, chips_back, half + chips_back)
    group_normed = relative[position].reshape(group_rows, width)

    partial = (dot(group_normed, back_columns, FIRST) * (1.0 / group_rows)).astype(BF16)
    pieces = lax.all_to_all(partial.reshape(m, width // m, columns), "rep", 0, 0, tiled=True)
    reduced = jnp.sum(pieces.astype(F32), axis=0).astype(BF16)
    gains = lax.all_gather(gain_term, "rep")
    gain_sum = jnp.sum(gains, axis=0)
    proj_rows = lax.all_gather(reduced, "loop")
    proj_grad = jnp.transpose(proj_rows, (1, 0, 2)).reshape(width // m, n * columns).astype(F32)
    gain_gradient = jnp.sum(lax.all_gather(gain_sum, "loop"), axis=0)

    group_unit = jnp.concatenate(
        [img_unit] + [unit_rows(dot(block, proj))[0].astype(BF16) for block in other_normed]
    )
    text_weights = weights(own_txt_unit, group_unit)
    txt_back = logit_scale * dot(text_weights, group_unit)
    text_grad = (
        (txt_back - txt_dir * jnp.sum(txt_dir * txt_back, axis=-1, keepdims=True)) * txt_inv
    ).astype(BF16)
    return feature_grad[:, None, :], text_grad[:, None, :], proj_grad, gain_gradient


VMEM = pl.BlockSpec(memory_space=pltpu.VMEM)
SMEM = pl.BlockSpec(memory_space=pltpu.SMEM)
HBM = pl.BlockSpec(memory_space=pltpu.HBM)
LANES = 128
BAND = 16
TOKEN = ((8, LANES), F32)


def call(body, outs, scratch=(), smem=0, hbm=0, limit=24, flops=0, moved=0):
    def run(*operands):
        specs = [SMEM] * smem + [HBM] * hbm + [VMEM] * (len(operands) - smem - hbm)
        return pl.pallas_call(
            body,
            out_shape=[jax.ShapeDtypeStruct(shape, kind) for shape, kind in outs],
            in_specs=specs,
            out_specs=[VMEM] * len(outs),
            scratch_shapes=[pltpu.VMEM(shape, kind) for shape, kind in scratch]
            + [pltpu.SemaphoreType.DMA((hbm,))] * bool(hbm),
            compiler_params=pltpu.CompilerParams(vmem_limit_bytes=limit * 2**20),
            cost_estimate=pl.CostEstimate(flops=flops, bytes_accessed=moved, transcendentals=0),
        )(*operands)

    return run


def over_rows(count, step, body):
    def turn(index, _):
        body(pl.ds(pl.multiple_of(index * step, step), step))
        return 0

    lax.fori_loop(0, count // step, turn, 0, unroll=min(4, count // step))


def sums(values):
    return jnp.sum(values, axis=-1, keepdims=True)


def normalize_into(source, gain, target, at):
    rows, width = source.shape

    def chunk(where):
        values = source[where, :].astype(F32)
        centred = values - sums(values) * (1.0 / width)
        inverse = lax.rsqrt(sums(centred * centred) * (1.0 / width) + 1e-06)
        target[pl.ds(at + where.start, where.size), :] = (centred * inverse * gain[...]).astype(BF16)

    over_rows(rows, 32, chunk)


def unit_into(source, target, at, inverses=None):
    rows = source.shape[0]

    def chunk(where):
        values = source[where, :].astype(F32)
        inverse = lax.rsqrt(sums(values * values) + 1e-06)
        place = pl.ds(at + where.start, where.size)
        target[place, :] = (values * inverse).astype(BF16)
        if inverses is not None:
            inverses[place, :] = jnp.broadcast_to(inverse, (where.size, LANES))

    over_rows(rows, 32, chunk)


def weigh(dots, scale, bias, diagonal, weights):
    texts, images = dots.shape

    def chunk(index, total):
        where = pl.ds(pl.multiple_of(index * BAND, BAND), BAND)
        product = dots[where, :]
        weight = jnp.tanh((0.5 * scale) * product + 0.5 * bias)
        offset = 0.5
        if diagonal is not None:
            text = index * BAND + diagonal + lax.broadcasted_iota(jnp.int32, product.shape, 0)
            image = lax.broadcasted_iota(jnp.int32, product.shape, 1)
            offset = jnp.where(text == image, -0.5, 0.5)
        weight = (0.5 * weight + offset).astype(BF16)
        weights[where, :] = weight
        both = weight.astype(F32) * product
        return total + both[:8, :] + both[8:, :]

    total = lax.fori_loop(0, texts // BAND, chunk, jnp.zeros((8, images), F32), unroll=4)
    return jnp.sum(total, axis=0, keepdims=True)


def take_columns(place, source, target):
    columns = target.shape[1]
    for member in range(source.shape[1] // columns):

        @pl.when(place[0] == member)
        def _():
            target[...] = source[:, member * columns : (member + 1) * columns]


def near_body(
    f0_far, proj_far, t0_far, f1, t1, gain,
    f0, proj, t0, normed, unit, factors, text_unit, token, projected, semaphores,
):
    rows = f0.shape[0]
    copies = [
        pltpu.make_async_copy(source, target, semaphores.at[at])
        for at, (source, target) in enumerate(((f0_far, f0), (proj_far, proj), (t0_far, t0)))
    ]
    for copy in copies:
        copy.start()
    normalize_into(f1, gain, normed, rows)
    unit_into(t1, text_unit, rows)
    copies[0].wait()
    normalize_into(f0, gain, normed, 0)
    copies[1].wait()
    projected[...] = dot(normed[...], proj[...])
    copies[2].wait()
    unit_into(t0, text_unit, 0)
    unit_into(projected, unit, 0, factors)
    token[...] = jnp.zeros_like(token)


def near_pairs_body(
    scale, bias, place, normed, unit, factors, text_unit, proj, before,
    normed_turned, unit_turned, inverse, text_columns, weights, totals, proj_columns, dots, turned,
):
    dots[...] = dot(text_unit[...], unit[...], LAST)
    totals[...] = weigh(dots, scale[0], bias[0], 0, weights)
    take_columns(place, text_unit, text_columns)
    take_columns(place, proj, proj_columns)
    turn_own(place, unit, factors, turned, unit_turned, inverse)
    normed_turned[...] = normed[...].T


def turn_own(place, unit, factors, turned, unit_turned, inverse):
    columns = unit_turned.shape[0]
    turned[...] = unit[...].T
    unit_turned[...] = turned[pl.ds(pl.multiple_of(place[0] * columns, BAND), columns), :]
    inverse[...] = factors[...].T[:1, :]


def far_body(
    scale, bias, place, f2, f3, proj, gain, text_near, before,
    normed_turned, unit, unit_turned, inverse, weights, totals, token,
    normed, projected, dots, turned, factors,
):
    rows = f2.shape[0]
    normalize_into(f2, gain, normed, 0)
    normalize_into(f3, gain, normed, rows)
    projected[...] = dot(normed[...], proj[...])
    unit_into(projected, unit, 0, factors)
    dots[...] = dot(text_near[...], unit[...], LAST)
    totals[...] = weigh(dots, scale[0], bias[0], None, weights)
    turn_own(place, unit, factors, turned, unit_turned, inverse)
    normed_turned[...] = normed[...].T
    token[...] = jnp.zeros_like(token)


def third_body(
    scale, bias, place, t2, unit_near, unit_far, weights_near, weights_far, totals_near, totals_far, text_columns_near,
    before, text_unit, weights, back_near, back_far, totals,
    text_columns, dots,
):
    rows = t2.shape[0]
    near = 2 * rows
    unit_into(t2, text_unit, 0)
    take_columns(place, text_unit, text_columns)
    dots[:, :near] = dot(text_unit[...], unit_near[...], LAST)
    dots[:, near:] = dot(text_unit[...], unit_far[...], LAST)
    added = weigh(dots, scale[0], bias[0], near, weights)
    totals[:, :near] = totals_near[...] + added[:, :near]
    totals[:, near:] = totals_far[...] + added[:, near:]
    back_near[...] = dot(text_columns_near[...], weights_near[...], FIRST) + dot(
        text_columns[...], weights[:, :near], FIRST
    )
    back_far[...] = dot(text_columns_near[...], weights_far[...], FIRST) + dot(
        text_columns[...], weights[:, near:], FIRST
    )


def pack_into(target, block, full):
    rows, columns = block.shape
    rest = columns - full
    target[:rows, :] = block[:, :full].astype(BF16)
    per_band = full // rest
    tail = block[:, full:]
    chunks = [tail[at : at + BAND, :] for at in range(0, rows, BAND)]
    for band in range(0, len(chunks), per_band):
        part = chunks[band : band + per_band]
        if len(part) < per_band:
            part.append(jnp.zeros((BAND, full - rest * len(part)), block.dtype))
        at = rows + (band // per_band) * BAND
        target[at : at + BAND, :] = jnp.concatenate(part, axis=1).astype(BF16)


def partial_body(
    members, groups, lead, scale, bias, place, t3, unit_near, unit_far, totals, back_near, back_far, unit_turned_near,
    unit_turned_far, inverse_near, inverse_far, turned_near, turned_far, proj_columns, gain, *refs,
):
    (across, keep_lead, keep_tail), refs = refs[:3], refs[3:]
    along, refs = refs[: groups // 2 - 1], refs[groups // 2 - 1 :]
    text_unit, weights, text_columns, dots, packed = refs
    rows = t3.shape[0]
    near = 2 * rows
    every = members * rows
    width = unit_near.shape[1]
    columns = width // members
    count, full = packed.shape[1:]
    scale, bias = scale[0], bias[0]
    unit_into(t3, text_unit, 0)
    take_columns(place, text_unit, text_columns)
    dots[:, :near] = dot(text_unit[...], unit_near[...], LAST)
    dots[:, near:] = dot(text_unit[...], unit_far[...], LAST)
    total = totals[...] + weigh(dots, scale, bias, near + rows, weights)
    product = None
    for where, earlier, unit_turned, inverse, turned in (
        (slice(0, near), back_near, unit_turned_near, inverse_near, turned_near),
        (slice(near, every), back_far, unit_turned_far, inverse_far, turned_far),
    ):
        whole = earlier[...] + dot(text_columns[...], weights[:, where], FIRST)
        back = (whole - unit_turned[...].astype(F32) * total[:, where]) * (inverse[...] * scale)
        part = dot(turned[...], back.astype(BF16), LAST)
        product = part if product is None else product + part
    each = width // groups
    product = product * (1.0 / every)
    for group in range(groups):
        pack_into(packed.at[group], product[group * each : (group + 1) * each, :], full)

    terms = product * proj_columns[...].astype(F32)
    folded = jnp.concatenate([terms[:, full:], jnp.zeros((width, full + LANES - columns), F32)], axis=1)
    for at in range(0, full, LANES):
        folded = folded + terms[:, at : at + LANES]
    high = folded.astype(BF16)
    low = (folded - high.astype(F32)).astype(BF16)
    ones = jnp.ones((BAND, 2 * LANES), BF16)
    gain_row = dot(ones, jnp.concatenate([high, low], axis=1), LAST)[:1, :] / gain[...]
    pieces = [gain_row[:, at : at + LANES] for at in range(0, width, LANES)]
    pieces.append(jnp.zeros((BAND - len(pieces), LANES), F32))
    gain_tile = jnp.concatenate(pieces, axis=0).astype(BF16)
    for group in range(groups):
        packed[group, count - BAND :, full - LANES :] = gain_tile

    own = place[1]
    for step in range(groups // 2):
        across[step] = packed[own ^ 1 ^ (2 * step), :lead, :]
        keep_lead[step] = packed[own ^ (2 * step), :lead, :]
    for other in range(2):
        keep_tail[other] = packed[own ^ other, lead:, :]
        for step in range(1, groups // 2):
            along[step - 1][other] = packed[own ^ (2 * step) ^ other, lead:, :]


def image_body(
    scale, features, proj, gain, text_near, text_third, text_fourth, weights_near, weights_third, weights_fourth,
    unit, factors, feature_grad, token, back, product,
):
    rows, width = features.shape
    scale = scale[0]
    product[...] = (
        dot(weights_near[:, :rows], text_near[...], FIRST)
        + dot(weights_third[:, :rows], text_third[...], FIRST)
        + dot(weights_fourth[:, :rows], text_fourth[...], FIRST)
    )

    def image_chunk(where):
        values = product[where, :] * scale
        direction = unit[where, :].astype(F32)
        back[where, :] = (
            (values - direction * sums(direction * values)) * factors[where, :1]
        ).astype(BF16)

    over_rows(rows, 32, image_chunk)
    product[...] = dot(back[...], proj[...], LAST)

    def feature_chunk(where):
        values = features[where, :].astype(F32)
        centred = values - sums(values) * (1.0 / width)
        deviation = lax.rsqrt(sums(centred * centred) * (1.0 / width) + 1e-06)
        xhat = centred * deviation
        scaled = product[where, :] * gain[...]
        feature_grad[where, :] = (
            deviation
            * (scaled - sums(scaled) * (1.0 / width) - xhat * (sums(scaled * xhat) * (1.0 / width)))
        ).astype(BF16)

    over_rows(rows, 32, feature_chunk)
    token[...] = jnp.zeros_like(token)


def text_body(scale, text, weights_near, weights_far, unit_near, unit_far, text_grad, token, product):
    rows = text.shape[0]
    scale = scale[0]
    product[...] = dot(weights_near[:rows, :], unit_near[...]) + dot(weights_far[:rows, :], unit_far[...])

    def text_chunk(where):
        values = product[where, :] * scale
        own = text[where, :].astype(F32)
        own_inverse = lax.rsqrt(sums(own * own) + 1e-06)
        direction = own * own_inverse
        text_grad[where, :] = (
            (values - direction * sums(direction * values)) * own_inverse
        ).astype(BF16)

    over_rows(rows, 32, text_chunk)
    token[...] = jnp.zeros_like(token)


def first_sum_body(place, token, keep_lead, across, keep_tail, *refs):
    steps = keep_lead.shape[0]
    along, refs = refs[: steps - 1], refs[steps - 1 :]
    leads, (tail, tail_across, ordered) = refs[:steps], refs[steps:]
    for step in range(steps):
        leads[step][...] = (keep_lead[step].astype(F32) + across[step].astype(F32)).astype(BF16)
    own = place[1] // 2
    ordered[own] = keep_tail[...]
    for step in range(1, steps):
        ordered[own ^ step] = along[steps - 1 - step][...]
    value = ordered[0].astype(F32)
    for step in range(1, steps):
        value = value + ordered[step].astype(F32)
    tail[...] = value[0].astype(BF16)
    tail_across[...] = value[1].astype(BF16)


def last_sum_body(tail, tail_across, *refs):
    leads, total = refs[:-1], refs[-1]
    split = leads[0].shape[0]
    value = leads[0][...].astype(F32)
    for lead in leads[1:]:
        value = value + lead[...].astype(F32)
    total[:split, :] = value.astype(BF16)
    total[split:, :] = (tail[...].astype(F32) + tail_across[...].astype(F32)).astype(BF16)


def finish_body(members, place, *refs):
    packets, (proj_grad, gain_gradient, ordered) = refs[:members], refs[members:]
    count, full = packets[0].shape
    rows, width = proj_grad.shape
    columns = width // members
    rest = columns - full
    per_band = full // rest
    for own in range(members):

        @pl.when(place[0] == own)
        def _():
            for k in range(members):
                base = (own ^ k) * columns
                packet = packets[k]
                main = packet[:rows, :].astype(F32)
                tails = []
                for index in range(rows // BAND):
                    at = rows + (index // per_band) * BAND
                    lane = (index % per_band) * rest
                    tails.append(packet[at : at + BAND, lane : lane + rest].astype(F32))
                proj_grad[:, base : base + full] = main
                proj_grad[:, base + full : base + columns] = jnp.concatenate(tails, axis=0)

    for k in range(members):
        ordered[place[0] ^ k] = packets[k][count - BAND :, full - LANES :].astype(F32)
    value = ordered[0]
    for member in range(1, members):
        value = value + ordered[member]
    for at in range(width // LANES):
        gain_gradient[at * LANES : (at + 1) * LANES] = value[at]


def local_four(features, text, proj, gain, scale, bias):
    members = lax.axis_size("loop")
    groups = lax.axis_size("rep")
    place = jnp.stack([lax.axis_index("loop"), lax.axis_index("rep")]).astype(jnp.int32)
    rows, width = features.shape[0], features.shape[2]
    near, every = 2 * rows, 4 * rows
    columns = width // members
    full = columns // LANES * LANES
    each = width // groups
    bands = -(-(each // BAND) // (full // (columns - full)))
    packet = (each + bands * BAND, full)
    gain_row = gain.reshape(1, width)

    lead = (3 * packet[0] // BAND // 4) * BAND
    tail = packet[0] - lead
    steps = groups // 2

    f0, t0 = features[:, 0, :], text[:, 0, :]
    f2 = send(f0, "loop", lambda p: p ^ 2)
    f1 = send(f0, "loop", lambda p: p ^ 1)
    t1 = send(t0, "loop", lambda p: p ^ 1)

    wide, half = ((near, width), BF16), ((rows, width), BF16)
    square, part, turned = ((near, near), BF16), ((near, columns), BF16), ((width, near), BF16)

    line, mine = ((1, near), F32), ((columns, near), BF16)
    kept = ((width, width), BF16)
    f0_kept, proj_kept, t0_kept, normed_near, unit_near, factors, text_near, token = call(
        near_body,
        [half, kept, half, wide, wide, ((near, LANES), F32), wide, TOKEN],
        [((near, width), F32)],
        hbm=3,
        limit=36,
        flops=2 * near * width * width,
        moved=8 * near * width,
    )(f0, proj, t0, f1, t1, gain_row)

    t_after, f2_after, token = lax.optimization_barrier((t0, f2, token))
    t2 = send(t_after, "loop", lambda p: p ^ 2)
    f3 = send(f2_after, "loop", lambda p: p ^ 1)

    (
        turned_near, unit_turned_near, inverse_near, text_columns_near, weights_near, totals_near, proj_columns,
    ) = call(
        near_pairs_body,
        [turned, mine, line, part, square, line, ((width, columns), BF16)],
        [((near, near), F32), turned],
        smem=3,
        flops=near * width * width,
        moved=8 * near * width,
    )(scale, bias, place, normed_near, unit_near, factors, text_near, proj_kept, token)

    turned_far, unit_far, unit_turned_far, inverse_far, weights_far, totals_far, token = call(
        far_body,
        [turned, wide, mine, line, square, line, TOKEN],
        [wide, ((near, width), F32), ((near, near), F32), turned, ((near, LANES), F32)],
        smem=3,
        flops=3 * near * width * width,
        moved=8 * near * width,
    )(scale, bias, place, f2, f3, proj_kept, gain_row, text_near, totals_near)

    text_grad, token = call(
        text_body,
        [half, TOKEN],
        [((rows, width), F32)],
        smem=1,
        flops=2 * near * width * width,
        moved=6 * near * width,
    )(scale, t0_kept, weights_near, weights_far, unit_near, unit_far)

    t2_after, token = lax.optimization_barrier((t2, token))
    t3 = send(t2_after, "loop", lambda p: p ^ 1)

    narrow, back_kind = ((rows, every), BF16), ((columns, near), F32)
    text_third, weights_third, back_near, back_far, totals = call(
        third_body,
        [half, narrow, back_kind, back_kind, ((1, every), F32)],
        [((rows, columns), BF16), ((rows, every), F32)],
        smem=3,
        flops=2 * near * width * width,
        moved=8 * near * width,
    )(
        scale, bias, place, t2, unit_near, unit_far, weights_near, weights_far, totals_near, totals_far,
        text_columns_near, token,
    )

    outs = call(
        functools.partial(partial_body, members, groups, lead),
        [((steps, lead, full), BF16), ((steps, lead, full), BF16)] + [((2, tail, full), BF16)] * steps + [half, narrow],
        [((rows, columns), BF16), ((rows, every), F32), ((groups,) + packet, BF16)],
        smem=3,
        flops=4 * near * width * width,
        moved=16 * near * width,
    )(
        scale, bias, place, t3, unit_near, unit_far, totals, back_near, back_far, unit_turned_near, unit_turned_far,
        inverse_near, inverse_far, turned_near, turned_far, proj_columns, gain_row,
    )
    across, keep_lead, keep_tail = outs[:3]
    along, (text_fourth, weights_fourth) = outs[3 : 2 + steps], outs[2 + steps :]

    across = send(across, "rep", lambda p: p ^ 1)
    along = [send(along[step - 1], "rep", lambda p: p ^ (2 * step)) for step in reversed(range(1, steps))]

    feature_grad, token = call(
        image_body,
        [half, TOKEN],
        [half, ((rows, width), F32)],
        smem=1,
        flops=4 * near * width * width,
        moved=12 * near * width,
    )(
        scale, f0_kept, proj_kept, gain_row, text_near, text_third, text_fourth, weights_near, weights_third,
        weights_fourth, unit_near, factors,
    )

    outs = call(
        first_sum_body,
        [((lead, full), BF16)] * steps + [((tail, full), BF16)] * 2,
        [((steps, 2, tail, full), BF16)],
        smem=1,
        moved=4 * each * width,
    )(place, token, keep_lead, across, keep_tail, *along)
    leads = [outs[0]] + [send(outs[step], "rep", lambda p: p ^ (2 * step)) for step in reversed(range(1, steps))]
    tail_across = send(outs[steps + 1], "rep", lambda p: p ^ 1)

    (reduced,) = call(
        last_sum_body,
        [(packet, BF16)],
        moved=4 * each * width,
    )(outs[steps], tail_across, *leads)
    far_block = send(reduced, "loop", lambda p: p ^ 2)
    near_block = send(reduced, "loop", lambda p: p ^ 1)
    blocks = [reduced, near_block, far_block, send(far_block, "loop", lambda p: p ^ 1)]

    proj_grad, gain_gradient = call(
        functools.partial(finish_body, members),
        [((each, width), F32), ((width,), F32)],
        [((members, BAND, LANES), F32)],
        smem=1,
        moved=8 * each * width,
    )(place, *blocks)
    return feature_grad[:, None, :], text_grad[:, None, :], proj_grad, gain_gradient


def four_fits(mesh, rows_shape):
    members, groups = mesh.shape["loop"], mesh.shape["rep"]
    rows, width = rows_shape[0] // members, rows_shape[2]
    if members != 4 or groups & (groups - 1) or width % (members * groups) or width % LANES:
        return False
    columns, each = width // members, width // groups
    full = columns // LANES * LANES
    rest = columns - full
    if rest == 0 or full < LANES or full % rest or each % BAND or rows % 64 or width // LANES > BAND:
        return False
    chunks = each // BAND
    used = (chunks - 1) % (full // rest) + 1
    return used * rest <= full - LANES


def solution(mesh):
    def run(features, text, proj, gain, scale, bias):
        body = local_four if four_fits(mesh, features.shape) else local_any_size
        return jax.shard_map(
            body,
            mesh=mesh,
            in_specs=(P("loop", "rep", None), P("loop", "rep", None), P(), P(), P(), P()),
            out_specs=(P("loop", "rep", None), P("loop", "rep", None), P("rep", None), P()),
            check_vma=False,
        )(features, text, proj, gain, scale, bias)

    return run
```

```python
import functools

import jax
import jax.numpy as jnp
from jax import lax
from jax.experimental import pallas as pl
from jax.experimental.pallas import tpu as pltpu
from jax.sharding import PartitionSpec as P

F32 = jnp.float32
BF16 = jnp.bfloat16
LAST = (((1,), (1,)), ((), ()))
FIRST = (((0,), (0,)), ((), ()))


def dot(a, b, dims=(((1,), (0,)), ((), ()))):
    return lax.dot_general(a, b, dims, preferred_element_type=F32)


def unit_rows(values):
    inverse = lax.rsqrt(jnp.sum(values * values, axis=-1, keepdims=True) + 1e-06)
    return values * inverse, inverse


def standardize(rows):
    values = rows.astype(F32)
    centred = values - jnp.mean(values, axis=-1, keepdims=True)
    inverse = lax.rsqrt(jnp.mean(centred * centred, axis=-1, keepdims=True) + 1e-06)
    return centred * inverse, inverse


def send(value, axis, target):
    count = lax.axis_size(axis)
    return lax.ppermute(value, axis, [(p, target(p)) for p in range(count)])


def gather_group(value, count):
    mine = [value]
    for step in range(1, count // 2):
        mine.append(send(value, "loop", lambda p: (p + 2 * step) % count))
    mates = [send(block, "loop", lambda p: p ^ 1) for block in mine]
    return mine + mates


def local_any_size(features, text, proj, gain, scale, bias):
    n = lax.axis_size("loop")
    m = lax.axis_size("rep")
    me = lax.axis_index("loop")
    half = n // 2
    rows, width = features.shape[0], features.shape[2]
    columns = proj.shape[1] // n
    group_rows = rows * n
    logit_scale, logit_bias = scale[0], bias[0]

    own_features = features[:, 0, :]
    own_text = text[:, 0, :]
    text_blocks = gather_group(own_text, n)
    feature_blocks = gather_group(own_features, n)

    xhat, deviation = standardize(own_features)
    normed = (xhat * gain).astype(BF16)
    img_dir, img_inv = unit_rows(dot(normed, proj))
    img_unit = img_dir.astype(BF16)

    txt_dir, txt_inv = unit_rows(own_text.astype(F32))
    own_txt_unit = txt_dir.astype(BF16)
    txt_unit = jnp.concatenate(
        [own_txt_unit] + [unit_rows(block.astype(F32))[0].astype(BF16) for block in text_blocks[1:]]
    )
    row_ids = lax.broadcasted_iota(jnp.int32, (rows, group_rows), 0)
    column_ids = lax.broadcasted_iota(jnp.int32, (rows, group_rows), 1)
    diagonal = (row_ids == column_ids).astype(F32)

    def weights(left, right):
        logits = logit_scale * dot(left, right, LAST) + logit_bias
        return (jax.nn.sigmoid(logits) - diagonal).astype(BF16)

    img_back = logit_scale * dot(weights(img_unit, txt_unit), txt_unit)
    proj_back = (
        (img_back - img_dir * jnp.sum(img_dir * img_back, axis=-1, keepdims=True)) * img_inv
    ).astype(BF16)

    blocks = jnp.transpose(proj_back.reshape(rows, n, columns), (1, 0, 2))
    blocks = lax.all_to_all(blocks, "loop", 0, 0, tiled=True)
    back_columns = blocks.reshape(group_rows, columns)

    norm_back = dot(proj_back, proj, LAST)
    scaled = norm_back * gain
    feature_grad = (
        deviation
        * (
            scaled
            - jnp.mean(scaled, axis=-1, keepdims=True)
            - xhat * jnp.mean(scaled * xhat, axis=-1, keepdims=True)
        )
    ).astype(BF16)
    gain_term = jnp.sum(norm_back * xhat, axis=0) * (1.0 / group_rows)

    other_normed = [(standardize(block)[0] * gain).astype(BF16) for block in feature_blocks[1:]]
    relative = jnp.stack([normed] + other_normed)
    member = jnp.arange(n)
    same_core = (member % 2) == (me % 2)
    chips_back = ((me // 2 - member // 2) % half)
    position = jnp.where(same_core, chips_back, half + chips_back)
    group_normed = relative[position].reshape(group_rows, width)

    partial = (dot(group_normed, back_columns, FIRST) * (1.0 / group_rows)).astype(BF16)
    pieces = lax.all_to_all(partial.reshape(m, width // m, columns), "rep", 0, 0, tiled=True)
    reduced = jnp.sum(pieces.astype(F32), axis=0).astype(BF16)
    gains = lax.all_gather(gain_term, "rep")
    gain_sum = jnp.sum(gains, axis=0)
    proj_rows = lax.all_gather(reduced, "loop")
    proj_grad = jnp.transpose(proj_rows, (1, 0, 2)).reshape(width // m, n * columns).astype(F32)
    gain_gradient = jnp.sum(lax.all_gather(gain_sum, "loop"), axis=0)

    group_unit = jnp.concatenate(
        [img_unit] + [unit_rows(dot(block, proj))[0].astype(BF16) for block in other_normed]
    )
    text_weights = weights(own_txt_unit, group_unit)
    txt_back = logit_scale * dot(text_weights, group_unit)
    text_grad = (
        (txt_back - txt_dir * jnp.sum(txt_dir * txt_back, axis=-1, keepdims=True)) * txt_inv
    ).astype(BF16)
    return feature_grad[:, None, :], text_grad[:, None, :], proj_grad, gain_gradient


VMEM = pl.BlockSpec(memory_space=pltpu.VMEM)
SMEM = pl.BlockSpec(memory_space=pltpu.SMEM)
HBM = pl.BlockSpec(memory_space=pltpu.HBM)
LANES = 128
BAND = 16
TOKEN = ((8, LANES), F32)


def call(body, outs, scratch=(), smem=0, hbm=0, limit=24, flops=0, moved=0):
    def run(*operands):
        specs = [SMEM] * smem + [HBM] * hbm + [VMEM] * (len(operands) - smem - hbm)
        return pl.pallas_call(
            body,
            out_shape=[jax.ShapeDtypeStruct(shape, kind) for shape, kind in outs],
            in_specs=specs,
            out_specs=[VMEM] * len(outs),
            scratch_shapes=[pltpu.VMEM(shape, kind) for shape, kind in scratch]
            + [pltpu.SemaphoreType.DMA((hbm,))] * bool(hbm),
            compiler_params=pltpu.CompilerParams(vmem_limit_bytes=limit * 2**20),
            cost_estimate=pl.CostEstimate(flops=flops, bytes_accessed=moved, transcendentals=0),
        )(*operands)

    return run


def over_rows(count, step, body):
    def turn(index, _):
        body(pl.ds(pl.multiple_of(index * step, step), step))
        return 0

    lax.fori_loop(0, count // step, turn, 0, unroll=min(4, count // step))


def sums(values):
    return jnp.sum(values, axis=-1, keepdims=True)


def normalize_into(source, gain, target, at):
    rows, width = source.shape

    def chunk(where):
        values = source[where, :].astype(F32)
        centred = values - sums(values) * (1.0 / width)
        inverse = lax.rsqrt(sums(centred * centred) * (1.0 / width) + 1e-06)
        target[pl.ds(at + where.start, where.size), :] = (centred * inverse * gain[...]).astype(BF16)

    over_rows(rows, 32, chunk)


def unit_into(source, target, at, inverses=None):
    rows = source.shape[0]

    def chunk(where):
        values = source[where, :].astype(F32)
        inverse = lax.rsqrt(sums(values * values) + 1e-06)
        place = pl.ds(at + where.start, where.size)
        target[place, :] = (values * inverse).astype(BF16)
        if inverses is not None:
            inverses[place, :] = jnp.broadcast_to(inverse, (where.size, LANES))

    over_rows(rows, 32, chunk)


def weigh(dots, scale, bias, diagonal, weights):
    texts, images = dots.shape

    def chunk(index, total):
        where = pl.ds(pl.multiple_of(index * BAND, BAND), BAND)
        product = dots[where, :]
        weight = jnp.tanh((0.5 * scale) * product + 0.5 * bias)
        offset = 0.5
        if diagonal is not None:
            text = index * BAND + diagonal + lax.broadcasted_iota(jnp.int32, product.shape, 0)
            image = lax.broadcasted_iota(jnp.int32, product.shape, 1)
            offset = jnp.where(text == image, -0.5, 0.5)
        weight = (0.5 * weight + offset).astype(BF16)
        weights[where, :] = weight
        both = weight.astype(F32) * product
        return total + both[:8, :] + both[8:, :]

    total = lax.fori_loop(0, texts // BAND, chunk, jnp.zeros((8, images), F32), unroll=4)
    return jnp.sum(total, axis=0, keepdims=True)


def take_columns(place, source, target):
    columns = target.shape[1]
    for member in range(source.shape[1] // columns):

        @pl.when(place[0] == member)
        def _():
            target[...] = source[:, member * columns : (member + 1) * columns]


def near_body(
    scale, bias, place, f0_far, proj_far, t0_far, f1, t1, gain,
    f0, proj, t0, normed, unit, factors, text_unit, token, projected, semaphores,
):
    rows = f0.shape[0]
    copies = [
        pltpu.make_async_copy(source, target, semaphores.at[at])
        for at, (source, target) in enumerate(((f0_far, f0), (proj_far, proj), (t0_far, t0)))
    ]
    for copy in copies:
        copy.start()
    normalize_into(f1, gain, normed, rows)
    unit_into(t1, text_unit, rows)
    copies[0].wait()
    normalize_into(f0, gain, normed, 0)
    copies[1].wait()
    projected[...] = dot(normed[...], proj[...])
    copies[2].wait()
    unit_into(t0, text_unit, 0)
    unit_into(projected, unit, 0, factors)
    token[...] = jnp.zeros_like(token)


def near_pairs_body(
    scale, bias, place, normed, unit, factors, text_unit, proj, before,
    normed_turned, unit_turned, inverse, text_columns, weights, totals, proj_columns, dots, turned,
):
    dots[...] = dot(text_unit[...], unit[...], LAST)
    totals[...] = weigh(dots, scale[0], bias[0], 0, weights)
    take_columns(place, text_unit, text_columns)
    take_columns(place, proj, proj_columns)
    turn_own(place, unit, factors, turned, unit_turned, inverse)
    normed_turned[...] = normed[...].T


def turn_own(place, unit, factors, turned, unit_turned, inverse):
    columns = unit_turned.shape[0]
    turned[...] = unit[...].T
    unit_turned[...] = turned[pl.ds(pl.multiple_of(place[0] * columns, BAND), columns), :]
    inverse[...] = factors[...].T[:1, :]


def far_body(
    scale, bias, place, f2, f3, proj, gain, text_near, before,
    normed_turned, unit, unit_turned, inverse, weights, totals, token,
    normed, projected, dots, turned, factors,
):
    rows = f2.shape[0]
    normalize_into(f2, gain, normed, 0)
    normalize_into(f3, gain, normed, rows)
    projected[...] = dot(normed[...], proj[...])
    unit_into(projected, unit, 0, factors)
    dots[...] = dot(text_near[...], unit[...], LAST)
    totals[...] = weigh(dots, scale[0], bias[0], None, weights)
    turn_own(place, unit, factors, turned, unit_turned, inverse)
    normed_turned[...] = normed[...].T
    token[...] = jnp.zeros_like(token)


def third_body(
    scale, bias, place, t2, unit_near, unit_far, weights_near, weights_far, totals_near, totals_far, text_columns_near,
    before, text_unit, weights, back_near, back_far, totals,
    text_columns, dots,
):
    rows = t2.shape[0]
    near = 2 * rows
    unit_into(t2, text_unit, 0)
    take_columns(place, text_unit, text_columns)
    dots[:, :near] = dot(text_unit[...], unit_near[...], LAST)
    dots[:, near:] = dot(text_unit[...], unit_far[...], LAST)
    added = weigh(dots, scale[0], bias[0], near, weights)
    totals[:, :near] = totals_near[...] + added[:, :near]
    totals[:, near:] = totals_far[...] + added[:, near:]
    back_near[...] = dot(text_columns_near[...], weights_near[...], FIRST) + dot(
        text_columns[...], weights[:, :near], FIRST
    )
    back_far[...] = dot(text_columns_near[...], weights_far[...], FIRST) + dot(
        text_columns[...], weights[:, near:], FIRST
    )


def pack_into(target, block, full):
    rows, columns = block.shape
    rest = columns - full
    target[:rows, :] = block[:, :full].astype(BF16)
    per_band = full // rest
    tail = block[:, full:]
    chunks = [tail[at : at + BAND, :] for at in range(0, rows, BAND)]
    for band in range(0, len(chunks), per_band):
        part = chunks[band : band + per_band]
        if len(part) < per_band:
            part.append(jnp.zeros((BAND, full - rest * len(part)), block.dtype))
        at = rows + (band // per_band) * BAND
        target[at : at + BAND, :] = jnp.concatenate(part, axis=1).astype(BF16)


def partial_body(
    members, groups, lead, scale, bias, place, t3, unit_near, unit_far, totals, back_near, back_far, unit_turned_near,
    unit_turned_far, inverse_near, inverse_far, turned_near, turned_far, proj_columns, gain, *refs,
):
    (across, keep_lead, keep_tail), refs = refs[:3], refs[3:]
    along, refs = refs[: groups // 2 - 1], refs[groups // 2 - 1 :]
    text_unit, weights, text_columns, dots, packed = refs
    rows = t3.shape[0]
    near = 2 * rows
    every = members * rows
    width = unit_near.shape[1]
    columns = width // members
    count, full = packed.shape[1:]
    scale, bias = scale[0], bias[0]
    unit_into(t3, text_unit, 0)
    take_columns(place, text_unit, text_columns)
    dots[:, :near] = dot(text_unit[...], unit_near[...], LAST)
    dots[:, near:] = dot(text_unit[...], unit_far[...], LAST)
    total = totals[...] + weigh(dots, scale, bias, near + rows, weights)
    product = None
    for where, earlier, unit_turned, inverse, turned in (
        (slice(0, near), back_near, unit_turned_near, inverse_near, turned_near),
        (slice(near, every), back_far, unit_turned_far, inverse_far, turned_far),
    ):
        whole = earlier[...] + dot(text_columns[...], weights[:, where], FIRST)
        back = (whole - unit_turned[...].astype(F32) * total[:, where]) * (inverse[...] * scale)
        part = dot(turned[...], back.astype(BF16), LAST)
        product = part if product is None else product + part
    each = width // groups
    product = product * (1.0 / every)
    for group in range(groups):
        pack_into(packed.at[group], product[group * each : (group + 1) * each, :], full)

    terms = product * proj_columns[...].astype(F32)
    folded = jnp.concatenate([terms[:, full:], jnp.zeros((width, full + LANES - columns), F32)], axis=1)
    for at in range(0, full, LANES):
        folded = folded + terms[:, at : at + LANES]
    high = folded.astype(BF16)
    low = (folded - high.astype(F32)).astype(BF16)
    ones = jnp.ones((BAND, 2 * LANES), BF16)
    gain_row = dot(ones, jnp.concatenate([high, low], axis=1), LAST)[:1, :] / gain[...]
    pieces = [gain_row[:, at : at + LANES] for at in range(0, width, LANES)]
    pieces.append(jnp.zeros((BAND - len(pieces), LANES), F32))
    gain_tile = jnp.concatenate(pieces, axis=0).astype(BF16)
    for group in range(groups):
        packed[group, count - BAND :, full - LANES :] = gain_tile

    own = place[1]
    for step in range(groups // 2):
        across[step] = packed[own ^ 1 ^ (2 * step), :lead, :]
        keep_lead[step] = packed[own ^ (2 * step), :lead, :]
    for other in range(2):
        keep_tail[other] = packed[own ^ other, lead:, :]
        for step in range(1, groups // 2):
            along[step - 1][other] = packed[own ^ (2 * step) ^ other, lead:, :]


def image_body(
    scale, features, proj, gain, text_near, text_third, text_fourth, weights_near, weights_third, weights_fourth,
    unit, factors, feature_grad, token, back, product,
):
    rows, width = features.shape
    scale = scale[0]
    product[...] = (
        dot(weights_near[:, :rows], text_near[...], FIRST)
        + dot(weights_third[:, :rows], text_third[...], FIRST)
        + dot(weights_fourth[:, :rows], text_fourth[...], FIRST)
    )

    def image_chunk(where):
        values = product[where, :] * scale
        direction = unit[where, :].astype(F32)
        back[where, :] = (
            (values - direction * sums(direction * values)) * factors[where, :1]
        ).astype(BF16)

    over_rows(rows, 32, image_chunk)
    product[...] = dot(back[...], proj[...], LAST)

    def feature_chunk(where):
        values = features[where, :].astype(F32)
        centred = values - sums(values) * (1.0 / width)
        deviation = lax.rsqrt(sums(centred * centred) * (1.0 / width) + 1e-06)
        xhat = centred * deviation
        scaled = product[where, :] * gain[...]
        feature_grad[where, :] = (
            deviation
            * (scaled - sums(scaled) * (1.0 / width) - xhat * (sums(scaled * xhat) * (1.0 / width)))
        ).astype(BF16)

    over_rows(rows, 32, feature_chunk)
    token[...] = jnp.zeros_like(token)


def text_body(scale, text, weights_near, weights_far, unit_near, unit_far, text_grad, token, product):
    rows = text.shape[0]
    scale = scale[0]
    product[...] = dot(weights_near[:rows, :], unit_near[...]) + dot(weights_far[:rows, :], unit_far[...])

    def text_chunk(where):
        values = product[where, :] * scale
        own = text[where, :].astype(F32)
        own_inverse = lax.rsqrt(sums(own * own) + 1e-06)
        direction = own * own_inverse
        text_grad[where, :] = (
            (values - direction * sums(direction * values)) * own_inverse
        ).astype(BF16)

    over_rows(rows, 32, text_chunk)
    token[...] = jnp.zeros_like(token)


def first_sum_body(place, token, keep_lead, across, keep_tail, *refs):
    steps = keep_lead.shape[0]
    along, refs = refs[: steps - 1], refs[steps - 1 :]
    leads, (tail, tail_across, ordered) = refs[:steps], refs[steps:]
    for step in range(steps):
        leads[step][...] = (keep_lead[step].astype(F32) + across[step].astype(F32)).astype(BF16)
    own = place[1] // 2
    ordered[own] = keep_tail[...]
    for step in range(1, steps):
        ordered[own ^ step] = along[steps - 1 - step][...]
    value = ordered[0].astype(F32)
    for step in range(1, steps):
        value = value + ordered[step].astype(F32)
    tail[...] = value[0].astype(BF16)
    tail_across[...] = value[1].astype(BF16)


def last_sum_body(tail, tail_across, *refs):
    leads, total = refs[:-1], refs[-1]
    split = leads[0].shape[0]
    value = leads[0][...].astype(F32)
    for lead in leads[1:]:
        value = value + lead[...].astype(F32)
    total[:split, :] = value.astype(BF16)
    total[split:, :] = (tail[...].astype(F32) + tail_across[...].astype(F32)).astype(BF16)


def finish_body(members, place, *refs):
    packets, (proj_grad, gain_gradient, ordered) = refs[:members], refs[members:]
    count, full = packets[0].shape
    rows, width = proj_grad.shape
    columns = width // members
    rest = columns - full
    per_band = full // rest
    for own in range(members):

        @pl.when(place[0] == own)
        def _():
            for k in range(members):
                base = (own ^ k) * columns
                packet = packets[k]
                main = packet[:rows, :].astype(F32)
                tails = []
                for index in range(rows // BAND):
                    at = rows + (index // per_band) * BAND
                    lane = (index % per_band) * rest
                    tails.append(packet[at : at + BAND, lane : lane + rest].astype(F32))
                proj_grad[:, base : base + full] = main
                proj_grad[:, base + full : base + columns] = jnp.concatenate(tails, axis=0)

    for k in range(members):
        ordered[place[0] ^ k] = packets[k][count - BAND :, full - LANES :].astype(F32)
    value = ordered[0]
    for member in range(1, members):
        value = value + ordered[member]
    for at in range(width // LANES):
        gain_gradient[at * LANES : (at + 1) * LANES] = value[at]


def local_four(features, text, proj, gain, scale, bias):
    members = lax.axis_size("loop")
    groups = lax.axis_size("rep")
    place = jnp.stack([lax.axis_index("loop"), lax.axis_index("rep")]).astype(jnp.int32)
    rows, width = features.shape[0], features.shape[2]
    near, every = 2 * rows, 4 * rows
    columns = width // members
    full = columns // LANES * LANES
    each = width // groups
    bands = -(-(each // BAND) // (full // (columns - full)))
    packet = (each + bands * BAND, full)
    gain_row = gain.reshape(1, width)

    lead = (3 * packet[0] // BAND // 4) * BAND
    tail = packet[0] - lead
    steps = groups // 2

    f0, t0 = features[:, 0, :], text[:, 0, :]
    f2 = send(f0, "loop", lambda p: p ^ 2)
    f1 = send(f0, "loop", lambda p: p ^ 1)
    t1 = send(t0, "loop", lambda p: p ^ 1)

    wide, half = ((near, width), BF16), ((rows, width), BF16)
    square, part, turned = ((near, near), BF16), ((near, columns), BF16), ((width, near), BF16)

    line, mine = ((1, near), F32), ((columns, near), BF16)
    kept = ((width, width), BF16)
    f0_kept, proj_kept, t0_kept, normed_near, unit_near, factors, text_near, token = call(
        near_body,
        [half, kept, half, wide, wide, ((near, LANES), F32), wide, TOKEN],
        [((near, width), F32)],
        smem=3,
        hbm=3,
        limit=36,
        flops=2 * near * width * width,
        moved=8 * near * width,
    )(scale, bias, place, f0, proj, t0, f1, t1, gain_row)

    t_after, f2_after, token = lax.optimization_barrier((t0, f2, token))
    t2 = send(t_after, "loop", lambda p: p ^ 2)
    f3 = send(f2_after, "loop", lambda p: p ^ 1)

    (
        turned_near, unit_turned_near, inverse_near, text_columns_near, weights_near, totals_near, proj_columns,
    ) = call(
        near_pairs_body,
        [turned, mine, line, part, square, line, ((width, columns), BF16)],
        [((near, near), F32), turned],
        smem=3,
        flops=near * width * width,
        moved=8 * near * width,
    )(scale, bias, place, normed_near, unit_near, factors, text_near, proj_kept, token)

    turned_far, unit_far, unit_turned_far, inverse_far, weights_far, totals_far, token = call(
        far_body,
        [turned, wide, mine, line, square, line, TOKEN],
        [wide, ((near, width), F32), ((near, near), F32), turned, ((near, LANES), F32)],
        smem=3,
        flops=3 * near * width * width,
        moved=8 * near * width,
    )(scale, bias, place, f2, f3, proj_kept, gain_row, text_near, totals_near)

    text_grad, token = call(
        text_body,
        [half, TOKEN],
        [((rows, width), F32)],
        smem=1,
        flops=2 * near * width * width,
        moved=6 * near * width,
    )(scale, t0_kept, weights_near, weights_far, unit_near, unit_far)

    t2_after, token = lax.optimization_barrier((t2, token))
    t3 = send(t2_after, "loop", lambda p: p ^ 1)

    narrow, back_kind = ((rows, every), BF16), ((columns, near), F32)
    text_third, weights_third, back_near, back_far, totals = call(
        third_body,
        [half, narrow, back_kind, back_kind, ((1, every), F32)],
        [((rows, columns), BF16), ((rows, every), F32)],
        smem=3,
        flops=2 * near * width * width,
        moved=8 * near * width,
    )(
        scale, bias, place, t2, unit_near, unit_far, weights_near, weights_far, totals_near, totals_far,
        text_columns_near, token,
    )

    outs = call(
        functools.partial(partial_body, members, groups, lead),
        [((steps, lead, full), BF16), ((steps, lead, full), BF16)] + [((2, tail, full), BF16)] * steps + [half, narrow],
        [((rows, columns), BF16), ((rows, every), F32), ((groups,) + packet, BF16)],
        smem=3,
        flops=4 * near * width * width,
        moved=16 * near * width,
    )(
        scale, bias, place, t3, unit_near, unit_far, totals, back_near, back_far, unit_turned_near, unit_turned_far,
        inverse_near, inverse_far, turned_near, turned_far, proj_columns, gain_row,
    )
    across, keep_lead, keep_tail = outs[:3]
    along, (text_fourth, weights_fourth) = outs[3 : 2 + steps], outs[2 + steps :]

    across = send(across, "rep", lambda p: p ^ 1)
    along = [send(along[step - 1], "rep", lambda p: p ^ (2 * step)) for step in reversed(range(1, steps))]

    feature_grad, token = call(
        image_body,
        [half, TOKEN],
        [half, ((rows, width), F32)],
        smem=1,
        flops=4 * near * width * width,
        moved=12 * near * width,
    )(
        scale, f0_kept, proj_kept, gain_row, text_near, text_third, text_fourth, weights_near, weights_third,
        weights_fourth, unit_near, factors,
    )

    outs = call(
        first_sum_body,
        [((lead, full), BF16)] * steps + [((tail, full), BF16)] * 2,
        [((steps, 2, tail, full), BF16)],
        smem=1,
        moved=4 * each * width,
    )(place, token, keep_lead, across, keep_tail, *along)
    leads = [outs[0]] + [send(outs[step], "rep", lambda p: p ^ (2 * step)) for step in reversed(range(1, steps))]
    tail_across = send(outs[steps + 1], "rep", lambda p: p ^ 1)

    (reduced,) = call(
        last_sum_body,
        [(packet, BF16)],
        moved=4 * each * width,
    )(outs[steps], tail_across, *leads)
    far_block = send(reduced, "loop", lambda p: p ^ 2)
    near_block = send(reduced, "loop", lambda p: p ^ 1)
    blocks = [reduced, near_block, far_block, send(far_block, "loop", lambda p: p ^ 1)]

    proj_grad, gain_gradient = call(
        functools.partial(finish_body, members),
        [((each, width), F32), ((width,), F32)],
        [((members, BAND, LANES), F32)],
        smem=1,
        moved=8 * each * width,
    )(place, *blocks)
    return feature_grad[:, None, :], text_grad[:, None, :], proj_grad, gain_gradient


def four_fits(mesh, rows_shape):
    members, groups = mesh.shape["loop"], mesh.shape["rep"]
    rows, width = rows_shape[0] // members, rows_shape[2]
    if members != 4 or groups & (groups - 1) or width % (members * groups) or width % LANES:
        return False
    columns, each = width // members, width // groups
    full = columns // LANES * LANES
    rest = columns - full
    if rest == 0 or full < LANES or full % rest or each % BAND or rows % 64 or width // LANES > BAND:
        return False
    chunks = each // BAND
    used = (chunks - 1) % (full // rest) + 1
    return used * rest <= full - LANES


def solution(mesh):
    def run(features, text, proj, gain, scale, bias):
        body = local_four if four_fits(mesh, features.shape) else local_any_size
        return jax.shard_map(
            body,
            mesh=mesh,
            in_specs=(P("loop", "rep", None), P("loop", "rep", None), P(), P(), P(), P()),
            out_specs=(P("loop", "rep", None), P("loop", "rep", None), P("rep", None), P()),
            check_vma=False,
        )(features, text, proj, gain, scale, bias)

    return run
```

```python
import functools

import jax
import jax.numpy as jnp
from jax import lax
from jax.experimental import pallas as pl
from jax.experimental.pallas import tpu as pltpu
from jax.sharding import PartitionSpec as P

F32 = jnp.float32
BF16 = jnp.bfloat16
LAST = (((1,), (1,)), ((), ()))
FIRST = (((0,), (0,)), ((), ()))


def dot(a, b, dims=(((1,), (0,)), ((), ()))):
    return lax.dot_general(a, b, dims, preferred_element_type=F32)


def unit_rows(values):
    inverse = lax.rsqrt(jnp.sum(values * values, axis=-1, keepdims=True) + 1e-06)
    return values * inverse, inverse


def standardize(rows):
    values = rows.astype(F32)
    centred = values - jnp.mean(values, axis=-1, keepdims=True)
    inverse = lax.rsqrt(jnp.mean(centred * centred, axis=-1, keepdims=True) + 1e-06)
    return centred * inverse, inverse


def send(value, axis, target):
    count = lax.axis_size(axis)
    return lax.ppermute(value, axis, [(p, target(p)) for p in range(count)])


def gather_group(value, count):
    mine = [value]
    for step in range(1, count // 2):
        mine.append(send(value, "loop", lambda p: (p + 2 * step) % count))
    mates = [send(block, "loop", lambda p: p ^ 1) for block in mine]
    return mine + mates


def local_any_size(features, text, proj, gain, scale, bias):
    n = lax.axis_size("loop")
    m = lax.axis_size("rep")
    me = lax.axis_index("loop")
    half = n // 2
    rows, width = features.shape[0], features.shape[2]
    columns = proj.shape[1] // n
    group_rows = rows * n
    logit_scale, logit_bias = scale[0], bias[0]

    own_features = features[:, 0, :]
    own_text = text[:, 0, :]
    text_blocks = gather_group(own_text, n)
    feature_blocks = gather_group(own_features, n)

    xhat, deviation = standardize(own_features)
    normed = (xhat * gain).astype(BF16)
    img_dir, img_inv = unit_rows(dot(normed, proj))
    img_unit = img_dir.astype(BF16)

    txt_dir, txt_inv = unit_rows(own_text.astype(F32))
    own_txt_unit = txt_dir.astype(BF16)
    txt_unit = jnp.concatenate(
        [own_txt_unit] + [unit_rows(block.astype(F32))[0].astype(BF16) for block in text_blocks[1:]]
    )
    row_ids = lax.broadcasted_iota(jnp.int32, (rows, group_rows), 0)
    column_ids = lax.broadcasted_iota(jnp.int32, (rows, group_rows), 1)
    diagonal = (row_ids == column_ids).astype(F32)

    def weights(left, right):
        logits = logit_scale * dot(left, right, LAST) + logit_bias
        return (jax.nn.sigmoid(logits) - diagonal).astype(BF16)

    img_back = logit_scale * dot(weights(img_unit, txt_unit), txt_unit)
    proj_back = (
        (img_back - img_dir * jnp.sum(img_dir * img_back, axis=-1, keepdims=True)) * img_inv
    ).astype(BF16)

    blocks = jnp.transpose(proj_back.reshape(rows, n, columns), (1, 0, 2))
    blocks = lax.all_to_all(blocks, "loop", 0, 0, tiled=True)
    back_columns = blocks.reshape(group_rows, columns)

    norm_back = dot(proj_back, proj, LAST)
    scaled = norm_back * gain
    feature_grad = (
        deviation
        * (
            scaled
            - jnp.mean(scaled, axis=-1, keepdims=True)
            - xhat * jnp.mean(scaled * xhat, axis=-1, keepdims=True)
        )
    ).astype(BF16)
    gain_term = jnp.sum(norm_back * xhat, axis=0) * (1.0 / group_rows)

    other_normed = [(standardize(block)[0] * gain).astype(BF16) for block in feature_blocks[1:]]
    relative = jnp.stack([normed] + other_normed)
    member = jnp.arange(n)
    same_core = (member % 2) == (me % 2)
    chips_back = ((me // 2 - member // 2) % half)
    position = jnp.where(same_core, chips_back, half + chips_back)
    group_normed = relative[position].reshape(group_rows, width)

    partial = (dot(group_normed, back_columns, FIRST) * (1.0 / group_rows)).astype(BF16)
    pieces = lax.all_to_all(partial.reshape(m, width // m, columns), "rep", 0, 0, tiled=True)
    reduced = jnp.sum(pieces.astype(F32), axis=0).astype(BF16)
    gains = lax.all_gather(gain_term, "rep")
    gain_sum = jnp.sum(gains, axis=0)
    proj_rows = lax.all_gather(reduced, "loop")
    proj_grad = jnp.transpose(proj_rows, (1, 0, 2)).reshape(width // m, n * columns).astype(F32)
    gain_gradient = jnp.sum(lax.all_gather(gain_sum, "loop"), axis=0)

    group_unit = jnp.concatenate(
        [img_unit] + [unit_rows(dot(block, proj))[0].astype(BF16) for block in other_normed]
    )
    text_weights = weights(own_txt_unit, group_unit)
    txt_back = logit_scale * dot(text_weights, group_unit)
    text_grad = (
        (txt_back - txt_dir * jnp.sum(txt_dir * txt_back, axis=-1, keepdims=True)) * txt_inv
    ).astype(BF16)
    return feature_grad[:, None, :], text_grad[:, None, :], proj_grad, gain_gradient


VMEM = pl.BlockSpec(memory_space=pltpu.VMEM)
SMEM = pl.BlockSpec(memory_space=pltpu.SMEM)
HBM = pl.BlockSpec(memory_space=pltpu.HBM)
LANES = 128
BAND = 16
TOKEN = ((8, LANES), F32)


def call(body, outs, scratch=(), smem=0, hbm=0, limit=24, flops=0, moved=0):
    def run(*operands):
        specs = [SMEM] * smem + [HBM] * hbm + [VMEM] * (len(operands) - smem - hbm)
        return pl.pallas_call(
            body,
            out_shape=[jax.ShapeDtypeStruct(shape, kind) for shape, kind in outs],
            in_specs=specs,
            out_specs=[VMEM] * len(outs),
            scratch_shapes=[pltpu.VMEM(shape, kind) for shape, kind in scratch]
            + [pltpu.SemaphoreType.DMA((hbm,))] * bool(hbm),
            compiler_params=pltpu.CompilerParams(vmem_limit_bytes=limit * 2**20),
            cost_estimate=pl.CostEstimate(flops=flops, bytes_accessed=moved, transcendentals=0),
        )(*operands)

    return run


def over_rows(count, step, body):
    def turn(index, _):
        body(pl.ds(pl.multiple_of(index * step, step), step))
        return 0

    lax.fori_loop(0, count // step, turn, 0, unroll=min(4, count // step))


def sums(values):
    return jnp.sum(values, axis=-1, keepdims=True)


def normalize_into(source, gain, target, at):
    rows, width = source.shape

    def chunk(where):
        values = source[where, :].astype(F32)
        centred = values - sums(values) * (1.0 / width)
        inverse = lax.rsqrt(sums(centred * centred) * (1.0 / width) + 1e-06)
        target[pl.ds(at + where.start, where.size), :] = (centred * inverse * gain[...]).astype(BF16)

    over_rows(rows, 32, chunk)


def unit_into(source, target, at, inverses=None):
    rows = source.shape[0]

    def chunk(where):
        values = source[where, :].astype(F32)
        inverse = lax.rsqrt(sums(values * values) + 1e-06)
        place = pl.ds(at + where.start, where.size)
        target[place, :] = (values * inverse).astype(BF16)
        if inverses is not None:
            inverses[place, :] = jnp.broadcast_to(inverse, (where.size, LANES))

    over_rows(rows, 32, chunk)


def weigh(dots, scale, bias, diagonal, weights):
    texts, images = dots.shape

    def chunk(index, total):
        where = pl.ds(pl.multiple_of(index * BAND, BAND), BAND)
        product = dots[where, :]
        weight = jnp.tanh((0.5 * scale) * product + 0.5 * bias)
        offset = 0.5
        if diagonal is not None:
            text = index * BAND + diagonal + lax.broadcasted_iota(jnp.int32, product.shape, 0)
            image = lax.broadcasted_iota(jnp.int32, product.shape, 1)
            offset = jnp.where(text == image, -0.5, 0.5)
        weight = (0.5 * weight + offset).astype(BF16)
        weights[where, :] = weight
        both = weight.astype(F32) * product
        return total + both[:8, :] + both[8:, :]

    total = lax.fori_loop(0, texts // BAND, chunk, jnp.zeros((8, images), F32), unroll=4)
    return jnp.sum(total, axis=0, keepdims=True)


def take_columns(place, source, target):
    members = source.shape[1] // target.shape[1]
    full = target.shape[1] // LANES * LANES
    rest = target.shape[1] - full
    target[:, :full] = source[:, pl.ds(pl.multiple_of(place[0] * full, LANES), full)]
    for member in range(members):

        @pl.when(place[0] == member)
        def _():
            target[:, full:] = source[:, members * full + member * rest : members * full + (member + 1) * rest]


def near_body(
    scale, bias, place, f0_far, proj_far, t0_far, f1, t1, gain,
    f0, proj, t0, normed, unit, factors, text_unit, token, projected, semaphores,
):
    rows = f0.shape[0]
    copies = [
        pltpu.make_async_copy(source, target, semaphores.at[at])
        for at, (source, target) in enumerate(((f0_far, f0), (proj_far, proj), (t0_far, t0)))
    ]
    for copy in copies:
        copy.start()
    normalize_into(f1, gain, normed, rows)
    unit_into(t1, text_unit, rows)
    copies[0].wait()
    normalize_into(f0, gain, normed, 0)
    copies[1].wait()
    projected[...] = dot(normed[...], proj[...])
    copies[2].wait()
    unit_into(t0, text_unit, 0)
    unit_into(projected, unit, 0, factors)
    token[...] = jnp.zeros_like(token)


def near_pairs_body(
    scale, bias, place, normed, unit, factors, text_unit, proj, before,
    normed_turned, unit_turned, inverse, text_columns, weights, totals, proj_columns, dots, turned,
):
    dots[...] = dot(text_unit[...], unit[...], LAST)
    totals[...] = weigh(dots, scale[0], bias[0], 0, weights)
    take_columns(place, text_unit, text_columns)
    take_columns(place, proj, proj_columns)
    turn_own(place, unit, factors, turned, unit_turned, inverse)
    normed_turned[...] = normed[...].T


def turn_own(place, unit, factors, turned, unit_turned, inverse):
    columns = unit_turned.shape[0]
    full = columns // LANES * LANES
    rest = columns - full
    turned[...] = unit[...].T
    unit_turned[:full, :] = turned[pl.ds(pl.multiple_of(place[0] * full, LANES), full), :]
    begin = turned.shape[0] // columns * full
    unit_turned[full:, :] = turned[pl.ds(pl.multiple_of(begin + place[0] * rest, BAND), rest), :]
    inverse[...] = factors[...].T[:1, :]


def far_body(
    scale, bias, place, f2, f3, proj, gain, text_near, before,
    normed_turned, unit, unit_turned, inverse, weights, totals, token,
    normed, projected, dots, turned, factors,
):
    rows = f2.shape[0]
    normalize_into(f2, gain, normed, 0)
    normalize_into(f3, gain, normed, rows)
    projected[...] = dot(normed[...], proj[...])
    unit_into(projected, unit, 0, factors)
    dots[...] = dot(text_near[...], unit[...], LAST)
    totals[...] = weigh(dots, scale[0], bias[0], None, weights)
    turn_own(place, unit, factors, turned, unit_turned, inverse)
    normed_turned[...] = normed[...].T
    token[...] = jnp.zeros_like(token)


def third_body(
    scale, bias, place, t2, unit_near, unit_far, weights_near, weights_far, totals_near, totals_far, text_columns_near,
    before, text_unit, weights, back_near, back_far, totals,
    text_columns, dots,
):
    rows = t2.shape[0]
    near = 2 * rows
    unit_into(t2, text_unit, 0)
    take_columns(place, text_unit, text_columns)
    dots[:, :near] = dot(text_unit[...], unit_near[...], LAST)
    dots[:, near:] = dot(text_unit[...], unit_far[...], LAST)
    added = weigh(dots, scale[0], bias[0], near, weights)
    totals[:, :near] = totals_near[...] + added[:, :near]
    totals[:, near:] = totals_far[...] + added[:, near:]
    back_near[...] = dot(text_columns_near[...], weights_near[...], FIRST) + dot(
        text_columns[...], weights[:, :near], FIRST
    )
    back_far[...] = dot(text_columns_near[...], weights_far[...], FIRST) + dot(
        text_columns[...], weights[:, near:], FIRST
    )


def pack_into(target, block, full):
    rows, columns = block.shape
    rest = columns - full
    target[:rows, :] = block[:, :full].astype(BF16)
    per_band = full // rest
    tail = block[:, full:]
    chunks = [tail[at : at + BAND, :] for at in range(0, rows, BAND)]
    for band in range(0, len(chunks), per_band):
        part = chunks[band : band + per_band]
        if len(part) < per_band:
            part.append(jnp.zeros((BAND, full - rest * len(part)), block.dtype))
        at = rows + (band // per_band) * BAND
        target[at : at + BAND, :] = jnp.concatenate(part, axis=1).astype(BF16)


def partial_body(
    members, groups, lead, scale, bias, place, t3, unit_near, unit_far, totals, back_near, back_far, unit_turned_near,
    unit_turned_far, inverse_near, inverse_far, turned_near, turned_far, proj_columns, gain,
    send_lead, keep_lead, send_tail, keep_tail, text_unit, weights, text_columns, dots, packed,
):
    rows = t3.shape[0]
    near = 2 * rows
    every = members * rows
    width = unit_near.shape[1]
    columns = width // members
    count, full = packed.shape[1:]
    scale, bias = scale[0], bias[0]
    unit_into(t3, text_unit, 0)
    take_columns(place, text_unit, text_columns)
    dots[:, :near] = dot(text_unit[...], unit_near[...], LAST)
    dots[:, near:] = dot(text_unit[...], unit_far[...], LAST)
    total = totals[...] + weigh(dots, scale, bias, near + rows, weights)
    added = dot(text_columns[...], weights[...], FIRST)
    back = []
    for where, earlier, unit_turned, inverse in (
        (slice(0, near), back_near, unit_turned_near, inverse_near),
        (slice(near, every), back_far, unit_turned_far, inverse_far),
    ):
        whole = earlier[...] + added[:, where]
        part = (whole - unit_turned[...].astype(F32) * total[:, where]) * (inverse[...] * scale)
        back.append(part.astype(BF16))
    turned = jnp.concatenate([turned_near[...], turned_far[...]], axis=1)
    product = dot(turned, jnp.concatenate(back, axis=1), LAST)
    each = width // groups
    product = product * (1.0 / every)
    for group in range(groups):
        pack_into(packed.at[group], product[group * each : (group + 1) * each, :], full)

    terms = product * proj_columns[...].astype(F32)
    folded = jnp.concatenate([terms[:, full:], jnp.zeros((width, full + LANES - columns), F32)], axis=1)
    for at in range(0, full, LANES):
        folded = folded + terms[:, at : at + LANES]
    high = folded.astype(BF16)
    low = (folded - high.astype(F32)).astype(BF16)
    ones = jnp.ones((BAND, 2 * LANES), BF16)
    gain_row = dot(ones, jnp.concatenate([high, low], axis=1), LAST)[:1, :] / gain[...]
    pieces = [gain_row[:, at : at + LANES] for at in range(0, width, LANES)]
    pieces.append(jnp.zeros((BAND - len(pieces), LANES), F32))
    gain_tile = jnp.concatenate(pieces, axis=0).astype(BF16)
    for group in range(groups):
        packed[group, count - BAND :, full - LANES :] = gain_tile

    own = place[1]
    for at in range(4):
        send_lead[at] = packed[own ^ 1 ^ (2 * at), :lead, :]
        keep_lead[at] = packed[own ^ (2 * at), :lead, :]
        other = (at % 2) + 4 * (at // 2)
        send_tail[at] = packed[own ^ 2 ^ other, lead:, :]
        keep_tail[at] = packed[own ^ other, lead:, :]


def image_body(
    scale, features, proj, gain, text_near, text_third, text_fourth, weights_near, weights_third, weights_fourth,
    unit, factors, feature_grad, token, back, product,
):
    rows, width = features.shape
    scale = scale[0]
    product[...] = (
        dot(weights_near[:, :rows], text_near[...], FIRST)
        + dot(weights_third[:, :rows], text_third[...], FIRST)
        + dot(weights_fourth[:, :rows], text_fourth[...], FIRST)
    )

    def image_chunk(where):
        values = product[where, :] * scale
        direction = unit[where, :].astype(F32)
        back[where, :] = (
            (values - direction * sums(direction * values)) * factors[where, :1]
        ).astype(BF16)

    over_rows(rows, 32, image_chunk)
    product[...] = dot(back[...], proj[...], LAST)

    def feature_chunk(where):
        values = features[where, :].astype(F32)
        centred = values - sums(values) * (1.0 / width)
        deviation = lax.rsqrt(sums(centred * centred) * (1.0 / width) + 1e-06)
        xhat = centred * deviation
        scaled = product[where, :] * gain[...]
        feature_grad[where, :] = (
            deviation
            * (scaled - sums(scaled) * (1.0 / width) - xhat * (sums(scaled * xhat) * (1.0 / width)))
        ).astype(BF16)

    over_rows(rows, 32, feature_chunk)
    token[...] = jnp.zeros_like(token)


def text_body(scale, text, weights_near, weights_far, unit_near, unit_far, text_grad, token, product):
    rows = text.shape[0]
    scale = scale[0]
    product[...] = dot(weights_near[:rows, :], unit_near[...]) + dot(weights_far[:rows, :], unit_far[...])

    def text_chunk(where):
        values = product[where, :] * scale
        own = text[where, :].astype(F32)
        own_inverse = lax.rsqrt(sums(own * own) + 1e-06)
        direction = own * own_inverse
        text_grad[where, :] = (
            (values - direction * sums(direction * values)) * own_inverse
        ).astype(BF16)

    over_rows(rows, 32, text_chunk)
    token[...] = jnp.zeros_like(token)


def halve_body(before, kept_lead, come_lead, kept_tail, come_tail, send_lead, keep_lead, send_tail, keep_tail):
    for kept, come, send_next, keep in (
        (kept_lead, come_lead, send_lead, keep_lead),
        (kept_tail, come_tail, send_tail, keep_tail),
    ):
        for at in range(2):
            keep[at] = (kept[2 * at].astype(F32) + come[2 * at].astype(F32)).astype(BF16)
            send_next[at] = (kept[2 * at + 1].astype(F32) + come[2 * at + 1].astype(F32)).astype(BF16)


def quarter_body(kept_lead, come_lead, kept_tail, come_tail, send_next, keep):
    lead = kept_lead.shape[1]
    for target, at in ((keep, 0), (send_next, 1)):
        target[:lead, :] = (kept_lead[at].astype(F32) + come_lead[at].astype(F32)).astype(BF16)
        target[lead:, :] = (kept_tail[at].astype(F32) + come_tail[at].astype(F32)).astype(BF16)


def last_sum_body(kept, come, total):
    total[...] = (kept[...].astype(F32) + come[...].astype(F32)).astype(BF16)


def finish_body(members, place, *refs):
    packets, (proj_grad, gain_gradient, ordered) = refs[:members], refs[members:]
    count, full = packets[0].shape
    rows, width = proj_grad.shape
    rest = width // members - full
    per_band = full // rest
    for k in range(members):
        member = place[0] ^ k
        proj_grad[:, pl.ds(pl.multiple_of(member * full, LANES), full)] = packets[k][:rows, :].astype(F32)
        ordered[member] = packets[k][rows:, :].astype(F32)
    tails = []
    for index in range(rows // BAND):
        at, lane = (index // per_band) * BAND, (index % per_band) * rest
        tails.append(
            jnp.concatenate([ordered[member][at : at + BAND, lane : lane + rest] for member in range(members)], axis=1)
        )
    proj_grad[:, members * full :] = jnp.concatenate(tails, axis=0)
    value = ordered[0][count - rows - BAND :, full - LANES :]
    for member in range(1, members):
        value = value + ordered[member][count - rows - BAND :, full - LANES :]
    for at in range(width // LANES):
        gain_gradient[at * LANES : (at + 1) * LANES] = value[at]


def local_four(features, text, proj, gain, scale, bias):
    members = lax.axis_size("loop")
    groups = lax.axis_size("rep")
    place = jnp.stack([lax.axis_index("loop"), lax.axis_index("rep")]).astype(jnp.int32)
    rows, width = features.shape[0], features.shape[2]
    near, every = 2 * rows, 4 * rows
    columns = width // members
    full = columns // LANES * LANES
    each = width // groups
    bands = -(-(each // BAND) // (full // (columns - full)))
    packet = (each + bands * BAND, full)
    gain_row = gain.reshape(1, width)

    lead = (2 * packet[0] // BAND // 3) * BAND
    tail = packet[0] - lead

    f0, t0 = features[:, 0, :], text[:, 0, :]
    f2 = send(f0, "loop", lambda p: p ^ 2)
    f1 = send(f0, "loop", lambda p: p ^ 1)
    t1 = send(t0, "loop", lambda p: p ^ 1)

    wide, half = ((near, width), BF16), ((rows, width), BF16)
    square, part, turned = ((near, near), BF16), ((near, columns), BF16), ((width, near), BF16)

    line, mine = ((1, near), F32), ((columns, near), BF16)
    kept = ((width, width), BF16)
    f0_kept, proj_kept, t0_kept, normed_near, unit_near, factors, text_near, token = call(
        near_body,
        [half, kept, half, wide, wide, ((near, LANES), F32), wide, TOKEN],
        [((near, width), F32)],
        smem=3,
        hbm=3,
        limit=36,
        flops=2 * near * width * width,
        moved=8 * near * width,
    )(scale, bias, place, f0, proj, t0, f1, t1, gain_row)

    t_after, f2_after, token = lax.optimization_barrier((t0, f2, token))
    t2 = send(t_after, "loop", lambda p: p ^ 2)
    f3 = send(f2_after, "loop", lambda p: p ^ 1)

    (
        turned_near, unit_turned_near, inverse_near, text_columns_near, weights_near, totals_near, proj_columns,
    ) = call(
        near_pairs_body,
        [turned, mine, line, part, square, line, ((width, columns), BF16)],
        [((near, near), F32), turned],
        smem=3,
        flops=near * width * width,
        moved=8 * near * width,
    )(scale, bias, place, normed_near, unit_near, factors, text_near, proj_kept, token)

    turned_far, unit_far, unit_turned_far, inverse_far, weights_far, totals_far, token = call(
        far_body,
        [turned, wide, mine, line, square, line, TOKEN],
        [wide, ((near, width), F32), ((near, near), F32), turned, ((near, LANES), F32)],
        smem=3,
        flops=3 * near * width * width,
        moved=8 * near * width,
    )(scale, bias, place, f2, f3, proj_kept, gain_row, text_near, totals_near)

    text_grad, token = call(
        text_body,
        [half, TOKEN],
        [((rows, width), F32)],
        smem=1,
        flops=2 * near * width * width,
        moved=6 * near * width,
    )(scale, t0_kept, weights_near, weights_far, unit_near, unit_far)

    t2_after, token = lax.optimization_barrier((t2, token))
    t3 = send(t2_after, "loop", lambda p: p ^ 1)

    narrow, back_kind = ((rows, every), BF16), ((columns, near), F32)
    text_third, weights_third, back_near, back_far, totals = call(
        third_body,
        [half, narrow, back_kind, back_kind, ((1, every), F32)],
        [((rows, columns), BF16), ((rows, every), F32)],
        smem=3,
        flops=2 * near * width * width,
        moved=8 * near * width,
    )(
        scale, bias, place, t2, unit_near, unit_far, weights_near, weights_far, totals_near, totals_far,
        text_columns_near, token,
    )

    outs = call(
        functools.partial(partial_body, members, groups, lead),
        [((4, lead, full), BF16)] * 2 + [((4, tail, full), BF16)] * 2 + [half, narrow],
        [((rows, columns), BF16), ((rows, every), F32), ((groups,) + packet, BF16)],
        smem=3,
        flops=4 * near * width * width,
        moved=16 * near * width,
    )(
        scale, bias, place, t3, unit_near, unit_far, totals, back_near, back_far, unit_turned_near, unit_turned_far,
        inverse_near, inverse_far, turned_near, turned_far, proj_columns, gain_row,
    )
    send_lead, keep_lead, send_tail, keep_tail, text_fourth, weights_fourth = outs
    come_lead = send(send_lead, "rep", lambda p: p ^ 1)
    come_tail = send(send_tail, "rep", lambda p: p ^ 2)

    feature_grad, token = call(
        image_body,
        [half, TOKEN],
        [half, ((rows, width), F32)],
        smem=1,
        flops=4 * near * width * width,
        moved=12 * near * width,
    )(
        scale, f0_kept, proj_kept, gain_row, text_near, text_third, text_fourth, weights_near, weights_third,
        weights_fourth, unit_near, factors,
    )

    send_lead, keep_lead, send_tail, keep_tail = call(
        halve_body,
        [((2, lead, full), BF16)] * 2 + [((2, tail, full), BF16)] * 2,
        moved=4 * each * width,
    )(token, keep_lead, come_lead, keep_tail, come_tail)
    come_lead = send(send_lead, "rep", lambda p: p ^ 2)
    come_tail = send(send_tail, "rep", lambda p: p ^ 1)
    send_all, keep_all = call(quarter_body, [(packet, BF16)] * 2, moved=2 * each * width)(
        keep_lead, come_lead, keep_tail, come_tail
    )
    come_all = send(send_all, "rep", lambda p: p ^ 4)
    (reduced,) = call(last_sum_body, [(packet, BF16)], moved=each * width)(keep_all, come_all)
    far_block = send(reduced, "loop", lambda p: p ^ 2)
    near_block = send(reduced, "loop", lambda p: p ^ 1)
    blocks = [reduced, near_block, far_block, send(far_block, "loop", lambda p: p ^ 1)]

    proj_grad, gain_gradient = call(
        functools.partial(finish_body, members),
        [((each, width), F32), ((width,), F32)],
        [((members, bands * BAND, full), F32)],
        smem=1,
        moved=8 * each * width,
    )(place, *blocks)
    return feature_grad[:, None, :], text_grad[:, None, :], proj_grad, gain_gradient


def four_fits(mesh, rows_shape):
    members, groups = mesh.shape["loop"], mesh.shape["rep"]
    rows, width = rows_shape[0] // members, rows_shape[2]
    if members != 4 or groups != 8 or width % (members * groups) or width % LANES:
        return False
    columns, each = width // members, width // groups
    full = columns // LANES * LANES
    rest = columns - full
    if rest == 0 or full < LANES or full % rest or each % BAND or rows % 64 or width // LANES > BAND:
        return False
    chunks = each // BAND
    used = (chunks - 1) % (full // rest) + 1
    return used * rest <= full - LANES


def solution(mesh):
    def run(features, text, proj, gain, scale, bias):
        body = local_four if four_fits(mesh, features.shape) else local_any_size
        return jax.shard_map(
            body,
            mesh=mesh,
            in_specs=(P("loop", "rep", None), P("loop", "rep", None), P(), P(), P(), P()),
            out_specs=(P("loop", "rep", None), P("loop", "rep", None), P("rep", None), P()),
            check_vma=False,
        )(features, text, proj, gain, scale, bias)

    return run
```

```python
import functools

import jax
import jax.numpy as jnp
from jax import lax
from jax.experimental import pallas as pl
from jax.experimental.pallas import tpu as pltpu
from jax.sharding import PartitionSpec as P

F32 = jnp.float32
BF16 = jnp.bfloat16
LAST = (((1,), (1,)), ((), ()))
FIRST = (((0,), (0,)), ((), ()))


def dot(a, b, dims=(((1,), (0,)), ((), ()))):
    return lax.dot_general(a, b, dims, preferred_element_type=F32)


def unit_rows(values):
    inverse = lax.rsqrt(jnp.sum(values * values, axis=-1, keepdims=True) + 1e-06)
    return values * inverse, inverse


def standardize(rows):
    values = rows.astype(F32)
    centred = values - jnp.mean(values, axis=-1, keepdims=True)
    inverse = lax.rsqrt(jnp.mean(centred * centred, axis=-1, keepdims=True) + 1e-06)
    return centred * inverse, inverse


def send(value, axis, target):
    count = lax.axis_size(axis)
    return lax.ppermute(value, axis, [(p, target(p)) for p in range(count)])


def gather_group(value, count):
    mine = [value]
    for step in range(1, count // 2):
        mine.append(send(value, "loop", lambda p: (p + 2 * step) % count))
    mates = [send(block, "loop", lambda p: p ^ 1) for block in mine]
    return mine + mates


def local_any_size(features, text, proj, gain, scale, bias):
    n = lax.axis_size("loop")
    m = lax.axis_size("rep")
    me = lax.axis_index("loop")
    half = n // 2
    rows, width = features.shape[0], features.shape[2]
    columns = proj.shape[1] // n
    group_rows = rows * n
    logit_scale, logit_bias = scale[0], bias[0]

    own_features = features[:, 0, :]
    own_text = text[:, 0, :]
    text_blocks = gather_group(own_text, n)
    feature_blocks = gather_group(own_features, n)

    xhat, deviation = standardize(own_features)
    normed = (xhat * gain).astype(BF16)
    img_dir, img_inv = unit_rows(dot(normed, proj))
    img_unit = img_dir.astype(BF16)

    txt_dir, txt_inv = unit_rows(own_text.astype(F32))
    own_txt_unit = txt_dir.astype(BF16)
    txt_unit = jnp.concatenate(
        [own_txt_unit] + [unit_rows(block.astype(F32))[0].astype(BF16) for block in text_blocks[1:]]
    )
    row_ids = lax.broadcasted_iota(jnp.int32, (rows, group_rows), 0)
    column_ids = lax.broadcasted_iota(jnp.int32, (rows, group_rows), 1)
    diagonal = (row_ids == column_ids).astype(F32)

    def weights(left, right):
        logits = logit_scale * dot(left, right, LAST) + logit_bias
        return (jax.nn.sigmoid(logits) - diagonal).astype(BF16)

    img_back = logit_scale * dot(weights(img_unit, txt_unit), txt_unit)
    proj_back = (
        (img_back - img_dir * jnp.sum(img_dir * img_back, axis=-1, keepdims=True)) * img_inv
    ).astype(BF16)

    blocks = jnp.transpose(proj_back.reshape(rows, n, columns), (1, 0, 2))
    blocks = lax.all_to_all(blocks, "loop", 0, 0, tiled=True)
    back_columns = blocks.reshape(group_rows, columns)

    norm_back = dot(proj_back, proj, LAST)
    scaled = norm_back * gain
    feature_grad = (
        deviation
        * (
            scaled
            - jnp.mean(scaled, axis=-1, keepdims=True)
            - xhat * jnp.mean(scaled * xhat, axis=-1, keepdims=True)
        )
    ).astype(BF16)
    gain_term = jnp.sum(norm_back * xhat, axis=0) * (1.0 / group_rows)

    other_normed = [(standardize(block)[0] * gain).astype(BF16) for block in feature_blocks[1:]]
    relative = jnp.stack([normed] + other_normed)
    member = jnp.arange(n)
    same_core = (member % 2) == (me % 2)
    chips_back = ((me // 2 - member // 2) % half)
    position = jnp.where(same_core, chips_back, half + chips_back)
    group_normed = relative[position].reshape(group_rows, width)

    partial = (dot(group_normed, back_columns, FIRST) * (1.0 / group_rows)).astype(BF16)
    pieces = lax.all_to_all(partial.reshape(m, width // m, columns), "rep", 0, 0, tiled=True)
    reduced = jnp.sum(pieces.astype(F32), axis=0).astype(BF16)
    gains = lax.all_gather(gain_term, "rep")
    gain_sum = jnp.sum(gains, axis=0)
    proj_rows = lax.all_gather(reduced, "loop")
    proj_grad = jnp.transpose(proj_rows, (1, 0, 2)).reshape(width // m, n * columns).astype(F32)
    gain_gradient = jnp.sum(lax.all_gather(gain_sum, "loop"), axis=0)

    group_unit = jnp.concatenate(
        [img_unit] + [unit_rows(dot(block, proj))[0].astype(BF16) for block in other_normed]
    )
    text_weights = weights(own_txt_unit, group_unit)
    txt_back = logit_scale * dot(text_weights, group_unit)
    text_grad = (
        (txt_back - txt_dir * jnp.sum(txt_dir * txt_back, axis=-1, keepdims=True)) * txt_inv
    ).astype(BF16)
    return feature_grad[:, None, :], text_grad[:, None, :], proj_grad, gain_gradient


VMEM = pl.BlockSpec(memory_space=pltpu.VMEM)
SMEM = pl.BlockSpec(memory_space=pltpu.SMEM)
HBM = pl.BlockSpec(memory_space=pltpu.HBM)
LANES = 128
BAND = 16
TOKEN = ((8, LANES), F32)


def call(body, outs, scratch=(), smem=0, hbm=0, limit=24, flops=0, moved=0):
    def run(*operands):
        specs = [SMEM] * smem + [HBM] * hbm + [VMEM] * (len(operands) - smem - hbm)
        return pl.pallas_call(
            body,
            out_shape=[jax.ShapeDtypeStruct(shape, kind) for shape, kind in outs],
            in_specs=specs,
            out_specs=[VMEM] * len(outs),
            scratch_shapes=[pltpu.VMEM(shape, kind) for shape, kind in scratch]
            + [pltpu.SemaphoreType.DMA((hbm,))] * bool(hbm),
            compiler_params=pltpu.CompilerParams(vmem_limit_bytes=limit * 2**20),
            cost_estimate=pl.CostEstimate(flops=flops, bytes_accessed=moved, transcendentals=0),
        )(*operands)

    return run


def over_rows(count, step, body):
    def turn(index, _):
        body(pl.ds(pl.multiple_of(index * step, step), step))
        return 0

    lax.fori_loop(0, count // step, turn, 0, unroll=min(4, count // step))


def sums(values):
    return jnp.sum(values, axis=-1, keepdims=True)


def normalize_into(source, gain, target, at):
    rows, width = source.shape

    def chunk(where):
        values = source[where, :].astype(F32)
        centred = values - sums(values) * (1.0 / width)
        inverse = lax.rsqrt(sums(centred * centred) * (1.0 / width) + 1e-06)
        target[pl.ds(at + where.start, where.size), :] = (centred * inverse * gain[...]).astype(BF16)

    over_rows(rows, 32, chunk)


def unit_into(source, target, at, inverses=None):
    rows = source.shape[0]

    def chunk(where):
        values = source[where, :].astype(F32)
        inverse = lax.rsqrt(sums(values * values) + 1e-06)
        place = pl.ds(at + where.start, where.size)
        target[place, :] = (values * inverse).astype(BF16)
        if inverses is not None:
            inverses[place, :] = jnp.broadcast_to(inverse, (where.size, LANES))

    over_rows(rows, 32, chunk)


def weigh(dots, scale, bias, diagonal, weights):
    texts, images = dots.shape

    def chunk(index, total):
        where = pl.ds(pl.multiple_of(index * BAND, BAND), BAND)
        product = dots[where, :]
        weight = jnp.tanh((0.5 * scale) * product + 0.5 * bias)
        offset = 0.5
        if diagonal is not None:
            text = index * BAND + diagonal + lax.broadcasted_iota(jnp.int32, product.shape, 0)
            image = lax.broadcasted_iota(jnp.int32, product.shape, 1)
            offset = jnp.where(text == image, -0.5, 0.5)
        weight = (0.5 * weight + offset).astype(BF16)
        weights[where, :] = weight
        both = weight.astype(F32) * product
        return total + both[:8, :] + both[8:, :]

    total = lax.fori_loop(0, texts // BAND, chunk, jnp.zeros((8, images), F32), unroll=4)
    return jnp.sum(total, axis=0, keepdims=True)


def take_columns(place, source, target):
    members = source.shape[1] // target.shape[1]
    full = target.shape[1] // LANES * LANES
    rest = target.shape[1] - full
    target[:, :full] = source[:, pl.ds(pl.multiple_of(place[0] * full, LANES), full)]
    for member in range(members):

        @pl.when(place[0] == member)
        def _():
            target[:, full:] = source[:, members * full + member * rest : members * full + (member + 1) * rest]


def near_body(
    scale, bias, place, f0_far, proj_far, t0_far, f1, t1, gain_line,
    f0, proj, t_sent, gain, normed, unit, factors, text_unit, token, projected, semaphores,
):
    rows = f0.shape[0]
    copies = [
        pltpu.make_async_copy(source, target, semaphores.at[at])
        for at, (source, target) in enumerate(((f0_far, f0), (proj_far, proj), (t0_far, t_sent.at[: f0.shape[0]])))
    ]
    for copy in copies:
        copy.start()
    for at in range(0, gain.shape[1], LANES):
        gain[:, at : at + LANES] = gain_line[at : at + LANES].reshape(1, LANES)
    normalize_into(f1, gain, normed, rows)
    unit_into(t1, text_unit, rows)
    copies[0].wait()
    normalize_into(f0, gain, normed, 0)
    copies[1].wait()
    projected[...] = dot(normed[...], proj[...])
    copies[2].wait()
    t_sent[rows:, :] = jnp.zeros((t_sent.shape[0] - rows, t_sent.shape[1]), BF16)
    unit_into(t_sent.at[:rows], text_unit, 0)
    unit_into(projected, unit, 0, factors)
    token[...] = jnp.zeros_like(token)


def near_pairs_body(
    scale, bias, place, normed, unit, factors, text_unit, proj, before,
    normed_turned, unit_turned, inverse, text_columns, weights, totals, proj_columns, token, dots, turned,
):
    token[...] = jnp.zeros_like(token)
    dots[...] = dot(text_unit[...], unit[...], LAST)
    totals[...] = weigh(dots, scale[0], bias[0], 0, weights)
    take_columns(place, text_unit, text_columns)
    take_columns(place, proj, proj_columns)
    turn_own(place, unit, factors, turned, unit_turned, inverse)
    normed_turned[...] = normed[...].T


def turn_own(place, unit, factors, turned, unit_turned, inverse):
    columns = unit_turned.shape[0]
    full = columns // LANES * LANES
    rest = columns - full
    turned[...] = unit[...].T
    unit_turned[:full, :] = turned[pl.ds(pl.multiple_of(place[0] * full, LANES), full), :]
    begin = turned.shape[0] // columns * full
    unit_turned[full:, :] = turned[pl.ds(pl.multiple_of(begin + place[0] * rest, BAND), rest), :]
    inverse[...] = factors[...].T[:1, :]


def far_body(
    scale, bias, place, f2, f3, proj, gain, text_near, before,
    normed_turned, unit, unit_turned, inverse, weights, totals, token,
    normed, projected, dots, turned, factors,
):
    rows = f2.shape[0]
    normalize_into(f2, gain, normed, 0)
    normalize_into(f3, gain, normed, rows)
    projected[...] = dot(normed[...], proj[...])
    unit_into(projected, unit, 0, factors)
    dots[...] = dot(text_near[...], unit[...], LAST)
    totals[...] = weigh(dots, scale[0], bias[0], None, weights)
    turn_own(place, unit, factors, turned, unit_turned, inverse)
    normed_turned[...] = normed[...].T
    token[...] = jnp.zeros_like(token)


def third_body(
    scale, bias, place, t2, unit_near, unit_far, totals_near, totals_far, early_near, early_far,
    before, text_unit, weights, back_near, back_far, totals,
    text_columns, dots,
):
    rows = text_unit.shape[0]
    near = 2 * rows
    unit_into(t2.at[:rows], text_unit, 0)
    take_columns(place, text_unit, text_columns)
    dots[:, :near] = dot(text_unit[...], unit_near[...], LAST)
    dots[:, near:] = dot(text_unit[...], unit_far[...], LAST)
    added = weigh(dots, scale[0], bias[0], near, weights)
    totals[:, :near] = totals_near[...] + added[:, :near]
    totals[:, near:] = totals_far[...] + added[:, near:]
    added = dot(text_columns[...], weights[...], FIRST)
    back_near[...] = early_near[...] + added[:, :near]
    back_far[...] = early_far[...] + added[:, near:]


def pack_into(target, block, full):
    rows, columns = block.shape
    rest = columns - full
    target[:rows, :] = block[:, :full].astype(BF16)
    per_band = full // rest
    tail = block[:, full:]
    chunks = [tail[at : at + BAND, :] for at in range(0, rows, BAND)]
    for band in range(0, len(chunks), per_band):
        part = chunks[band : band + per_band]
        if len(part) < per_band:
            part.append(jnp.zeros((BAND, full - rest * len(part)), block.dtype))
        at = rows + (band // per_band) * BAND
        target[at : at + BAND, :] = jnp.concatenate(part, axis=1).astype(BF16)


def partial_body(
    members, groups, lead, scale, bias, place, t3, unit_near, unit_far, totals, back_near, back_far, unit_turned_near,
    unit_turned_far, inverse_near, inverse_far, turned_near, turned_far, proj_columns, gain,
    across, keep_lead, keep_tail, *refs,
):
    along, (text_unit, weights, text_columns, dots, packed) = refs[: groups // 2 - 1], refs[groups // 2 - 1 :]
    rows = text_unit.shape[0]
    near = 2 * rows
    every = members * rows
    width = unit_near.shape[1]
    columns = width // members
    count, full = packed.shape[1:]
    scale, bias = scale[0], bias[0]
    unit_into(t3.at[:rows], text_unit, 0)
    take_columns(place, text_unit, text_columns)
    dots[:, :near] = dot(text_unit[...], unit_near[...], LAST)
    dots[:, near:] = dot(text_unit[...], unit_far[...], LAST)
    total = totals[...] + weigh(dots, scale, bias, near + rows, weights)
    added = dot(text_columns[...], weights[...], FIRST)
    back = []
    for where, earlier, unit_turned, inverse in (
        (slice(0, near), back_near, unit_turned_near, inverse_near),
        (slice(near, every), back_far, unit_turned_far, inverse_far),
    ):
        whole = earlier[...] + added[:, where]
        part = (whole - unit_turned[...].astype(F32) * total[:, where]) * (inverse[...] * scale)
        back.append(part.astype(BF16))
    turned = jnp.concatenate([turned_near[...], turned_far[...]], axis=1)
    product = dot(turned, jnp.concatenate(back, axis=1), LAST)
    each = width // groups
    product = product * (1.0 / every)
    for group in range(groups):
        pack_into(packed.at[group], product[group * each : (group + 1) * each, :], full)

    terms = product * proj_columns[...].astype(F32)
    folded = jnp.concatenate([terms[:, full:], jnp.zeros((width, full + LANES - columns), F32)], axis=1)
    for at in range(0, full, LANES):
        folded = folded + terms[:, at : at + LANES]
    high = folded.astype(BF16)
    low = (folded - high.astype(F32)).astype(BF16)
    ones = jnp.ones((BAND, 2 * LANES), BF16)
    gain_row = dot(ones, jnp.concatenate([high, low], axis=1), LAST)[:1, :] / gain[...]
    pieces = [gain_row[:, at : at + LANES] for at in range(0, width, LANES)]
    pieces.append(jnp.zeros((BAND - len(pieces), LANES), F32))
    gain_tile = jnp.concatenate(pieces, axis=0).astype(BF16)
    for group in range(groups):
        packed[group, count - BAND :, full - LANES :] = gain_tile

    own = place[1]
    for step in range(groups // 2):
        across[step] = packed[own ^ 1 ^ (2 * step), :lead, :]
        keep_lead[step] = packed[own ^ (2 * step), :lead, :]
    for other in range(2):
        keep_tail[other] = packed[own ^ other, lead:, :]
        for step in range(1, groups // 2):
            along[step - 1][other] = packed[own ^ (2 * step) ^ other, lead:, :]


def image_body(
    scale, features, proj, gain, text_near, text_third, text_fourth, weights_near, weights_third, weights_fourth,
    unit, factors, feature_grad, token, back, product,
):
    rows, width = features.shape
    scale = scale[0]
    product[...] = (
        dot(weights_near[:, :rows], text_near[...], FIRST)
        + dot(weights_third[:, :rows], text_third[...], FIRST)
        + dot(weights_fourth[:, :rows], text_fourth[...], FIRST)
    )

    def image_chunk(where):
        values = product[where, :] * scale
        direction = unit[where, :].astype(F32)
        back[where, :] = (
            (values - direction * sums(direction * values)) * factors[where, :1]
        ).astype(BF16)

    over_rows(rows, 32, image_chunk)
    product[...] = dot(back[...], proj[...], LAST)

    def feature_chunk(where):
        values = features[where, :].astype(F32)
        centred = values - sums(values) * (1.0 / width)
        deviation = lax.rsqrt(sums(centred * centred) * (1.0 / width) + 1e-06)
        xhat = centred * deviation
        scaled = product[where, :] * gain[...]
        feature_grad[where, :] = (
            deviation
            * (scaled - sums(scaled) * (1.0 / width) - xhat * (sums(scaled * xhat) * (1.0 / width)))
        ).astype(BF16)

    over_rows(rows, 32, feature_chunk)
    token[...] = jnp.zeros_like(token)


def text_body(
    scale, text, weights_near, weights_far, unit_near, unit_far, text_columns, before,
    text_grad, back_near, back_far, token, product,
):
    rows = text_grad.shape[0]
    scale = scale[0]
    product[...] = dot(weights_near[:rows, :], unit_near[...]) + dot(weights_far[:rows, :], unit_far[...])

    def text_chunk(where):
        values = product[where, :] * scale
        own = text[where, :].astype(F32)
        own_inverse = lax.rsqrt(sums(own * own) + 1e-06)
        direction = own * own_inverse
        text_grad[where, :] = (
            (values - direction * sums(direction * values)) * own_inverse
        ).astype(BF16)

    over_rows(rows, 32, text_chunk)
    back_near[...] = dot(text_columns[...], weights_near[...], FIRST)
    back_far[...] = dot(text_columns[...], weights_far[...], FIRST)
    token[...] = jnp.zeros_like(token)


def first_sum_body(place, token, keep_lead, across, keep_tail, *refs):
    steps = keep_lead.shape[0]
    along, refs = refs[: steps - 1], refs[steps - 1 :]
    leads, (tail, tail_across, ordered) = refs[:steps], refs[steps:]
    for step in range(steps):
        leads[step][...] = (keep_lead[step].astype(F32) + across[step].astype(F32)).astype(BF16)
    own = place[1] // 2
    ordered[own] = keep_tail[...]
    for step in range(1, steps):
        ordered[own ^ step] = along[steps - 1 - step][...]
    value = ordered[0].astype(F32)
    for step in range(1, steps):
        value = value + ordered[step].astype(F32)
    tail[...] = value[0].astype(BF16)
    tail_across[...] = value[1].astype(BF16)


def last_sum_body(tail, tail_across, *refs):
    leads, total = refs[:-1], refs[-1]
    split = leads[0].shape[0]
    value = leads[0][...].astype(F32)
    for lead in leads[1:]:
        value = value + lead[...].astype(F32)
    total[:split, :] = value.astype(BF16)
    total[split:, :] = (tail[...].astype(F32) + tail_across[...].astype(F32)).astype(BF16)


def place_main(packet, member, buffer, out, semaphore):
    rows, full = buffer.shape
    buffer[...] = packet[:rows, :].astype(F32)
    where = pl.ds(pl.multiple_of(member * full, LANES), full)
    copy = pltpu.make_async_copy(buffer, out.at[:, where], semaphore)
    copy.start()
    return copy


def finish_most_body(place, own, near, far, out, first, second, third, semaphores):
    copies = [
        place_main(packet, place[0] ^ k, buffer, out, semaphores.at[k])
        for k, (packet, buffer) in enumerate(((own, first), (near, second), (far, third)))
    ]
    for copy in copies:
        copy.wait()


def finish_body(members, place, begun, *refs):
    packets, (out, gain_gradient, ordered, main, last, semaphores) = refs[:members], refs[members:]
    count, full = packets[0].shape
    rows, width = out.shape
    rest = width // members - full
    per_band = full // rest
    main_out = place_main(packets[-1], place[0] ^ (members - 1), main, out, semaphores.at[0])
    for k in range(members):
        ordered[place[0] ^ k] = packets[k][rows:, :].astype(F32)
    tails = []
    for index in range(rows // BAND):
        at, lane = (index // per_band) * BAND, (index % per_band) * rest
        tails.append(
            jnp.concatenate([ordered[member][at : at + BAND, lane : lane + rest] for member in range(members)], axis=1)
        )
    last[...] = jnp.concatenate(tails, axis=0)
    last_out = pltpu.make_async_copy(last, out.at[:, members * full :], semaphores.at[1])
    last_out.start()
    value = ordered[0][count - rows - BAND :, full - LANES :]
    for member in range(1, members):
        value = value + ordered[member][count - rows - BAND :, full - LANES :]
    for at in range(width // LANES):
        gain_gradient[at * LANES : (at + 1) * LANES] = value[at]
    main_out.wait()
    last_out.wait()


def local_four(features, text, proj, gain, scale, bias):
    members = lax.axis_size("loop")
    groups = lax.axis_size("rep")
    place = jnp.stack([lax.axis_index("loop"), lax.axis_index("rep")]).astype(jnp.int32)
    rows, width = features.shape[0], features.shape[2]
    near, every = 2 * rows, 4 * rows
    columns = width // members
    full = columns // LANES * LANES
    each = width // groups
    bands = -(-(each // BAND) // (full // (columns - full)))
    packet = (each + bands * BAND, full)

    lead = (3 * packet[0] // BAND // 4) * BAND
    tail = packet[0] - lead
    steps = groups // 2

    f0, t0 = features[:, 0, :], text[:, 0, :]
    f2 = send(f0, "loop", lambda p: p ^ 2)
    f1 = send(f0, "loop", lambda p: p ^ 1)
    t1 = send(t0, "loop", lambda p: p ^ 1)

    wide, half = ((near, width), BF16), ((rows, width), BF16)
    square, part, turned = ((near, near), BF16), ((near, columns), BF16), ((width, near), BF16)

    line, mine = ((1, near), F32), ((columns, near), BF16)
    kept = ((width, width), BF16)
    f0_kept, proj_kept, t_sent, gain_row, normed_near, unit_near, factors, text_near, token = call(
        near_body,
        [half, kept, ((rows + BAND, width), BF16), ((1, width), F32), wide, wide, ((near, LANES), F32), wide, TOKEN],
        [((near, width), F32)],
        smem=3,
        hbm=3,
        limit=46,
        flops=2 * near * width * width,
        moved=8 * near * width,
    )(scale, bias, place, f0, proj, t0, f1, t1, gain)

    f2_after, f2_token = lax.optimization_barrier((f2, token))
    f3 = send(f2_after, "loop", lambda p: p ^ 1)
    t2 = send(t_sent, "loop", lambda p: p ^ 2)

    (
        turned_near, unit_turned_near, inverse_near, text_columns_near, weights_near, totals_near, proj_columns,
        token,
    ) = call(
        near_pairs_body,
        [turned, mine, line, part, square, line, ((width, columns), BF16), TOKEN],
        [((near, near), F32), turned],
        smem=3,
        flops=1000,
        moved=1000,
    )(scale, bias, place, normed_near, unit_near, factors, text_near, proj_kept, token)

    turned_far, unit_far, unit_turned_far, inverse_far, weights_far, totals_far, token = call(
        far_body,
        [turned, wide, mine, line, square, line, TOKEN],
        [wide, ((near, width), F32), ((near, near), F32), turned, ((near, LANES), F32)],
        smem=3,
        flops=1000,
        moved=1000,
    )(scale, bias, place, f2, f3, proj_kept, gain_row, text_near, f2_token)

    back_kind = ((columns, near), F32)
    text_grad, early_near, early_far, token = call(
        text_body,
        [half, back_kind, back_kind, TOKEN],
        [((rows, width), F32)],
        smem=1,
        flops=1000,
        moved=1000,
    )(scale, t_sent, weights_near, weights_far, unit_near, unit_far, text_columns_near, token)

    t2_after, token = lax.optimization_barrier((t2, token))
    t3 = send(t2_after, "loop", lambda p: p ^ 1)

    narrow = ((rows, every), BF16)
    text_third, weights_third, back_near, back_far, totals = call(
        third_body,
        [half, narrow, back_kind, back_kind, ((1, every), F32)],
        [((rows, columns), BF16), ((rows, every), F32)],
        smem=3,
        flops=2 * near * width * width,
        moved=8 * near * width,
    )(
        scale, bias, place, t2, unit_near, unit_far, totals_near, totals_far, early_near, early_far, token,
    )

    outs = call(
        functools.partial(partial_body, members, groups, lead),
        [((steps, lead, full), BF16)] * 2 + [((2, tail, full), BF16)] * steps + [half, narrow],
        [((rows, columns), BF16), ((rows, every), F32), ((groups,) + packet, BF16)],
        smem=3,
        flops=4 * near * width * width,
        moved=16 * near * width,
    )(
        scale, bias, place, t3, unit_near, unit_far, totals, back_near, back_far, unit_turned_near, unit_turned_far,
        inverse_near, inverse_far, turned_near, turned_far, proj_columns, gain_row,
    )
    across, keep_lead, keep_tail = outs[:3]
    along, (text_fourth, weights_fourth) = outs[3 : 2 + steps], outs[2 + steps :]

    across = send(across, "rep", lambda p: p ^ 1)
    along = [send(along[step - 1], "rep", lambda p: p ^ (2 * step)) for step in reversed(range(1, steps))]

    feature_grad, token = call(
        image_body,
        [half, TOKEN],
        [half, ((rows, width), F32)],
        smem=1,
        flops=4 * near * width * width,
        moved=12 * near * width,
    )(
        scale, f0_kept, proj_kept, gain_row, text_near, text_third, text_fourth, weights_near, weights_third,
        weights_fourth, unit_near, factors,
    )

    outs = call(
        first_sum_body,
        [((lead, full), BF16)] * steps + [((tail, full), BF16)] * 2,
        [((steps, 2, tail, full), BF16)],
        smem=1,
        moved=4 * each * width,
    )(place, token, keep_lead, across, keep_tail, *along)
    leads = [outs[0]] + [send(outs[step], "rep", lambda p: p ^ (2 * step)) for step in reversed(range(1, steps))]
    tail_across = send(outs[steps + 1], "rep", lambda p: p ^ 1)

    (reduced,) = call(
        last_sum_body,
        [(packet, BF16)],
        moved=4 * each * width,
    )(outs[steps], tail_across, *leads)
    far_block = send(reduced, "loop", lambda p: p ^ 2)
    near_block = send(reduced, "loop", lambda p: p ^ 1)
    last_block = send(far_block, "loop", lambda p: p ^ 1)
    out_kind = jax.ShapeDtypeStruct((each, width), F32)
    main_room = pltpu.VMEM((each, full), F32)
    begun = pl.pallas_call(
        finish_most_body,
        out_shape=out_kind,
        in_specs=[SMEM] + [VMEM] * 3,
        out_specs=HBM,
        scratch_shapes=[main_room] * 3 + [pltpu.SemaphoreType.DMA((3,))],
        compiler_params=pltpu.CompilerParams(vmem_limit_bytes=24 * 2**20),
        cost_estimate=pl.CostEstimate(flops=0, bytes_accessed=8 * each * width, transcendentals=0),
    )(place, reduced, near_block, far_block)
    proj_grad, gain_gradient = pl.pallas_call(
        functools.partial(finish_body, members),
        out_shape=[out_kind, jax.ShapeDtypeStruct((width,), F32)],
        in_specs=[SMEM, HBM] + [VMEM] * members,
        out_specs=[HBM, VMEM],
        input_output_aliases={1: 0},
        scratch_shapes=[
            pltpu.VMEM((members, bands * BAND, full), F32),
            main_room,
            pltpu.VMEM((each, width - members * full), F32),
            pltpu.SemaphoreType.DMA((2,)),
        ],
        compiler_params=pltpu.CompilerParams(vmem_limit_bytes=24 * 2**20),
        cost_estimate=pl.CostEstimate(flops=0, bytes_accessed=2 * each * width, transcendentals=0),
    )(place, begun, reduced, near_block, far_block, last_block)
    return feature_grad[:, None, :], text_grad[:, None, :], proj_grad, gain_gradient


def four_fits(mesh, rows_shape):
    members, groups = mesh.shape["loop"], mesh.shape["rep"]
    rows, width = rows_shape[0] // members, rows_shape[2]
    if members != 4 or groups != 8 or width % (members * groups) or width % LANES:
        return False
    columns, each = width // members, width // groups
    full = columns // LANES * LANES
    rest = columns - full
    if rest == 0 or full < LANES or full % rest or each % BAND or rows % 64 or width // LANES > BAND:
        return False
    chunks = each // BAND
    used = (chunks - 1) % (full // rest) + 1
    return used * rest <= full - LANES


def solution(mesh):
    def run(features, text, proj, gain, scale, bias):
        body = local_four if four_fits(mesh, features.shape) else local_any_size
        return jax.shard_map(
            body,
            mesh=mesh,
            in_specs=(P("loop", "rep", None), P("loop", "rep", None), P(), P(), P(), P()),
            out_specs=(P("loop", "rep", None), P("loop", "rep", None), P("rep", None), P()),
            check_vma=False,
        )(features, text, proj, gain, scale, bias)

    return run
```

```python
import functools

import jax
import jax.numpy as jnp
from jax import lax
from jax.experimental import pallas as pl
from jax.experimental.pallas import tpu as pltpu
from jax.sharding import PartitionSpec as P

F32 = jnp.float32
BF16 = jnp.bfloat16
LAST = (((1,), (1,)), ((), ()))
FIRST = (((0,), (0,)), ((), ()))


def dot(a, b, dims=(((1,), (0,)), ((), ()))):
    return lax.dot_general(a, b, dims, preferred_element_type=F32)


def unit_rows(values):
    inverse = lax.rsqrt(jnp.sum(values * values, axis=-1, keepdims=True) + 1e-06)
    return values * inverse, inverse


def standardize(rows):
    values = rows.astype(F32)
    centred = values - jnp.mean(values, axis=-1, keepdims=True)
    inverse = lax.rsqrt(jnp.mean(centred * centred, axis=-1, keepdims=True) + 1e-06)
    return centred * inverse, inverse


def send(value, axis, target):
    count = lax.axis_size(axis)
    return lax.ppermute(value, axis, [(p, target(p)) for p in range(count)])


def gather_group(value, count):
    mine = [value]
    for step in range(1, count // 2):
        mine.append(send(value, "loop", lambda p: (p + 2 * step) % count))
    mates = [send(block, "loop", lambda p: p ^ 1) for block in mine]
    return mine + mates


def local_any_size(features, text, proj, gain, scale, bias):
    n = lax.axis_size("loop")
    m = lax.axis_size("rep")
    me = lax.axis_index("loop")
    half = n // 2
    rows, width = features.shape[0], features.shape[2]
    columns = proj.shape[1] // n
    group_rows = rows * n
    logit_scale, logit_bias = scale[0], bias[0]

    own_features = features[:, 0, :]
    own_text = text[:, 0, :]
    text_blocks = gather_group(own_text, n)
    feature_blocks = gather_group(own_features, n)

    xhat, deviation = standardize(own_features)
    normed = (xhat * gain).astype(BF16)
    img_dir, img_inv = unit_rows(dot(normed, proj))
    img_unit = img_dir.astype(BF16)

    txt_dir, txt_inv = unit_rows(own_text.astype(F32))
    own_txt_unit = txt_dir.astype(BF16)
    txt_unit = jnp.concatenate(
        [own_txt_unit] + [unit_rows(block.astype(F32))[0].astype(BF16) for block in text_blocks[1:]]
    )
    row_ids = lax.broadcasted_iota(jnp.int32, (rows, group_rows), 0)
    column_ids = lax.broadcasted_iota(jnp.int32, (rows, group_rows), 1)
    diagonal = (row_ids == column_ids).astype(F32)

    def weights(left, right):
        logits = logit_scale * dot(left, right, LAST) + logit_bias
        return (jax.nn.sigmoid(logits) - diagonal).astype(BF16)

    img_back = logit_scale * dot(weights(img_unit, txt_unit), txt_unit)
    proj_back = (
        (img_back - img_dir * jnp.sum(img_dir * img_back, axis=-1, keepdims=True)) * img_inv
    ).astype(BF16)

    blocks = jnp.transpose(proj_back.reshape(rows, n, columns), (1, 0, 2))
    blocks = lax.all_to_all(blocks, "loop", 0, 0, tiled=True)
    back_columns = blocks.reshape(group_rows, columns)

    norm_back = dot(proj_back, proj, LAST)
    scaled = norm_back * gain
    feature_grad = (
        deviation
        * (
            scaled
            - jnp.mean(scaled, axis=-1, keepdims=True)
            - xhat * jnp.mean(scaled * xhat, axis=-1, keepdims=True)
        )
    ).astype(BF16)
    gain_term = jnp.sum(norm_back * xhat, axis=0) * (1.0 / group_rows)

    other_normed = [(standardize(block)[0] * gain).astype(BF16) for block in feature_blocks[1:]]
    relative = jnp.stack([normed] + other_normed)
    member = jnp.arange(n)
    same_core = (member % 2) == (me % 2)
    chips_back = ((me // 2 - member // 2) % half)
    position = jnp.where(same_core, chips_back, half + chips_back)
    group_normed = relative[position].reshape(group_rows, width)

    partial = (dot(group_normed, back_columns, FIRST) * (1.0 / group_rows)).astype(BF16)
    pieces = lax.all_to_all(partial.reshape(m, width // m, columns), "rep", 0, 0, tiled=True)
    reduced = jnp.sum(pieces.astype(F32), axis=0).astype(BF16)
    gains = lax.all_gather(gain_term, "rep")
    gain_sum = jnp.sum(gains, axis=0)
    proj_rows = lax.all_gather(reduced, "loop")
    proj_grad = jnp.transpose(proj_rows, (1, 0, 2)).reshape(width // m, n * columns).astype(F32)
    gain_gradient = jnp.sum(lax.all_gather(gain_sum, "loop"), axis=0)

    group_unit = jnp.concatenate(
        [img_unit] + [unit_rows(dot(block, proj))[0].astype(BF16) for block in other_normed]
    )
    text_weights = weights(own_txt_unit, group_unit)
    txt_back = logit_scale * dot(text_weights, group_unit)
    text_grad = (
        (txt_back - txt_dir * jnp.sum(txt_dir * txt_back, axis=-1, keepdims=True)) * txt_inv
    ).astype(BF16)
    return feature_grad[:, None, :], text_grad[:, None, :], proj_grad, gain_gradient


VMEM = pl.BlockSpec(memory_space=pltpu.VMEM)
SMEM = pl.BlockSpec(memory_space=pltpu.SMEM)
HBM = pl.BlockSpec(memory_space=pltpu.HBM)
LANES = 128
BAND = 16
TOKEN = ((8, LANES), F32)


def call(body, outs, scratch=(), smem=0, hbm=0, limit=24, flops=0, moved=0):
    def run(*operands):
        specs = [SMEM] * smem + [HBM] * hbm + [VMEM] * (len(operands) - smem - hbm)
        return pl.pallas_call(
            body,
            out_shape=[jax.ShapeDtypeStruct(shape, kind) for shape, kind in outs],
            in_specs=specs,
            out_specs=[VMEM] * len(outs),
            scratch_shapes=[pltpu.VMEM(shape, kind) for shape, kind in scratch]
            + [pltpu.SemaphoreType.DMA((hbm,))] * bool(hbm),
            compiler_params=pltpu.CompilerParams(vmem_limit_bytes=limit * 2**20),
            cost_estimate=pl.CostEstimate(flops=flops, bytes_accessed=moved, transcendentals=0),
        )(*operands)

    return run


def over_rows(count, step, body):
    def turn(index, _):
        body(pl.ds(pl.multiple_of(index * step, step), step))
        return 0

    lax.fori_loop(0, count // step, turn, 0, unroll=min(4, count // step))


def sums(values):
    return jnp.sum(values, axis=-1, keepdims=True)


def normalize_into(source, gain, target, at):
    rows, width = source.shape

    def chunk(where):
        values = source[where, :].astype(F32)
        centred = values - sums(values) * (1.0 / width)
        inverse = lax.rsqrt(sums(centred * centred) * (1.0 / width) + 1e-06)
        target[pl.ds(at + where.start, where.size), :] = (centred * inverse * gain[...]).astype(BF16)

    over_rows(rows, 32, chunk)


def unit_into(source, target, at, inverses=None):
    rows = source.shape[0]

    def chunk(where):
        values = source[where, :].astype(F32)
        inverse = lax.rsqrt(sums(values * values) + 1e-06)
        place = pl.ds(at + where.start, where.size)
        target[place, :] = (values * inverse).astype(BF16)
        if inverses is not None:
            inverses[place, :] = jnp.broadcast_to(inverse, (where.size, LANES))

    over_rows(rows, 32, chunk)


def weigh(dots, scale, bias, diagonal, weights):
    texts, images = dots.shape

    def chunk(index, total):
        where = pl.ds(pl.multiple_of(index * BAND, BAND), BAND)
        product = dots[where, :]
        weight = jnp.tanh((0.5 * scale) * product + 0.5 * bias)
        offset = 0.5
        if diagonal is not None:
            text = index * BAND + diagonal + lax.broadcasted_iota(jnp.int32, product.shape, 0)
            image = lax.broadcasted_iota(jnp.int32, product.shape, 1)
            offset = jnp.where(text == image, -0.5, 0.5)
        weight = (0.5 * weight + offset).astype(BF16)
        weights[where, :] = weight
        both = weight.astype(F32) * product
        return total + both[:8, :] + both[8:, :]

    total = lax.fori_loop(0, texts // BAND, chunk, jnp.zeros((8, images), F32), unroll=4)
    return jnp.sum(total, axis=0, keepdims=True)


def take_columns(place, source, target):
    members = source.shape[1] // target.shape[1]
    full = target.shape[1] // LANES * LANES
    rest = target.shape[1] - full
    target[:, :full] = source[:, pl.ds(pl.multiple_of(place[0] * full, LANES), full)]
    for member in range(members):

        @pl.when(place[0] == member)
        def _():
            target[:, full:] = source[:, members * full + member * rest : members * full + (member + 1) * rest]


def near_body(
    scale, bias, place, f0_far, proj_far, t0_far, f1, gain_line,
    f0, proj, t0, gain, normed, unit, factors, text_unit, token, projected, semaphores,
):
    rows = f0.shape[0]
    copies = [
        pltpu.make_async_copy(source, target, semaphores.at[at])
        for at, (source, target) in enumerate(((f0_far, f0), (proj_far, proj), (t0_far, t0)))
    ]
    for copy in copies:
        copy.start()
    for at in range(0, gain.shape[1], LANES):
        gain[:, at : at + LANES] = gain_line[at : at + LANES].reshape(1, LANES)
    normalize_into(f1, gain, normed, rows)
    copies[0].wait()
    normalize_into(f0, gain, normed, 0)
    copies[1].wait()
    projected[...] = dot(normed[...], proj[...])
    copies[2].wait()
    unit_into(t0, text_unit, 0)
    unit_into(projected, unit, 0, factors)
    token[...] = jnp.zeros_like(token)


def near_pairs_body(
    scale, bias, place, normed, unit, factors, text_own, t1, proj, before,
    text_unit, normed_turned, unit_turned, inverse, text_columns, weights, totals, proj_columns, token, dots, turned,
):
    token[...] = jnp.zeros_like(token)
    rows = t1.shape[0]
    text_unit[:rows, :] = text_own[...]
    unit_into(t1, text_unit, rows)
    dots[...] = dot(text_unit[...], unit[...], LAST)
    totals[...] = weigh(dots, scale[0], bias[0], 0, weights)
    take_columns(place, text_unit, text_columns)
    take_columns(place, proj, proj_columns)
    turn_own(place, unit, factors, turned, unit_turned, inverse)
    normed_turned[...] = normed[...].T


def turn_own(place, unit, factors, turned, unit_turned, inverse):
    columns = unit_turned.shape[0]
    full = columns // LANES * LANES
    rest = columns - full
    turned[...] = unit[...].T
    unit_turned[:full, :] = turned[pl.ds(pl.multiple_of(place[0] * full, LANES), full), :]
    begin = turned.shape[0] // columns * full
    unit_turned[full:, :] = turned[pl.ds(pl.multiple_of(begin + place[0] * rest, BAND), rest), :]
    inverse[...] = factors[...].T[:1, :]


def split_body(f2, before, head, tail):
    head[...] = f2[: head.shape[0], :]
    tail[...] = f2[head.shape[0] :, :]


def far_body(
    scale, bias, place, f2, f3_head, f3_tail, proj, gain, text_near,
    normed_turned, unit, unit_turned, inverse, weights, totals, token,
    normed, projected, dots, turned, factors,
):
    rows = f2.shape[0]
    normalize_into(f2, gain, normed, 0)
    normalize_into(f3_head, gain, normed, rows)
    normalize_into(f3_tail, gain, normed, rows + f3_head.shape[0])
    projected[...] = dot(normed[...], proj[...])
    unit_into(projected, unit, 0, factors)
    dots[...] = dot(text_near[...], unit[...], LAST)
    totals[...] = weigh(dots, scale[0], bias[0], None, weights)
    turn_own(place, unit, factors, turned, unit_turned, inverse)
    normed_turned[...] = normed[...].T
    token[...] = jnp.zeros_like(token)


def third_body(
    scale, bias, place, t2, unit_near, unit_far, totals_near, totals_far, early_near, early_far,
    before, text_unit, weights, back_near, back_far, totals,
    text_columns, dots,
):
    rows = text_unit.shape[0]
    near = 2 * rows
    unit_into(t2, text_unit, 0)
    take_columns(place, text_unit, text_columns)
    dots[:, :near] = dot(text_unit[...], unit_near[...], LAST)
    dots[:, near:] = dot(text_unit[...], unit_far[...], LAST)
    added = weigh(dots, scale[0], bias[0], near, weights)
    totals[:, :near] = totals_near[...] + added[:, :near]
    totals[:, near:] = totals_far[...] + added[:, near:]
    added = dot(text_columns[...], weights[...], FIRST)
    back_near[...] = early_near[...] + added[:, :near]
    back_far[...] = early_far[...] + added[:, near:]


def pack_into(target, block, full):
    rows, columns = block.shape
    rest = columns - full
    target[:rows, :] = block[:, :full].astype(BF16)
    per_band = full // rest
    tail = block[:, full:]
    chunks = [tail[at : at + BAND, :] for at in range(0, rows, BAND)]
    for band in range(0, len(chunks), per_band):
        part = chunks[band : band + per_band]
        if len(part) < per_band:
            part.append(jnp.zeros((BAND, full - rest * len(part)), block.dtype))
        at = rows + (band // per_band) * BAND
        target[at : at + BAND, :] = jnp.concatenate(part, axis=1).astype(BF16)


def partial_body(
    members, groups, lead, scale, bias, place, t3, unit_near, unit_far, totals, back_near, back_far, unit_turned_near,
    unit_turned_far, inverse_near, inverse_far, turned_near, turned_far, proj_columns, gain,
    across, keep_lead, keep_tail, *refs,
):
    along, (text_unit, weights, text_columns, dots, packed) = refs[: groups // 2 - 1], refs[groups // 2 - 1 :]
    rows = text_unit.shape[0]
    near = 2 * rows
    every = members * rows
    width = unit_near.shape[1]
    columns = width // members
    count, full = packed.shape[1:]
    scale, bias = scale[0], bias[0]
    unit_into(t3, text_unit, 0)
    take_columns(place, text_unit, text_columns)
    dots[:, :near] = dot(text_unit[...], unit_near[...], LAST)
    dots[:, near:] = dot(text_unit[...], unit_far[...], LAST)
    total = totals[...] + weigh(dots, scale, bias, near + rows, weights)
    added = dot(text_columns[...], weights[...], FIRST)
    back = []
    for where, earlier, unit_turned, inverse in (
        (slice(0, near), back_near, unit_turned_near, inverse_near),
        (slice(near, every), back_far, unit_turned_far, inverse_far),
    ):
        whole = earlier[...] + added[:, where]
        part = (whole - unit_turned[...].astype(F32) * total[:, where]) * (inverse[...] * scale)
        back.append(part.astype(BF16))
    turned = jnp.concatenate([turned_near[...], turned_far[...]], axis=1)
    product = dot(turned, jnp.concatenate(back, axis=1), LAST)
    each = width // groups
    product = product * (1.0 / every)
    for group in range(groups):
        pack_into(packed.at[group], product[group * each : (group + 1) * each, :], full)

    terms = product * proj_columns[...].astype(F32)
    folded = jnp.concatenate([terms[:, full:], jnp.zeros((width, full + LANES - columns), F32)], axis=1)
    for at in range(0, full, LANES):
        folded = folded + terms[:, at : at + LANES]
    high = folded.astype(BF16)
    low = (folded - high.astype(F32)).astype(BF16)
    ones = jnp.ones((BAND, 2 * LANES), BF16)
    gain_row = dot(ones, jnp.concatenate([high, low], axis=1), LAST)[:1, :] / gain[...]
    pieces = [gain_row[:, at : at + LANES] for at in range(0, width, LANES)]
    pieces.append(jnp.zeros((BAND - len(pieces), LANES), F32))
    gain_tile = jnp.concatenate(pieces, axis=0).astype(BF16)
    for group in range(groups):
        packed[group, count - BAND :, full - LANES :] = gain_tile

    own = place[1]
    for step in range(groups // 2):
        across[step] = packed[own ^ 1 ^ (2 * step), :lead, :]
        keep_lead[step] = packed[own ^ (2 * step), :lead, :]
    for other in range(2):
        keep_tail[other] = packed[own ^ other, lead:, :]
        for step in range(1, groups // 2):
            along[step - 1][other] = packed[own ^ (2 * step) ^ other, lead:, :]


def image_body(
    scale, proj, text_near, text_third, text_fourth, weights_near, weights_third, weights_fourth,
    unit, factors, norm_back, token, back, product,
):
    rows = back.shape[0]
    scale = scale[0]
    product[...] = (
        dot(weights_near[:, :rows], text_near[...], FIRST)
        + dot(weights_third[:, :rows], text_third[...], FIRST)
        + dot(weights_fourth[:, :rows], text_fourth[...], FIRST)
    )

    def image_chunk(where):
        values = product[where, :] * scale
        direction = unit[where, :].astype(F32)
        back[where, :] = (
            (values - direction * sums(direction * values)) * factors[where, :1]
        ).astype(BF16)

    over_rows(rows, 32, image_chunk)
    norm_back[...] = dot(back[...], proj[...], LAST)
    token[...] = jnp.zeros_like(token)


def feature_body(features, gain, norm_back, before, feature_grad, token):
    rows, width = features.shape

    def feature_chunk(where):
        values = features[where, :].astype(F32)
        centred = values - sums(values) * (1.0 / width)
        deviation = lax.rsqrt(sums(centred * centred) * (1.0 / width) + 1e-06)
        xhat = centred * deviation
        scaled = norm_back[where, :] * gain[...]
        feature_grad[where, :] = (
            deviation
            * (scaled - sums(scaled) * (1.0 / width) - xhat * (sums(scaled * xhat) * (1.0 / width)))
        ).astype(BF16)

    over_rows(rows, 32, feature_chunk)
    token[...] = jnp.zeros_like(token)


def text_body(
    scale, text, weights_near, weights_far, unit_near, unit_far, text_columns, before,
    text_grad, back_near, back_far, token, product,
):
    rows = text_grad.shape[0]
    scale = scale[0]
    product[...] = dot(weights_near[:rows, :], unit_near[...]) + dot(weights_far[:rows, :], unit_far[...])

    def text_chunk(where):
        values = product[where, :] * scale
        own = text[where, :].astype(F32)
        own_inverse = lax.rsqrt(sums(own * own) + 1e-06)
        direction = own * own_inverse
        text_grad[where, :] = (
            (values - direction * sums(direction * values)) * own_inverse
        ).astype(BF16)

    over_rows(rows, 32, text_chunk)
    back_near[...] = dot(text_columns[...], weights_near[...], FIRST)
    back_far[...] = dot(text_columns[...], weights_far[...], FIRST)
    token[...] = jnp.zeros_like(token)


def first_sum_body(place, token, keep_lead, across, keep_tail, *refs):
    steps = keep_lead.shape[0]
    along, refs = refs[: steps - 1], refs[steps - 1 :]
    leads, (tail, tail_across, ordered) = refs[:steps], refs[steps:]
    for step in range(steps):
        leads[step][...] = (keep_lead[step].astype(F32) + across[step].astype(F32)).astype(BF16)
    own = place[1] // 2
    ordered[own] = keep_tail[...]
    for step in range(1, steps):
        ordered[own ^ step] = along[steps - 1 - step][...]
    value = ordered[0].astype(F32)
    for step in range(1, steps):
        value = value + ordered[step].astype(F32)
    tail[...] = value[0].astype(BF16)
    tail_across[...] = value[1].astype(BF16)


def last_sum_body(before, tail, tail_across, *refs):
    leads, total = refs[:-1], refs[-1]
    split = leads[0].shape[0]
    value = leads[0][...].astype(F32)
    for lead in leads[1:]:
        value = value + lead[...].astype(F32)
    total[:split, :] = value.astype(BF16)
    total[split:, :] = (tail[...].astype(F32) + tail_across[...].astype(F32)).astype(BF16)


def finish_body(members, place, *refs):
    packets, (proj_grad, gain_gradient, ordered) = refs[:members], refs[members:]
    count, full = packets[0].shape
    rows, width = proj_grad.shape
    rest = width // members - full
    per_band = full // rest
    for k in range(members):
        member = place[0] ^ k
        proj_grad[:, pl.ds(pl.multiple_of(member * full, LANES), full)] = packets[k][:rows, :].astype(F32)
        ordered[member] = packets[k][rows:, :].astype(F32)
    tails = []
    for index in range(rows // BAND):
        at, lane = (index // per_band) * BAND, (index % per_band) * rest
        tails.append(
            jnp.concatenate([ordered[member][at : at + BAND, lane : lane + rest] for member in range(members)], axis=1)
        )
    proj_grad[:, members * full :] = jnp.concatenate(tails, axis=0)
    value = ordered[0][count - rows - BAND :, full - LANES :]
    for member in range(1, members):
        value = value + ordered[member][count - rows - BAND :, full - LANES :]
    for at in range(width // LANES):
        gain_gradient[at * LANES : (at + 1) * LANES] = value[at]


def local_four(features, text, proj, gain, scale, bias):
    members = lax.axis_size("loop")
    groups = lax.axis_size("rep")
    place = jnp.stack([lax.axis_index("loop"), lax.axis_index("rep")]).astype(jnp.int32)
    rows, width = features.shape[0], features.shape[2]
    near, every = 2 * rows, 4 * rows
    columns = width // members
    full = columns // LANES * LANES
    each = width // groups
    bands = -(-(each // BAND) // (full // (columns - full)))
    packet = (each + bands * BAND, full)

    lead = (5 * packet[0] // BAND // 6) * BAND
    tail = packet[0] - lead
    steps = groups // 2

    f0, t0 = features[:, 0, :], text[:, 0, :]
    f2 = send(f0, "loop", lambda p: p ^ 2)
    f1 = send(f0, "loop", lambda p: p ^ 1)

    wide, half = ((near, width), BF16), ((rows, width), BF16)
    square, part, turned = ((near, near), BF16), ((near, columns), BF16), ((width, near), BF16)

    line, mine = ((1, near), F32), ((columns, near), BF16)
    kept = ((width, width), BF16)
    f0_kept, proj_kept, t_sent, gain_row, normed_near, unit_near, factors, text_own, token = call(
        near_body,
        [half, kept, half, ((1, width), F32), wide, wide, ((near, LANES), F32), half, TOKEN],
        [((near, width), F32)],
        smem=3,
        hbm=3,
        limit=46,
        flops=2 * near * width * width,
        moved=8 * near * width,
    )(scale, bias, place, f0, proj, t0, f1, gain)

    t2 = send(t_sent, "loop", lambda p: p ^ 2)
    t1 = send(t_sent, "loop", lambda p: p ^ 1)
    head = rows // 6 * 5
    f3_head, f3_tail = call(split_body, [((head, width), BF16), ((rows - head, width), BF16)], moved=1000)(f2, token)
    f3_head = send(f3_head, "loop", lambda p: p ^ 1)
    f3_tail = send(f3_tail, "loop", lambda p: p ^ 1)

    (
        text_near, turned_near, unit_turned_near, inverse_near, text_columns_near, weights_near, totals_near, proj_columns,
        token,
    ) = call(
        near_pairs_body,
        [wide, turned, mine, line, part, square, line, ((width, columns), BF16), TOKEN],
        [((near, near), F32), turned],
        smem=3,
        flops=1000,
        moved=1000,
    )(scale, bias, place, normed_near, unit_near, factors, text_own, t1, proj_kept, token)

    turned_far, unit_far, unit_turned_far, inverse_far, weights_far, totals_far, token = call(
        far_body,
        [turned, wide, mine, line, square, line, TOKEN],
        [wide, ((near, width), F32), ((near, near), F32), turned, ((near, LANES), F32)],
        smem=3,
        flops=1000,
        moved=1000,
    )(scale, bias, place, f2, f3_head, f3_tail, proj_kept, gain_row, text_near)

    back_kind = ((columns, near), F32)
    text_grad, early_near, early_far, token = call(
        text_body,
        [half, back_kind, back_kind, TOKEN],
        [((rows, width), F32)],
        smem=1,
        flops=1000,
        moved=1000,
    )(scale, t_sent, weights_near, weights_far, unit_near, unit_far, text_columns_near, token)

    t2_after, token = lax.optimization_barrier((t2, token))
    t3 = send(t2_after, "loop", lambda p: p ^ 1)

    narrow = ((rows, every), BF16)
    text_third, weights_third, back_near, back_far, totals = call(
        third_body,
        [half, narrow, back_kind, back_kind, ((1, every), F32)],
        [((rows, columns), BF16), ((rows, every), F32)],
        smem=3,
        flops=2 * near * width * width,
        moved=8 * near * width,
    )(
        scale, bias, place, t2, unit_near, unit_far, totals_near, totals_far, early_near, early_far, token,
    )

    outs = call(
        functools.partial(partial_body, members, groups, lead),
        [((steps, lead, full), BF16)] * 2 + [((2, tail, full), BF16)] * steps + [half, narrow],
        [((rows, columns), BF16), ((rows, every), F32), ((groups,) + packet, BF16)],
        smem=3,
        flops=4 * near * width * width,
        moved=16 * near * width,
    )(
        scale, bias, place, t3, unit_near, unit_far, totals, back_near, back_far, unit_turned_near, unit_turned_far,
        inverse_near, inverse_far, turned_near, turned_far, proj_columns, gain_row,
    )
    across, keep_lead, keep_tail = outs[:3]
    along, (text_fourth, weights_fourth) = outs[3 : 2 + steps], outs[2 + steps :]

    across = send(across, "rep", lambda p: p ^ 1)
    along = [send(along[step - 1], "rep", lambda p: p ^ (2 * step)) for step in reversed(range(1, steps))]

    norm_back, token = call(
        image_body,
        [((rows, width), F32), TOKEN],
        [half, ((rows, width), F32)],
        smem=1,
        flops=4 * near * width * width,
        moved=12 * near * width,
    )(
        scale, proj_kept, text_near, text_third, text_fourth, weights_near, weights_third, weights_fourth,
        unit_near, factors,
    )

    outs = call(
        first_sum_body,
        [((lead, full), BF16)] * steps + [((tail, full), BF16)] * 2,
        [((steps, 2, tail, full), BF16)],
        smem=1,
        moved=4 * each * width,
    )(place, token, keep_lead, across, keep_tail, *along)
    leads = [outs[0]] + [send(outs[step], "rep", lambda p: p ^ (2 * step)) for step in reversed(range(1, steps))]
    tail_across = send(outs[steps + 1], "rep", lambda p: p ^ 1)

    feature_grad, token = call(feature_body, [half, TOKEN], moved=12 * near * width)(
        f0_kept, gain_row, norm_back, outs[steps]
    )

    (reduced,) = call(
        last_sum_body,
        [(packet, BF16)],
        moved=4 * each * width,
    )(token, outs[steps], tail_across, *leads)
    far_block = send(reduced, "loop", lambda p: p ^ 2)
    near_block = send(reduced, "loop", lambda p: p ^ 1)
    blocks = [reduced, near_block, far_block, send(far_block, "loop", lambda p: p ^ 1)]

    proj_grad, gain_gradient = call(
        functools.partial(finish_body, members),
        [((each, width), F32), ((width,), F32)],
        [((members, bands * BAND, full), F32)],
        smem=1,
        moved=8 * each * width,
    )(place, *blocks)
    return feature_grad[:, None, :], text_grad[:, None, :], proj_grad, gain_gradient


def four_fits(mesh, rows_shape):
    members, groups = mesh.shape["loop"], mesh.shape["rep"]
    rows, width = rows_shape[0] // members, rows_shape[2]
    if members != 4 or groups != 8 or width % (members * groups) or width % LANES:
        return False
    columns, each = width // members, width // groups
    full = columns // LANES * LANES
    rest = columns - full
    if rest == 0 or full < LANES or full % rest or each % BAND or rows % 64 or width // LANES > BAND:
        return False
    chunks = each // BAND
    used = (chunks - 1) % (full // rest) + 1
    return used * rest <= full - LANES


def solution(mesh):
    def run(features, text, proj, gain, scale, bias):
        body = local_four if four_fits(mesh, features.shape) else local_any_size
        return jax.shard_map(
            body,
            mesh=mesh,
            in_specs=(P("loop", "rep", None), P("loop", "rep", None), P(), P(), P(), P()),
            out_specs=(P("loop", "rep", None), P("loop", "rep", None), P("rep", None), P()),
            check_vma=False,
        )(features, text, proj, gain, scale, bias)

    return run
```

```python
import functools

import jax
import jax.numpy as jnp
from jax import lax
from jax.experimental import pallas as pl
from jax.experimental.pallas import tpu as pltpu
from jax.sharding import PartitionSpec as P

F32 = jnp.float32
BF16 = jnp.bfloat16
LAST = (((1,), (1,)), ((), ()))
FIRST = (((0,), (0,)), ((), ()))


def dot(a, b, dims=(((1,), (0,)), ((), ()))):
    return lax.dot_general(a, b, dims, preferred_element_type=F32)


def unit_rows(values):
    inverse = lax.rsqrt(jnp.sum(values * values, axis=-1, keepdims=True) + 1e-06)
    return values * inverse, inverse


def standardize(rows):
    values = rows.astype(F32)
    centred = values - jnp.mean(values, axis=-1, keepdims=True)
    inverse = lax.rsqrt(jnp.mean(centred * centred, axis=-1, keepdims=True) + 1e-06)
    return centred * inverse, inverse


def send(value, axis, target):
    count = lax.axis_size(axis)
    return lax.ppermute(value, axis, [(p, target(p)) for p in range(count)])


def gather_group(value, count):
    mine = [value]
    for step in range(1, count // 2):
        mine.append(send(value, "loop", lambda p: (p + 2 * step) % count))
    mates = [send(block, "loop", lambda p: p ^ 1) for block in mine]
    return mine + mates


def local_any_size(features, text, proj, gain, scale, bias):
    n = lax.axis_size("loop")
    m = lax.axis_size("rep")
    me = lax.axis_index("loop")
    half = n // 2
    rows, width = features.shape[0], features.shape[2]
    columns = proj.shape[1] // n
    group_rows = rows * n
    logit_scale, logit_bias = scale[0], bias[0]

    own_features = features[:, 0, :]
    own_text = text[:, 0, :]
    text_blocks = gather_group(own_text, n)
    feature_blocks = gather_group(own_features, n)

    xhat, deviation = standardize(own_features)
    normed = (xhat * gain).astype(BF16)
    img_dir, img_inv = unit_rows(dot(normed, proj))
    img_unit = img_dir.astype(BF16)

    txt_dir, txt_inv = unit_rows(own_text.astype(F32))
    own_txt_unit = txt_dir.astype(BF16)
    txt_unit = jnp.concatenate(
        [own_txt_unit] + [unit_rows(block.astype(F32))[0].astype(BF16) for block in text_blocks[1:]]
    )
    row_ids = lax.broadcasted_iota(jnp.int32, (rows, group_rows), 0)
    column_ids = lax.broadcasted_iota(jnp.int32, (rows, group_rows), 1)
    diagonal = (row_ids == column_ids).astype(F32)

    def weights(left, right):
        logits = logit_scale * dot(left, right, LAST) + logit_bias
        return (jax.nn.sigmoid(logits) - diagonal).astype(BF16)

    img_back = logit_scale * dot(weights(img_unit, txt_unit), txt_unit)
    proj_back = (
        (img_back - img_dir * jnp.sum(img_dir * img_back, axis=-1, keepdims=True)) * img_inv
    ).astype(BF16)

    blocks = jnp.transpose(proj_back.reshape(rows, n, columns), (1, 0, 2))
    blocks = lax.all_to_all(blocks, "loop", 0, 0, tiled=True)
    back_columns = blocks.reshape(group_rows, columns)

    norm_back = dot(proj_back, proj, LAST)
    scaled = norm_back * gain
    feature_grad = (
        deviation
        * (
            scaled
            - jnp.mean(scaled, axis=-1, keepdims=True)
            - xhat * jnp.mean(scaled * xhat, axis=-1, keepdims=True)
        )
    ).astype(BF16)
    gain_term = jnp.sum(norm_back * xhat, axis=0) * (1.0 / group_rows)

    other_normed = [(standardize(block)[0] * gain).astype(BF16) for block in feature_blocks[1:]]
    relative = jnp.stack([normed] + other_normed)
    member = jnp.arange(n)
    same_core = (member % 2) == (me % 2)
    chips_back = ((me // 2 - member // 2) % half)
    position = jnp.where(same_core, chips_back, half + chips_back)
    group_normed = relative[position].reshape(group_rows, width)

    partial = (dot(group_normed, back_columns, FIRST) * (1.0 / group_rows)).astype(BF16)
    pieces = lax.all_to_all(partial.reshape(m, width // m, columns), "rep", 0, 0, tiled=True)
    reduced = jnp.sum(pieces.astype(F32), axis=0).astype(BF16)
    gains = lax.all_gather(gain_term, "rep")
    gain_sum = jnp.sum(gains, axis=0)
    proj_rows = lax.all_gather(reduced, "loop")
    proj_grad = jnp.transpose(proj_rows, (1, 0, 2)).reshape(width // m, n * columns).astype(F32)
    gain_gradient = jnp.sum(lax.all_gather(gain_sum, "loop"), axis=0)

    group_unit = jnp.concatenate(
        [img_unit] + [unit_rows(dot(block, proj))[0].astype(BF16) for block in other_normed]
    )
    text_weights = weights(own_txt_unit, group_unit)
    txt_back = logit_scale * dot(text_weights, group_unit)
    text_grad = (
        (txt_back - txt_dir * jnp.sum(txt_dir * txt_back, axis=-1, keepdims=True)) * txt_inv
    ).astype(BF16)
    return feature_grad[:, None, :], text_grad[:, None, :], proj_grad, gain_gradient


VMEM = pl.BlockSpec(memory_space=pltpu.VMEM)
SMEM = pl.BlockSpec(memory_space=pltpu.SMEM)
HBM = pl.BlockSpec(memory_space=pltpu.HBM)
LANES = 128
BAND = 16
TOKEN = ((8, LANES), F32)


def call(body, outs, scratch=(), smem=0, hbm=0, limit=24, flops=0, moved=0):
    def run(*operands):
        specs = [SMEM] * smem + [HBM] * hbm + [VMEM] * (len(operands) - smem - hbm)
        return pl.pallas_call(
            body,
            out_shape=[jax.ShapeDtypeStruct(shape, kind) for shape, kind in outs],
            in_specs=specs,
            out_specs=[VMEM] * len(outs),
            scratch_shapes=[pltpu.VMEM(shape, kind) for shape, kind in scratch]
            + [pltpu.SemaphoreType.DMA((hbm,))] * bool(hbm),
            compiler_params=pltpu.CompilerParams(vmem_limit_bytes=limit * 2**20),
            cost_estimate=pl.CostEstimate(flops=flops, bytes_accessed=moved, transcendentals=0),
        )(*operands)

    return run


def over_rows(count, step, body):
    def turn(index, _):
        body(pl.ds(pl.multiple_of(index * step, step), step))
        return 0

    lax.fori_loop(0, count // step, turn, 0, unroll=min(4, count // step))


def sums(values):
    return jnp.sum(values, axis=-1, keepdims=True)


def normalize_into(source, gain, target, at):
    rows, width = source.shape

    def chunk(where):
        values = source[where, :].astype(F32)
        centred = values - sums(values) * (1.0 / width)
        inverse = lax.rsqrt(sums(centred * centred) * (1.0 / width) + 1e-06)
        target[pl.ds(at + where.start, where.size), :] = (centred * inverse * gain[...]).astype(BF16)

    over_rows(rows, 32, chunk)


def unit_into(source, target, at, inverses=None):
    rows = source.shape[0]

    def chunk(where):
        values = source[where, :].astype(F32)
        inverse = lax.rsqrt(sums(values * values) + 1e-06)
        place = pl.ds(at + where.start, where.size)
        target[place, :] = (values * inverse).astype(BF16)
        if inverses is not None:
            inverses[place, :] = jnp.broadcast_to(inverse, (where.size, LANES))

    over_rows(rows, 32, chunk)


def weigh(dots, scale, bias, diagonal, weights):
    texts, images = dots.shape

    def chunk(index, total):
        where = pl.ds(pl.multiple_of(index * BAND, BAND), BAND)
        product = dots[where, :]
        weight = jnp.tanh((0.5 * scale) * product + 0.5 * bias)
        offset = 0.5
        if diagonal is not None:
            text = index * BAND + diagonal + lax.broadcasted_iota(jnp.int32, product.shape, 0)
            image = lax.broadcasted_iota(jnp.int32, product.shape, 1)
            offset = jnp.where(text == image, -0.5, 0.5)
        weight = (0.5 * weight + offset).astype(BF16)
        weights[where, :] = weight
        both = weight.astype(F32) * product
        return total + both[:8, :] + both[8:, :]

    total = lax.fori_loop(0, texts // BAND, chunk, jnp.zeros((8, images), F32), unroll=4)
    return jnp.sum(total, axis=0, keepdims=True)


def take_columns(place, source, target):
    members = source.shape[1] // target.shape[1]
    full = target.shape[1] // LANES * LANES
    rest = target.shape[1] - full
    target[:, :full] = source[:, pl.ds(pl.multiple_of(place[0] * full, LANES), full)]
    for member in range(members):

        @pl.when(place[0] == member)
        def _():
            target[:, full:] = source[:, members * full + member * rest : members * full + (member + 1) * rest]


def near_body(
    scale, bias, place, f0_far, proj_far, t0_far, f1, gain_line,
    f0, proj, t0, gain, normed, unit, factors, text_unit, token, projected, semaphores,
):
    rows = f0.shape[0]
    copies = [
        pltpu.make_async_copy(source, target, semaphores.at[at])
        for at, (source, target) in enumerate(((f0_far, f0), (proj_far, proj), (t0_far, t0)))
    ]
    for copy in copies:
        copy.start()
    for at in range(0, gain.shape[1], LANES):
        gain[:, at : at + LANES] = gain_line[at : at + LANES].reshape(1, LANES)
    normalize_into(f1, gain, normed, rows)
    copies[0].wait()
    normalize_into(f0, gain, normed, 0)
    copies[1].wait()
    projected[...] = dot(normed[...], proj[...])
    copies[2].wait()
    unit_into(t0, text_unit, 0)
    unit_into(projected, unit, 0, factors)
    token[...] = jnp.zeros_like(token)


def near_pairs_body(
    scale, bias, place, normed, unit, factors, text_own, t1, proj, before,
    text_unit, normed_turned, turned, unit_turned, inverse, text_columns, weights, totals, proj_columns, token, dots,
):
    token[...] = jnp.zeros_like(token)
    rows = t1.shape[0]
    text_unit[:rows, :] = text_own[...]
    text_unit[rows:, :] = t1[...]
    dots[...] = dot(text_unit[...], unit[...], LAST)
    totals[...] = weigh(dots, scale[0], bias[0], 0, weights)
    take_columns(place, text_unit, text_columns)
    take_columns(place, proj, proj_columns)
    turn_own(place, unit, factors, turned, unit_turned, inverse)
    normed_turned[...] = normed[...].T


def turn_own(place, unit, factors, turned, unit_turned, inverse):
    columns = unit_turned.shape[0]
    full = columns // LANES * LANES
    rest = columns - full
    turned[...] = unit[...].T
    unit_turned[:full, :] = turned[pl.ds(pl.multiple_of(place[0] * full, LANES), full), :]
    begin = turned.shape[0] // columns * full
    unit_turned[full:, :] = turned[pl.ds(pl.multiple_of(begin + place[0] * rest, BAND), rest), :]
    inverse[...] = factors[...].T[:1, :]


def split_body(f2, before, head, tail):
    head[...] = f2[: head.shape[0], :]
    tail[...] = f2[head.shape[0] :, :]


def far_body(
    scale, bias, place, f2, f3_head, f3_tail, proj, gain, text_near, text_columns, weights_near,
    normed_turned, unit, turned, unit_turned, inverse, weights, totals, early_near, early_far, token,
    normed, projected, dots, factors,
):
    rows = f2.shape[0]
    normalize_into(f2, gain, normed, 0)
    normalize_into(f3_head, gain, normed, rows)
    normalize_into(f3_tail, gain, normed, rows + f3_head.shape[0])
    projected[...] = dot(normed[...], proj[...])
    unit_into(projected, unit, 0, factors)
    dots[...] = dot(text_near[...], unit[...], LAST)
    totals[...] = weigh(dots, scale[0], bias[0], None, weights)
    turn_own(place, unit, factors, turned, unit_turned, inverse)
    normed_turned[...] = normed[...].T
    early_near[...] = dot(text_columns[...], weights_near[...], FIRST)
    early_far[...] = dot(text_columns[...], weights[...], FIRST)
    token[...] = jnp.zeros_like(token)


def third_body(
    scale, bias, place, text_unit, flat_near, flat_far, totals_near, totals_far, early_near, early_far,
    before, weights, back_near, back_far, totals,
    text_columns, dots,
):
    rows = text_unit.shape[0]
    near = 2 * rows
    take_columns(place, text_unit, text_columns)
    dots[:, :near] = dot(text_unit[...], flat_near[...])
    dots[:, near:] = dot(text_unit[...], flat_far[...])
    added = weigh(dots, scale[0], bias[0], near, weights)
    totals[:, :near] = totals_near[...] + added[:, :near]
    totals[:, near:] = totals_far[...] + added[:, near:]
    added = dot(text_columns[...], weights[...], FIRST)
    back_near[...] = early_near[...] + added[:, :near]
    back_far[...] = early_far[...] + added[:, near:]


def pack_into(target, block, full):
    rows, columns = block.shape
    rest = columns - full
    target[:rows, :] = block[:, :full].astype(BF16)
    per_band = full // rest
    tail = block[:, full:]
    chunks = [tail[at : at + BAND, :] for at in range(0, rows, BAND)]
    for band in range(0, len(chunks), per_band):
        part = chunks[band : band + per_band]
        if len(part) < per_band:
            part.append(jnp.zeros((BAND, full - rest * len(part)), block.dtype))
        at = rows + (band // per_band) * BAND
        target[at : at + BAND, :] = jnp.concatenate(part, axis=1).astype(BF16)


def partial_body(
    members, groups, lead, scale, bias, place, text_unit, flat_near, flat_far, totals, back_near, back_far, unit_turned_near,
    unit_turned_far, inverse_near, inverse_far, turned_near, turned_far, proj_columns, gain,
    across, keep_lead, keep_tail, *refs,
):
    along, (weights, text_columns, dots, packed) = refs[: groups // 2 - 1], refs[groups // 2 - 1 :]
    rows = text_unit.shape[0]
    near = 2 * rows
    every = members * rows
    width = text_unit.shape[1]
    columns = width // members
    count, full = packed.shape[1:]
    scale, bias = scale[0], bias[0]
    take_columns(place, text_unit, text_columns)
    dots[:, :near] = dot(text_unit[...], flat_near[...])
    dots[:, near:] = dot(text_unit[...], flat_far[...])
    total = totals[...] + weigh(dots, scale, bias, near + rows, weights)
    added = dot(text_columns[...], weights[...], FIRST)
    back = []
    for where, earlier, unit_turned, inverse in (
        (slice(0, near), back_near, unit_turned_near, inverse_near),
        (slice(near, every), back_far, unit_turned_far, inverse_far),
    ):
        whole = earlier[...] + added[:, where]
        part = (whole - unit_turned[...].astype(F32) * total[:, where]) * (inverse[...] * scale)
        back.append(part.astype(BF16))
    turned = jnp.concatenate([turned_near[...], turned_far[...]], axis=1)
    product = dot(turned, jnp.concatenate(back, axis=1), LAST)
    each = width // groups
    product = product * (1.0 / every)
    for group in range(groups):
        pack_into(packed.at[group], product[group * each : (group + 1) * each, :], full)

    terms = product * proj_columns[...].astype(F32)
    folded = jnp.concatenate([terms[:, full:], jnp.zeros((width, full + LANES - columns), F32)], axis=1)
    for at in range(0, full, LANES):
        folded = folded + terms[:, at : at + LANES]
    high = folded.astype(BF16)
    low = (folded - high.astype(F32)).astype(BF16)
    ones = jnp.ones((BAND, 2 * LANES), BF16)
    gain_row = dot(ones, jnp.concatenate([high, low], axis=1), LAST)[:1, :] / gain[...]
    pieces = [gain_row[:, at : at + LANES] for at in range(0, width, LANES)]
    pieces.append(jnp.zeros((BAND - len(pieces), LANES), F32))
    gain_tile = jnp.concatenate(pieces, axis=0).astype(BF16)
    for group in range(groups):
        packed[group, count - BAND :, full - LANES :] = gain_tile

    own = place[1]
    for step in range(groups // 2):
        across[step] = packed[own ^ 1 ^ (2 * step), :lead, :]
        keep_lead[step] = packed[own ^ (2 * step), :lead, :]
    for other in range(2):
        keep_tail[other] = packed[own ^ other, lead:, :]
        for step in range(1, groups // 2):
            along[step - 1][other] = packed[own ^ (2 * step) ^ other, lead:, :]


def image_body(
    scale, proj, text_near, text_third, text_fourth, weights_near, weights_third, weights_fourth,
    unit, factors, norm_back, token, back, product,
):
    rows = back.shape[0]
    scale = scale[0]
    product[...] = (
        dot(weights_near[:, :rows], text_near[...], FIRST)
        + dot(weights_third[:, :rows], text_third[...], FIRST)
        + dot(weights_fourth[:, :rows], text_fourth[...], FIRST)
    )

    def image_chunk(where):
        values = product[where, :] * scale
        direction = unit[where, :].astype(F32)
        back[where, :] = (
            (values - direction * sums(direction * values)) * factors[where, :1]
        ).astype(BF16)

    over_rows(rows, 32, image_chunk)
    norm_back[...] = dot(back[...], proj[...], LAST)
    token[...] = jnp.zeros_like(token)


def feature_body(features, gain, norm_back, before, feature_grad, token):
    rows, width = features.shape

    def feature_chunk(where):
        values = features[where, :].astype(F32)
        centred = values - sums(values) * (1.0 / width)
        deviation = lax.rsqrt(sums(centred * centred) * (1.0 / width) + 1e-06)
        xhat = centred * deviation
        scaled = norm_back[where, :] * gain[...]
        feature_grad[where, :] = (
            deviation
            * (scaled - sums(scaled) * (1.0 / width) - xhat * (sums(scaled * xhat) * (1.0 / width)))
        ).astype(BF16)

    over_rows(rows, 32, feature_chunk)
    token[...] = jnp.zeros_like(token)


def text_body(
    scale, text, weights_near, weights_far, unit_near, unit_far, before, text_grad, token, product,
):
    rows = text_grad.shape[0]
    scale = scale[0]
    product[...] = dot(weights_near[:rows, :], unit_near[...]) + dot(weights_far[:rows, :], unit_far[...])

    def text_chunk(where):
        values = product[where, :] * scale
        own = text[where, :].astype(F32)
        own_inverse = lax.rsqrt(sums(own * own) + 1e-06)
        direction = own * own_inverse
        text_grad[where, :] = (
            (values - direction * sums(direction * values)) * own_inverse
        ).astype(BF16)

    over_rows(rows, 32, text_chunk)
    token[...] = jnp.zeros_like(token)


def first_sum_body(place, token, keep_lead, across, keep_tail, *refs):
    steps = keep_lead.shape[0]
    along, refs = refs[: steps - 1], refs[steps - 1 :]
    leads, (tail, tail_across, ordered) = refs[:steps], refs[steps:]
    for step in range(steps):
        leads[step][...] = (keep_lead[step].astype(F32) + across[step].astype(F32)).astype(BF16)
    own = place[1] // 2
    ordered[own] = keep_tail[...]
    for step in range(1, steps):
        ordered[own ^ step] = along[steps - 1 - step][...]
    value = ordered[0].astype(F32)
    for step in range(1, steps):
        value = value + ordered[step].astype(F32)
    tail[...] = value[0].astype(BF16)
    tail_across[...] = value[1].astype(BF16)


def last_sum_body(before, tail, tail_across, *refs):
    leads, total = refs[:-1], refs[-1]
    split = leads[0].shape[0]
    value = leads[0][...].astype(F32)
    for lead in leads[1:]:
        value = value + lead[...].astype(F32)
    total[:split, :] = value.astype(BF16)
    total[split:, :] = (tail[...].astype(F32) + tail_across[...].astype(F32)).astype(BF16)


def finish_body(members, place, before, *refs):
    packets, (proj_grad, gain_gradient, ordered) = refs[:members], refs[members:]
    count, full = packets[0].shape
    rows, width = proj_grad.shape
    rest = width // members - full
    per_band = full // rest
    for k in range(members):
        member = place[0] ^ k
        proj_grad[:, pl.ds(pl.multiple_of(member * full, LANES), full)] = packets[k][:rows, :].astype(F32)
        ordered[member] = packets[k][rows:, :].astype(F32)
    tails = []
    for index in range(rows // BAND):
        at, lane = (index // per_band) * BAND, (index % per_band) * rest
        tails.append(
            jnp.concatenate([ordered[member][at : at + BAND, lane : lane + rest] for member in range(members)], axis=1)
        )
    proj_grad[:, members * full :] = jnp.concatenate(tails, axis=0)
    value = ordered[0][count - rows - BAND :, full - LANES :]
    for member in range(1, members):
        value = value + ordered[member][count - rows - BAND :, full - LANES :]
    for at in range(width // LANES):
        gain_gradient[at * LANES : (at + 1) * LANES] = value[at]


def local_four(features, text, proj, gain, scale, bias):
    members = lax.axis_size("loop")
    groups = lax.axis_size("rep")
    place = jnp.stack([lax.axis_index("loop"), lax.axis_index("rep")]).astype(jnp.int32)
    rows, width = features.shape[0], features.shape[2]
    near, every = 2 * rows, 4 * rows
    columns = width // members
    full = columns // LANES * LANES
    each = width // groups
    bands = -(-(each // BAND) // (full // (columns - full)))
    packet = (each + bands * BAND, full)

    lead = (5 * packet[0] // BAND // 6) * BAND
    tail = packet[0] - lead
    steps = groups // 2

    f0, t0 = features[:, 0, :], text[:, 0, :]
    f2 = send(f0, "loop", lambda p: p ^ 2)
    f1 = send(f0, "loop", lambda p: p ^ 1)

    wide, half = ((near, width), BF16), ((rows, width), BF16)
    square, part, turned = ((near, near), BF16), ((near, columns), BF16), ((width, near), BF16)

    line, mine = ((1, near), F32), ((columns, near), BF16)
    kept = ((width, width), BF16)
    f0_kept, proj_kept, t0_kept, gain_row, normed_near, unit_near, factors, text_own, token = call(
        near_body,
        [half, kept, half, ((1, width), F32), wide, wide, ((near, LANES), F32), half, TOKEN],
        [((near, width), F32)],
        smem=3,
        hbm=3,
        limit=46,
        flops=2 * near * width * width,
        moved=8 * near * width,
    )(scale, bias, place, f0, proj, t0, f1, gain)

    t2 = send(text_own, "loop", lambda p: p ^ 2)
    t1 = send(text_own, "loop", lambda p: p ^ 1)
    head = rows // 6 * 5
    f3_head, f3_tail = call(split_body, [((head, width), BF16), ((rows - head, width), BF16)], moved=1000)(f2, token)
    f3_head = send(f3_head, "loop", lambda p: p ^ 1)
    f3_tail = send(f3_tail, "loop", lambda p: p ^ 1)

    (
        text_near, turned_near, flat_near, unit_turned_near, inverse_near, text_columns_near, weights_near, totals_near, proj_columns,
        token,
    ) = call(
        near_pairs_body,
        [wide, turned, turned, mine, line, part, square, line, ((width, columns), BF16), TOKEN],
        [((near, near), F32)],
        smem=3,
        flops=1000,
        moved=1000,
    )(scale, bias, place, normed_near, unit_near, factors, text_own, t1, proj_kept, token)

    back_kind = ((columns, near), F32)
    (
        turned_far, unit_far, flat_far, unit_turned_far, inverse_far, weights_far, totals_far, early_near, early_far,
        token,
    ) = call(
        far_body,
        [turned, wide, turned, mine, line, square, line, back_kind, back_kind, TOKEN],
        [wide, ((near, width), F32), ((near, near), F32), ((near, LANES), F32)],
        smem=3,
        flops=1000,
        moved=1000,
    )(
        scale, bias, place, f2, f3_head, f3_tail, proj_kept, gain_row, text_near, text_columns_near, weights_near,
    )

    t2_after, token = lax.optimization_barrier((t2, token))
    t3 = send(t2_after, "loop", lambda p: p ^ 1)

    narrow = ((rows, every), BF16)
    weights_third, back_near, back_far, totals = call(
        third_body,
        [narrow, back_kind, back_kind, ((1, every), F32)],
        [((rows, columns), BF16), ((rows, every), F32)],
        smem=3,
        flops=2 * near * width * width,
        moved=8 * near * width,
    )(
        scale, bias, place, t2, flat_near, flat_far, totals_near, totals_far, early_near, early_far, token,
    )

    outs = call(
        functools.partial(partial_body, members, groups, lead),
        [((steps, lead, full), BF16)] * 2 + [((2, tail, full), BF16)] * steps + [narrow],
        [((rows, columns), BF16), ((rows, every), F32), ((groups,) + packet, BF16)],
        smem=3,
        flops=4 * near * width * width,
        moved=16 * near * width,
    )(
        scale, bias, place, t3, flat_near, flat_far, totals, back_near, back_far, unit_turned_near, unit_turned_far,
        inverse_near, inverse_far, turned_near, turned_far, proj_columns, gain_row,
    )
    across, keep_lead, keep_tail = outs[:3]
    along, weights_fourth = outs[3 : 2 + steps], outs[2 + steps]

    across = send(across, "rep", lambda p: p ^ 1)
    along = [send(along[step - 1], "rep", lambda p: p ^ (2 * step)) for step in reversed(range(1, steps))]

    norm_back, token = call(
        image_body,
        [((rows, width), F32), TOKEN],
        [half, ((rows, width), F32)],
        smem=1,
        flops=4 * near * width * width,
        moved=12 * near * width,
    )(
        scale, proj_kept, text_near, t2, t3, weights_near, weights_third, weights_fourth,
        unit_near, factors,
    )

    outs = call(
        first_sum_body,
        [((lead, full), BF16)] * steps + [((tail, full), BF16)] * 2,
        [((steps, 2, tail, full), BF16)],
        smem=1,
        moved=4 * each * width,
    )(place, token, keep_lead, across, keep_tail, *along)
    leads = [outs[0]] + [send(outs[step], "rep", lambda p: p ^ (2 * step)) for step in reversed(range(1, steps))]
    tail_across = send(outs[steps + 1], "rep", lambda p: p ^ 1)

    feature_grad, token = call(feature_body, [half, TOKEN], moved=12 * near * width)(
        f0_kept, gain_row, norm_back, outs[steps]
    )

    (reduced,) = call(
        last_sum_body,
        [(packet, BF16)],
        moved=4 * each * width,
    )(token, outs[steps], tail_across, *leads)
    far_block = send(reduced, "loop", lambda p: p ^ 2)
    near_block = send(reduced, "loop", lambda p: p ^ 1)
    text_grad, token = call(
        text_body,
        [half, TOKEN],
        [((rows, width), F32)],
        smem=1,
        flops=2 * near * width * width,
        moved=6 * near * width,
    )(scale, t0_kept, weights_near, weights_far, unit_near, unit_far, reduced)
    far_block, token = lax.optimization_barrier((far_block, token))
    blocks = [reduced, near_block, far_block, send(far_block, "loop", lambda p: p ^ 1)]

    proj_grad, gain_gradient = call(
        functools.partial(finish_body, members),
        [((each, width), F32), ((width,), F32)],
        [((members, bands * BAND, full), F32)],
        smem=1,
        moved=8 * each * width,
    )(place, token, *blocks)
    return feature_grad[:, None, :], text_grad[:, None, :], proj_grad, gain_gradient


def four_fits(mesh, rows_shape):
    members, groups = mesh.shape["loop"], mesh.shape["rep"]
    rows, width = rows_shape[0] // members, rows_shape[2]
    if members != 4 or groups != 8 or width % (members * groups) or width % LANES:
        return False
    columns, each = width // members, width // groups
    full = columns // LANES * LANES
    rest = columns - full
    if rest == 0 or full < LANES or full % rest or each % BAND or rows % 64 or width // LANES > BAND:
        return False
    chunks = each // BAND
    used = (chunks - 1) % (full // rest) + 1
    return used * rest <= full - LANES


def solution(mesh):
    def run(features, text, proj, gain, scale, bias):
        body = local_four if four_fits(mesh, features.shape) else local_any_size
        return jax.shard_map(
            body,
            mesh=mesh,
            in_specs=(P("loop", "rep", None), P("loop", "rep", None), P(), P(), P(), P()),
            out_specs=(P("loop", "rep", None), P("loop", "rep", None), P("rep", None), P()),
            check_vma=False,
        )(features, text, proj, gain, scale, bias)

    return run
```

```python
import functools

import jax
import jax.numpy as jnp
from jax import lax
from jax.experimental import pallas as pl
from jax.experimental.pallas import tpu as pltpu
from jax.sharding import PartitionSpec as P

F32 = jnp.float32
BF16 = jnp.bfloat16
LAST = (((1,), (1,)), ((), ()))
FIRST = (((0,), (0,)), ((), ()))


def dot(a, b, dims=(((1,), (0,)), ((), ()))):
    return lax.dot_general(a, b, dims, preferred_element_type=F32)


def unit_rows(values):
    inverse = lax.rsqrt(jnp.sum(values * values, axis=-1, keepdims=True) + 1e-06)
    return values * inverse, inverse


def standardize(rows):
    values = rows.astype(F32)
    centred = values - jnp.mean(values, axis=-1, keepdims=True)
    inverse = lax.rsqrt(jnp.mean(centred * centred, axis=-1, keepdims=True) + 1e-06)
    return centred * inverse, inverse


def send(value, axis, target):
    count = lax.axis_size(axis)
    return lax.ppermute(value, axis, [(p, target(p)) for p in range(count)])


def gather_group(value, count):
    mine = [value]
    for step in range(1, count // 2):
        mine.append(send(value, "loop", lambda p: (p + 2 * step) % count))
    mates = [send(block, "loop", lambda p: p ^ 1) for block in mine]
    return mine + mates


def local_any_size(features, text, proj, gain, scale, bias):
    n = lax.axis_size("loop")
    m = lax.axis_size("rep")
    me = lax.axis_index("loop")
    half = n // 2
    rows, width = features.shape[0], features.shape[2]
    columns = proj.shape[1] // n
    group_rows = rows * n
    logit_scale, logit_bias = scale[0], bias[0]

    own_features = features[:, 0, :]
    own_text = text[:, 0, :]
    text_blocks = gather_group(own_text, n)
    feature_blocks = gather_group(own_features, n)

    xhat, deviation = standardize(own_features)
    normed = (xhat * gain).astype(BF16)
    img_dir, img_inv = unit_rows(dot(normed, proj))
    img_unit = img_dir.astype(BF16)

    txt_dir, txt_inv = unit_rows(own_text.astype(F32))
    own_txt_unit = txt_dir.astype(BF16)
    txt_unit = jnp.concatenate(
        [own_txt_unit] + [unit_rows(block.astype(F32))[0].astype(BF16) for block in text_blocks[1:]]
    )
    row_ids = lax.broadcasted_iota(jnp.int32, (rows, group_rows), 0)
    column_ids = lax.broadcasted_iota(jnp.int32, (rows, group_rows), 1)
    diagonal = (row_ids == column_ids).astype(F32)

    def weights(left, right):
        logits = logit_scale * dot(left, right, LAST) + logit_bias
        return (jax.nn.sigmoid(logits) - diagonal).astype(BF16)

    img_back = logit_scale * dot(weights(img_unit, txt_unit), txt_unit)
    proj_back = (
        (img_back - img_dir * jnp.sum(img_dir * img_back, axis=-1, keepdims=True)) * img_inv
    ).astype(BF16)

    blocks = jnp.transpose(proj_back.reshape(rows, n, columns), (1, 0, 2))
    blocks = lax.all_to_all(blocks, "loop", 0, 0, tiled=True)
    back_columns = blocks.reshape(group_rows, columns)

    norm_back = dot(proj_back, proj, LAST)
    scaled = norm_back * gain
    feature_grad = (
        deviation
        * (
            scaled
            - jnp.mean(scaled, axis=-1, keepdims=True)
            - xhat * jnp.mean(scaled * xhat, axis=-1, keepdims=True)
        )
    ).astype(BF16)
    gain_term = jnp.sum(norm_back * xhat, axis=0) * (1.0 / group_rows)

    other_normed = [(standardize(block)[0] * gain).astype(BF16) for block in feature_blocks[1:]]
    relative = jnp.stack([normed] + other_normed)
    member = jnp.arange(n)
    same_core = (member % 2) == (me % 2)
    chips_back = ((me // 2 - member // 2) % half)
    position = jnp.where(same_core, chips_back, half + chips_back)
    group_normed = relative[position].reshape(group_rows, width)

    partial = (dot(group_normed, back_columns, FIRST) * (1.0 / group_rows)).astype(BF16)
    pieces = lax.all_to_all(partial.reshape(m, width // m, columns), "rep", 0, 0, tiled=True)
    reduced = jnp.sum(pieces.astype(F32), axis=0).astype(BF16)
    gains = lax.all_gather(gain_term, "rep")
    gain_sum = jnp.sum(gains, axis=0)
    proj_rows = lax.all_gather(reduced, "loop")
    proj_grad = jnp.transpose(proj_rows, (1, 0, 2)).reshape(width // m, n * columns).astype(F32)
    gain_gradient = jnp.sum(lax.all_gather(gain_sum, "loop"), axis=0)

    group_unit = jnp.concatenate(
        [img_unit] + [unit_rows(dot(block, proj))[0].astype(BF16) for block in other_normed]
    )
    text_weights = weights(own_txt_unit, group_unit)
    txt_back = logit_scale * dot(text_weights, group_unit)
    text_grad = (
        (txt_back - txt_dir * jnp.sum(txt_dir * txt_back, axis=-1, keepdims=True)) * txt_inv
    ).astype(BF16)
    return feature_grad[:, None, :], text_grad[:, None, :], proj_grad, gain_gradient


VMEM = pl.BlockSpec(memory_space=pltpu.VMEM)
SMEM = pl.BlockSpec(memory_space=pltpu.SMEM)
HBM = pl.BlockSpec(memory_space=pltpu.HBM)
LANES = 128
BAND = 16
TOKEN = ((8, LANES), F32)


def call(body, outs, scratch=(), smem=0, hbm=0, limit=24, flops=0, moved=0):
    def run(*operands):
        specs = [SMEM] * smem + [HBM] * hbm + [VMEM] * (len(operands) - smem - hbm)
        return pl.pallas_call(
            body,
            out_shape=[jax.ShapeDtypeStruct(shape, kind) for shape, kind in outs],
            in_specs=specs,
            out_specs=[VMEM] * len(outs),
            scratch_shapes=[pltpu.VMEM(shape, kind) for shape, kind in scratch]
            + [pltpu.SemaphoreType.DMA((hbm,))] * bool(hbm),
            compiler_params=pltpu.CompilerParams(vmem_limit_bytes=limit * 2**20),
            cost_estimate=pl.CostEstimate(flops=flops, bytes_accessed=moved, transcendentals=0),
        )(*operands)

    return run


def over_rows(count, step, body):
    def turn(index, _):
        body(pl.ds(pl.multiple_of(index * step, step), step))
        return 0

    lax.fori_loop(0, count // step, turn, 0, unroll=min(4, count // step))


def sums(values):
    return jnp.sum(values, axis=-1, keepdims=True)


def normalize_into(source, gain, target, at):
    rows, width = source.shape

    def chunk(where):
        values = source[where, :].astype(F32)
        centred = values - sums(values) * (1.0 / width)
        inverse = lax.rsqrt(sums(centred * centred) * (1.0 / width) + 1e-06)
        target[pl.ds(at + where.start, where.size), :] = (centred * inverse * gain[...]).astype(BF16)

    over_rows(rows, 32, chunk)


def unit_into(source, target, at, inverses=None):
    rows = source.shape[0]

    def chunk(where):
        values = source[where, :].astype(F32)
        inverse = lax.rsqrt(sums(values * values) + 1e-06)
        place = pl.ds(at + where.start, where.size)
        target[place, :] = (values * inverse).astype(BF16)
        if inverses is not None:
            inverses[place, :] = jnp.broadcast_to(inverse, (where.size, LANES))

    over_rows(rows, 32, chunk)


def weigh(dots, scale, bias, diagonal, weights):
    texts, images = dots.shape

    def chunk(index, total):
        where = pl.ds(pl.multiple_of(index * BAND, BAND), BAND)
        product = dots[where, :]
        weight = jnp.tanh((0.5 * scale) * product + 0.5 * bias)
        offset = 0.5
        if diagonal is not None:
            text = index * BAND + diagonal + lax.broadcasted_iota(jnp.int32, product.shape, 0)
            image = lax.broadcasted_iota(jnp.int32, product.shape, 1)
            offset = jnp.where(text == image, -0.5, 0.5)
        weight = (0.5 * weight + offset).astype(BF16)
        weights[where, :] = weight
        both = weight.astype(F32) * product
        return total + both[:8, :] + both[8:, :]

    total = lax.fori_loop(0, texts // BAND, chunk, jnp.zeros((8, images), F32), unroll=4)
    return jnp.sum(total, axis=0, keepdims=True)


def take_columns(source, target):
    members = source.shape[1] // target.shape[1]
    full = target.shape[1] // LANES * LANES
    rest = target.shape[1] - full
    target[:, :full] = source[:, pl.ds(pl.multiple_of(lax.axis_index("loop") * full, LANES), full)]
    for member in range(members):

        @pl.when(lax.axis_index("loop") == member)
        def _():
            target[:, full:] = source[:, members * full + member * rest : members * full + (member + 1) * rest]


def near_body(
    scale, bias, f0_far, proj_far, t0_far, f1, gain_line,
    f0, proj, t0, gain, normed, unit, factors, text_unit, token, projected, semaphores,
):
    rows = f0.shape[0]
    copies = [
        pltpu.make_async_copy(source, target, semaphores.at[at])
        for at, (source, target) in enumerate(((f0_far, f0), (proj_far, proj), (t0_far, t0)))
    ]
    for copy in copies:
        copy.start()
    for at in range(0, gain.shape[1], LANES):
        gain[:, at : at + LANES] = gain_line[at : at + LANES].reshape(1, LANES)
    normalize_into(f1, gain, normed, rows)
    copies[0].wait()
    normalize_into(f0, gain, normed, 0)
    copies[1].wait()
    projected[...] = dot(normed[...], proj[...])
    copies[2].wait()
    unit_into(t0, text_unit, 0)
    unit_into(projected, unit, 0, factors)
    token[...] = jnp.zeros_like(token)


def near_pairs_body(
    scale, bias, normed, unit, factors, text_own, t1, proj, before,
    text_unit, normed_turned, turned, unit_turned, inverse, text_columns, weights, totals, proj_columns, token, dots,
):
    token[...] = jnp.zeros_like(token)
    rows = t1.shape[0]
    text_unit[:rows, :] = text_own[...]
    text_unit[rows:, :] = t1[...]
    dots[...] = dot(text_unit[...], unit[...], LAST)
    totals[...] = weigh(dots, scale[0], bias[0], 0, weights)
    take_columns(text_unit, text_columns)
    take_columns(proj, proj_columns)
    turn_own(unit, factors, turned, unit_turned, inverse)
    normed_turned[...] = normed[...].T


def turn_own(unit, factors, turned, unit_turned, inverse):
    columns = unit_turned.shape[0]
    full = columns // LANES * LANES
    rest = columns - full
    turned[...] = unit[...].T
    unit_turned[:full, :] = turned[pl.ds(pl.multiple_of(lax.axis_index("loop") * full, LANES), full), :]
    begin = turned.shape[0] // columns * full
    unit_turned[full:, :] = turned[pl.ds(pl.multiple_of(begin + lax.axis_index("loop") * rest, BAND), rest), :]
    inverse[...] = factors[...].T[:1, :]


def split_body(f2, before, head, tail):
    head[...] = f2[: head.shape[0], :]
    tail[...] = f2[head.shape[0] :, :]


def far_body(
    scale, bias, f2, f3_head, f3_tail, proj, gain, text_near, text_columns, weights_near,
    normed_turned, unit, turned, unit_turned, inverse, weights, totals, early_near, early_far, token,
    normed, projected, dots, factors,
):
    rows = f2.shape[0]
    normalize_into(f2, gain, normed, 0)
    normalize_into(f3_head, gain, normed, rows)
    normalize_into(f3_tail, gain, normed, rows + f3_head.shape[0])
    projected[...] = dot(normed[...], proj[...])
    unit_into(projected, unit, 0, factors)
    dots[...] = dot(text_near[...], unit[...], LAST)
    totals[...] = weigh(dots, scale[0], bias[0], None, weights)
    turn_own(unit, factors, turned, unit_turned, inverse)
    normed_turned[...] = normed[...].T
    early_near[...] = dot(text_columns[...], weights_near[...], FIRST)
    early_far[...] = dot(text_columns[...], weights[...], FIRST)
    token[...] = jnp.zeros_like(token)


def third_body(
    scale, bias, text_unit, flat_near, flat_far, totals_near, totals_far, early_near, early_far,
    before, weights, back_near, back_far, totals,
    text_columns, dots,
):
    rows = text_unit.shape[0]
    near = 2 * rows
    take_columns(text_unit, text_columns)
    dots[:, :near] = dot(text_unit[...], flat_near[...])
    dots[:, near:] = dot(text_unit[...], flat_far[...])
    added = weigh(dots, scale[0], bias[0], near, weights)
    totals[:, :near] = totals_near[...] + added[:, :near]
    totals[:, near:] = totals_far[...] + added[:, near:]
    added = dot(text_columns[...], weights[...], FIRST)
    back_near[...] = early_near[...] + added[:, :near]
    back_far[...] = early_far[...] + added[:, near:]


def pack_into(target, block, full):
    rows, columns = block.shape
    rest = columns - full
    target[:rows, :] = block[:, :full].astype(BF16)
    per_band = full // rest
    tail = block[:, full:]
    chunks = [tail[at : at + BAND, :] for at in range(0, rows, BAND)]
    for band in range(0, len(chunks), per_band):
        part = chunks[band : band + per_band]
        if len(part) < per_band:
            part.append(jnp.zeros((BAND, full - rest * len(part)), block.dtype))
        at = rows + (band // per_band) * BAND
        target[at : at + BAND, :] = jnp.concatenate(part, axis=1).astype(BF16)


def partial_body(
    members, groups, lead, scale, bias, text_unit, flat_near, flat_far, totals, back_near, back_far, unit_turned_near,
    unit_turned_far, inverse_near, inverse_far, turned_near, turned_far, proj_columns, gain,
    across, keep_lead, keep_tail, *refs,
):
    along, (weights, text_columns, dots, packed) = refs[: groups // 2 - 1], refs[groups // 2 - 1 :]
    rows = text_unit.shape[0]
    near = 2 * rows
    every = members * rows
    width = text_unit.shape[1]
    columns = width // members
    count, full = packed.shape[1:]
    scale, bias = scale[0], bias[0]
    take_columns(text_unit, text_columns)
    dots[:, :near] = dot(text_unit[...], flat_near[...])
    dots[:, near:] = dot(text_unit[...], flat_far[...])
    total = totals[...] + weigh(dots, scale, bias, near + rows, weights)
    added = dot(text_columns[...], weights[...], FIRST)
    back = []
    for where, earlier, unit_turned, inverse in (
        (slice(0, near), back_near, unit_turned_near, inverse_near),
        (slice(near, every), back_far, unit_turned_far, inverse_far),
    ):
        whole = earlier[...] + added[:, where]
        part = (whole - unit_turned[...].astype(F32) * total[:, where]) * (inverse[...] * scale)
        back.append(part.astype(BF16))
    turned = jnp.concatenate([turned_near[...], turned_far[...]], axis=1)
    product = dot(turned, jnp.concatenate(back, axis=1), LAST)
    each = width // groups
    product = product * (1.0 / every)
    for group in range(groups):
        pack_into(packed.at[group], product[group * each : (group + 1) * each, :], full)

    terms = product * proj_columns[...].astype(F32)
    folded = jnp.concatenate([terms[:, full:], jnp.zeros((width, full + LANES - columns), F32)], axis=1)
    for at in range(0, full, LANES):
        folded = folded + terms[:, at : at + LANES]
    high = folded.astype(BF16)
    low = (folded - high.astype(F32)).astype(BF16)
    ones = jnp.ones((BAND, 2 * LANES), BF16)
    gain_row = dot(ones, jnp.concatenate([high, low], axis=1), LAST)[:1, :] / gain[...]
    pieces = [gain_row[:, at : at + LANES] for at in range(0, width, LANES)]
    pieces.append(jnp.zeros((BAND - len(pieces), LANES), F32))
    gain_tile = jnp.concatenate(pieces, axis=0).astype(BF16)
    for group in range(groups):
        packed[group, count - BAND :, full - LANES :] = gain_tile

    own = lax.axis_index("rep")
    for step in range(groups // 2):
        across[step] = packed[own ^ 1 ^ (2 * step), :lead, :]
        keep_lead[step] = packed[own ^ (2 * step), :lead, :]
    for other in range(2):
        keep_tail[other] = packed[own ^ other, lead:, :]
        for step in range(1, groups // 2):
            along[step - 1][other] = packed[own ^ (2 * step) ^ other, lead:, :]


def image_body(
    scale, proj, text_near, text_third, text_fourth, weights_near, weights_third, weights_fourth,
    unit, factors, norm_back, token, back, product,
):
    rows = back.shape[0]
    scale = scale[0]
    product[...] = (
        dot(weights_near[:, :rows], text_near[...], FIRST)
        + dot(weights_third[:, :rows], text_third[...], FIRST)
        + dot(weights_fourth[:, :rows], text_fourth[...], FIRST)
    )

    def image_chunk(where):
        values = product[where, :] * scale
        direction = unit[where, :].astype(F32)
        back[where, :] = (
            (values - direction * sums(direction * values)) * factors[where, :1]
        ).astype(BF16)

    over_rows(rows, 32, image_chunk)
    norm_back[...] = dot(back[...], proj[...], LAST)
    token[...] = jnp.zeros_like(token)


def feature_body(features, gain, norm_back, before, feature_grad, token):
    rows, width = features.shape

    def feature_chunk(where):
        values = features[where, :].astype(F32)
        centred = values - sums(values) * (1.0 / width)
        deviation = lax.rsqrt(sums(centred * centred) * (1.0 / width) + 1e-06)
        xhat = centred * deviation
        scaled = norm_back[where, :] * gain[...]
        feature_grad[where, :] = (
            deviation
            * (scaled - sums(scaled) * (1.0 / width) - xhat * (sums(scaled * xhat) * (1.0 / width)))
        ).astype(BF16)

    over_rows(rows, 32, feature_chunk)
    token[...] = jnp.zeros_like(token)


def text_body(
    scale, text, weights_near, weights_far, unit_near, unit_far, before, text_grad, token, product,
):
    rows = text_grad.shape[0]
    scale = scale[0]
    product[...] = dot(weights_near[:rows, :], unit_near[...]) + dot(weights_far[:rows, :], unit_far[...])

    def text_chunk(where):
        values = product[where, :] * scale
        own = text[where, :].astype(F32)
        own_inverse = lax.rsqrt(sums(own * own) + 1e-06)
        direction = own * own_inverse
        text_grad[where, :] = (
            (values - direction * sums(direction * values)) * own_inverse
        ).astype(BF16)

    over_rows(rows, 32, text_chunk)
    token[...] = jnp.zeros_like(token)


def first_sum_body(token, keep_lead, across, keep_tail, *refs):
    steps = keep_lead.shape[0]
    along, refs = refs[: steps - 1], refs[steps - 1 :]
    leads, (tail, tail_across, ordered) = refs[:steps], refs[steps:]
    for step in range(steps):
        leads[step][...] = (keep_lead[step].astype(F32) + across[step].astype(F32)).astype(BF16)
    own = lax.axis_index("rep") // 2
    ordered[own] = keep_tail[...]
    for step in range(1, steps):
        ordered[own ^ step] = along[steps - 1 - step][...]
    value = ordered[0].astype(F32)
    for step in range(1, steps):
        value = value + ordered[step].astype(F32)
    tail[...] = value[0].astype(BF16)
    tail_across[...] = value[1].astype(BF16)


def last_sum_body(before, tail, tail_across, *refs):
    leads, total = refs[:-1], refs[-1]
    split = leads[0].shape[0]
    value = leads[0][...].astype(F32)
    for lead in leads[1:]:
        value = value + lead[...].astype(F32)
    total[:split, :] = value.astype(BF16)
    total[split:, :] = (tail[...].astype(F32) + tail_across[...].astype(F32)).astype(BF16)


def finish_body(members, before, *refs):
    packets, (proj_grad, gain_gradient, ordered) = refs[:members], refs[members:]
    count, full = packets[0].shape
    rows, width = proj_grad.shape
    rest = width // members - full
    per_band = full // rest
    for k in range(members):
        member = lax.axis_index("loop") ^ k
        proj_grad[:, pl.ds(pl.multiple_of(member * full, LANES), full)] = packets[k][:rows, :].astype(F32)
        ordered[member] = packets[k][rows:, :].astype(F32)
    tails = []
    for index in range(rows // BAND):
        at, lane = (index // per_band) * BAND, (index % per_band) * rest
        tails.append(
            jnp.concatenate([ordered[member][at : at + BAND, lane : lane + rest] for member in range(members)], axis=1)
        )
    proj_grad[:, members * full :] = jnp.concatenate(tails, axis=0)
    value = ordered[0][count - rows - BAND :, full - LANES :]
    for member in range(1, members):
        value = value + ordered[member][count - rows - BAND :, full - LANES :]
    for at in range(width // LANES):
        gain_gradient[at * LANES : (at + 1) * LANES] = value[at]


def local_four(features, text, proj, gain, scale, bias):
    members = lax.axis_size("loop")
    groups = lax.axis_size("rep")
    rows, width = features.shape[0], features.shape[2]
    near, every = 2 * rows, 4 * rows
    columns = width // members
    full = columns // LANES * LANES
    each = width // groups
    bands = -(-(each // BAND) // (full // (columns - full)))
    packet = (each + bands * BAND, full)

    lead = (5 * packet[0] // BAND // 6) * BAND
    tail = packet[0] - lead
    steps = groups // 2

    f0, t0 = features[:, 0, :], text[:, 0, :]
    f2 = send(f0, "loop", lambda p: p ^ 2)
    f1 = send(f0, "loop", lambda p: p ^ 1)

    wide, half = ((near, width), BF16), ((rows, width), BF16)
    square, part, turned = ((near, near), BF16), ((near, columns), BF16), ((width, near), BF16)

    line, mine = ((1, near), F32), ((columns, near), BF16)
    kept = ((width, width), BF16)
    f0_kept, proj_kept, t0_kept, gain_row, normed_near, unit_near, factors, text_own, token = call(
        near_body,
        [half, kept, half, ((1, width), F32), wide, wide, ((near, LANES), F32), half, TOKEN],
        [((near, width), F32)],
        smem=2,
        hbm=3,
        limit=46,
        flops=2 * near * width * width,
        moved=8 * near * width,
    )(scale, bias, f0, proj, t0, f1, gain)

    t2 = send(text_own, "loop", lambda p: p ^ 2)
    t1 = send(text_own, "loop", lambda p: p ^ 1)
    head = rows // 6 * 5
    f3_head, f3_tail = call(split_body, [((head, width), BF16), ((rows - head, width), BF16)], moved=1000)(f2, token)
    f3_head = send(f3_head, "loop", lambda p: p ^ 1)
    f3_tail = send(f3_tail, "loop", lambda p: p ^ 1)

    (
        text_near, turned_near, flat_near, unit_turned_near, inverse_near, text_columns_near, weights_near, totals_near, proj_columns,
        token,
    ) = call(
        near_pairs_body,
        [wide, turned, turned, mine, line, part, square, line, ((width, columns), BF16), TOKEN],
        [((near, near), F32)],
        smem=2,
        flops=1000,
        moved=1000,
    )(scale, bias, normed_near, unit_near, factors, text_own, t1, proj_kept, token)

    back_kind = ((columns, near), F32)
    (
        turned_far, unit_far, flat_far, unit_turned_far, inverse_far, weights_far, totals_far, early_near, early_far,
        token,
    ) = call(
        far_body,
        [turned, wide, turned, mine, line, square, line, back_kind, back_kind, TOKEN],
        [wide, ((near, width), F32), ((near, near), F32), ((near, LANES), F32)],
        smem=2,
        flops=1000,
        moved=1000,
    )(
        scale, bias, f2, f3_head, f3_tail, proj_kept, gain_row, text_near, text_columns_near, weights_near,
    )

    t2_after, token = lax.optimization_barrier((t2, token))
    t3 = send(t2_after, "loop", lambda p: p ^ 1)

    narrow = ((rows, every), BF16)
    weights_third, back_near, back_far, totals = call(
        third_body,
        [narrow, back_kind, back_kind, ((1, every), F32)],
        [((rows, columns), BF16), ((rows, every), F32)],
        smem=2,
        flops=2 * near * width * width,
        moved=8 * near * width,
    )(
        scale, bias, t2, flat_near, flat_far, totals_near, totals_far, early_near, early_far, token,
    )

    outs = call(
        functools.partial(partial_body, members, groups, lead),
        [((steps, lead, full), BF16)] * 2 + [((2, tail, full), BF16)] * steps + [narrow],
        [((rows, columns), BF16), ((rows, every), F32), ((groups,) + packet, BF16)],
        smem=2,
        flops=4 * near * width * width,
        moved=16 * near * width,
    )(
        scale, bias, t3, flat_near, flat_far, totals, back_near, back_far, unit_turned_near, unit_turned_far,
        inverse_near, inverse_far, turned_near, turned_far, proj_columns, gain_row,
    )
    across, keep_lead, keep_tail = outs[:3]
    along, weights_fourth = outs[3 : 2 + steps], outs[2 + steps]

    across = send(across, "rep", lambda p: p ^ 1)
    along = [send(along[step - 1], "rep", lambda p: p ^ (2 * step)) for step in reversed(range(1, steps))]

    norm_back, token = call(
        image_body,
        [((rows, width), F32), TOKEN],
        [half, ((rows, width), F32)],
        smem=1,
        flops=4 * near * width * width,
        moved=12 * near * width,
    )(
        scale, proj_kept, text_near, t2, t3, weights_near, weights_third, weights_fourth,
        unit_near, factors,
    )

    outs = call(
        first_sum_body,
        [((lead, full), BF16)] * steps + [((tail, full), BF16)] * 2,
        [((steps, 2, tail, full), BF16)],
        moved=4 * each * width,
    )(token, keep_lead, across, keep_tail, *along)
    leads = [outs[0]] + [send(outs[step], "rep", lambda p: p ^ (2 * step)) for step in reversed(range(1, steps))]
    tail_across = send(outs[steps + 1], "rep", lambda p: p ^ 1)

    feature_grad, token = call(feature_body, [half, TOKEN], moved=12 * near * width)(
        f0_kept, gain_row, norm_back, outs[steps]
    )

    (reduced,) = call(
        last_sum_body,
        [(packet, BF16)],
        moved=4 * each * width,
    )(token, outs[steps], tail_across, *leads)
    far_block = send(reduced, "loop", lambda p: p ^ 2)
    text_grad, token = call(
        text_body,
        [half, TOKEN],
        [((rows, width), F32)],
        smem=1,
        flops=2 * near * width * width,
        moved=6 * near * width,
    )(scale, t0_kept, weights_near, weights_far, unit_near, unit_far, reduced)
    reduced, token = lax.optimization_barrier((reduced, token))
    near_block = send(reduced, "loop", lambda p: p ^ 1)
    blocks = [reduced, near_block, far_block, send(far_block, "loop", lambda p: p ^ 1)]

    proj_grad, gain_gradient = call(
        functools.partial(finish_body, members),
        [((each, width), F32), ((width,), F32)],
        [((members, bands * BAND, full), F32)],
        moved=8 * each * width,
    )(token, *blocks)
    return feature_grad[:, None, :], text_grad[:, None, :], proj_grad, gain_gradient


def four_fits(mesh, rows_shape):
    members, groups = mesh.shape["loop"], mesh.shape["rep"]
    rows, width = rows_shape[0] // members, rows_shape[2]
    if members != 4 or groups != 8 or width % (members * groups) or width % LANES:
        return False
    columns, each = width // members, width // groups
    full = columns // LANES * LANES
    rest = columns - full
    if rest == 0 or full < LANES or full % rest or each % BAND or rows % 64 or width // LANES > BAND:
        return False
    chunks = each // BAND
    used = (chunks - 1) % (full // rest) + 1
    return used * rest <= full - LANES


def solution(mesh):
    def run(features, text, proj, gain, scale, bias):
        body = local_four if four_fits(mesh, features.shape) else local_any_size
        return jax.shard_map(
            body,
            mesh=mesh,
            in_specs=(P("loop", "rep", None), P("loop", "rep", None), P(), P(), P(), P()),
            out_specs=(P("loop", "rep", None), P("loop", "rep", None), P("rep", None), P()),
            check_vma=False,
        )(features, text, proj, gain, scale, bias)

    return run
```

```python
import functools

import jax
import jax.numpy as jnp
from jax import lax
from jax.experimental import pallas as pl
from jax.experimental.pallas import tpu as pltpu
from jax.sharding import PartitionSpec as P

F32 = jnp.float32
BF16 = jnp.bfloat16
LAST = (((1,), (1,)), ((), ()))
FIRST = (((0,), (0,)), ((), ()))


def dot(a, b, dims=(((1,), (0,)), ((), ()))):
    return lax.dot_general(a, b, dims, preferred_element_type=F32)


def unit_rows(values):
    inverse = lax.rsqrt(jnp.sum(values * values, axis=-1, keepdims=True) + 1e-06)
    return values * inverse, inverse


def standardize(rows):
    values = rows.astype(F32)
    centred = values - jnp.mean(values, axis=-1, keepdims=True)
    inverse = lax.rsqrt(jnp.mean(centred * centred, axis=-1, keepdims=True) + 1e-06)
    return centred * inverse, inverse


def send(value, axis, target):
    count = lax.axis_size(axis)
    return lax.ppermute(value, axis, [(p, target(p)) for p in range(count)])


def gather_group(value, count):
    mine = [value]
    for step in range(1, count // 2):
        mine.append(send(value, "loop", lambda p: (p + 2 * step) % count))
    mates = [send(block, "loop", lambda p: p ^ 1) for block in mine]
    return mine + mates


def local_any_size(features, text, proj, gain, scale, bias):
    n = lax.axis_size("loop")
    m = lax.axis_size("rep")
    me = lax.axis_index("loop")
    half = n // 2
    rows, width = features.shape[0], features.shape[2]
    columns = proj.shape[1] // n
    group_rows = rows * n
    logit_scale, logit_bias = scale[0], bias[0]

    own_features = features[:, 0, :]
    own_text = text[:, 0, :]
    text_blocks = gather_group(own_text, n)
    feature_blocks = gather_group(own_features, n)

    xhat, deviation = standardize(own_features)
    normed = (xhat * gain).astype(BF16)
    img_dir, img_inv = unit_rows(dot(normed, proj))
    img_unit = img_dir.astype(BF16)

    txt_dir, txt_inv = unit_rows(own_text.astype(F32))
    own_txt_unit = txt_dir.astype(BF16)
    txt_unit = jnp.concatenate(
        [own_txt_unit] + [unit_rows(block.astype(F32))[0].astype(BF16) for block in text_blocks[1:]]
    )
    row_ids = lax.broadcasted_iota(jnp.int32, (rows, group_rows), 0)
    column_ids = lax.broadcasted_iota(jnp.int32, (rows, group_rows), 1)
    diagonal = (row_ids == column_ids).astype(F32)

    def weights(left, right):
        logits = logit_scale * dot(left, right, LAST) + logit_bias
        return (jax.nn.sigmoid(logits) - diagonal).astype(BF16)

    img_back = logit_scale * dot(weights(img_unit, txt_unit), txt_unit)
    proj_back = (
        (img_back - img_dir * jnp.sum(img_dir * img_back, axis=-1, keepdims=True)) * img_inv
    ).astype(BF16)

    blocks = jnp.transpose(proj_back.reshape(rows, n, columns), (1, 0, 2))
    blocks = lax.all_to_all(blocks, "loop", 0, 0, tiled=True)
    back_columns = blocks.reshape(group_rows, columns)

    norm_back = dot(proj_back, proj, LAST)
    scaled = norm_back * gain
    feature_grad = (
        deviation
        * (
            scaled
            - jnp.mean(scaled, axis=-1, keepdims=True)
            - xhat * jnp.mean(scaled * xhat, axis=-1, keepdims=True)
        )
    ).astype(BF16)
    gain_term = jnp.sum(norm_back * xhat, axis=0) * (1.0 / group_rows)

    other_normed = [(standardize(block)[0] * gain).astype(BF16) for block in feature_blocks[1:]]
    relative = jnp.stack([normed] + other_normed)
    member = jnp.arange(n)
    same_core = (member % 2) == (me % 2)
    chips_back = ((me // 2 - member // 2) % half)
    position = jnp.where(same_core, chips_back, half + chips_back)
    group_normed = relative[position].reshape(group_rows, width)

    partial = (dot(group_normed, back_columns, FIRST) * (1.0 / group_rows)).astype(BF16)
    pieces = lax.all_to_all(partial.reshape(m, width // m, columns), "rep", 0, 0, tiled=True)
    reduced = jnp.sum(pieces.astype(F32), axis=0).astype(BF16)
    gains = lax.all_gather(gain_term, "rep")
    gain_sum = jnp.sum(gains, axis=0)
    proj_rows = lax.all_gather(reduced, "loop")
    proj_grad = jnp.transpose(proj_rows, (1, 0, 2)).reshape(width // m, n * columns).astype(F32)
    gain_gradient = jnp.sum(lax.all_gather(gain_sum, "loop"), axis=0)

    group_unit = jnp.concatenate(
        [img_unit] + [unit_rows(dot(block, proj))[0].astype(BF16) for block in other_normed]
    )
    text_weights = weights(own_txt_unit, group_unit)
    txt_back = logit_scale * dot(text_weights, group_unit)
    text_grad = (
        (txt_back - txt_dir * jnp.sum(txt_dir * txt_back, axis=-1, keepdims=True)) * txt_inv
    ).astype(BF16)
    return feature_grad[:, None, :], text_grad[:, None, :], proj_grad, gain_gradient


VMEM = pl.BlockSpec(memory_space=pltpu.VMEM)
SMEM = pl.BlockSpec(memory_space=pltpu.SMEM)
HBM = pl.BlockSpec(memory_space=pltpu.HBM)
LANES = 128
BAND = 16
TOKEN = ((8, LANES), F32)
Z_ORDER = (2, 3, 1)


def call(body, outs, scratch=(), smem=0, hbm=0, limit=24, flops=0, moved=0):
    def run(*operands):
        specs = [SMEM] * smem + [HBM] * hbm + [VMEM] * (len(operands) - smem - hbm)
        return pl.pallas_call(
            body,
            out_shape=[jax.ShapeDtypeStruct(shape, kind) for shape, kind in outs],
            in_specs=specs,
            out_specs=[VMEM] * len(outs),
            scratch_shapes=[pltpu.VMEM(shape, kind) for shape, kind in scratch]
            + [pltpu.SemaphoreType.DMA((hbm,))] * bool(hbm),
            compiler_params=pltpu.CompilerParams(vmem_limit_bytes=limit * 2**20),
            cost_estimate=pl.CostEstimate(flops=flops, bytes_accessed=moved, transcendentals=0),
        )(*operands)

    return run


def over_rows(count, step, body):
    def turn(index, _):
        body(pl.ds(pl.multiple_of(index * step, step), step))
        return 0

    lax.fori_loop(0, count // step, turn, 0, unroll=min(4, count // step))


def sums(values):
    return jnp.sum(values, axis=-1, keepdims=True)


def normalize_into(source, gain, target, at):
    rows, width = source.shape

    def chunk(where):
        values = source[where, :].astype(F32)
        centred = values - sums(values) * (1.0 / width)
        inverse = lax.rsqrt(sums(centred * centred) * (1.0 / width) + 1e-06)
        target[pl.ds(at + where.start, where.size), :] = (centred * inverse * gain[...]).astype(BF16)

    over_rows(rows, 32, chunk)


def unit_into(source, target, at, inverses=None):
    rows = source.shape[0]

    def chunk(where):
        values = source[where, :].astype(F32)
        inverse = lax.rsqrt(sums(values * values) + 1e-06)
        place = pl.ds(at + where.start, where.size)
        target[place, :] = (values * inverse).astype(BF16)
        if inverses is not None:
            inverses[place, :] = jnp.broadcast_to(inverse, (where.size, LANES))

    over_rows(rows, 32, chunk)


def weigh(dots, scale, bias, diagonal, weights):
    texts, images = dots.shape

    def chunk(index, total):
        where = pl.ds(pl.multiple_of(index * BAND, BAND), BAND)
        product = dots[where, :]
        weight = jnp.tanh((0.5 * scale) * product + 0.5 * bias)
        offset = 0.5
        if diagonal is not None:
            text = index * BAND + diagonal + lax.broadcasted_iota(jnp.int32, product.shape, 0)
            image = lax.broadcasted_iota(jnp.int32, product.shape, 1)
            offset = jnp.where(text == image, -0.5, 0.5)
        weight = (0.5 * weight + offset).astype(BF16)
        weights[where, :] = weight
        both = weight.astype(F32) * product
        return total + both[:8, :] + both[8:, :]

    total = lax.fori_loop(0, texts // BAND, chunk, jnp.zeros((8, images), F32), unroll=4)
    return jnp.sum(total, axis=0, keepdims=True)


def take_columns(source, target):
    members = source.shape[1] // target.shape[1]
    full = target.shape[1] // LANES * LANES
    rest = target.shape[1] - full
    target[:, :full] = source[:, pl.ds(pl.multiple_of(lax.axis_index("loop") * full, LANES), full)]
    for member in range(members):

        @pl.when(lax.axis_index("loop") == member)
        def _():
            target[:, full:] = source[:, members * full + member * rest : members * full + (member + 1) * rest]


def near_body(
    scale, bias, f0_far, proj_far, t0_far, f1, gain_line,
    f0, proj, t0, gain, normed, unit, factors, text_unit, token, projected, semaphores,
):
    rows = f0.shape[0]
    copies = [
        pltpu.make_async_copy(source, target, semaphores.at[at])
        for at, (source, target) in enumerate(((f0_far, f0), (proj_far, proj), (t0_far, t0)))
    ]
    for copy in copies:
        copy.start()
    for at in range(0, gain.shape[1], LANES):
        gain[:, at : at + LANES] = gain_line[at : at + LANES].reshape(1, LANES)
    normalize_into(f1, gain, normed, rows)
    copies[0].wait()
    normalize_into(f0, gain, normed, 0)
    copies[1].wait()
    projected[...] = dot(normed[...], proj[...])
    copies[2].wait()
    unit_into(t0, text_unit, 0)
    unit_into(projected, unit, 0, factors)
    token[...] = jnp.zeros_like(token)


def near_pairs_body(
    scale, bias, normed, unit, factors, text_own, t1, proj, before,
    text_unit, normed_turned, turned, unit_turned, inverse, text_columns, weights, totals, proj_columns, token, dots,
):
    token[...] = jnp.zeros_like(token)
    rows = t1.shape[0]
    text_unit[:rows, :] = text_own[...]
    text_unit[rows:, :] = t1[...]
    dots[...] = dot(text_unit[...], unit[...], LAST)
    totals[...] = weigh(dots, scale[0], bias[0], 0, weights)
    take_columns(text_unit, text_columns)
    take_columns(proj, proj_columns)
    turn_own(unit, factors, turned, unit_turned, inverse)
    normed_turned[...] = normed[...].T


def turn_own(unit, factors, turned, unit_turned, inverse):
    columns = unit_turned.shape[0]
    full = columns // LANES * LANES
    rest = columns - full
    turned[...] = unit[...].T
    unit_turned[:full, :] = turned[pl.ds(pl.multiple_of(lax.axis_index("loop") * full, LANES), full), :]
    begin = turned.shape[0] // columns * full
    unit_turned[full:, :] = turned[pl.ds(pl.multiple_of(begin + lax.axis_index("loop") * rest, BAND), rest), :]
    inverse[...] = factors[...].T[:1, :]


def split_body(f2, before, head, tail):
    head[...] = f2[: head.shape[0], :]
    tail[...] = f2[head.shape[0] :, :]


def far_body(
    scale, bias, f2, f3_head, f3_tail, proj, gain, text_near, text_columns, weights_near,
    normed_turned, unit, turned, unit_turned, inverse, weights, totals, early_near, early_far, token,
    normed, projected, dots, factors,
):
    rows = f2.shape[0]
    normalize_into(f2, gain, normed, 0)
    normalize_into(f3_head, gain, normed, rows)
    normalize_into(f3_tail, gain, normed, rows + f3_head.shape[0])
    projected[...] = dot(normed[...], proj[...])
    unit_into(projected, unit, 0, factors)
    dots[...] = dot(text_near[...], unit[...], LAST)
    totals[...] = weigh(dots, scale[0], bias[0], None, weights)
    turn_own(unit, factors, turned, unit_turned, inverse)
    normed_turned[...] = normed[...].T
    early_near[...] = dot(text_columns[...], weights_near[...], FIRST)
    early_far[...] = dot(text_columns[...], weights[...], FIRST)
    token[...] = jnp.zeros_like(token)


def third_body(
    scale, bias, text_unit, flat_near, flat_far, totals_near, totals_far, early_near, early_far,
    before, weights, back_near, back_far, totals,
    text_columns, dots,
):
    rows = text_unit.shape[0]
    near = 2 * rows
    take_columns(text_unit, text_columns)
    dots[:, :near] = dot(text_unit[...], flat_near[...])
    dots[:, near:] = dot(text_unit[...], flat_far[...])
    added = weigh(dots, scale[0], bias[0], near, weights)
    totals[:, :near] = totals_near[...] + added[:, :near]
    totals[:, near:] = totals_far[...] + added[:, near:]
    added = dot(text_columns[...], weights[...], FIRST)
    back_near[...] = early_near[...] + added[:, :near]
    back_far[...] = early_far[...] + added[:, near:]


def pack_into(target, block, full):
    rows, columns = block.shape
    rest = columns - full
    target[:rows, :] = block[:, :full].astype(BF16)
    per_band = full // rest
    tail = block[:, full:]
    chunks = [tail[at : at + BAND, :] for at in range(0, rows, BAND)]
    for band in range(0, len(chunks), per_band):
        part = chunks[band : band + per_band]
        if len(part) < per_band:
            part.append(jnp.zeros((BAND, full - rest * len(part)), block.dtype))
        at = rows + (band // per_band) * BAND
        target[at : at + BAND, :] = jnp.concatenate(part, axis=1).astype(BF16)


def partial_body(
    members, groups, lead, scale, bias, text_unit, flat_near, flat_far, totals, back_near, back_far, unit_turned_near,
    unit_turned_far, inverse_near, inverse_far, turned_near, turned_far, proj_columns, gain,
    across, keep_lead, keep_tail, *refs,
):
    along, (weights, text_columns, dots, packed) = refs[: groups // 2 - 1], refs[groups // 2 - 1 :]
    rows = text_unit.shape[0]
    near = 2 * rows
    every = members * rows
    width = text_unit.shape[1]
    columns = width // members
    count, full = packed.shape[1:]
    scale, bias = scale[0], bias[0]
    take_columns(text_unit, text_columns)
    dots[:, :near] = dot(text_unit[...], flat_near[...])
    dots[:, near:] = dot(text_unit[...], flat_far[...])
    total = totals[...] + weigh(dots, scale, bias, near + rows, weights)
    added = dot(text_columns[...], weights[...], FIRST)
    back = []
    for where, earlier, unit_turned, inverse in (
        (slice(0, near), back_near, unit_turned_near, inverse_near),
        (slice(near, every), back_far, unit_turned_far, inverse_far),
    ):
        whole = earlier[...] + added[:, where]
        part = (whole - unit_turned[...].astype(F32) * total[:, where]) * (inverse[...] * scale)
        back.append(part.astype(BF16))
    turned = jnp.concatenate([turned_near[...], turned_far[...]], axis=1)
    product = dot(turned, jnp.concatenate(back, axis=1), LAST)
    each = width // groups
    product = product * (1.0 / every)
    for group in range(groups):
        pack_into(packed.at[group], product[group * each : (group + 1) * each, :], full)

    terms = product * proj_columns[...].astype(F32)
    folded = jnp.concatenate([terms[:, full:], jnp.zeros((width, full + LANES - columns), F32)], axis=1)
    for at in range(0, full, LANES):
        folded = folded + terms[:, at : at + LANES]
    high = folded.astype(BF16)
    low = (folded - high.astype(F32)).astype(BF16)
    ones = jnp.ones((BAND, 2 * LANES), BF16)
    gain_row = dot(ones, jnp.concatenate([high, low], axis=1), LAST)[:1, :] / gain[...]
    pieces = [gain_row[:, at : at + LANES] for at in range(0, width, LANES)]
    pieces.append(jnp.zeros((BAND - len(pieces), LANES), F32))
    gain_tile = jnp.concatenate(pieces, axis=0).astype(BF16)
    for group in range(groups):
        packed[group, count - BAND :, full - LANES :] = gain_tile

    own = lax.axis_index("rep")
    for step in range(groups // 2):
        across[step] = packed[own ^ 1 ^ (2 * step), :lead, :]
        keep_lead[step] = packed[own ^ (2 * step), :lead, :]
    for other in range(2):
        keep_tail[other] = packed[own ^ other, lead:, :]
        for step in range(1, groups // 2):
            along[step - 1][other] = packed[own ^ (2 * step) ^ other, lead:, :]


def image_body(
    scale, proj, text_near, text_third, text_fourth, weights_near, weights_third, weights_fourth,
    unit, factors, norm_back, token, back, product,
):
    rows = back.shape[0]
    scale = scale[0]
    product[...] = (
        dot(weights_near[:, :rows], text_near[...], FIRST)
        + dot(weights_third[:, :rows], text_third[...], FIRST)
        + dot(weights_fourth[:, :rows], text_fourth[...], FIRST)
    )

    def image_chunk(where):
        values = product[where, :] * scale
        direction = unit[where, :].astype(F32)
        back[where, :] = (
            (values - direction * sums(direction * values)) * factors[where, :1]
        ).astype(BF16)

    over_rows(rows, 32, image_chunk)
    norm_back[...] = dot(back[...], proj[...], LAST)
    token[...] = jnp.zeros_like(token)


def feature_body(features, gain, norm_back, before, feature_grad, token):
    rows, width = features.shape

    def feature_chunk(where):
        values = features[where, :].astype(F32)
        centred = values - sums(values) * (1.0 / width)
        deviation = lax.rsqrt(sums(centred * centred) * (1.0 / width) + 1e-06)
        xhat = centred * deviation
        scaled = norm_back[where, :] * gain[...]
        feature_grad[where, :] = (
            deviation
            * (scaled - sums(scaled) * (1.0 / width) - xhat * (sums(scaled * xhat) * (1.0 / width)))
        ).astype(BF16)

    over_rows(rows, 32, feature_chunk)
    token[...] = jnp.zeros_like(token)


def text_body(
    scale, text, weights_near, weights_far, unit_near, unit_far, before, text_grad, token, product,
):
    rows = text_grad.shape[0]
    scale = scale[0]
    product[...] = dot(weights_near[:rows, :], unit_near[...]) + dot(weights_far[:rows, :], unit_far[...])

    def text_chunk(where):
        values = product[where, :] * scale
        own = text[where, :].astype(F32)
        own_inverse = lax.rsqrt(sums(own * own) + 1e-06)
        direction = own * own_inverse
        text_grad[where, :] = (
            (values - direction * sums(direction * values)) * own_inverse
        ).astype(BF16)

    over_rows(rows, 32, text_chunk)
    token[...] = jnp.zeros_like(token)


def first_sum_body(token, keep_lead, across, keep_tail, *refs):
    steps = keep_lead.shape[0]
    along, refs = refs[: steps - 1], refs[steps - 1 :]
    leads, (tail, tail_across, ordered) = refs[:steps], refs[steps:]
    for step in range(steps):
        leads[step][...] = (keep_lead[step].astype(F32) + across[step].astype(F32)).astype(BF16)
    own = lax.axis_index("rep") // 2
    ordered[own] = keep_tail[...]
    for step in range(1, steps):
        ordered[own ^ step] = along[Z_ORDER.index(step)][...]
    value = ordered[0].astype(F32)
    for step in range(1, steps):
        value = value + ordered[step].astype(F32)
    tail[...] = value[0].astype(BF16)
    tail_across[...] = value[1].astype(BF16)


def last_sum_body(before, tail, tail_across, *refs):
    leads, total = refs[:-1], refs[-1]
    split = leads[0].shape[0]
    value = leads[0][...].astype(F32)
    for lead in leads[1:]:
        value = value + lead[...].astype(F32)
    total[:split, :] = value.astype(BF16)
    total[split:, :] = (tail[...].astype(F32) + tail_across[...].astype(F32)).astype(BF16)


def finish_body(members, before, *refs):
    packets, (proj_grad, gain_gradient, ordered) = refs[:members], refs[members:]
    count, full = packets[0].shape
    rows, width = proj_grad.shape
    rest = width // members - full
    per_band = full // rest
    for k in range(members):
        member = lax.axis_index("loop") ^ k
        proj_grad[:, pl.ds(pl.multiple_of(member * full, LANES), full)] = packets[k][:rows, :].astype(F32)
        ordered[member] = packets[k][rows:, :].astype(F32)
    tails = []
    for index in range(rows // BAND):
        at, lane = (index // per_band) * BAND, (index % per_band) * rest
        tails.append(
            jnp.concatenate([ordered[member][at : at + BAND, lane : lane + rest] for member in range(members)], axis=1)
        )
    proj_grad[:, members * full :] = jnp.concatenate(tails, axis=0)
    value = ordered[0][count - rows - BAND :, full - LANES :]
    for member in range(1, members):
        value = value + ordered[member][count - rows - BAND :, full - LANES :]
    for at in range(width // LANES):
        gain_gradient[at * LANES : (at + 1) * LANES] = value[at]


def local_four(features, text, proj, gain, scale, bias):
    members = lax.axis_size("loop")
    groups = lax.axis_size("rep")
    rows, width = features.shape[0], features.shape[2]
    near, every = 2 * rows, 4 * rows
    columns = width // members
    full = columns // LANES * LANES
    each = width // groups
    bands = -(-(each // BAND) // (full // (columns - full)))
    packet = (each + bands * BAND, full)

    lead = (5 * packet[0] // BAND // 6) * BAND
    tail = packet[0] - lead
    steps = groups // 2

    f0, t0 = features[:, 0, :], text[:, 0, :]
    f2 = send(f0, "loop", lambda p: p ^ 2)
    f1 = send(f0, "loop", lambda p: p ^ 1)

    wide, half = ((near, width), BF16), ((rows, width), BF16)
    square, part, turned = ((near, near), BF16), ((near, columns), BF16), ((width, near), BF16)

    line, mine = ((1, near), F32), ((columns, near), BF16)
    kept = ((width, width), BF16)
    f0_kept, proj_kept, t0_kept, gain_row, normed_near, unit_near, factors, text_own, token = call(
        near_body,
        [half, kept, half, ((1, width), F32), wide, wide, ((near, LANES), F32), half, TOKEN],
        [((near, width), F32)],
        smem=2,
        hbm=3,
        limit=46,
        flops=2 * near * width * width,
        moved=8 * near * width,
    )(scale, bias, f0, proj, t0, f1, gain)

    t2 = send(text_own, "loop", lambda p: p ^ 2)
    t1 = send(text_own, "loop", lambda p: p ^ 1)
    head = rows // 6 * 5
    f3_head, f3_tail = call(split_body, [((head, width), BF16), ((rows - head, width), BF16)], moved=1000)(f2, token)
    f3_head = send(f3_head, "loop", lambda p: p ^ 1)
    f3_tail = send(f3_tail, "loop", lambda p: p ^ 1)

    (
        text_near, turned_near, flat_near, unit_turned_near, inverse_near, text_columns_near, weights_near, totals_near, proj_columns,
        token,
    ) = call(
        near_pairs_body,
        [wide, turned, turned, mine, line, part, square, line, ((width, columns), BF16), TOKEN],
        [((near, near), F32)],
        smem=2,
        flops=1000,
        moved=1000,
    )(scale, bias, normed_near, unit_near, factors, text_own, t1, proj_kept, token)

    back_kind = ((columns, near), F32)
    (
        turned_far, unit_far, flat_far, unit_turned_far, inverse_far, weights_far, totals_far, early_near, early_far,
        token,
    ) = call(
        far_body,
        [turned, wide, turned, mine, line, square, line, back_kind, back_kind, TOKEN],
        [wide, ((near, width), F32), ((near, near), F32), ((near, LANES), F32)],
        smem=2,
        flops=1000,
        moved=1000,
    )(
        scale, bias, f2, f3_head, f3_tail, proj_kept, gain_row, text_near, text_columns_near, weights_near,
    )

    t2_after, token = lax.optimization_barrier((t2, token))
    t3 = send(t2_after, "loop", lambda p: p ^ 1)

    narrow = ((rows, every), BF16)
    weights_third, back_near, back_far, totals = call(
        third_body,
        [narrow, back_kind, back_kind, ((1, every), F32)],
        [((rows, columns), BF16), ((rows, every), F32)],
        smem=2,
        flops=2 * near * width * width,
        moved=8 * near * width,
    )(
        scale, bias, t2, flat_near, flat_far, totals_near, totals_far, early_near, early_far, token,
    )

    outs = call(
        functools.partial(partial_body, members, groups, lead),
        [((steps, lead, full), BF16)] * 2 + [((2, tail, full), BF16)] * steps + [narrow],
        [((rows, columns), BF16), ((rows, every), F32), ((groups,) + packet, BF16)],
        smem=2,
        flops=4 * near * width * width,
        moved=16 * near * width,
    )(
        scale, bias, t3, flat_near, flat_far, totals, back_near, back_far, unit_turned_near, unit_turned_far,
        inverse_near, inverse_far, turned_near, turned_far, proj_columns, gain_row,
    )
    across, keep_lead, keep_tail = outs[:3]
    along, weights_fourth = outs[3 : 2 + steps], outs[2 + steps]

    across = send(across, "rep", lambda p: p ^ 1)
    along = [send(along[step - 1], "rep", lambda p: p ^ (2 * step)) for step in Z_ORDER]

    norm_back, token = call(
        image_body,
        [((rows, width), F32), TOKEN],
        [half, ((rows, width), F32)],
        smem=1,
        flops=4 * near * width * width,
        moved=12 * near * width,
    )(
        scale, proj_kept, text_near, t2, t3, weights_near, weights_third, weights_fourth,
        unit_near, factors,
    )

    outs = call(
        first_sum_body,
        [((lead, full), BF16)] * steps + [((tail, full), BF16)] * 2,
        [((steps, 2, tail, full), BF16)],
        moved=4 * each * width,
    )(token, keep_lead, across, keep_tail, *along)
    leads = [outs[0]] + [send(outs[step], "rep", lambda p: p ^ (2 * step)) for step in Z_ORDER]
    tail_across = send(outs[steps + 1], "rep", lambda p: p ^ 1)

    feature_grad, token = call(feature_body, [half, TOKEN], moved=12 * near * width)(
        f0_kept, gain_row, norm_back, outs[steps]
    )

    (reduced,) = call(
        last_sum_body,
        [(packet, BF16)],
        moved=4 * each * width,
    )(token, outs[steps], tail_across, *leads)
    far_block = send(reduced, "loop", lambda p: p ^ 2)
    text_grad, token = call(
        text_body,
        [half, TOKEN],
        [((rows, width), F32)],
        smem=1,
        flops=2 * near * width * width,
        moved=6 * near * width,
    )(scale, t0_kept, weights_near, weights_far, unit_near, unit_far, reduced)
    reduced, token = lax.optimization_barrier((reduced, token))
    near_block = send(reduced, "loop", lambda p: p ^ 1)
    blocks = [reduced, near_block, far_block, send(far_block, "loop", lambda p: p ^ 1)]

    proj_grad, gain_gradient = call(
        functools.partial(finish_body, members),
        [((each, width), F32), ((width,), F32)],
        [((members, bands * BAND, full), F32)],
        moved=8 * each * width,
    )(token, *blocks)
    return feature_grad[:, None, :], text_grad[:, None, :], proj_grad, gain_gradient


def four_fits(mesh, rows_shape):
    members, groups = mesh.shape["loop"], mesh.shape["rep"]
    rows, width = rows_shape[0] // members, rows_shape[2]
    if members != 4 or groups != 8 or width % (members * groups) or width % LANES:
        return False
    columns, each = width // members, width // groups
    full = columns // LANES * LANES
    rest = columns - full
    if rest == 0 or full < LANES or full % rest or each % BAND or rows % 64 or width // LANES > BAND:
        return False
    chunks = each // BAND
    used = (chunks - 1) % (full // rest) + 1
    return used * rest <= full - LANES


def solution(mesh):
    def run(features, text, proj, gain, scale, bias):
        body = local_four if four_fits(mesh, features.shape) else local_any_size
        return jax.shard_map(
            body,
            mesh=mesh,
            in_specs=(P("loop", "rep", None), P("loop", "rep", None), P(), P(), P(), P()),
            out_specs=(P("loop", "rep", None), P("loop", "rep", None), P("rep", None), P()),
            check_vma=False,
        )(features, text, proj, gain, scale, bias)

    return run
```

```python
import functools

import jax
import jax.numpy as jnp
from jax import lax
from jax.experimental import pallas as pl
from jax.experimental.pallas import tpu as pltpu
from jax.sharding import PartitionSpec as P

F32 = jnp.float32
BF16 = jnp.bfloat16
LAST = (((1,), (1,)), ((), ()))
FIRST = (((0,), (0,)), ((), ()))


def dot(a, b, dims=(((1,), (0,)), ((), ()))):
    return lax.dot_general(a, b, dims, preferred_element_type=F32)


def unit_rows(values):
    inverse = lax.rsqrt(jnp.sum(values * values, axis=-1, keepdims=True) + 1e-06)
    return values * inverse, inverse


def standardize(rows):
    values = rows.astype(F32)
    centred = values - jnp.mean(values, axis=-1, keepdims=True)
    inverse = lax.rsqrt(jnp.mean(centred * centred, axis=-1, keepdims=True) + 1e-06)
    return centred * inverse, inverse


def send(value, axis, target):
    count = lax.axis_size(axis)
    return lax.ppermute(value, axis, [(p, target(p)) for p in range(count)])


def gather_group(value, count):
    mine = [value]
    for step in range(1, count // 2):
        mine.append(send(value, "loop", lambda p: (p + 2 * step) % count))
    mates = [send(block, "loop", lambda p: p ^ 1) for block in mine]
    return mine + mates


def local_any_size(features, text, proj, gain, scale, bias):
    n = lax.axis_size("loop")
    m = lax.axis_size("rep")
    me = lax.axis_index("loop")
    half = n // 2
    rows, width = features.shape[0], features.shape[2]
    columns = proj.shape[1] // n
    group_rows = rows * n
    logit_scale, logit_bias = scale[0], bias[0]

    own_features = features[:, 0, :]
    own_text = text[:, 0, :]
    text_blocks = gather_group(own_text, n)
    feature_blocks = gather_group(own_features, n)

    xhat, deviation = standardize(own_features)
    normed = (xhat * gain).astype(BF16)
    img_dir, img_inv = unit_rows(dot(normed, proj))
    img_unit = img_dir.astype(BF16)

    txt_dir, txt_inv = unit_rows(own_text.astype(F32))
    own_txt_unit = txt_dir.astype(BF16)
    txt_unit = jnp.concatenate(
        [own_txt_unit] + [unit_rows(block.astype(F32))[0].astype(BF16) for block in text_blocks[1:]]
    )
    row_ids = lax.broadcasted_iota(jnp.int32, (rows, group_rows), 0)
    column_ids = lax.broadcasted_iota(jnp.int32, (rows, group_rows), 1)
    diagonal = (row_ids == column_ids).astype(F32)

    def weights(left, right):
        logits = logit_scale * dot(left, right, LAST) + logit_bias
        return (jax.nn.sigmoid(logits) - diagonal).astype(BF16)

    img_back = logit_scale * dot(weights(img_unit, txt_unit), txt_unit)
    proj_back = (
        (img_back - img_dir * jnp.sum(img_dir * img_back, axis=-1, keepdims=True)) * img_inv
    ).astype(BF16)

    blocks = jnp.transpose(proj_back.reshape(rows, n, columns), (1, 0, 2))
    blocks = lax.all_to_all(blocks, "loop", 0, 0, tiled=True)
    back_columns = blocks.reshape(group_rows, columns)

    norm_back = dot(proj_back, proj, LAST)
    scaled = norm_back * gain
    feature_grad = (
        deviation
        * (
            scaled
            - jnp.mean(scaled, axis=-1, keepdims=True)
            - xhat * jnp.mean(scaled * xhat, axis=-1, keepdims=True)
        )
    ).astype(BF16)
    gain_term = jnp.sum(norm_back * xhat, axis=0) * (1.0 / group_rows)

    other_normed = [(standardize(block)[0] * gain).astype(BF16) for block in feature_blocks[1:]]
    relative = jnp.stack([normed] + other_normed)
    member = jnp.arange(n)
    same_core = (member % 2) == (me % 2)
    chips_back = ((me // 2 - member // 2) % half)
    position = jnp.where(same_core, chips_back, half + chips_back)
    group_normed = relative[position].reshape(group_rows, width)

    partial = (dot(group_normed, back_columns, FIRST) * (1.0 / group_rows)).astype(BF16)
    pieces = lax.all_to_all(partial.reshape(m, width // m, columns), "rep", 0, 0, tiled=True)
    reduced = jnp.sum(pieces.astype(F32), axis=0).astype(BF16)
    gains = lax.all_gather(gain_term, "rep")
    gain_sum = jnp.sum(gains, axis=0)
    proj_rows = lax.all_gather(reduced, "loop")
    proj_grad = jnp.transpose(proj_rows, (1, 0, 2)).reshape(width // m, n * columns).astype(F32)
    gain_gradient = jnp.sum(lax.all_gather(gain_sum, "loop"), axis=0)

    group_unit = jnp.concatenate(
        [img_unit] + [unit_rows(dot(block, proj))[0].astype(BF16) for block in other_normed]
    )
    text_weights = weights(own_txt_unit, group_unit)
    txt_back = logit_scale * dot(text_weights, group_unit)
    text_grad = (
        (txt_back - txt_dir * jnp.sum(txt_dir * txt_back, axis=-1, keepdims=True)) * txt_inv
    ).astype(BF16)
    return feature_grad[:, None, :], text_grad[:, None, :], proj_grad, gain_gradient


VMEM = pl.BlockSpec(memory_space=pltpu.VMEM)
SMEM = pl.BlockSpec(memory_space=pltpu.SMEM)
HBM = pl.BlockSpec(memory_space=pltpu.HBM)
LANES = 128
BAND = 16
TOKEN = ((8, LANES), F32)


def call(body, outs, scratch=(), smem=0, hbm=0, limit=24, flops=0, moved=0):
    def run(*operands):
        specs = [SMEM] * smem + [HBM] * hbm + [VMEM] * (len(operands) - smem - hbm)
        return pl.pallas_call(
            body,
            out_shape=[jax.ShapeDtypeStruct(shape, kind) for shape, kind in outs],
            in_specs=specs,
            out_specs=[VMEM] * len(outs),
            scratch_shapes=[pltpu.VMEM(shape, kind) for shape, kind in scratch]
            + [pltpu.SemaphoreType.DMA((hbm,))] * bool(hbm),
            compiler_params=pltpu.CompilerParams(vmem_limit_bytes=limit * 2**20),
            cost_estimate=pl.CostEstimate(flops=flops, bytes_accessed=moved, transcendentals=0),
        )(*operands)

    return run


def over_rows(count, step, body):
    def turn(index, _):
        body(pl.ds(pl.multiple_of(index * step, step), step))
        return 0

    lax.fori_loop(0, count // step, turn, 0, unroll=min(4, count // step))


def sums(values):
    return jnp.sum(values, axis=-1, keepdims=True)


def normalize_into(source, gain, target, at):
    rows, width = source.shape

    def chunk(where):
        values = source[where, :].astype(F32)
        centred = values - sums(values) * (1.0 / width)
        inverse = lax.rsqrt(sums(centred * centred) * (1.0 / width) + 1e-06)
        target[pl.ds(at + where.start, where.size), :] = (centred * inverse * gain[...]).astype(BF16)

    over_rows(rows, 32, chunk)


def unit_into(source, target, at, inverses=None):
    rows = source.shape[0]

    def chunk(where):
        values = source[where, :].astype(F32)
        inverse = lax.rsqrt(sums(values * values) + 1e-06)
        place = pl.ds(at + where.start, where.size)
        target[place, :] = (values * inverse).astype(BF16)
        if inverses is not None:
            inverses[place, :] = jnp.broadcast_to(inverse, (where.size, LANES))

    over_rows(rows, 32, chunk)


def weigh(dots, scale, bias, diagonal, weights):
    texts, images = dots.shape

    def chunk(index, total):
        where = pl.ds(pl.multiple_of(index * BAND, BAND), BAND)
        product = dots[where, :]
        weight = jnp.tanh((0.5 * scale) * product + 0.5 * bias)
        offset = 0.5
        if diagonal is not None:
            text = index * BAND + diagonal + lax.broadcasted_iota(jnp.int32, product.shape, 0)
            image = lax.broadcasted_iota(jnp.int32, product.shape, 1)
            offset = jnp.where(text == image, -0.5, 0.5)
        weight = (0.5 * weight + offset).astype(BF16)
        weights[where, :] = weight
        both = weight.astype(F32) * product
        return total + both[:8, :] + both[8:, :]

    total = lax.fori_loop(0, texts // BAND, chunk, jnp.zeros((8, images), F32), unroll=4)
    return jnp.sum(total, axis=0, keepdims=True)


def take_columns(source, target):
    members = source.shape[1] // target.shape[1]
    full = target.shape[1] // LANES * LANES
    rest = target.shape[1] - full
    target[:, :full] = source[:, pl.ds(pl.multiple_of(lax.axis_index("loop") * full, LANES), full)]
    for member in range(members):

        @pl.when(lax.axis_index("loop") == member)
        def _():
            target[:, full:] = source[:, members * full + member * rest : members * full + (member + 1) * rest]


def near_body(
    scale, bias, f0_far, proj_far, t0_far, f1, gain_line,
    f0, proj, t0, gain, normed, unit, factors, text_unit, token, projected, semaphores,
):
    rows = f0.shape[0]
    copies = [
        pltpu.make_async_copy(source, target, semaphores.at[at])
        for at, (source, target) in enumerate(((f0_far, f0), (proj_far, proj), (t0_far, t0)))
    ]
    for copy in copies:
        copy.start()
    for at in range(0, gain.shape[1], LANES):
        gain[:, at : at + LANES] = gain_line[at : at + LANES].reshape(1, LANES)
    normalize_into(f1, gain, normed, rows)
    copies[0].wait()
    normalize_into(f0, gain, normed, 0)
    copies[1].wait()
    projected[...] = dot(normed[...], proj[...])
    copies[2].wait()
    unit_into(t0, text_unit, 0)
    unit_into(projected, unit, 0, factors)
    token[...] = jnp.zeros_like(token)


def near_pairs_body(
    scale, bias, normed, unit, factors, text_own, t1, proj, before,
    text_unit, normed_turned, turned, unit_turned, inverse, text_columns, weights, totals, proj_columns, token, dots,
):
    token[...] = jnp.zeros_like(token)
    rows = t1.shape[0]
    text_unit[:rows, :] = text_own[...]
    text_unit[rows:, :] = t1[...]
    dots[...] = dot(text_unit[...], unit[...], LAST)
    totals[...] = weigh(dots, scale[0], bias[0], 0, weights)
    take_columns(text_unit, text_columns)
    take_columns(proj, proj_columns)
    turn_own(unit, factors, turned, unit_turned, inverse)
    normed_turned[...] = normed[...].T


def turn_own(unit, factors, turned, unit_turned, inverse):
    columns = unit_turned.shape[0]
    full = columns // LANES * LANES
    rest = columns - full
    turned[...] = unit[...].T
    unit_turned[:full, :] = turned[pl.ds(pl.multiple_of(lax.axis_index("loop") * full, LANES), full), :]
    begin = turned.shape[0] // columns * full
    unit_turned[full:, :] = turned[pl.ds(pl.multiple_of(begin + lax.axis_index("loop") * rest, BAND), rest), :]
    inverse[...] = factors[...].T[:1, :]


def split_body(f2, before, head, tail):
    head[...] = f2[: head.shape[0], :]
    tail[...] = f2[head.shape[0] :, :]


def far_body(
    scale, bias, f2, f3_head, f3_tail, proj, gain, text_near, text_columns, weights_near,
    normed_turned, unit, turned, unit_turned, inverse, weights, totals, early_near, early_far, token,
    normed, projected, dots, factors,
):
    rows = f2.shape[0]
    normalize_into(f2, gain, normed, 0)
    normalize_into(f3_head, gain, normed, rows)
    normalize_into(f3_tail, gain, normed, rows + f3_head.shape[0])
    projected[...] = dot(normed[...], proj[...])
    unit_into(projected, unit, 0, factors)
    dots[...] = dot(text_near[...], unit[...], LAST)
    totals[...] = weigh(dots, scale[0], bias[0], None, weights)
    turn_own(unit, factors, turned, unit_turned, inverse)
    normed_turned[...] = normed[...].T
    early_near[...] = dot(text_columns[...], weights_near[...], FIRST)
    early_far[...] = dot(text_columns[...], weights[...], FIRST)
    token[...] = jnp.zeros_like(token)


def third_body(
    scale, bias, text_unit, flat_near, flat_far, totals_near, totals_far, early_near, early_far,
    before, weights, back_near, back_far, totals,
    text_columns, dots,
):
    rows = text_unit.shape[0]
    near = 2 * rows
    take_columns(text_unit, text_columns)
    dots[:, :near] = dot(text_unit[...], flat_near[...])
    dots[:, near:] = dot(text_unit[...], flat_far[...])
    added = weigh(dots, scale[0], bias[0], near, weights)
    totals[:, :near] = totals_near[...] + added[:, :near]
    totals[:, near:] = totals_far[...] + added[:, near:]
    added = dot(text_columns[...], weights[...], FIRST)
    back_near[...] = early_near[...] + added[:, :near]
    back_far[...] = early_far[...] + added[:, near:]


def pack_into(target, block, full):
    rows, columns = block.shape
    rest = columns - full
    target[:rows, :] = block[:, :full].astype(BF16)
    per_band = full // rest
    tail = block[:, full:]
    chunks = [tail[at : at + BAND, :] for at in range(0, rows, BAND)]
    for band in range(0, len(chunks), per_band):
        part = chunks[band : band + per_band]
        if len(part) < per_band:
            part.append(jnp.zeros((BAND, full - rest * len(part)), block.dtype))
        at = rows + (band // per_band) * BAND
        target[at : at + BAND, :] = jnp.concatenate(part, axis=1).astype(BF16)


def partial_body(
    members, groups, scale, bias, text_unit, flat_near, flat_far, totals, back_near, back_far, unit_turned_near,
    unit_turned_far, inverse_near, inverse_far, turned_near, turned_far, proj_columns, gain,
    across_first, across_later, keep, weights, text_columns, dots, packed,
):
    rows = text_unit.shape[0]
    near = 2 * rows
    every = members * rows
    width = text_unit.shape[1]
    columns = width // members
    count, full = packed.shape[1:]
    scale, bias = scale[0], bias[0]
    take_columns(text_unit, text_columns)
    dots[:, :near] = dot(text_unit[...], flat_near[...])
    dots[:, near:] = dot(text_unit[...], flat_far[...])
    total = totals[...] + weigh(dots, scale, bias, near + rows, weights)
    added = dot(text_columns[...], weights[...], FIRST)
    back = []
    for where, earlier, unit_turned, inverse in (
        (slice(0, near), back_near, unit_turned_near, inverse_near),
        (slice(near, every), back_far, unit_turned_far, inverse_far),
    ):
        whole = earlier[...] + added[:, where]
        part = (whole - unit_turned[...].astype(F32) * total[:, where]) * (inverse[...] * scale)
        back.append(part.astype(BF16))
    turned = jnp.concatenate([turned_near[...], turned_far[...]], axis=1)
    product = dot(turned, jnp.concatenate(back, axis=1), LAST)
    each = width // groups
    product = product * (1.0 / every)
    for group in range(groups):
        pack_into(packed.at[group], product[group * each : (group + 1) * each, :], full)

    terms = product * proj_columns[...].astype(F32)
    folded = jnp.concatenate([terms[:, full:], jnp.zeros((width, full + LANES - columns), F32)], axis=1)
    for at in range(0, full, LANES):
        folded = folded + terms[:, at : at + LANES]
    high = folded.astype(BF16)
    low = (folded - high.astype(F32)).astype(BF16)
    ones = jnp.ones((BAND, 2 * LANES), BF16)
    gain_row = dot(ones, jnp.concatenate([high, low], axis=1), LAST)[:1, :] / gain[...]
    pieces = [gain_row[:, at : at + LANES] for at in range(0, width, LANES)]
    pieces.append(jnp.zeros((BAND - len(pieces), LANES), F32))
    gain_tile = jnp.concatenate(pieces, axis=0).astype(BF16)
    for group in range(groups):
        packed[group, count - BAND :, full - LANES :] = gain_tile

    own = lax.axis_index("rep")
    for at in range(2):
        across_first[at] = packed[own ^ 1 ^ (4 + 2 * at)]
        across_later[at] = packed[own ^ 1 ^ (2 * at)]
    for at in range(4):
        keep[at] = packed[own ^ (2 * at)]


def image_body(
    scale, proj, text_near, text_third, text_fourth, weights_near, weights_third, weights_fourth,
    unit, factors, norm_back, token, back, product,
):
    rows = back.shape[0]
    scale = scale[0]
    product[...] = (
        dot(weights_near[:, :rows], text_near[...], FIRST)
        + dot(weights_third[:, :rows], text_third[...], FIRST)
        + dot(weights_fourth[:, :rows], text_fourth[...], FIRST)
    )

    def image_chunk(where):
        values = product[where, :] * scale
        direction = unit[where, :].astype(F32)
        back[where, :] = (
            (values - direction * sums(direction * values)) * factors[where, :1]
        ).astype(BF16)

    over_rows(rows, 32, image_chunk)
    norm_back[...] = dot(back[...], proj[...], LAST)
    token[...] = jnp.zeros_like(token)


def feature_body(features, gain, norm_back, before, feature_grad, token):
    rows, width = features.shape

    def feature_chunk(where):
        values = features[where, :].astype(F32)
        centred = values - sums(values) * (1.0 / width)
        deviation = lax.rsqrt(sums(centred * centred) * (1.0 / width) + 1e-06)
        xhat = centred * deviation
        scaled = norm_back[where, :] * gain[...]
        feature_grad[where, :] = (
            deviation
            * (scaled - sums(scaled) * (1.0 / width) - xhat * (sums(scaled * xhat) * (1.0 / width)))
        ).astype(BF16)

    over_rows(rows, 32, feature_chunk)
    token[...] = jnp.zeros_like(token)


def text_body(
    scale, text, weights_near, weights_far, unit_near, unit_far, before, text_grad, token, product,
):
    rows = text_grad.shape[0]
    scale = scale[0]
    product[...] = dot(weights_near[:rows, :], unit_near[...]) + dot(weights_far[:rows, :], unit_far[...])

    def text_chunk(where):
        values = product[where, :] * scale
        own = text[where, :].astype(F32)
        own_inverse = lax.rsqrt(sums(own * own) + 1e-06)
        direction = own * own_inverse
        text_grad[where, :] = (
            (values - direction * sums(direction * values)) * own_inverse
        ).astype(BF16)

    over_rows(rows, 32, text_chunk)
    token[...] = jnp.zeros_like(token)


def pair_sum_body(first, before, keep, come, low, high):
    for at, target in enumerate((low, high)):
        target[...] = (keep[first + at].astype(F32) + come[at].astype(F32)).astype(BF16)


def far_sum_body(before, two_on, three_on, total):
    total[...] = two_on[...].astype(F32) + three_on[...].astype(F32)


def last_sum_body(far, own, next_one, two_on, three_on, total, ordered):
    parts = (own, next_one, two_on, three_on)
    total[...] = (own[...].astype(F32) + next_one[...].astype(F32) + far[...]).astype(BF16)
    count, full = total.shape
    z = lax.axis_index("rep") // 2
    for step, part in enumerate(parts):
        ordered[z ^ step] = part[count - BAND :, full - LANES :].astype(F32)
    value = ordered[0]
    for at in range(1, len(parts)):
        value = value + ordered[at]
    total[count - BAND :, full - LANES :] = value.astype(BF16)


def finish_body(members, *refs):
    packets, (proj_grad, gain_gradient, ordered) = refs[:members], refs[members:]
    count, full = packets[0].shape
    rows, width = proj_grad.shape
    rest = width // members - full
    per_band = full // rest
    for k in range(members):
        member = lax.axis_index("loop") ^ k
        proj_grad[:, pl.ds(pl.multiple_of(member * full, LANES), full)] = packets[k][:rows, :].astype(F32)
        ordered[member] = packets[k][rows:, :].astype(F32)
    tails = []
    for index in range(rows // BAND):
        at, lane = (index // per_band) * BAND, (index % per_band) * rest
        tails.append(
            jnp.concatenate([ordered[member][at : at + BAND, lane : lane + rest] for member in range(members)], axis=1)
        )
    proj_grad[:, members * full :] = jnp.concatenate(tails, axis=0)
    value = ordered[0][count - rows - BAND :, full - LANES :]
    for member in range(1, members):
        value = value + ordered[member][count - rows - BAND :, full - LANES :]
    for at in range(width // LANES):
        gain_gradient[at * LANES : (at + 1) * LANES] = value[at]


def local_four(features, text, proj, gain, scale, bias):
    members = lax.axis_size("loop")
    groups = lax.axis_size("rep")
    rows, width = features.shape[0], features.shape[2]
    near, every = 2 * rows, 4 * rows
    columns = width // members
    full = columns // LANES * LANES
    each = width // groups
    bands = -(-(each // BAND) // (full // (columns - full)))
    packet = (each + bands * BAND, full)


    f0, t0 = features[:, 0, :], text[:, 0, :]
    f2 = send(f0, "loop", lambda p: p ^ 2)
    f1 = send(f0, "loop", lambda p: p ^ 1)

    wide, half = ((near, width), BF16), ((rows, width), BF16)
    square, part, turned = ((near, near), BF16), ((near, columns), BF16), ((width, near), BF16)

    line, mine = ((1, near), F32), ((columns, near), BF16)
    kept = ((width, width), BF16)
    f0_kept, proj_kept, t0_kept, gain_row, normed_near, unit_near, factors, text_own, token = call(
        near_body,
        [half, kept, half, ((1, width), F32), wide, wide, ((near, LANES), F32), half, TOKEN],
        [((near, width), F32)],
        smem=2,
        hbm=3,
        limit=46,
        flops=2 * near * width * width,
        moved=8 * near * width,
    )(scale, bias, f0, proj, t0, f1, gain)

    t2 = send(text_own, "loop", lambda p: p ^ 2)
    t1 = send(text_own, "loop", lambda p: p ^ 1)
    head = rows // 6 * 5
    f3_head, f3_tail = call(split_body, [((head, width), BF16), ((rows - head, width), BF16)], moved=1000)(f2, token)
    f3_head = send(f3_head, "loop", lambda p: p ^ 1)
    f3_tail = send(f3_tail, "loop", lambda p: p ^ 1)

    (
        text_near, turned_near, flat_near, unit_turned_near, inverse_near, text_columns_near, weights_near, totals_near, proj_columns,
        token,
    ) = call(
        near_pairs_body,
        [wide, turned, turned, mine, line, part, square, line, ((width, columns), BF16), TOKEN],
        [((near, near), F32)],
        smem=2,
        flops=1000,
        moved=1000,
    )(scale, bias, normed_near, unit_near, factors, text_own, t1, proj_kept, token)

    back_kind = ((columns, near), F32)
    (
        turned_far, unit_far, flat_far, unit_turned_far, inverse_far, weights_far, totals_far, early_near, early_far,
        token,
    ) = call(
        far_body,
        [turned, wide, turned, mine, line, square, line, back_kind, back_kind, TOKEN],
        [wide, ((near, width), F32), ((near, near), F32), ((near, LANES), F32)],
        smem=2,
        flops=1000,
        moved=1000,
    )(
        scale, bias, f2, f3_head, f3_tail, proj_kept, gain_row, text_near, text_columns_near, weights_near,
    )

    text_grad, token = call(
        text_body,
        [half, TOKEN],
        [((rows, width), F32)],
        smem=1,
        flops=1000,
        moved=1000,
    )(scale, t0_kept, weights_near, weights_far, unit_near, unit_far, token)

    t2_after, token = lax.optimization_barrier((t2, token))
    t3 = send(t2_after, "loop", lambda p: p ^ 1)

    narrow = ((rows, every), BF16)
    weights_third, back_near, back_far, totals = call(
        third_body,
        [narrow, back_kind, back_kind, ((1, every), F32)],
        [((rows, columns), BF16), ((rows, every), F32)],
        smem=2,
        flops=2 * near * width * width,
        moved=8 * near * width,
    )(
        scale, bias, t2, flat_near, flat_far, totals_near, totals_far, early_near, early_far, token,
    )

    outs = call(
        functools.partial(partial_body, members, groups),
        [((2,) + packet, BF16)] * 2 + [((4,) + packet, BF16), narrow],
        [((rows, columns), BF16), ((rows, every), F32), ((groups,) + packet, BF16)],
        smem=2,
        flops=4 * near * width * width,
        moved=16 * near * width,
    )(
        scale, bias, t3, flat_near, flat_far, totals, back_near, back_far, unit_turned_near, unit_turned_far,
        inverse_near, inverse_far, turned_near, turned_far, proj_columns, gain_row,
    )
    across_first, across_later, keep, weights_fourth = outs
    come_first = send(across_first, "rep", lambda p: p ^ 1)
    norm_back, token = call(
        image_body,
        [((rows, width), F32), TOKEN],
        [half, ((rows, width), F32)],
        smem=1,
        flops=1000,
        moved=1000,
    )(
        scale, proj_kept, text_near, t2, t3, weights_near, weights_third, weights_fourth,
        unit_near, factors,
    )

    across_later, token = lax.optimization_barrier((across_later, token))
    come_later = send(across_later, "rep", lambda p: p ^ 1)
    two_on, three_on = call(functools.partial(pair_sum_body, 2), [(packet, BF16)] * 2, moved=1000)(
        token, keep, come_first
    )
    first_two = two_on
    two_on = send(two_on, "rep", lambda p: p ^ 4)
    three_on = send(three_on, "rep", lambda p: p ^ 6)
    own_sum, next_one = call(functools.partial(pair_sum_body, 0), [(packet, BF16)] * 2, moved=1000)(
        first_two, keep, come_later
    )
    next_one = send(next_one, "rep", lambda p: p ^ 2)
    feature_grad, token = call(feature_body, [half, TOKEN], moved=12 * near * width)(
        f0_kept, gain_row, norm_back, own_sum
    )
    (far_sum,) = call(far_sum_body, [(packet, F32)], moved=1000)(token, two_on, three_on)
    (reduced,) = call(last_sum_body, [(packet, BF16)], [((4, BAND, LANES), F32)], moved=1000)(
        far_sum, own_sum, next_one, two_on, three_on
    )
    far_block = send(reduced, "loop", lambda p: p ^ 2)
    near_block = send(reduced, "loop", lambda p: p ^ 1)
    blocks = [reduced, near_block, far_block, send(far_block, "loop", lambda p: p ^ 1)]

    proj_grad, gain_gradient = call(
        functools.partial(finish_body, members),
        [((each, width), F32), ((width,), F32)],
        [((members, bands * BAND, full), F32)],
        moved=8 * each * width,
    )(*blocks)
    return feature_grad[:, None, :], text_grad[:, None, :], proj_grad, gain_gradient


def four_fits(mesh, rows_shape):
    members, groups = mesh.shape["loop"], mesh.shape["rep"]
    rows, width = rows_shape[0] // members, rows_shape[2]
    if members != 4 or groups != 8 or width % (members * groups) or width % LANES:
        return False
    columns, each = width // members, width // groups
    full = columns // LANES * LANES
    rest = columns - full
    if rest == 0 or full < LANES or full % rest or each % BAND or rows % 64 or width // LANES > BAND:
        return False
    chunks = each // BAND
    used = (chunks - 1) % (full // rest) + 1
    return used * rest <= full - LANES


def solution(mesh):
    def run(features, text, proj, gain, scale, bias):
        body = local_four if four_fits(mesh, features.shape) else local_any_size
        return jax.shard_map(
            body,
            mesh=mesh,
            in_specs=(P("loop", "rep", None), P("loop", "rep", None), P(), P(), P(), P()),
            out_specs=(P("loop", "rep", None), P("loop", "rep", None), P("rep", None), P()),
            check_vma=False,
        )(features, text, proj, gain, scale, bias)

    return run
```

```python
import functools

import jax
import jax.numpy as jnp
from jax import lax
from jax.experimental import pallas as pl
from jax.experimental.pallas import tpu as pltpu
from jax.sharding import PartitionSpec as P

F32 = jnp.float32
BF16 = jnp.bfloat16
LAST = (((1,), (1,)), ((), ()))
FIRST = (((0,), (0,)), ((), ()))


def dot(a, b, dims=(((1,), (0,)), ((), ()))):
    return lax.dot_general(a, b, dims, preferred_element_type=F32)


def unit_rows(values):
    inverse = lax.rsqrt(jnp.sum(values * values, axis=-1, keepdims=True) + 1e-06)
    return values * inverse, inverse


def standardize(rows):
    values = rows.astype(F32)
    centred = values - jnp.mean(values, axis=-1, keepdims=True)
    inverse = lax.rsqrt(jnp.mean(centred * centred, axis=-1, keepdims=True) + 1e-06)
    return centred * inverse, inverse


def send(value, axis, target):
    count = lax.axis_size(axis)
    return lax.ppermute(value, axis, [(p, target(p)) for p in range(count)])


def gather_group(value, count):
    mine = [value]
    for step in range(1, count // 2):
        mine.append(send(value, "loop", lambda p: (p + 2 * step) % count))
    mates = [send(block, "loop", lambda p: p ^ 1) for block in mine]
    return mine + mates


def local_any_size(features, text, proj, gain, scale, bias):
    n = lax.axis_size("loop")
    m = lax.axis_size("rep")
    me = lax.axis_index("loop")
    half = n // 2
    rows, width = features.shape[0], features.shape[2]
    columns = proj.shape[1] // n
    group_rows = rows * n
    logit_scale, logit_bias = scale[0], bias[0]

    own_features = features[:, 0, :]
    own_text = text[:, 0, :]
    text_blocks = gather_group(own_text, n)
    feature_blocks = gather_group(own_features, n)

    xhat, deviation = standardize(own_features)
    normed = (xhat * gain).astype(BF16)
    img_dir, img_inv = unit_rows(dot(normed, proj))
    img_unit = img_dir.astype(BF16)

    txt_dir, txt_inv = unit_rows(own_text.astype(F32))
    own_txt_unit = txt_dir.astype(BF16)
    txt_unit = jnp.concatenate(
        [own_txt_unit] + [unit_rows(block.astype(F32))[0].astype(BF16) for block in text_blocks[1:]]
    )
    row_ids = lax.broadcasted_iota(jnp.int32, (rows, group_rows), 0)
    column_ids = lax.broadcasted_iota(jnp.int32, (rows, group_rows), 1)
    diagonal = (row_ids == column_ids).astype(F32)

    def weights(left, right):
        logits = logit_scale * dot(left, right, LAST) + logit_bias
        return (jax.nn.sigmoid(logits) - diagonal).astype(BF16)

    img_back = logit_scale * dot(weights(img_unit, txt_unit), txt_unit)
    proj_back = (
        (img_back - img_dir * jnp.sum(img_dir * img_back, axis=-1, keepdims=True)) * img_inv
    ).astype(BF16)

    blocks = jnp.transpose(proj_back.reshape(rows, n, columns), (1, 0, 2))
    blocks = lax.all_to_all(blocks, "loop", 0, 0, tiled=True)
    back_columns = blocks.reshape(group_rows, columns)

    norm_back = dot(proj_back, proj, LAST)
    scaled = norm_back * gain
    feature_grad = (
        deviation
        * (
            scaled
            - jnp.mean(scaled, axis=-1, keepdims=True)
            - xhat * jnp.mean(scaled * xhat, axis=-1, keepdims=True)
        )
    ).astype(BF16)
    gain_term = jnp.sum(norm_back * xhat, axis=0) * (1.0 / group_rows)

    other_normed = [(standardize(block)[0] * gain).astype(BF16) for block in feature_blocks[1:]]
    relative = jnp.stack([normed] + other_normed)
    member = jnp.arange(n)
    same_core = (member % 2) == (me % 2)
    chips_back = ((me // 2 - member // 2) % half)
    position = jnp.where(same_core, chips_back, half + chips_back)
    group_normed = relative[position].reshape(group_rows, width)

    partial = (dot(group_normed, back_columns, FIRST) * (1.0 / group_rows)).astype(BF16)
    pieces = lax.all_to_all(partial.reshape(m, width // m, columns), "rep", 0, 0, tiled=True)
    reduced = jnp.sum(pieces.astype(F32), axis=0).astype(BF16)
    gains = lax.all_gather(gain_term, "rep")
    gain_sum = jnp.sum(gains, axis=0)
    proj_rows = lax.all_gather(reduced, "loop")
    proj_grad = jnp.transpose(proj_rows, (1, 0, 2)).reshape(width // m, n * columns).astype(F32)
    gain_gradient = jnp.sum(lax.all_gather(gain_sum, "loop"), axis=0)

    group_unit = jnp.concatenate(
        [img_unit] + [unit_rows(dot(block, proj))[0].astype(BF16) for block in other_normed]
    )
    text_weights = weights(own_txt_unit, group_unit)
    txt_back = logit_scale * dot(text_weights, group_unit)
    text_grad = (
        (txt_back - txt_dir * jnp.sum(txt_dir * txt_back, axis=-1, keepdims=True)) * txt_inv
    ).astype(BF16)
    return feature_grad[:, None, :], text_grad[:, None, :], proj_grad, gain_gradient


VMEM = pl.BlockSpec(memory_space=pltpu.VMEM)
SMEM = pl.BlockSpec(memory_space=pltpu.SMEM)
HBM = pl.BlockSpec(memory_space=pltpu.HBM)
LANES = 128
BAND = 16
TOKEN = ((8, LANES), F32)


def call(body, outs, scratch=(), smem=0, hbm=0, limit=24, flops=0, moved=0):
    def run(*operands):
        specs = [SMEM] * smem + [HBM] * hbm + [VMEM] * (len(operands) - smem - hbm)
        return pl.pallas_call(
            body,
            out_shape=[jax.ShapeDtypeStruct(shape, kind) for shape, kind in outs],
            in_specs=specs,
            out_specs=[VMEM] * len(outs),
            scratch_shapes=[pltpu.VMEM(shape, kind) for shape, kind in scratch]
            + [pltpu.SemaphoreType.DMA((hbm,))] * bool(hbm),
            compiler_params=pltpu.CompilerParams(vmem_limit_bytes=limit * 2**20),
            cost_estimate=pl.CostEstimate(flops=flops, bytes_accessed=moved, transcendentals=0),
        )(*operands)

    return run


def over_rows(count, step, body):
    def turn(index, _):
        body(pl.ds(pl.multiple_of(index * step, step), step))
        return 0

    lax.fori_loop(0, count // step, turn, 0, unroll=min(4, count // step))


def sums(values):
    return jnp.sum(values, axis=-1, keepdims=True)


def normalize_into(source, gain, target, at):
    rows, width = source.shape

    def chunk(where):
        values = source[where, :].astype(F32)
        centred = values - sums(values) * (1.0 / width)
        inverse = lax.rsqrt(sums(centred * centred) * (1.0 / width) + 1e-06)
        target[pl.ds(at + where.start, where.size), :] = (centred * inverse * gain[...]).astype(BF16)

    over_rows(rows, 32, chunk)


def unit_into(source, target, at, inverses=None):
    rows = source.shape[0]

    def chunk(where):
        values = source[where, :].astype(F32)
        inverse = lax.rsqrt(sums(values * values) + 1e-06)
        place = pl.ds(at + where.start, where.size)
        target[place, :] = (values * inverse).astype(BF16)
        if inverses is not None:
            inverses[place, :] = jnp.broadcast_to(inverse, (where.size, LANES))

    over_rows(rows, 32, chunk)


def weigh(dots, scale, bias, diagonal, weights):
    texts, images = dots.shape

    def chunk(index, total):
        where = pl.ds(pl.multiple_of(index * BAND, BAND), BAND)
        product = dots[where, :]
        weight = jnp.tanh((0.5 * scale) * product + 0.5 * bias)
        offset = 0.5
        if diagonal is not None:
            text = index * BAND + diagonal + lax.broadcasted_iota(jnp.int32, product.shape, 0)
            image = lax.broadcasted_iota(jnp.int32, product.shape, 1)
            offset = jnp.where(text == image, -0.5, 0.5)
        weight = (0.5 * weight + offset).astype(BF16)
        weights[where, :] = weight
        both = weight.astype(F32) * product
        return total + both[:8, :] + both[8:, :]

    total = lax.fori_loop(0, texts // BAND, chunk, jnp.zeros((8, images), F32), unroll=4)
    return jnp.sum(total, axis=0, keepdims=True)


def take_columns(source, target):
    members = source.shape[1] // target.shape[1]
    full = target.shape[1] // LANES * LANES
    rest = target.shape[1] - full
    target[:, :full] = source[:, pl.ds(pl.multiple_of(lax.axis_index("loop") * full, LANES), full)]
    for member in range(members):

        @pl.when(lax.axis_index("loop") == member)
        def _():
            target[:, full:] = source[:, members * full + member * rest : members * full + (member + 1) * rest]


def near_body(
    scale, bias, f0_far, proj_far, t0_far, f1, gain_line,
    f0, proj, t0, gain, normed, unit, factors, text_unit, token, projected, semaphores,
):
    rows = f0.shape[0]
    copies = [
        pltpu.make_async_copy(source, target, semaphores.at[at])
        for at, (source, target) in enumerate(((f0_far, f0), (proj_far, proj), (t0_far, t0)))
    ]
    for copy in copies:
        copy.start()
    for at in range(0, gain.shape[1], LANES):
        gain[:, at : at + LANES] = gain_line[at : at + LANES].reshape(1, LANES)
    normalize_into(f1, gain, normed, rows)
    copies[0].wait()
    normalize_into(f0, gain, normed, 0)
    copies[1].wait()
    projected[...] = dot(normed[...], proj[...])
    copies[2].wait()
    unit_into(t0, text_unit, 0)
    unit_into(projected, unit, 0, factors)
    token[...] = jnp.zeros_like(token)


def near_pairs_body(
    scale, bias, normed, unit, factors, text_own, t1, proj, before,
    text_unit, normed_turned, turned, unit_turned, inverse, text_columns, weights, totals, proj_columns, token, dots,
):
    token[...] = jnp.zeros_like(token)
    rows = t1.shape[0]
    text_unit[:rows, :] = text_own[...]
    text_unit[rows:, :] = t1[...]
    dots[...] = dot(text_unit[...], unit[...], LAST)
    totals[...] = weigh(dots, scale[0], bias[0], 0, weights)
    take_columns(text_unit, text_columns)
    take_columns(proj, proj_columns)
    turn_own(unit, factors, turned, unit_turned, inverse)
    normed_turned[...] = normed[...].T


def turn_own(unit, factors, turned, unit_turned, inverse):
    columns = unit_turned.shape[0]
    full = columns // LANES * LANES
    rest = columns - full
    turned[...] = unit[...].T
    unit_turned[:full, :] = turned[pl.ds(pl.multiple_of(lax.axis_index("loop") * full, LANES), full), :]
    begin = turned.shape[0] // columns * full
    unit_turned[full:, :] = turned[pl.ds(pl.multiple_of(begin + lax.axis_index("loop") * rest, BAND), rest), :]
    inverse[...] = factors[...].T[:1, :]


def split_body(f2, before, head, tail):
    head[...] = f2[: head.shape[0], :]
    tail[...] = f2[head.shape[0] :, :]


def far_body(
    scale, bias, f2, f3_head, f3_tail, proj, gain, text_near, text_columns, weights_near,
    normed_turned, unit, turned, unit_turned, inverse, weights, totals, early_near, early_far, token,
    normed, projected, dots, factors,
):
    rows = f2.shape[0]
    normalize_into(f2, gain, normed, 0)
    normalize_into(f3_head, gain, normed, rows)
    normalize_into(f3_tail, gain, normed, rows + f3_head.shape[0])
    projected[...] = dot(normed[...], proj[...])
    unit_into(projected, unit, 0, factors)
    dots[...] = dot(text_near[...], unit[...], LAST)
    totals[...] = weigh(dots, scale[0], bias[0], None, weights)
    turn_own(unit, factors, turned, unit_turned, inverse)
    normed_turned[...] = normed[...].T
    early_near[...] = dot(text_columns[...], weights_near[...], FIRST)
    early_far[...] = dot(text_columns[...], weights[...], FIRST)
    token[...] = jnp.zeros_like(token)


def third_body(
    scale, bias, text_unit, flat_near, flat_far, totals_near, totals_far, early_near, early_far,
    before, weights, back_near, back_far, totals,
    text_columns, dots,
):
    rows = text_unit.shape[0]
    near = 2 * rows
    take_columns(text_unit, text_columns)
    dots[:, :near] = dot(text_unit[...], flat_near[...])
    dots[:, near:] = dot(text_unit[...], flat_far[...])
    added = weigh(dots, scale[0], bias[0], near, weights)
    totals[:, :near] = totals_near[...] + added[:, :near]
    totals[:, near:] = totals_far[...] + added[:, near:]
    added = dot(text_columns[...], weights[...], FIRST)
    back_near[...] = early_near[...] + added[:, :near]
    back_far[...] = early_far[...] + added[:, near:]


def pack_into(target, block, full):
    rows, columns = block.shape
    rest = columns - full
    target[:rows, :] = block[:, :full].astype(BF16)
    per_band = full // rest
    tail = block[:, full:]
    chunks = [tail[at : at + BAND, :] for at in range(0, rows, BAND)]
    for band in range(0, len(chunks), per_band):
        part = chunks[band : band + per_band]
        if len(part) < per_band:
            part.append(jnp.zeros((BAND, full - rest * len(part)), block.dtype))
        at = rows + (band // per_band) * BAND
        target[at : at + BAND, :] = jnp.concatenate(part, axis=1).astype(BF16)


def partial_body(
    members, groups, scale, bias, text_unit, flat_near, flat_far, totals, back_near, back_far, unit_turned_near,
    unit_turned_far, inverse_near, inverse_far, turned_near, turned_far, proj_columns, gain,
    across_three, across_near, across_own, keep, weights, text_columns, dots, packed,
):
    rows = text_unit.shape[0]
    near = 2 * rows
    every = members * rows
    width = text_unit.shape[1]
    columns = width // members
    count, full = packed.shape[1:]
    scale, bias = scale[0], bias[0]
    take_columns(text_unit, text_columns)
    dots[:, :near] = dot(text_unit[...], flat_near[...])
    dots[:, near:] = dot(text_unit[...], flat_far[...])
    total = totals[...] + weigh(dots, scale, bias, near + rows, weights)
    added = dot(text_columns[...], weights[...], FIRST)
    back = []
    for where, earlier, unit_turned, inverse in (
        (slice(0, near), back_near, unit_turned_near, inverse_near),
        (slice(near, every), back_far, unit_turned_far, inverse_far),
    ):
        whole = earlier[...] + added[:, where]
        part = (whole - unit_turned[...].astype(F32) * total[:, where]) * (inverse[...] * scale)
        back.append(part.astype(BF16))
    turned = jnp.concatenate([turned_near[...], turned_far[...]], axis=1)
    product = dot(turned, jnp.concatenate(back, axis=1), LAST)
    each = width // groups
    product = product * (1.0 / every)
    for group in range(groups):
        pack_into(packed.at[group], product[group * each : (group + 1) * each, :], full)

    terms = product * proj_columns[...].astype(F32)
    folded = jnp.concatenate([terms[:, full:], jnp.zeros((width, full + LANES - columns), F32)], axis=1)
    for at in range(0, full, LANES):
        folded = folded + terms[:, at : at + LANES]
    high = folded.astype(BF16)
    low = (folded - high.astype(F32)).astype(BF16)
    ones = jnp.ones((BAND, 2 * LANES), BF16)
    gain_row = dot(ones, jnp.concatenate([high, low], axis=1), LAST)[:1, :] / gain[...]
    pieces = [gain_row[:, at : at + LANES] for at in range(0, width, LANES)]
    pieces.append(jnp.zeros((BAND - len(pieces), LANES), F32))
    gain_tile = jnp.concatenate(pieces, axis=0).astype(BF16)
    for group in range(groups):
        packed[group, count - BAND :, full - LANES :] = gain_tile

    own = lax.axis_index("rep")
    across_three[...] = packed[own ^ 7]
    across_near[0] = packed[own ^ 3]
    across_near[1] = packed[own ^ 5]
    across_own[...] = packed[own ^ 1]
    for at in range(4):
        keep[at] = packed[own ^ (2 * at)]


def image_body(
    scale, proj, text_near, text_third, text_fourth, weights_near, weights_third, weights_fourth,
    unit, factors, norm_back, token, back, product,
):
    rows = back.shape[0]
    scale = scale[0]
    product[...] = (
        dot(weights_near[:, :rows], text_near[...], FIRST)
        + dot(weights_third[:, :rows], text_third[...], FIRST)
        + dot(weights_fourth[:, :rows], text_fourth[...], FIRST)
    )

    def image_chunk(where):
        values = product[where, :] * scale
        direction = unit[where, :].astype(F32)
        back[where, :] = (
            (values - direction * sums(direction * values)) * factors[where, :1]
        ).astype(BF16)

    over_rows(rows, 32, image_chunk)
    norm_back[...] = dot(back[...], proj[...], LAST)
    token[...] = jnp.zeros_like(token)


def feature_body(features, gain, norm_back, before, feature_grad, token):
    rows, width = features.shape

    def feature_chunk(where):
        values = features[where, :].astype(F32)
        centred = values - sums(values) * (1.0 / width)
        deviation = lax.rsqrt(sums(centred * centred) * (1.0 / width) + 1e-06)
        xhat = centred * deviation
        scaled = norm_back[where, :] * gain[...]
        feature_grad[where, :] = (
            deviation
            * (scaled - sums(scaled) * (1.0 / width) - xhat * (sums(scaled * xhat) * (1.0 / width)))
        ).astype(BF16)

    over_rows(rows, 32, feature_chunk)
    token[...] = jnp.zeros_like(token)


def text_body(
    scale, text, weights_near, weights_far, unit_near, unit_far, before, text_grad, token, product,
):
    rows = text_grad.shape[0]
    scale = scale[0]
    product[...] = dot(weights_near[:rows, :], unit_near[...]) + dot(weights_far[:rows, :], unit_far[...])

    def text_chunk(where):
        values = product[where, :] * scale
        own = text[where, :].astype(F32)
        own_inverse = lax.rsqrt(sums(own * own) + 1e-06)
        direction = own * own_inverse
        text_grad[where, :] = (
            (values - direction * sums(direction * values)) * own_inverse
        ).astype(BF16)

    over_rows(rows, 32, text_chunk)
    token[...] = jnp.zeros_like(token)


def three_sum_body(before, keep, come, total):
    total[...] = (keep[3].astype(F32) + come[...].astype(F32)).astype(BF16)


def near_sum_body(before, keep, come, next_one, two_on):
    for at, target in enumerate((next_one, two_on)):
        target[...] = (keep[1 + at].astype(F32) + come[at].astype(F32)).astype(BF16)


def far_sum_body(before, two_on, three_on, total):
    total[...] = two_on[...].astype(F32) + three_on[...].astype(F32)


def last_sum_body(far, keep, come, next_one, two_on, three_on, total, ordered, own):
    own[...] = (keep[0].astype(F32) + come[...].astype(F32)).astype(BF16)
    parts = (own, next_one, two_on, three_on)
    total[...] = (own[...].astype(F32) + next_one[...].astype(F32) + far[...]).astype(BF16)
    count, full = total.shape
    z = lax.axis_index("rep") // 2
    for step, part in enumerate(parts):
        ordered[z ^ step] = part[count - BAND :, full - LANES :].astype(F32)
    value = ordered[0]
    for at in range(1, len(parts)):
        value = value + ordered[at]
    total[count - BAND :, full - LANES :] = value.astype(BF16)


def finish_body(members, *refs):
    packets, (proj_grad, gain_gradient, ordered) = refs[:members], refs[members:]
    count, full = packets[0].shape
    rows, width = proj_grad.shape
    rest = width // members - full
    per_band = full // rest
    for k in range(members):
        member = lax.axis_index("loop") ^ k
        proj_grad[:, pl.ds(pl.multiple_of(member * full, LANES), full)] = packets[k][:rows, :].astype(F32)
        ordered[member] = packets[k][rows:, :].astype(F32)
    tails = []
    for index in range(rows // BAND):
        at, lane = (index // per_band) * BAND, (index % per_band) * rest
        tails.append(
            jnp.concatenate([ordered[member][at : at + BAND, lane : lane + rest] for member in range(members)], axis=1)
        )
    proj_grad[:, members * full :] = jnp.concatenate(tails, axis=0)
    value = ordered[0][count - rows - BAND :, full - LANES :]
    for member in range(1, members):
        value = value + ordered[member][count - rows - BAND :, full - LANES :]
    for at in range(width // LANES):
        gain_gradient[at * LANES : (at + 1) * LANES] = value[at]


def local_four(features, text, proj, gain, scale, bias):
    members = lax.axis_size("loop")
    groups = lax.axis_size("rep")
    rows, width = features.shape[0], features.shape[2]
    near, every = 2 * rows, 4 * rows
    columns = width // members
    full = columns // LANES * LANES
    each = width // groups
    bands = -(-(each // BAND) // (full // (columns - full)))
    packet = (each + bands * BAND, full)


    f0, t0 = features[:, 0, :], text[:, 0, :]
    f2 = send(f0, "loop", lambda p: p ^ 2)
    f1 = send(f0, "loop", lambda p: p ^ 1)

    wide, half = ((near, width), BF16), ((rows, width), BF16)
    square, part, turned = ((near, near), BF16), ((near, columns), BF16), ((width, near), BF16)

    line, mine = ((1, near), F32), ((columns, near), BF16)
    kept = ((width, width), BF16)
    f0_kept, proj_kept, t0_kept, gain_row, normed_near, unit_near, factors, text_own, token = call(
        near_body,
        [half, kept, half, ((1, width), F32), wide, wide, ((near, LANES), F32), half, TOKEN],
        [((near, width), F32)],
        smem=2,
        hbm=3,
        limit=46,
        flops=2 * near * width * width,
        moved=8 * near * width,
    )(scale, bias, f0, proj, t0, f1, gain)

    t2 = send(text_own, "loop", lambda p: p ^ 2)
    t1 = send(text_own, "loop", lambda p: p ^ 1)
    head = rows // 6 * 5
    f3_head, f3_tail = call(split_body, [((head, width), BF16), ((rows - head, width), BF16)], moved=1000)(f2, token)
    f3_head = send(f3_head, "loop", lambda p: p ^ 1)
    f3_tail = send(f3_tail, "loop", lambda p: p ^ 1)

    (
        text_near, turned_near, flat_near, unit_turned_near, inverse_near, text_columns_near, weights_near, totals_near, proj_columns,
        token,
    ) = call(
        near_pairs_body,
        [wide, turned, turned, mine, line, part, square, line, ((width, columns), BF16), TOKEN],
        [((near, near), F32)],
        smem=2,
        flops=1000,
        moved=1000,
    )(scale, bias, normed_near, unit_near, factors, text_own, t1, proj_kept, token)

    back_kind = ((columns, near), F32)
    (
        turned_far, unit_far, flat_far, unit_turned_far, inverse_far, weights_far, totals_far, early_near, early_far,
        token,
    ) = call(
        far_body,
        [turned, wide, turned, mine, line, square, line, back_kind, back_kind, TOKEN],
        [wide, ((near, width), F32), ((near, near), F32), ((near, LANES), F32)],
        smem=2,
        flops=1000,
        moved=1000,
    )(
        scale, bias, f2, f3_head, f3_tail, proj_kept, gain_row, text_near, text_columns_near, weights_near,
    )

    text_grad, token = call(
        text_body,
        [half, TOKEN],
        [((rows, width), F32)],
        smem=1,
        flops=1000,
        moved=1000,
    )(scale, t0_kept, weights_near, weights_far, unit_near, unit_far, token)

    t2_after, token = lax.optimization_barrier((t2, token))
    t3 = send(t2_after, "loop", lambda p: p ^ 1)

    narrow = ((rows, every), BF16)
    weights_third, back_near, back_far, totals = call(
        third_body,
        [narrow, back_kind, back_kind, ((1, every), F32)],
        [((rows, columns), BF16), ((rows, every), F32)],
        smem=2,
        flops=2 * near * width * width,
        moved=8 * near * width,
    )(
        scale, bias, t2, flat_near, flat_far, totals_near, totals_far, early_near, early_far, token,
    )

    outs = call(
        functools.partial(partial_body, members, groups),
        [(packet, BF16), ((2,) + packet, BF16), (packet, BF16), ((4,) + packet, BF16), narrow],
        [((rows, columns), BF16), ((rows, every), F32), ((groups,) + packet, BF16)],
        smem=2,
        flops=4 * near * width * width,
        moved=16 * near * width,
    )(
        scale, bias, t3, flat_near, flat_far, totals, back_near, back_far, unit_turned_near, unit_turned_far,
        inverse_near, inverse_far, turned_near, turned_far, proj_columns, gain_row,
    )
    across_three, across_near, across_own, keep, weights_fourth = outs
    come_three = send(across_three, "rep", lambda p: p ^ 1)
    norm_back, token = call(
        image_body,
        [((rows, width), F32), TOKEN],
        [half, ((rows, width), F32)],
        smem=1,
        flops=1000,
        moved=1000,
    )(
        scale, proj_kept, text_near, t2, t3, weights_near, weights_third, weights_fourth,
        unit_near, factors,
    )

    across_near, token = lax.optimization_barrier((across_near, token))
    come_near = send(across_near, "rep", lambda p: p ^ 1)
    (three_sum,) = call(three_sum_body, [(packet, BF16)], flops=3000000000, moved=1000)(token, keep, come_three)
    three_on = send(three_sum, "rep", lambda p: p ^ 6)
    next_sum, two_sum = call(near_sum_body, [(packet, BF16)] * 2, moved=1000)(three_sum, keep, come_near)
    two_on = send(two_sum, "rep", lambda p: p ^ 4)
    next_one = send(next_sum, "rep", lambda p: p ^ 2)
    across_own, next_sum = lax.optimization_barrier((across_own, next_sum))
    come_own = send(across_own, "rep", lambda p: p ^ 1)
    feature_grad, token = call(feature_body, [half, TOKEN], moved=12 * near * width)(
        f0_kept, gain_row, norm_back, next_sum
    )
    (far_sum,) = call(far_sum_body, [(packet, F32)], moved=1000)(token, two_on, three_on)
    (reduced,) = call(last_sum_body, [(packet, BF16)], [((4, BAND, LANES), F32), (packet, BF16)], moved=1000)(
        far_sum, keep, come_own, next_one, two_on, three_on
    )
    far_block = send(reduced, "loop", lambda p: p ^ 2)
    near_block = send(reduced, "loop", lambda p: p ^ 1)
    blocks = [reduced, near_block, far_block, send(far_block, "loop", lambda p: p ^ 1)]

    proj_grad, gain_gradient = call(
        functools.partial(finish_body, members),
        [((each, width), F32), ((width,), F32)],
        [((members, bands * BAND, full), F32)],
        moved=8 * each * width,
    )(*blocks)
    return feature_grad[:, None, :], text_grad[:, None, :], proj_grad, gain_gradient


def four_fits(mesh, rows_shape):
    members, groups = mesh.shape["loop"], mesh.shape["rep"]
    rows, width = rows_shape[0] // members, rows_shape[2]
    if members != 4 or groups != 8 or width % (members * groups) or width % LANES:
        return False
    columns, each = width // members, width // groups
    full = columns // LANES * LANES
    rest = columns - full
    if rest == 0 or full < LANES or full % rest or each % BAND or rows % 64 or width // LANES > BAND:
        return False
    chunks = each // BAND
    used = (chunks - 1) % (full // rest) + 1
    return used * rest <= full - LANES


def solution(mesh):
    def run(features, text, proj, gain, scale, bias):
        body = local_four if four_fits(mesh, features.shape) else local_any_size
        return jax.shard_map(
            body,
            mesh=mesh,
            in_specs=(P("loop", "rep", None), P("loop", "rep", None), P(), P(), P(), P()),
            out_specs=(P("loop", "rep", None), P("loop", "rep", None), P("rep", None), P()),
            check_vma=False,
        )(features, text, proj, gain, scale, bias)

    return run
```

```python
import functools

import jax
import jax.numpy as jnp
from jax import lax
from jax.experimental import pallas as pl
from jax.experimental.pallas import tpu as pltpu
from jax.sharding import PartitionSpec as P

F32 = jnp.float32
BF16 = jnp.bfloat16
LAST = (((1,), (1,)), ((), ()))
FIRST = (((0,), (0,)), ((), ()))


def dot(a, b, dims=(((1,), (0,)), ((), ()))):
    return lax.dot_general(a, b, dims, preferred_element_type=F32)


def unit_rows(values):
    inverse = lax.rsqrt(jnp.sum(values * values, axis=-1, keepdims=True) + 1e-06)
    return values * inverse, inverse


def standardize(rows):
    values = rows.astype(F32)
    centred = values - jnp.mean(values, axis=-1, keepdims=True)
    inverse = lax.rsqrt(jnp.mean(centred * centred, axis=-1, keepdims=True) + 1e-06)
    return centred * inverse, inverse


def send(value, axis, target):
    count = lax.axis_size(axis)
    return lax.ppermute(value, axis, [(p, target(p)) for p in range(count)])


def gather_group(value, count):
    mine = [value]
    for step in range(1, count // 2):
        mine.append(send(value, "loop", lambda p: (p + 2 * step) % count))
    mates = [send(block, "loop", lambda p: p ^ 1) for block in mine]
    return mine + mates


def local_any_size(features, text, proj, gain, scale, bias):
    n = lax.axis_size("loop")
    m = lax.axis_size("rep")
    me = lax.axis_index("loop")
    half = n // 2
    rows, width = features.shape[0], features.shape[2]
    columns = proj.shape[1] // n
    group_rows = rows * n
    logit_scale, logit_bias = scale[0], bias[0]

    own_features = features[:, 0, :]
    own_text = text[:, 0, :]
    text_blocks = gather_group(own_text, n)
    feature_blocks = gather_group(own_features, n)

    xhat, deviation = standardize(own_features)
    normed = (xhat * gain).astype(BF16)
    img_dir, img_inv = unit_rows(dot(normed, proj))
    img_unit = img_dir.astype(BF16)

    txt_dir, txt_inv = unit_rows(own_text.astype(F32))
    own_txt_unit = txt_dir.astype(BF16)
    txt_unit = jnp.concatenate(
        [own_txt_unit] + [unit_rows(block.astype(F32))[0].astype(BF16) for block in text_blocks[1:]]
    )
    row_ids = lax.broadcasted_iota(jnp.int32, (rows, group_rows), 0)
    column_ids = lax.broadcasted_iota(jnp.int32, (rows, group_rows), 1)
    diagonal = (row_ids == column_ids).astype(F32)

    def weights(left, right):
        logits = logit_scale * dot(left, right, LAST) + logit_bias
        return (jax.nn.sigmoid(logits) - diagonal).astype(BF16)

    img_back = logit_scale * dot(weights(img_unit, txt_unit), txt_unit)
    proj_back = (
        (img_back - img_dir * jnp.sum(img_dir * img_back, axis=-1, keepdims=True)) * img_inv
    ).astype(BF16)

    blocks = jnp.transpose(proj_back.reshape(rows, n, columns), (1, 0, 2))
    blocks = lax.all_to_all(blocks, "loop", 0, 0, tiled=True)
    back_columns = blocks.reshape(group_rows, columns)

    norm_back = dot(proj_back, proj, LAST)
    scaled = norm_back * gain
    feature_grad = (
        deviation
        * (
            scaled
            - jnp.mean(scaled, axis=-1, keepdims=True)
            - xhat * jnp.mean(scaled * xhat, axis=-1, keepdims=True)
        )
    ).astype(BF16)
    gain_term = jnp.sum(norm_back * xhat, axis=0) * (1.0 / group_rows)

    other_normed = [(standardize(block)[0] * gain).astype(BF16) for block in feature_blocks[1:]]
    relative = jnp.stack([normed] + other_normed)
    member = jnp.arange(n)
    same_core = (member % 2) == (me % 2)
    chips_back = ((me // 2 - member // 2) % half)
    position = jnp.where(same_core, chips_back, half + chips_back)
    group_normed = relative[position].reshape(group_rows, width)

    partial = (dot(group_normed, back_columns, FIRST) * (1.0 / group_rows)).astype(BF16)
    pieces = lax.all_to_all(partial.reshape(m, width // m, columns), "rep", 0, 0, tiled=True)
    reduced = jnp.sum(pieces.astype(F32), axis=0).astype(BF16)
    gains = lax.all_gather(gain_term, "rep")
    gain_sum = jnp.sum(gains, axis=0)
    proj_rows = lax.all_gather(reduced, "loop")
    proj_grad = jnp.transpose(proj_rows, (1, 0, 2)).reshape(width // m, n * columns).astype(F32)
    gain_gradient = jnp.sum(lax.all_gather(gain_sum, "loop"), axis=0)

    group_unit = jnp.concatenate(
        [img_unit] + [unit_rows(dot(block, proj))[0].astype(BF16) for block in other_normed]
    )
    text_weights = weights(own_txt_unit, group_unit)
    txt_back = logit_scale * dot(text_weights, group_unit)
    text_grad = (
        (txt_back - txt_dir * jnp.sum(txt_dir * txt_back, axis=-1, keepdims=True)) * txt_inv
    ).astype(BF16)
    return feature_grad[:, None, :], text_grad[:, None, :], proj_grad, gain_gradient


VMEM = pl.BlockSpec(memory_space=pltpu.VMEM)
SMEM = pl.BlockSpec(memory_space=pltpu.SMEM)
HBM = pl.BlockSpec(memory_space=pltpu.HBM)
LANES = 128
BAND = 16
TOKEN = ((8, LANES), F32)


def call(body, outs, scratch=(), smem=0, hbm=0, limit=24, flops=0, moved=0):
    def run(*operands):
        specs = [SMEM] * smem + [HBM] * hbm + [VMEM] * (len(operands) - smem - hbm)
        return pl.pallas_call(
            body,
            out_shape=[jax.ShapeDtypeStruct(shape, kind) for shape, kind in outs],
            in_specs=specs,
            out_specs=[VMEM] * len(outs),
            scratch_shapes=[pltpu.VMEM(shape, kind) for shape, kind in scratch]
            + [pltpu.SemaphoreType.DMA((hbm,))] * bool(hbm),
            compiler_params=pltpu.CompilerParams(vmem_limit_bytes=limit * 2**20),
            cost_estimate=pl.CostEstimate(flops=flops, bytes_accessed=moved, transcendentals=0),
        )(*operands)

    return run


def over_rows(count, step, body):
    def turn(index, _):
        body(pl.ds(pl.multiple_of(index * step, step), step))
        return 0

    lax.fori_loop(0, count // step, turn, 0, unroll=min(4, count // step))


def sums(values):
    return jnp.sum(values, axis=-1, keepdims=True)


def normalize_into(source, gain, target, at):
    rows, width = source.shape

    def chunk(where):
        values = source[where, :].astype(F32)
        centred = values - sums(values) * (1.0 / width)
        inverse = lax.rsqrt(sums(centred * centred) * (1.0 / width) + 1e-06)
        target[pl.ds(at + where.start, where.size), :] = (centred * inverse * gain[...]).astype(BF16)

    over_rows(rows, 32, chunk)


def unit_into(source, target, at, inverses=None):
    rows = source.shape[0]

    def chunk(where):
        values = source[where, :].astype(F32)
        inverse = lax.rsqrt(sums(values * values) + 1e-06)
        place = pl.ds(at + where.start, where.size)
        target[place, :] = (values * inverse).astype(BF16)
        if inverses is not None:
            inverses[place, :] = jnp.broadcast_to(inverse, (where.size, LANES))

    over_rows(rows, 32, chunk)


def weigh(dots, scale, bias, diagonal, weights):
    texts, images = dots.shape

    def chunk(index, total):
        where = pl.ds(pl.multiple_of(index * BAND, BAND), BAND)
        product = dots[where, :]
        weight = jnp.tanh((0.5 * scale) * product + 0.5 * bias)
        offset = 0.5
        if diagonal is not None:
            text = index * BAND + diagonal + lax.broadcasted_iota(jnp.int32, product.shape, 0)
            image = lax.broadcasted_iota(jnp.int32, product.shape, 1)
            offset = jnp.where(text == image, -0.5, 0.5)
        weight = (0.5 * weight + offset).astype(BF16)
        weights[where, :] = weight
        both = weight.astype(F32) * product
        return total + both[:8, :] + both[8:, :]

    total = lax.fori_loop(0, texts // BAND, chunk, jnp.zeros((8, images), F32), unroll=4)
    return jnp.sum(total, axis=0, keepdims=True)


def take_columns(source, target):
    members = source.shape[1] // target.shape[1]
    full = target.shape[1] // LANES * LANES
    rest = target.shape[1] - full
    target[:, :full] = source[:, pl.ds(pl.multiple_of(lax.axis_index("loop") * full, LANES), full)]
    for member in range(members):

        @pl.when(lax.axis_index("loop") == member)
        def _():
            target[:, full:] = source[:, members * full + member * rest : members * full + (member + 1) * rest]


def near_body(
    scale, bias, f0_far, proj_far, t0_far, f1, gain_line,
    f0, proj, t0, gain, normed, unit, factors, text_unit, token, projected, semaphores,
):
    rows = f0.shape[0]
    copies = [
        pltpu.make_async_copy(source, target, semaphores.at[at])
        for at, (source, target) in enumerate(((f0_far, f0), (proj_far, proj), (t0_far, t0)))
    ]
    for copy in copies:
        copy.start()
    for at in range(0, gain.shape[1], LANES):
        gain[:, at : at + LANES] = gain_line[at : at + LANES].reshape(1, LANES)
    normalize_into(f1, gain, normed, rows)
    copies[0].wait()
    normalize_into(f0, gain, normed, 0)
    copies[1].wait()
    projected[...] = dot(normed[...], proj[...])
    copies[2].wait()
    unit_into(t0, text_unit, 0)
    unit_into(projected, unit, 0, factors)
    token[...] = jnp.zeros_like(token)


def near_pairs_body(
    scale, bias, normed, unit, factors, text_own, t1, proj, before,
    text_unit, normed_turned, turned, unit_turned, inverse, text_columns, weights, totals, proj_columns, token, dots,
):
    token[...] = jnp.zeros_like(token)
    rows = t1.shape[0]
    text_unit[:rows, :] = text_own[...]
    text_unit[rows:, :] = t1[...]
    dots[...] = dot(text_unit[...], unit[...], LAST)
    totals[...] = weigh(dots, scale[0], bias[0], 0, weights)
    take_columns(text_unit, text_columns)
    take_columns(proj, proj_columns)
    turn_own(unit, factors, turned, unit_turned, inverse)
    normed_turned[...] = normed[...].T


def turn_own(unit, factors, turned, unit_turned, inverse):
    columns = unit_turned.shape[0]
    full = columns // LANES * LANES
    rest = columns - full
    turned[...] = unit[...].T
    unit_turned[:full, :] = turned[pl.ds(pl.multiple_of(lax.axis_index("loop") * full, LANES), full), :]
    begin = turned.shape[0] // columns * full
    unit_turned[full:, :] = turned[pl.ds(pl.multiple_of(begin + lax.axis_index("loop") * rest, BAND), rest), :]
    inverse[...] = factors[...].T[:1, :]


def split_body(f2, before, head, tail):
    head[...] = f2[: head.shape[0], :]
    tail[...] = f2[head.shape[0] :, :]


def far_body(
    scale, bias, f2, f3_head, f3_tail, proj, gain, text_near, text_columns, weights_near,
    normed_turned, unit, turned, unit_turned, inverse, weights, totals, early_near, early_far, token,
    normed, projected, dots, factors,
):
    rows = f2.shape[0]
    normalize_into(f2, gain, normed, 0)
    normalize_into(f3_head, gain, normed, rows)
    normalize_into(f3_tail, gain, normed, rows + f3_head.shape[0])
    projected[...] = dot(normed[...], proj[...])
    unit_into(projected, unit, 0, factors)
    dots[...] = dot(text_near[...], unit[...], LAST)
    totals[...] = weigh(dots, scale[0], bias[0], None, weights)
    turn_own(unit, factors, turned, unit_turned, inverse)
    normed_turned[...] = normed[...].T
    early_near[...] = dot(text_columns[...], weights_near[...], FIRST)
    early_far[...] = dot(text_columns[...], weights[...], FIRST)
    token[...] = jnp.zeros_like(token)


def third_body(
    scale, bias, text_unit, flat_near, flat_far, totals_near, totals_far, early_near, early_far,
    before, weights, back_near, back_far, totals,
    text_columns, dots,
):
    rows = text_unit.shape[0]
    near = 2 * rows
    take_columns(text_unit, text_columns)
    dots[:, :near] = dot(text_unit[...], flat_near[...])
    dots[:, near:] = dot(text_unit[...], flat_far[...])
    added = weigh(dots, scale[0], bias[0], near, weights)
    totals[:, :near] = totals_near[...] + added[:, :near]
    totals[:, near:] = totals_far[...] + added[:, near:]
    added = dot(text_columns[...], weights[...], FIRST)
    back_near[...] = early_near[...] + added[:, :near]
    back_far[...] = early_far[...] + added[:, near:]


def pack_into(target, block, full):
    rows, columns = block.shape
    rest = columns - full
    target[:rows, :] = block[:, :full].astype(BF16)
    per_band = full // rest
    tail = block[:, full:]
    chunks = [tail[at : at + BAND, :] for at in range(0, rows, BAND)]
    for band in range(0, len(chunks), per_band):
        part = chunks[band : band + per_band]
        if len(part) < per_band:
            part.append(jnp.zeros((BAND, full - rest * len(part)), block.dtype))
        at = rows + (band // per_band) * BAND
        target[at : at + BAND, :] = jnp.concatenate(part, axis=1).astype(BF16)


def far_packets_body(
    members, scale, bias, text_unit, flat_near, flat_far, totals, back_near, back_far, unit_turned_near,
    unit_turned_far, inverse_near, inverse_far, turned_near, turned_far, across, back, weights, text_columns, dots,
):
    rows = text_unit.shape[0]
    near = 2 * rows
    every = members * rows
    columns = text_columns.shape[1]
    each = turned_near.shape[0] // lax.axis_size("rep")
    full = across.shape[2]
    scale, bias = scale[0], bias[0]
    take_columns(text_unit, text_columns)
    dots[:, :near] = dot(text_unit[...], flat_near[...])
    dots[:, near:] = dot(text_unit[...], flat_far[...])
    total = totals[...] + weigh(dots, scale, bias, near + rows, weights)
    added = dot(text_columns[...], weights[...], FIRST)
    for where, earlier, unit_turned, inverse in (
        (slice(0, near), back_near, unit_turned_near, inverse_near),
        (slice(near, every), back_far, unit_turned_far, inverse_far),
    ):
        whole = earlier[...] + added[:, where]
        part = (whole - unit_turned[...].astype(F32) * total[:, where]) * (inverse[...] * scale)
        back[:, where] = part.astype(BF16)
    own = lax.axis_index("rep")
    picked = []
    for at in range(2):
        where = pl.ds(pl.multiple_of((own ^ (5 + 2 * at)) * each, BAND), each)
        picked.append(jnp.concatenate([turned_near[where, :], turned_far[where, :]], axis=1))
    product = dot(jnp.concatenate(picked, axis=0), back[...], LAST) * (1.0 / every)
    for at in range(2):
        pack_into(across.at[at], product[at * each : (at + 1) * each, :], full)


def partial_body(
    members, groups, back, turned_near, turned_far, proj_columns, gain, across_later, keep, token, packed,
):
    width = turned_near.shape[0]
    every = back.shape[1]
    columns = width // members
    count, full = packed.shape[1:]
    turned = jnp.concatenate([turned_near[...], turned_far[...]], axis=1)
    product = dot(turned, back[...], LAST)
    each = width // groups
    product = product * (1.0 / every)
    for group in range(groups):
        pack_into(packed.at[group], product[group * each : (group + 1) * each, :], full)

    terms = product * proj_columns[...].astype(F32)
    folded = jnp.concatenate([terms[:, full:], jnp.zeros((width, full + LANES - columns), F32)], axis=1)
    for at in range(0, full, LANES):
        folded = folded + terms[:, at : at + LANES]
    high = folded.astype(BF16)
    low = (folded - high.astype(F32)).astype(BF16)
    ones = jnp.ones((BAND, 2 * LANES), BF16)
    gain_row = dot(ones, jnp.concatenate([high, low], axis=1), LAST)[:1, :] / gain[...]
    pieces = [gain_row[:, at : at + LANES] for at in range(0, width, LANES)]
    pieces.append(jnp.zeros((BAND - len(pieces), LANES), F32))
    gain_tile = jnp.concatenate(pieces, axis=0).astype(BF16)
    for group in range(groups):
        packed[group, count - BAND :, full - LANES :] = gain_tile

    own = lax.axis_index("rep")
    for at in range(2):
        across_later[at] = packed[own ^ 1 ^ (2 * at)]
    for at in range(4):
        keep[at] = packed[own ^ (2 * at)]
    token[...] = jnp.zeros_like(token)


def image_body(
    scale, proj, text_near, text_third, text_fourth, weights_near, weights_third, weights_fourth,
    unit, factors, before, norm_back, token, back, product,
):
    rows = back.shape[0]
    scale = scale[0]
    product[...] = (
        dot(weights_near[:, :rows], text_near[...], FIRST)
        + dot(weights_third[:, :rows], text_third[...], FIRST)
        + dot(weights_fourth[:, :rows], text_fourth[...], FIRST)
    )

    def image_chunk(where):
        values = product[where, :] * scale
        direction = unit[where, :].astype(F32)
        back[where, :] = (
            (values - direction * sums(direction * values)) * factors[where, :1]
        ).astype(BF16)

    over_rows(rows, 32, image_chunk)
    norm_back[...] = dot(back[...], proj[...], LAST)
    token[...] = jnp.zeros_like(token)


def feature_body(features, gain, norm_back, before, feature_grad, token):
    rows, width = features.shape

    def feature_chunk(where):
        values = features[where, :].astype(F32)
        centred = values - sums(values) * (1.0 / width)
        deviation = lax.rsqrt(sums(centred * centred) * (1.0 / width) + 1e-06)
        xhat = centred * deviation
        scaled = norm_back[where, :] * gain[...]
        feature_grad[where, :] = (
            deviation
            * (scaled - sums(scaled) * (1.0 / width) - xhat * (sums(scaled * xhat) * (1.0 / width)))
        ).astype(BF16)

    over_rows(rows, 32, feature_chunk)
    token[...] = jnp.zeros_like(token)


def text_body(
    scale, text, weights_near, weights_far, unit_near, unit_far, before, text_grad, token, product,
):
    rows = text_grad.shape[0]
    scale = scale[0]
    product[...] = dot(weights_near[:rows, :], unit_near[...]) + dot(weights_far[:rows, :], unit_far[...])

    def text_chunk(where):
        values = product[where, :] * scale
        own = text[where, :].astype(F32)
        own_inverse = lax.rsqrt(sums(own * own) + 1e-06)
        direction = own * own_inverse
        text_grad[where, :] = (
            (values - direction * sums(direction * values)) * own_inverse
        ).astype(BF16)

    over_rows(rows, 32, text_chunk)
    token[...] = jnp.zeros_like(token)


def far_pair_sum_body(before, keep, come, two_on, three_on):
    for at, target in enumerate((two_on, three_on)):
        target[...] = (keep[2 + at].astype(F32) + come[at].astype(F32)).astype(BF16)


def near_pair_sum_body(before, keep, come, own, next_one, gain_rows):
    for at, target in enumerate((own, next_one)):
        target[...] = (keep[at].astype(F32) + come[at].astype(F32)).astype(BF16)
    count, full = own.shape
    gain_rows[...] = own[count - BAND :, full - LANES :]


def gain_sum_body(two_on, three_on, token):
    token[...] = jnp.zeros_like(token)


def far_sum_body(before, two_on, three_on, total):
    total[...] = two_on[...].astype(F32) + three_on[...].astype(F32)


def last_sum_body(far, own, next_one, gain_two, gain_three, total, ordered):
    total[...] = (own[...].astype(F32) + next_one[...].astype(F32) + far[...]).astype(BF16)
    count, full = total.shape
    z = lax.axis_index("rep") // 2
    ordered[z] = own[count - BAND :, full - LANES :].astype(F32)
    ordered[z ^ 1] = next_one[count - BAND :, full - LANES :].astype(F32)
    ordered[z ^ 2] = gain_two[...].astype(F32)
    ordered[z ^ 3] = gain_three[...].astype(F32)
    value = ordered[0]
    for at in range(1, 4):
        value = value + ordered[at]
    total[count - BAND :, full - LANES :] = value.astype(BF16)


def finish_body(members, before, *refs):
    packets, (proj_grad, gain_gradient, ordered) = refs[:members], refs[members:]
    count, full = packets[0].shape
    rows, width = proj_grad.shape
    rest = width // members - full
    per_band = full // rest
    for k in range(members):
        member = lax.axis_index("loop") ^ k
        proj_grad[:, pl.ds(pl.multiple_of(member * full, LANES), full)] = packets[k][:rows, :].astype(F32)
        ordered[member] = packets[k][rows:, :].astype(F32)
    tails = []
    for index in range(rows // BAND):
        at, lane = (index // per_band) * BAND, (index % per_band) * rest
        tails.append(
            jnp.concatenate([ordered[member][at : at + BAND, lane : lane + rest] for member in range(members)], axis=1)
        )
    proj_grad[:, members * full :] = jnp.concatenate(tails, axis=0)
    value = ordered[0][count - rows - BAND :, full - LANES :]
    for member in range(1, members):
        value = value + ordered[member][count - rows - BAND :, full - LANES :]
    for at in range(width // LANES):
        gain_gradient[at * LANES : (at + 1) * LANES] = value[at]


def local_four(features, text, proj, gain, scale, bias):
    members = lax.axis_size("loop")
    groups = lax.axis_size("rep")
    rows, width = features.shape[0], features.shape[2]
    near, every = 2 * rows, 4 * rows
    columns = width // members
    full = columns // LANES * LANES
    each = width // groups
    bands = -(-(each // BAND) // (full // (columns - full)))
    packet = (each + bands * BAND, full)


    f0, t0 = features[:, 0, :], text[:, 0, :]
    f2 = send(f0, "loop", lambda p: p ^ 2)
    f1 = send(f0, "loop", lambda p: p ^ 1)

    wide, half = ((near, width), BF16), ((rows, width), BF16)
    square, part, turned = ((near, near), BF16), ((near, columns), BF16), ((width, near), BF16)

    line, mine = ((1, near), F32), ((columns, near), BF16)
    kept = ((width, width), BF16)
    f0_kept, proj_kept, t0_kept, gain_row, normed_near, unit_near, factors, text_own, token = call(
        near_body,
        [half, kept, half, ((1, width), F32), wide, wide, ((near, LANES), F32), half, TOKEN],
        [((near, width), F32)],
        smem=2,
        hbm=3,
        limit=46,
        flops=2 * near * width * width,
        moved=8 * near * width,
    )(scale, bias, f0, proj, t0, f1, gain)

    t2 = send(text_own, "loop", lambda p: p ^ 2)
    t1 = send(text_own, "loop", lambda p: p ^ 1)
    head = rows // 6 * 5
    f3_head, f3_tail = call(split_body, [((head, width), BF16), ((rows - head, width), BF16)], moved=1000)(f2, token)
    f3_head = send(f3_head, "loop", lambda p: p ^ 1)
    f3_tail = send(f3_tail, "loop", lambda p: p ^ 1)

    (
        text_near, turned_near, flat_near, unit_turned_near, inverse_near, text_columns_near, weights_near, totals_near, proj_columns,
        token,
    ) = call(
        near_pairs_body,
        [wide, turned, turned, mine, line, part, square, line, ((width, columns), BF16), TOKEN],
        [((near, near), F32)],
        smem=2,
        flops=1000,
        moved=1000,
    )(scale, bias, normed_near, unit_near, factors, text_own, t1, proj_kept, token)

    back_kind = ((columns, near), F32)
    (
        turned_far, unit_far, flat_far, unit_turned_far, inverse_far, weights_far, totals_far, early_near, early_far,
        token,
    ) = call(
        far_body,
        [turned, wide, turned, mine, line, square, line, back_kind, back_kind, TOKEN],
        [wide, ((near, width), F32), ((near, near), F32), ((near, LANES), F32)],
        smem=2,
        flops=1000,
        moved=1000,
    )(
        scale, bias, f2, f3_head, f3_tail, proj_kept, gain_row, text_near, text_columns_near, weights_near,
    )

    text_grad, token = call(
        text_body,
        [half, TOKEN],
        [((rows, width), F32)],
        smem=1,
        flops=1000,
        moved=1000,
    )(scale, t0_kept, weights_near, weights_far, unit_near, unit_far, token)

    t2_after, token = lax.optimization_barrier((t2, token))
    t3 = send(t2_after, "loop", lambda p: p ^ 1)

    narrow = ((rows, every), BF16)
    weights_third, back_near, back_far, totals = call(
        third_body,
        [narrow, back_kind, back_kind, ((1, every), F32)],
        [((rows, columns), BF16), ((rows, every), F32)],
        smem=2,
        flops=2 * near * width * width,
        moved=8 * near * width,
    )(
        scale, bias, t2, flat_near, flat_far, totals_near, totals_far, early_near, early_far, token,
    )

    across_first, back, weights_fourth = call(
        functools.partial(far_packets_body, members),
        [((2,) + packet, BF16), ((columns, every), BF16), narrow],
        [((rows, columns), BF16), ((rows, every), F32)],
        smem=2,
        moved=1000,
    )(
        scale, bias, t3, flat_near, flat_far, totals, back_near, back_far, unit_turned_near, unit_turned_far,
        inverse_near, inverse_far, turned_near, turned_far,
    )
    come_first = send(across_first, "rep", lambda p: p ^ 1)
    across_later, keep, token = call(
        functools.partial(partial_body, members, groups),
        [((2,) + packet, BF16), ((4,) + packet, BF16), TOKEN],
        [((groups,) + packet, BF16)],
        moved=1000,
    )(back, turned_near, turned_far, proj_columns, gain_row)
    norm_back, token = call(
        image_body,
        [((rows, width), F32), TOKEN],
        [half, ((rows, width), F32)],
        smem=1,
        moved=1000,
    )(
        scale, proj_kept, text_near, t2, t3, weights_near, weights_third, weights_fourth,
        unit_near, factors, token,
    )

    across_later, token = lax.optimization_barrier((across_later, token))
    come_later = send(across_later, "rep", lambda p: p ^ 1)
    two_sum, three_sum = call(far_pair_sum_body, [(packet, BF16)] * 2, moved=1000)(token, keep, come_first)
    two_on = send(two_sum, "rep", lambda p: p ^ 4)
    three_on = send(three_sum, "rep", lambda p: p ^ 6)
    own_sum, next_one, gain_rows = call(
        near_pair_sum_body, [(packet, BF16)] * 2 + [((BAND, LANES), BF16)], moved=1000
    )(two_sum, keep, come_later)
    next_one = send(next_one, "rep", lambda p: p ^ 2)
    gain_two = send(gain_rows, "rep", lambda p: p ^ 4)
    gain_three = send(gain_rows, "rep", lambda p: p ^ 6)
    (token,) = call(gain_sum_body, [TOKEN], moved=1000)(gain_two, gain_three)
    (far_sum,) = call(far_sum_body, [(packet, F32)], moved=1000)(token, two_on, three_on)
    (reduced,) = call(last_sum_body, [(packet, BF16)], [((4, BAND, LANES), F32)], moved=1000)(
        far_sum, own_sum, next_one, gain_two, gain_three
    )
    far_block = send(reduced, "loop", lambda p: p ^ 2)
    near_block = send(reduced, "loop", lambda p: p ^ 1)
    feature_grad, token = call(feature_body, [half, TOKEN], moved=12 * near * width)(
        f0_kept, gain_row, norm_back, reduced
    )
    far_block, token = lax.optimization_barrier((far_block, token))
    blocks = [reduced, near_block, far_block, send(far_block, "loop", lambda p: p ^ 1)]

    proj_grad, gain_gradient = call(
        functools.partial(finish_body, members),
        [((each, width), F32), ((width,), F32)],
        [((members, bands * BAND, full), F32)],
        moved=8 * each * width,
    )(token, *blocks)
    return feature_grad[:, None, :], text_grad[:, None, :], proj_grad, gain_gradient


def four_fits(mesh, rows_shape):
    members, groups = mesh.shape["loop"], mesh.shape["rep"]
    rows, width = rows_shape[0] // members, rows_shape[2]
    if members != 4 or groups != 8 or width % (members * groups) or width % LANES:
        return False
    columns, each = width // members, width // groups
    full = columns // LANES * LANES
    rest = columns - full
    if rest == 0 or full < LANES or full % rest or each % BAND or rows % 64 or width // LANES > BAND:
        return False
    chunks = each // BAND
    used = (chunks - 1) % (full // rest) + 1
    return used * rest <= full - LANES


def solution(mesh):
    def run(features, text, proj, gain, scale, bias):
        body = local_four if four_fits(mesh, features.shape) else local_any_size
        return jax.shard_map(
            body,
            mesh=mesh,
            in_specs=(P("loop", "rep", None), P("loop", "rep", None), P(), P(), P(), P()),
            out_specs=(P("loop", "rep", None), P("loop", "rep", None), P("rep", None), P()),
            check_vma=False,
        )(features, text, proj, gain, scale, bias)

    return run
```

```python
import functools

import jax
import jax.numpy as jnp
from jax import lax
from jax.experimental import pallas as pl
from jax.experimental.pallas import tpu as pltpu
from jax.sharding import PartitionSpec as P

F32 = jnp.float32
BF16 = jnp.bfloat16
LAST = (((1,), (1,)), ((), ()))
FIRST = (((0,), (0,)), ((), ()))


def dot(a, b, dims=(((1,), (0,)), ((), ()))):
    return lax.dot_general(a, b, dims, preferred_element_type=F32)


def unit_rows(values):
    inverse = lax.rsqrt(jnp.sum(values * values, axis=-1, keepdims=True) + 1e-06)
    return values * inverse, inverse


def standardize(rows):
    values = rows.astype(F32)
    centred = values - jnp.mean(values, axis=-1, keepdims=True)
    inverse = lax.rsqrt(jnp.mean(centred * centred, axis=-1, keepdims=True) + 1e-06)
    return centred * inverse, inverse


def send(value, axis, target):
    count = lax.axis_size(axis)
    return lax.ppermute(value, axis, [(p, target(p)) for p in range(count)])


def gather_group(value, count):
    mine = [value]
    for step in range(1, count // 2):
        mine.append(send(value, "loop", lambda p: (p + 2 * step) % count))
    mates = [send(block, "loop", lambda p: p ^ 1) for block in mine]
    return mine + mates


def local_any_size(features, text, proj, gain, scale, bias):
    n = lax.axis_size("loop")
    m = lax.axis_size("rep")
    me = lax.axis_index("loop")
    half = n // 2
    rows, width = features.shape[0], features.shape[2]
    columns = proj.shape[1] // n
    group_rows = rows * n
    logit_scale, logit_bias = scale[0], bias[0]

    own_features = features[:, 0, :]
    own_text = text[:, 0, :]
    text_blocks = gather_group(own_text, n)
    feature_blocks = gather_group(own_features, n)

    xhat, deviation = standardize(own_features)
    normed = (xhat * gain).astype(BF16)
    img_dir, img_inv = unit_rows(dot(normed, proj))
    img_unit = img_dir.astype(BF16)

    txt_dir, txt_inv = unit_rows(own_text.astype(F32))
    own_txt_unit = txt_dir.astype(BF16)
    txt_unit = jnp.concatenate(
        [own_txt_unit] + [unit_rows(block.astype(F32))[0].astype(BF16) for block in text_blocks[1:]]
    )
    row_ids = lax.broadcasted_iota(jnp.int32, (rows, group_rows), 0)
    column_ids = lax.broadcasted_iota(jnp.int32, (rows, group_rows), 1)
    diagonal = (row_ids == column_ids).astype(F32)

    def weights(left, right):
        logits = logit_scale * dot(left, right, LAST) + logit_bias
        return (jax.nn.sigmoid(logits) - diagonal).astype(BF16)

    img_back = logit_scale * dot(weights(img_unit, txt_unit), txt_unit)
    proj_back = (
        (img_back - img_dir * jnp.sum(img_dir * img_back, axis=-1, keepdims=True)) * img_inv
    ).astype(BF16)

    blocks = jnp.transpose(proj_back.reshape(rows, n, columns), (1, 0, 2))
    blocks = lax.all_to_all(blocks, "loop", 0, 0, tiled=True)
    back_columns = blocks.reshape(group_rows, columns)

    norm_back = dot(proj_back, proj, LAST)
    scaled = norm_back * gain
    feature_grad = (
        deviation
        * (
            scaled
            - jnp.mean(scaled, axis=-1, keepdims=True)
            - xhat * jnp.mean(scaled * xhat, axis=-1, keepdims=True)
        )
    ).astype(BF16)
    gain_term = jnp.sum(norm_back * xhat, axis=0) * (1.0 / group_rows)

    other_normed = [(standardize(block)[0] * gain).astype(BF16) for block in feature_blocks[1:]]
    relative = jnp.stack([normed] + other_normed)
    member = jnp.arange(n)
    same_core = (member % 2) == (me % 2)
    chips_back = ((me // 2 - member // 2) % half)
    position = jnp.where(same_core, chips_back, half + chips_back)
    group_normed = relative[position].reshape(group_rows, width)

    partial = (dot(group_normed, back_columns, FIRST) * (1.0 / group_rows)).astype(BF16)
    pieces = lax.all_to_all(partial.reshape(m, width // m, columns), "rep", 0, 0, tiled=True)
    reduced = jnp.sum(pieces.astype(F32), axis=0).astype(BF16)
    gains = lax.all_gather(gain_term, "rep")
    gain_sum = jnp.sum(gains, axis=0)
    proj_rows = lax.all_gather(reduced, "loop")
    proj_grad = jnp.transpose(proj_rows, (1, 0, 2)).reshape(width // m, n * columns).astype(F32)
    gain_gradient = jnp.sum(lax.all_gather(gain_sum, "loop"), axis=0)

    group_unit = jnp.concatenate(
        [img_unit] + [unit_rows(dot(block, proj))[0].astype(BF16) for block in other_normed]
    )
    text_weights = weights(own_txt_unit, group_unit)
    txt_back = logit_scale * dot(text_weights, group_unit)
    text_grad = (
        (txt_back - txt_dir * jnp.sum(txt_dir * txt_back, axis=-1, keepdims=True)) * txt_inv
    ).astype(BF16)
    return feature_grad[:, None, :], text_grad[:, None, :], proj_grad, gain_gradient


VMEM = pl.BlockSpec(memory_space=pltpu.VMEM)
SMEM = pl.BlockSpec(memory_space=pltpu.SMEM)
HBM = pl.BlockSpec(memory_space=pltpu.HBM)
LANES = 128
BAND = 16
TOKEN = ((8, LANES), F32)


def call(body, outs, scratch=(), smem=0, hbm=0, limit=24, flops=0, moved=0):
    def run(*operands):
        specs = [SMEM] * smem + [HBM] * hbm + [VMEM] * (len(operands) - smem - hbm)
        return pl.pallas_call(
            body,
            out_shape=[jax.ShapeDtypeStruct(shape, kind) for shape, kind in outs],
            in_specs=specs,
            out_specs=[VMEM] * len(outs),
            scratch_shapes=[pltpu.VMEM(shape, kind) for shape, kind in scratch]
            + [pltpu.SemaphoreType.DMA((hbm,))] * bool(hbm),
            compiler_params=pltpu.CompilerParams(vmem_limit_bytes=limit * 2**20),
            cost_estimate=pl.CostEstimate(flops=flops, bytes_accessed=moved, transcendentals=0),
        )(*operands)

    return run


def over_rows(count, step, body):
    def turn(index, _):
        body(pl.ds(pl.multiple_of(index * step, step), step))
        return 0

    lax.fori_loop(0, count // step, turn, 0, unroll=min(4, count // step))


def sums(values):
    return jnp.sum(values, axis=-1, keepdims=True)


def normalize_into(source, gain, target, at):
    rows, width = source.shape

    def chunk(where):
        values = source[where, :].astype(F32)
        centred = values - sums(values) * (1.0 / width)
        inverse = lax.rsqrt(sums(centred * centred) * (1.0 / width) + 1e-06)
        target[pl.ds(at + where.start, where.size), :] = (centred * inverse * gain[...]).astype(BF16)

    over_rows(rows, 32, chunk)


def unit_into(source, target, at, inverses=None):
    rows = source.shape[0]

    def chunk(where):
        values = source[where, :].astype(F32)
        inverse = lax.rsqrt(sums(values * values) + 1e-06)
        place = pl.ds(at + where.start, where.size)
        target[place, :] = (values * inverse).astype(BF16)
        if inverses is not None:
            inverses[place, :] = jnp.broadcast_to(inverse, (where.size, LANES))

    over_rows(rows, 32, chunk)


def weigh(dots, scale, bias, diagonal, weights):
    texts, images = dots.shape

    def chunk(index, total):
        where = pl.ds(pl.multiple_of(index * BAND, BAND), BAND)
        product = dots[where, :]
        weight = jnp.tanh((0.5 * scale) * product + 0.5 * bias)
        offset = 0.5
        if diagonal is not None:
            text = index * BAND + diagonal + lax.broadcasted_iota(jnp.int32, product.shape, 0)
            image = lax.broadcasted_iota(jnp.int32, product.shape, 1)
            offset = jnp.where(text == image, -0.5, 0.5)
        weight = (0.5 * weight + offset).astype(BF16)
        weights[where, :] = weight
        both = weight.astype(F32) * product
        return total + both[:8, :] + both[8:, :]

    total = lax.fori_loop(0, texts // BAND, chunk, jnp.zeros((8, images), F32), unroll=4)
    return jnp.sum(total, axis=0, keepdims=True)


def take_columns(source, target):
    members = source.shape[1] // target.shape[1]
    full = target.shape[1] // LANES * LANES
    rest = target.shape[1] - full
    target[:, :full] = source[:, pl.ds(pl.multiple_of(lax.axis_index("loop") * full, LANES), full)]
    for member in range(members):

        @pl.when(lax.axis_index("loop") == member)
        def _():
            target[:, full:] = source[:, members * full + member * rest : members * full + (member + 1) * rest]


def near_body(
    scale, bias, f0_far, proj_far, t0_far, f1, gain_line,
    f0, proj, t0, gain, normed, unit, factors, text_unit, token, projected, semaphores,
):
    rows = f0.shape[0]
    copies = [
        pltpu.make_async_copy(source, target, semaphores.at[at])
        for at, (source, target) in enumerate(((f0_far, f0), (proj_far, proj), (t0_far, t0)))
    ]
    for copy in copies:
        copy.start()
    for at in range(0, gain.shape[1], LANES):
        gain[:, at : at + LANES] = gain_line[at : at + LANES].reshape(1, LANES)
    normalize_into(f1, gain, normed, rows)
    copies[0].wait()
    normalize_into(f0, gain, normed, 0)
    copies[1].wait()
    projected[...] = dot(normed[...], proj[...])
    copies[2].wait()
    unit_into(t0, text_unit, 0)
    unit_into(projected, unit, 0, factors)
    token[...] = jnp.zeros_like(token)


def near_pairs_body(
    scale, bias, normed, unit, factors, text_own, t1, proj, before,
    text_unit, normed_turned, turned, unit_turned, inverse, text_columns, weights, totals, proj_columns, token, dots,
):
    token[...] = jnp.zeros_like(token)
    rows = t1.shape[0]
    text_unit[:rows, :] = text_own[...]
    text_unit[rows:, :] = t1[...]
    dots[...] = dot(text_unit[...], unit[...], LAST)
    totals[...] = weigh(dots, scale[0], bias[0], 0, weights)
    take_columns(text_unit, text_columns)
    take_columns(proj, proj_columns)
    turn_own(unit, factors, turned, unit_turned, inverse)
    normed_turned[...] = normed[...].T


def turn_own(unit, factors, turned, unit_turned, inverse):
    columns = unit_turned.shape[0]
    full = columns // LANES * LANES
    rest = columns - full
    turned[...] = unit[...].T
    unit_turned[:full, :] = turned[pl.ds(pl.multiple_of(lax.axis_index("loop") * full, LANES), full), :]
    begin = turned.shape[0] // columns * full
    unit_turned[full:, :] = turned[pl.ds(pl.multiple_of(begin + lax.axis_index("loop") * rest, BAND), rest), :]
    inverse[...] = factors[...].T[:1, :]


def split_body(f2, before, head, tail):
    head[...] = f2[: head.shape[0], :]
    tail[...] = f2[head.shape[0] :, :]


def far_body(
    scale, bias, f2, f3_head, f3_tail, proj, gain, text_near, text_columns, weights_near,
    normed_turned, unit, turned, unit_turned, inverse, weights, totals, early_near, early_far, token,
    normed, projected, dots, factors,
):
    rows = f2.shape[0]
    normalize_into(f2, gain, normed, 0)
    normalize_into(f3_head, gain, normed, rows)
    normalize_into(f3_tail, gain, normed, rows + f3_head.shape[0])
    projected[...] = dot(normed[...], proj[...])
    unit_into(projected, unit, 0, factors)
    dots[...] = dot(text_near[...], unit[...], LAST)
    totals[...] = weigh(dots, scale[0], bias[0], None, weights)
    turn_own(unit, factors, turned, unit_turned, inverse)
    normed_turned[...] = normed[...].T
    early_near[...] = dot(text_columns[...], weights_near[...], FIRST)
    early_far[...] = dot(text_columns[...], weights[...], FIRST)
    token[...] = jnp.zeros_like(token)


def third_body(
    scale, bias, text_unit, flat_near, flat_far, totals_near, totals_far, early_near, early_far,
    before, weights, back_near, back_far, totals,
    text_columns, dots,
):
    rows = text_unit.shape[0]
    near = 2 * rows
    take_columns(text_unit, text_columns)
    dots[:, :near] = dot(text_unit[...], flat_near[...])
    dots[:, near:] = dot(text_unit[...], flat_far[...])
    added = weigh(dots, scale[0], bias[0], near, weights)
    totals[:, :near] = totals_near[...] + added[:, :near]
    totals[:, near:] = totals_far[...] + added[:, near:]
    added = dot(text_columns[...], weights[...], FIRST)
    back_near[...] = early_near[...] + added[:, :near]
    back_far[...] = early_far[...] + added[:, near:]


def pack_into(target, block, full):
    rows, columns = block.shape
    rest = columns - full
    target[:rows, :] = block[:, :full].astype(BF16)
    per_band = full // rest
    tail = block[:, full:]
    chunks = [tail[at : at + BAND, :] for at in range(0, rows, BAND)]
    for band in range(0, len(chunks), per_band):
        part = chunks[band : band + per_band]
        if len(part) < per_band:
            part.append(jnp.zeros((BAND, full - rest * len(part)), block.dtype))
        at = rows + (band // per_band) * BAND
        target[at : at + BAND, :] = jnp.concatenate(part, axis=1).astype(BF16)


def far_packets_body(
    members, scale, bias, text_unit, flat_near, flat_far, totals, back_near, back_far, unit_turned_near,
    unit_turned_far, inverse_near, inverse_far, turned_near, turned_far, across, back, weights, text_columns, dots,
):
    rows = text_unit.shape[0]
    near = 2 * rows
    every = members * rows
    columns = text_columns.shape[1]
    each = turned_near.shape[0] // lax.axis_size("rep")
    full = across.shape[2]
    scale, bias = scale[0], bias[0]
    take_columns(text_unit, text_columns)
    dots[:, :near] = dot(text_unit[...], flat_near[...])
    dots[:, near:] = dot(text_unit[...], flat_far[...])
    total = totals[...] + weigh(dots, scale, bias, near + rows, weights)
    added = dot(text_columns[...], weights[...], FIRST)
    for where, earlier, unit_turned, inverse in (
        (slice(0, near), back_near, unit_turned_near, inverse_near),
        (slice(near, every), back_far, unit_turned_far, inverse_far),
    ):
        whole = earlier[...] + added[:, where]
        part = (whole - unit_turned[...].astype(F32) * total[:, where]) * (inverse[...] * scale)
        back[:, where] = part.astype(BF16)
    own = lax.axis_index("rep")
    picked = []
    for at in range(2):
        where = pl.ds(pl.multiple_of((own ^ (5 + 2 * at)) * each, BAND), each)
        picked.append(jnp.concatenate([turned_near[where, :], turned_far[where, :]], axis=1))
    product = dot(jnp.concatenate(picked, axis=0), back[...], LAST) * (1.0 / every)
    for at in range(2):
        pack_into(across.at[at], product[at * each : (at + 1) * each, :], full)


def partial_body(
    members, groups, back, turned_near, turned_far, proj_columns, gain, across_later, keep, gain_rows, token, packed,
):
    width = turned_near.shape[0]
    every = back.shape[1]
    columns = width // members
    count, full = packed.shape[1:]
    turned = jnp.concatenate([turned_near[...], turned_far[...]], axis=1)
    product = dot(turned, back[...], LAST)
    each = width // groups
    product = product * (1.0 / every)
    for group in range(groups):
        pack_into(packed.at[group], product[group * each : (group + 1) * each, :], full)

    terms = product * proj_columns[...].astype(F32)
    folded = jnp.concatenate([terms[:, full:], jnp.zeros((width, full + LANES - columns), F32)], axis=1)
    for at in range(0, full, LANES):
        folded = folded + terms[:, at : at + LANES]
    high = folded.astype(BF16)
    low = (folded - high.astype(F32)).astype(BF16)
    ones = jnp.ones((BAND, 2 * LANES), BF16)
    gain_row = dot(ones, jnp.concatenate([high, low], axis=1), LAST)[:1, :] / gain[...]
    pieces = [gain_row[:, at : at + LANES] for at in range(0, width, LANES)]
    pieces.append(jnp.zeros((BAND - len(pieces), LANES), F32))
    gain_tile = jnp.concatenate(pieces, axis=0).astype(BF16)
    for group in range(groups):
        packed[group, count - BAND :, full - LANES :] = gain_tile
    gain_rows[...] = gain_tile

    own = lax.axis_index("rep")
    for at in range(2):
        across_later[at] = packed[own ^ 1 ^ (2 * at)]
    for at in range(4):
        keep[at] = packed[own ^ (2 * at)]
    token[...] = jnp.zeros_like(token)


def image_body(
    scale, proj, text_near, text_third, text_fourth, weights_near, weights_third, weights_fourth,
    unit, factors, before, norm_back, token, back, product,
):
    rows = back.shape[0]
    scale = scale[0]
    product[...] = (
        dot(weights_near[:, :rows], text_near[...], FIRST)
        + dot(weights_third[:, :rows], text_third[...], FIRST)
        + dot(weights_fourth[:, :rows], text_fourth[...], FIRST)
    )

    def image_chunk(where):
        values = product[where, :] * scale
        direction = unit[where, :].astype(F32)
        back[where, :] = (
            (values - direction * sums(direction * values)) * factors[where, :1]
        ).astype(BF16)

    over_rows(rows, 32, image_chunk)
    norm_back[...] = dot(back[...], proj[...], LAST)
    token[...] = jnp.zeros_like(token)


def feature_body(features, gain, norm_back, before, feature_grad, token):
    rows, width = features.shape

    def feature_chunk(where):
        values = features[where, :].astype(F32)
        centred = values - sums(values) * (1.0 / width)
        deviation = lax.rsqrt(sums(centred * centred) * (1.0 / width) + 1e-06)
        xhat = centred * deviation
        scaled = norm_back[where, :] * gain[...]
        feature_grad[where, :] = (
            deviation
            * (scaled - sums(scaled) * (1.0 / width) - xhat * (sums(scaled * xhat) * (1.0 / width)))
        ).astype(BF16)

    over_rows(rows, 32, feature_chunk)
    token[...] = jnp.zeros_like(token)


def text_body(
    scale, text, weights_near, weights_far, unit_near, unit_far, before, text_grad, token, product,
):
    rows = text_grad.shape[0]
    scale = scale[0]
    product[...] = dot(weights_near[:rows, :], unit_near[...]) + dot(weights_far[:rows, :], unit_far[...])

    def text_chunk(where):
        values = product[where, :] * scale
        own = text[where, :].astype(F32)
        own_inverse = lax.rsqrt(sums(own * own) + 1e-06)
        direction = own * own_inverse
        text_grad[where, :] = (
            (values - direction * sums(direction * values)) * own_inverse
        ).astype(BF16)

    over_rows(rows, 32, text_chunk)
    token[...] = jnp.zeros_like(token)


def far_pair_sum_body(before, keep, come, gain_rows, come_gain_rows, two_on, three_on):
    for at, target in enumerate((two_on, three_on)):
        target[...] = (keep[2 + at].astype(F32) + come[at].astype(F32)).astype(BF16)
        count, full = target.shape
        target[count - BAND :, full - LANES :] = (
            gain_rows[...].astype(F32) + come_gain_rows[...].astype(F32)
        ).astype(BF16)


def near_pair_sum_body(before, keep, come, own, next_one):
    for at, target in enumerate((own, next_one)):
        target[...] = (keep[at].astype(F32) + come[at].astype(F32)).astype(BF16)


def far_sum_body(before, two_on, three_on, total):
    total[...] = two_on[...].astype(F32) + three_on[...].astype(F32)


def last_sum_body(far, own, next_one, two_on, three_on, total, ordered):
    parts = (own, next_one, two_on, three_on)
    total[...] = (own[...].astype(F32) + next_one[...].astype(F32) + far[...]).astype(BF16)
    count, full = total.shape
    z = lax.axis_index("rep") // 2
    for step, part in enumerate(parts):
        ordered[z ^ step] = part[count - BAND :, full - LANES :].astype(F32)
    value = ordered[0]
    for at in range(1, len(parts)):
        value = value + ordered[at]
    total[count - BAND :, full - LANES :] = value.astype(BF16)


def finish_body(members, *refs):
    packets, (proj_grad, gain_gradient, ordered) = refs[:members], refs[members:]
    count, full = packets[0].shape
    rows, width = proj_grad.shape
    rest = width // members - full
    per_band = full // rest
    for k in range(members):
        member = lax.axis_index("loop") ^ k
        proj_grad[:, pl.ds(pl.multiple_of(member * full, LANES), full)] = packets[k][:rows, :].astype(F32)
        ordered[member] = packets[k][rows:, :].astype(F32)
    tails = []
    for index in range(rows // BAND):
        at, lane = (index // per_band) * BAND, (index % per_band) * rest
        tails.append(
            jnp.concatenate([ordered[member][at : at + BAND, lane : lane + rest] for member in range(members)], axis=1)
        )
    proj_grad[:, members * full :] = jnp.concatenate(tails, axis=0)
    value = ordered[0][count - rows - BAND :, full - LANES :]
    for member in range(1, members):
        value = value + ordered[member][count - rows - BAND :, full - LANES :]
    for at in range(width // LANES):
        gain_gradient[at * LANES : (at + 1) * LANES] = value[at]


def local_four(features, text, proj, gain, scale, bias):
    members = lax.axis_size("loop")
    groups = lax.axis_size("rep")
    rows, width = features.shape[0], features.shape[2]
    near, every = 2 * rows, 4 * rows
    columns = width // members
    full = columns // LANES * LANES
    each = width // groups
    bands = -(-(each // BAND) // (full // (columns - full)))
    packet = (each + bands * BAND, full)


    f0, t0 = features[:, 0, :], text[:, 0, :]
    f2 = send(f0, "loop", lambda p: p ^ 2)
    f1 = send(f0, "loop", lambda p: p ^ 1)

    wide, half = ((near, width), BF16), ((rows, width), BF16)
    square, part, turned = ((near, near), BF16), ((near, columns), BF16), ((width, near), BF16)

    line, mine = ((1, near), F32), ((columns, near), BF16)
    kept = ((width, width), BF16)
    f0_kept, proj_kept, t0_kept, gain_row, normed_near, unit_near, factors, text_own, token = call(
        near_body,
        [half, kept, half, ((1, width), F32), wide, wide, ((near, LANES), F32), half, TOKEN],
        [((near, width), F32)],
        smem=2,
        hbm=3,
        limit=46,
        flops=2 * near * width * width,
        moved=8 * near * width,
    )(scale, bias, f0, proj, t0, f1, gain)

    t2 = send(text_own, "loop", lambda p: p ^ 2)
    t1 = send(text_own, "loop", lambda p: p ^ 1)
    head = rows // 6 * 5
    f3_head, f3_tail = call(split_body, [((head, width), BF16), ((rows - head, width), BF16)], moved=1000)(f2, token)
    f3_head = send(f3_head, "loop", lambda p: p ^ 1)
    f3_tail = send(f3_tail, "loop", lambda p: p ^ 1)

    (
        text_near, turned_near, flat_near, unit_turned_near, inverse_near, text_columns_near, weights_near, totals_near, proj_columns,
        token,
    ) = call(
        near_pairs_body,
        [wide, turned, turned, mine, line, part, square, line, ((width, columns), BF16), TOKEN],
        [((near, near), F32)],
        smem=2,
        flops=1000,
        moved=1000,
    )(scale, bias, normed_near, unit_near, factors, text_own, t1, proj_kept, token)

    back_kind = ((columns, near), F32)
    (
        turned_far, unit_far, flat_far, unit_turned_far, inverse_far, weights_far, totals_far, early_near, early_far,
        token,
    ) = call(
        far_body,
        [turned, wide, turned, mine, line, square, line, back_kind, back_kind, TOKEN],
        [wide, ((near, width), F32), ((near, near), F32), ((near, LANES), F32)],
        smem=2,
        flops=1000,
        moved=1000,
    )(
        scale, bias, f2, f3_head, f3_tail, proj_kept, gain_row, text_near, text_columns_near, weights_near,
    )

    text_grad, token = call(
        text_body,
        [half, TOKEN],
        [((rows, width), F32)],
        smem=1,
        flops=1000,
        moved=1000,
    )(scale, t0_kept, weights_near, weights_far, unit_near, unit_far, token)

    t2_after, token = lax.optimization_barrier((t2, token))
    t3 = send(t2_after, "loop", lambda p: p ^ 1)

    narrow = ((rows, every), BF16)
    weights_third, back_near, back_far, totals = call(
        third_body,
        [narrow, back_kind, back_kind, ((1, every), F32)],
        [((rows, columns), BF16), ((rows, every), F32)],
        smem=2,
        flops=2 * near * width * width,
        moved=8 * near * width,
    )(
        scale, bias, t2, flat_near, flat_far, totals_near, totals_far, early_near, early_far, token,
    )

    across_first, back, weights_fourth = call(
        functools.partial(far_packets_body, members),
        [((2,) + packet, BF16), ((columns, every), BF16), narrow],
        [((rows, columns), BF16), ((rows, every), F32)],
        smem=2,
        moved=1000,
    )(
        scale, bias, t3, flat_near, flat_far, totals, back_near, back_far, unit_turned_near, unit_turned_far,
        inverse_near, inverse_far, turned_near, turned_far,
    )
    come_first = send(across_first, "rep", lambda p: p ^ 1)
    across_later, keep, gain_rows, token = call(
        functools.partial(partial_body, members, groups),
        [((2,) + packet, BF16), ((4,) + packet, BF16), ((BAND, LANES), BF16), TOKEN],
        [((groups,) + packet, BF16)],
        moved=1000,
    )(back, turned_near, turned_far, proj_columns, gain_row)
    norm_back, token = call(
        image_body,
        [((rows, width), F32), TOKEN],
        [half, ((rows, width), F32)],
        smem=1,
        moved=1000,
    )(
        scale, proj_kept, text_near, t2, t3, weights_near, weights_third, weights_fourth,
        unit_near, factors, token,
    )

    across_later, token = lax.optimization_barrier((across_later, token))
    come_later = send(across_later, "rep", lambda p: p ^ 1)
    come_gain_rows = send(gain_rows, "rep", lambda p: p ^ 1)
    two_sum, three_sum = call(far_pair_sum_body, [(packet, BF16)] * 2, moved=1000)(
        token, keep, come_first, gain_rows, come_gain_rows
    )
    two_on = send(two_sum, "rep", lambda p: p ^ 4)
    three_on = send(three_sum, "rep", lambda p: p ^ 6)
    own_sum, next_one = call(near_pair_sum_body, [(packet, BF16)] * 2, moved=1000)(two_sum, keep, come_later)
    next_one = send(next_one, "rep", lambda p: p ^ 2)
    feature_grad, token = call(feature_body, [half, TOKEN], moved=12 * near * width)(
        f0_kept, gain_row, norm_back, own_sum
    )
    (far_sum,) = call(far_sum_body, [(packet, F32)], moved=1000)(token, two_on, three_on)
    (reduced,) = call(last_sum_body, [(packet, BF16)], [((4, BAND, LANES), F32)], moved=1000)(
        far_sum, own_sum, next_one, two_on, three_on
    )
    far_block = send(reduced, "loop", lambda p: p ^ 2)
    near_block = send(reduced, "loop", lambda p: p ^ 1)
    blocks = [reduced, near_block, far_block, send(far_block, "loop", lambda p: p ^ 1)]

    proj_grad, gain_gradient = call(
        functools.partial(finish_body, members),
        [((each, width), F32), ((width,), F32)],
        [((members, bands * BAND, full), F32)],
        moved=8 * each * width,
    )(*blocks)
    return feature_grad[:, None, :], text_grad[:, None, :], proj_grad, gain_gradient


def four_fits(mesh, rows_shape):
    members, groups = mesh.shape["loop"], mesh.shape["rep"]
    rows, width = rows_shape[0] // members, rows_shape[2]
    if members != 4 or groups != 8 or width % (members * groups) or width % LANES:
        return False
    columns, each = width // members, width // groups
    full = columns // LANES * LANES
    rest = columns - full
    if rest == 0 or full < LANES or full % rest or each % BAND or rows % 64 or width // LANES > BAND:
        return False
    chunks = each // BAND
    used = (chunks - 1) % (full // rest) + 1
    return used * rest <= full - LANES


def solution(mesh):
    def run(features, text, proj, gain, scale, bias):
        body = local_four if four_fits(mesh, features.shape) else local_any_size
        return jax.shard_map(
            body,
            mesh=mesh,
            in_specs=(P("loop", "rep", None), P("loop", "rep", None), P(), P(), P(), P()),
            out_specs=(P("loop", "rep", None), P("loop", "rep", None), P("rep", None), P()),
            check_vma=False,
        )(features, text, proj, gain, scale, bias)

    return run
```

```python
import functools

import jax
import jax.numpy as jnp
from jax import lax
from jax.experimental import pallas as pl
from jax.experimental.pallas import tpu as pltpu
from jax.sharding import PartitionSpec as P

F32 = jnp.float32
BF16 = jnp.bfloat16
LAST = (((1,), (1,)), ((), ()))
FIRST = (((0,), (0,)), ((), ()))


def dot(a, b, dims=(((1,), (0,)), ((), ()))):
    return lax.dot_general(a, b, dims, preferred_element_type=F32)


def unit_rows(values):
    inverse = lax.rsqrt(jnp.sum(values * values, axis=-1, keepdims=True) + 1e-06)
    return values * inverse, inverse


def standardize(rows):
    values = rows.astype(F32)
    centred = values - jnp.mean(values, axis=-1, keepdims=True)
    inverse = lax.rsqrt(jnp.mean(centred * centred, axis=-1, keepdims=True) + 1e-06)
    return centred * inverse, inverse


def send(value, axis, target):
    count = lax.axis_size(axis)
    return lax.ppermute(value, axis, [(p, target(p)) for p in range(count)])


def gather_group(value, count):
    mine = [value]
    for step in range(1, count // 2):
        mine.append(send(value, "loop", lambda p: (p + 2 * step) % count))
    mates = [send(block, "loop", lambda p: p ^ 1) for block in mine]
    return mine + mates


def local_any_size(features, text, proj, gain, scale, bias):
    n = lax.axis_size("loop")
    m = lax.axis_size("rep")
    me = lax.axis_index("loop")
    half = n // 2
    rows, width = features.shape[0], features.shape[2]
    columns = proj.shape[1] // n
    group_rows = rows * n
    logit_scale, logit_bias = scale[0], bias[0]

    own_features = features[:, 0, :]
    own_text = text[:, 0, :]
    text_blocks = gather_group(own_text, n)
    feature_blocks = gather_group(own_features, n)

    xhat, deviation = standardize(own_features)
    normed = (xhat * gain).astype(BF16)
    img_dir, img_inv = unit_rows(dot(normed, proj))
    img_unit = img_dir.astype(BF16)

    txt_dir, txt_inv = unit_rows(own_text.astype(F32))
    own_txt_unit = txt_dir.astype(BF16)
    txt_unit = jnp.concatenate(
        [own_txt_unit] + [unit_rows(block.astype(F32))[0].astype(BF16) for block in text_blocks[1:]]
    )
    row_ids = lax.broadcasted_iota(jnp.int32, (rows, group_rows), 0)
    column_ids = lax.broadcasted_iota(jnp.int32, (rows, group_rows), 1)
    diagonal = (row_ids == column_ids).astype(F32)

    def weights(left, right):
        logits = logit_scale * dot(left, right, LAST) + logit_bias
        return (jax.nn.sigmoid(logits) - diagonal).astype(BF16)

    img_back = logit_scale * dot(weights(img_unit, txt_unit), txt_unit)
    proj_back = (
        (img_back - img_dir * jnp.sum(img_dir * img_back, axis=-1, keepdims=True)) * img_inv
    ).astype(BF16)

    blocks = jnp.transpose(proj_back.reshape(rows, n, columns), (1, 0, 2))
    blocks = lax.all_to_all(blocks, "loop", 0, 0, tiled=True)
    back_columns = blocks.reshape(group_rows, columns)

    norm_back = dot(proj_back, proj, LAST)
    scaled = norm_back * gain
    feature_grad = (
        deviation
        * (
            scaled
            - jnp.mean(scaled, axis=-1, keepdims=True)
            - xhat * jnp.mean(scaled * xhat, axis=-1, keepdims=True)
        )
    ).astype(BF16)
    gain_term = jnp.sum(norm_back * xhat, axis=0) * (1.0 / group_rows)

    other_normed = [(standardize(block)[0] * gain).astype(BF16) for block in feature_blocks[1:]]
    relative = jnp.stack([normed] + other_normed)
    member = jnp.arange(n)
    same_core = (member % 2) == (me % 2)
    chips_back = ((me // 2 - member // 2) % half)
    position = jnp.where(same_core, chips_back, half + chips_back)
    group_normed = relative[position].reshape(group_rows, width)

    partial = (dot(group_normed, back_columns, FIRST) * (1.0 / group_rows)).astype(BF16)
    pieces = lax.all_to_all(partial.reshape(m, width // m, columns), "rep", 0, 0, tiled=True)
    reduced = jnp.sum(pieces.astype(F32), axis=0).astype(BF16)
    gains = lax.all_gather(gain_term, "rep")
    gain_sum = jnp.sum(gains, axis=0)
    proj_rows = lax.all_gather(reduced, "loop")
    proj_grad = jnp.transpose(proj_rows, (1, 0, 2)).reshape(width // m, n * columns).astype(F32)
    gain_gradient = jnp.sum(lax.all_gather(gain_sum, "loop"), axis=0)

    group_unit = jnp.concatenate(
        [img_unit] + [unit_rows(dot(block, proj))[0].astype(BF16) for block in other_normed]
    )
    text_weights = weights(own_txt_unit, group_unit)
    txt_back = logit_scale * dot(text_weights, group_unit)
    text_grad = (
        (txt_back - txt_dir * jnp.sum(txt_dir * txt_back, axis=-1, keepdims=True)) * txt_inv
    ).astype(BF16)
    return feature_grad[:, None, :], text_grad[:, None, :], proj_grad, gain_gradient


VMEM = pl.BlockSpec(memory_space=pltpu.VMEM)
SMEM = pl.BlockSpec(memory_space=pltpu.SMEM)
HBM = pl.BlockSpec(memory_space=pltpu.HBM)
LANES = 128
BAND = 16
TOKEN = ((8, LANES), F32)


def call(body, outs, scratch=(), smem=0, hbm=0, limit=24, flops=0, moved=0):
    def run(*operands):
        specs = [SMEM] * smem + [HBM] * hbm + [VMEM] * (len(operands) - smem - hbm)
        return pl.pallas_call(
            body,
            out_shape=[jax.ShapeDtypeStruct(shape, kind) for shape, kind in outs],
            in_specs=specs,
            out_specs=[VMEM] * len(outs),
            scratch_shapes=[pltpu.VMEM(shape, kind) for shape, kind in scratch]
            + [pltpu.SemaphoreType.DMA((hbm,))] * bool(hbm),
            compiler_params=pltpu.CompilerParams(vmem_limit_bytes=limit * 2**20),
            cost_estimate=pl.CostEstimate(flops=flops, bytes_accessed=moved, transcendentals=0),
        )(*operands)

    return run


def over_rows(count, step, body):
    def turn(index, _):
        body(pl.ds(pl.multiple_of(index * step, step), step))
        return 0

    lax.fori_loop(0, count // step, turn, 0, unroll=min(4, count // step))


def sums(values):
    return jnp.sum(values, axis=-1, keepdims=True)


def normalize_into(source, gain, target, at):
    rows, width = source.shape

    def chunk(where):
        values = source[where, :].astype(F32)
        centred = values - sums(values) * (1.0 / width)
        inverse = lax.rsqrt(sums(centred * centred) * (1.0 / width) + 1e-06)
        target[pl.ds(at + where.start, where.size), :] = (centred * inverse * gain[...]).astype(BF16)

    over_rows(rows, 32, chunk)


def unit_into(source, target, at, inverses=None):
    rows = source.shape[0]

    def chunk(where):
        values = source[where, :].astype(F32)
        inverse = lax.rsqrt(sums(values * values) + 1e-06)
        place = pl.ds(at + where.start, where.size)
        target[place, :] = (values * inverse).astype(BF16)
        if inverses is not None:
            inverses[place, :] = jnp.broadcast_to(inverse, (where.size, LANES))

    over_rows(rows, 32, chunk)


def weigh(dots, scale, bias, diagonal, weights):
    texts, images = dots.shape

    def chunk(index, total):
        where = pl.ds(pl.multiple_of(index * BAND, BAND), BAND)
        product = dots[where, :]
        weight = jnp.tanh((0.5 * scale) * product + 0.5 * bias)
        offset = 0.5
        if diagonal is not None:
            text = index * BAND + diagonal + lax.broadcasted_iota(jnp.int32, product.shape, 0)
            image = lax.broadcasted_iota(jnp.int32, product.shape, 1)
            offset = jnp.where(text == image, -0.5, 0.5)
        weight = (0.5 * weight + offset).astype(BF16)
        weights[where, :] = weight
        both = weight.astype(F32) * product
        return total + both[:8, :] + both[8:, :]

    total = lax.fori_loop(0, texts // BAND, chunk, jnp.zeros((8, images), F32), unroll=4)
    return jnp.sum(total, axis=0, keepdims=True)


def take_columns(source, target):
    members = source.shape[1] // target.shape[1]
    full = target.shape[1] // LANES * LANES
    rest = target.shape[1] - full
    target[:, :full] = source[:, pl.ds(pl.multiple_of(lax.axis_index("loop") * full, LANES), full)]
    for member in range(members):

        @pl.when(lax.axis_index("loop") == member)
        def _():
            target[:, full:] = source[:, members * full + member * rest : members * full + (member + 1) * rest]


def near_body(
    scale, bias, f0_far, proj_far, t0_far, f1, gain_line,
    f0, proj, t0, gain, normed, unit, factors, text_unit, token, projected, semaphores,
):
    rows = f0.shape[0]
    copies = [
        pltpu.make_async_copy(source, target, semaphores.at[at])
        for at, (source, target) in enumerate(((f0_far, f0), (proj_far, proj), (t0_far, t0)))
    ]
    for copy in copies:
        copy.start()
    for at in range(0, gain.shape[1], LANES):
        gain[:, at : at + LANES] = gain_line[at : at + LANES].reshape(1, LANES)
    normalize_into(f1, gain, normed, rows)
    copies[0].wait()
    normalize_into(f0, gain, normed, 0)
    copies[1].wait()
    projected[...] = dot(normed[...], proj[...])
    copies[2].wait()
    unit_into(t0, text_unit, 0)
    unit_into(projected, unit, 0, factors)
    token[...] = jnp.zeros_like(token)


def near_pairs_body(
    scale, bias, normed, unit, factors, text_own, t1, proj, before,
    text_unit, normed_turned, turned, unit_turned, inverse, text_columns, weights, totals, proj_columns, token, dots,
):
    token[...] = jnp.zeros_like(token)
    rows = t1.shape[0]
    text_unit[:rows, :] = text_own[...]
    text_unit[rows:, :] = t1[...]
    dots[...] = dot(text_unit[...], unit[...], LAST)
    totals[...] = weigh(dots, scale[0], bias[0], 0, weights)
    take_columns(text_unit, text_columns)
    take_columns(proj, proj_columns)
    turn_own(unit, factors, turned, unit_turned, inverse)
    normed_turned[...] = normed[...].T


def turn_own(unit, factors, turned, unit_turned, inverse):
    columns = unit_turned.shape[0]
    full = columns // LANES * LANES
    rest = columns - full
    turned[...] = unit[...].T
    unit_turned[:full, :] = turned[pl.ds(pl.multiple_of(lax.axis_index("loop") * full, LANES), full), :]
    begin = turned.shape[0] // columns * full
    unit_turned[full:, :] = turned[pl.ds(pl.multiple_of(begin + lax.axis_index("loop") * rest, BAND), rest), :]
    inverse[...] = factors[...].T[:1, :]


def split_body(f2, before, head, tail):
    head[...] = f2[: head.shape[0], :]
    tail[...] = f2[head.shape[0] :, :]


def far_body(
    scale, bias, f2, f3_head, f3_tail, proj, gain, text_near, text_columns, weights_near,
    normed_turned, unit, turned, unit_turned, inverse, weights, totals, early_near, early_far, token,
    normed, projected, dots, factors,
):
    rows = f2.shape[0]
    normalize_into(f2, gain, normed, 0)
    normalize_into(f3_head, gain, normed, rows)
    normalize_into(f3_tail, gain, normed, rows + f3_head.shape[0])
    projected[...] = dot(normed[...], proj[...])
    unit_into(projected, unit, 0, factors)
    dots[...] = dot(text_near[...], unit[...], LAST)
    totals[...] = weigh(dots, scale[0], bias[0], None, weights)
    turn_own(unit, factors, turned, unit_turned, inverse)
    normed_turned[...] = normed[...].T
    early_near[...] = dot(text_columns[...], weights_near[...], FIRST)
    early_far[...] = dot(text_columns[...], weights[...], FIRST)
    token[...] = jnp.zeros_like(token)


def third_body(
    scale, bias, text_unit, flat_near, flat_far, totals_near, totals_far, early_near, early_far,
    before, weights, back_near, back_far, totals,
    text_columns, dots,
):
    rows = text_unit.shape[0]
    near = 2 * rows
    take_columns(text_unit, text_columns)
    dots[:, :near] = dot(text_unit[...], flat_near[...])
    dots[:, near:] = dot(text_unit[...], flat_far[...])
    added = weigh(dots, scale[0], bias[0], near, weights)
    totals[:, :near] = totals_near[...] + added[:, :near]
    totals[:, near:] = totals_far[...] + added[:, near:]
    added = dot(text_columns[...], weights[...], FIRST)
    back_near[...] = early_near[...] + added[:, :near]
    back_far[...] = early_far[...] + added[:, near:]


def pack_into(target, block, full):
    rows, columns = block.shape
    rest = columns - full
    target[:rows, :] = block[:, :full].astype(BF16)
    per_band = full // rest
    tail = block[:, full:]
    chunks = [tail[at : at + BAND, :] for at in range(0, rows, BAND)]
    for band in range(0, len(chunks), per_band):
        part = chunks[band : band + per_band]
        if len(part) < per_band:
            part.append(jnp.zeros((BAND, full - rest * len(part)), block.dtype))
        at = rows + (band // per_band) * BAND
        target[at : at + BAND, :] = jnp.concatenate(part, axis=1).astype(BF16)


def partial_body(
    members, groups, scale, bias, text_unit, flat_near, flat_far, totals, back_near, back_far, unit_turned_near,
    unit_turned_far, inverse_near, inverse_far, turned_near, turned_far, proj_columns, gain,
    across_three, across_two, across_later, keep, weights, text_columns, dots, packed,
):
    rows = text_unit.shape[0]
    near = 2 * rows
    every = members * rows
    width = text_unit.shape[1]
    columns = width // members
    count, full = packed.shape[1:]
    scale, bias = scale[0], bias[0]
    take_columns(text_unit, text_columns)
    dots[:, :near] = dot(text_unit[...], flat_near[...])
    dots[:, near:] = dot(text_unit[...], flat_far[...])
    total = totals[...] + weigh(dots, scale, bias, near + rows, weights)
    added = dot(text_columns[...], weights[...], FIRST)
    back = []
    for where, earlier, unit_turned, inverse in (
        (slice(0, near), back_near, unit_turned_near, inverse_near),
        (slice(near, every), back_far, unit_turned_far, inverse_far),
    ):
        whole = earlier[...] + added[:, where]
        part = (whole - unit_turned[...].astype(F32) * total[:, where]) * (inverse[...] * scale)
        back.append(part.astype(BF16))
    turned = jnp.concatenate([turned_near[...], turned_far[...]], axis=1)
    product = dot(turned, jnp.concatenate(back, axis=1), LAST)
    each = width // groups
    product = product * (1.0 / every)
    for group in range(groups):
        pack_into(packed.at[group], product[group * each : (group + 1) * each, :], full)

    terms = product * proj_columns[...].astype(F32)
    folded = jnp.concatenate([terms[:, full:], jnp.zeros((width, full + LANES - columns), F32)], axis=1)
    for at in range(0, full, LANES):
        folded = folded + terms[:, at : at + LANES]
    high = folded.astype(BF16)
    low = (folded - high.astype(F32)).astype(BF16)
    ones = jnp.ones((BAND, 2 * LANES), BF16)
    gain_row = dot(ones, jnp.concatenate([high, low], axis=1), LAST)[:1, :] / gain[...]
    pieces = [gain_row[:, at : at + LANES] for at in range(0, width, LANES)]
    pieces.append(jnp.zeros((BAND - len(pieces), LANES), F32))
    gain_tile = jnp.concatenate(pieces, axis=0).astype(BF16)
    for group in range(groups):
        packed[group, count - BAND :, full - LANES :] = gain_tile

    own = lax.axis_index("rep")
    across_three[...] = packed[own ^ 7]
    across_two[...] = packed[own ^ 5]
    for at in range(2):
        across_later[at] = packed[own ^ 1 ^ (2 * at)]
    for at in range(4):
        keep[at] = packed[own ^ (2 * at)]


def image_body(
    scale, proj, text_near, text_third, text_fourth, weights_near, weights_third, weights_fourth,
    unit, factors, norm_back, token, back, product,
):
    rows = back.shape[0]
    scale = scale[0]
    product[...] = (
        dot(weights_near[:, :rows], text_near[...], FIRST)
        + dot(weights_third[:, :rows], text_third[...], FIRST)
        + dot(weights_fourth[:, :rows], text_fourth[...], FIRST)
    )

    def image_chunk(where):
        values = product[where, :] * scale
        direction = unit[where, :].astype(F32)
        back[where, :] = (
            (values - direction * sums(direction * values)) * factors[where, :1]
        ).astype(BF16)

    over_rows(rows, 32, image_chunk)
    norm_back[...] = dot(back[...], proj[...], LAST)
    token[...] = jnp.zeros_like(token)


def feature_body(features, gain, norm_back, before, feature_grad, token):
    rows, width = features.shape

    def feature_chunk(where):
        values = features[where, :].astype(F32)
        centred = values - sums(values) * (1.0 / width)
        deviation = lax.rsqrt(sums(centred * centred) * (1.0 / width) + 1e-06)
        xhat = centred * deviation
        scaled = norm_back[where, :] * gain[...]
        feature_grad[where, :] = (
            deviation
            * (scaled - sums(scaled) * (1.0 / width) - xhat * (sums(scaled * xhat) * (1.0 / width)))
        ).astype(BF16)

    over_rows(rows, 32, feature_chunk)
    token[...] = jnp.zeros_like(token)


def text_body(
    scale, text, weights_near, weights_far, unit_near, unit_far, before, text_grad, token, product,
):
    rows = text_grad.shape[0]
    scale = scale[0]
    product[...] = dot(weights_near[:rows, :], unit_near[...]) + dot(weights_far[:rows, :], unit_far[...])

    def text_chunk(where):
        values = product[where, :] * scale
        own = text[where, :].astype(F32)
        own_inverse = lax.rsqrt(sums(own * own) + 1e-06)
        direction = own * own_inverse
        text_grad[where, :] = (
            (values - direction * sums(direction * values)) * own_inverse
        ).astype(BF16)

    over_rows(rows, 32, text_chunk)
    token[...] = jnp.zeros_like(token)


def one_sum_body(place, before, keep, come, total):
    total[...] = (keep[place].astype(F32) + come[...].astype(F32)).astype(BF16)


def pair_sum_body(before, keep, come, own, next_one):
    for at, target in enumerate((own, next_one)):
        target[...] = (keep[at].astype(F32) + come[at].astype(F32)).astype(BF16)


def far_sum_body(before, two_on, three_on, total):
    total[...] = two_on[...].astype(F32) + three_on[...].astype(F32)


def last_sum_body(far, own, next_one, two_on, three_on, total, ordered):
    parts = (own, next_one, two_on, three_on)
    total[...] = (own[...].astype(F32) + next_one[...].astype(F32) + far[...]).astype(BF16)
    count, full = total.shape
    z = lax.axis_index("rep") // 2
    for step, part in enumerate(parts):
        ordered[z ^ step] = part[count - BAND :, full - LANES :].astype(F32)
    value = ordered[0]
    for at in range(1, len(parts)):
        value = value + ordered[at]
    total[count - BAND :, full - LANES :] = value.astype(BF16)


def finish_body(members, *refs):
    packets, (proj_grad, gain_gradient, ordered) = refs[:members], refs[members:]
    count, full = packets[0].shape
    rows, width = proj_grad.shape
    rest = width // members - full
    per_band = full // rest
    for k in range(members):
        member = lax.axis_index("loop") ^ k
        proj_grad[:, pl.ds(pl.multiple_of(member * full, LANES), full)] = packets[k][:rows, :].astype(F32)
        ordered[member] = packets[k][rows:, :].astype(F32)
    tails = []
    for index in range(rows // BAND):
        at, lane = (index // per_band) * BAND, (index % per_band) * rest
        tails.append(
            jnp.concatenate([ordered[member][at : at + BAND, lane : lane + rest] for member in range(members)], axis=1)
        )
    proj_grad[:, members * full :] = jnp.concatenate(tails, axis=0)
    value = ordered[0][count - rows - BAND :, full - LANES :]
    for member in range(1, members):
        value = value + ordered[member][count - rows - BAND :, full - LANES :]
    for at in range(width // LANES):
        gain_gradient[at * LANES : (at + 1) * LANES] = value[at]


def local_four(features, text, proj, gain, scale, bias):
    members = lax.axis_size("loop")
    groups = lax.axis_size("rep")
    rows, width = features.shape[0], features.shape[2]
    near, every = 2 * rows, 4 * rows
    columns = width // members
    full = columns // LANES * LANES
    each = width // groups
    bands = -(-(each // BAND) // (full // (columns - full)))
    packet = (each + bands * BAND, full)


    f0, t0 = features[:, 0, :], text[:, 0, :]
    f2 = send(f0, "loop", lambda p: p ^ 2)
    f1 = send(f0, "loop", lambda p: p ^ 1)

    wide, half = ((near, width), BF16), ((rows, width), BF16)
    square, part, turned = ((near, near), BF16), ((near, columns), BF16), ((width, near), BF16)

    line, mine = ((1, near), F32), ((columns, near), BF16)
    kept = ((width, width), BF16)
    f0_kept, proj_kept, t0_kept, gain_row, normed_near, unit_near, factors, text_own, token = call(
        near_body,
        [half, kept, half, ((1, width), F32), wide, wide, ((near, LANES), F32), half, TOKEN],
        [((near, width), F32)],
        smem=2,
        hbm=3,
        limit=46,
        flops=2 * near * width * width,
        moved=8 * near * width,
    )(scale, bias, f0, proj, t0, f1, gain)

    t2 = send(text_own, "loop", lambda p: p ^ 2)
    t1 = send(text_own, "loop", lambda p: p ^ 1)
    head = rows // 6 * 5
    f3_head, f3_tail = call(split_body, [((head, width), BF16), ((rows - head, width), BF16)], moved=1000)(f2, token)
    f3_head = send(f3_head, "loop", lambda p: p ^ 1)
    f3_tail = send(f3_tail, "loop", lambda p: p ^ 1)

    (
        text_near, turned_near, flat_near, unit_turned_near, inverse_near, text_columns_near, weights_near, totals_near, proj_columns,
        token,
    ) = call(
        near_pairs_body,
        [wide, turned, turned, mine, line, part, square, line, ((width, columns), BF16), TOKEN],
        [((near, near), F32)],
        smem=2,
        flops=1000,
        moved=1000,
    )(scale, bias, normed_near, unit_near, factors, text_own, t1, proj_kept, token)

    back_kind = ((columns, near), F32)
    (
        turned_far, unit_far, flat_far, unit_turned_far, inverse_far, weights_far, totals_far, early_near, early_far,
        token,
    ) = call(
        far_body,
        [turned, wide, turned, mine, line, square, line, back_kind, back_kind, TOKEN],
        [wide, ((near, width), F32), ((near, near), F32), ((near, LANES), F32)],
        smem=2,
        flops=1000,
        moved=1000,
    )(
        scale, bias, f2, f3_head, f3_tail, proj_kept, gain_row, text_near, text_columns_near, weights_near,
    )

    text_grad, token = call(
        text_body,
        [half, TOKEN],
        [((rows, width), F32)],
        smem=1,
        flops=1000,
        moved=1000,
    )(scale, t0_kept, weights_near, weights_far, unit_near, unit_far, token)

    t2_after, token = lax.optimization_barrier((t2, token))
    t3 = send(t2_after, "loop", lambda p: p ^ 1)

    narrow = ((rows, every), BF16)
    weights_third, back_near, back_far, totals = call(
        third_body,
        [narrow, back_kind, back_kind, ((1, every), F32)],
        [((rows, columns), BF16), ((rows, every), F32)],
        smem=2,
        flops=2 * near * width * width,
        moved=8 * near * width,
    )(
        scale, bias, t2, flat_near, flat_far, totals_near, totals_far, early_near, early_far, token,
    )

    outs = call(
        functools.partial(partial_body, members, groups),
        [(packet, BF16)] * 2 + [((2,) + packet, BF16), ((4,) + packet, BF16), narrow],
        [((rows, columns), BF16), ((rows, every), F32), ((groups,) + packet, BF16)],
        smem=2,
        flops=4 * near * width * width,
        moved=16 * near * width,
    )(
        scale, bias, t3, flat_near, flat_far, totals, back_near, back_far, unit_turned_near, unit_turned_far,
        inverse_near, inverse_far, turned_near, turned_far, proj_columns, gain_row,
    )
    across_three, across_two, across_later, keep, weights_fourth = outs
    come_three = send(across_three, "rep", lambda p: p ^ 1)
    come_two = send(across_two, "rep", lambda p: p ^ 1)
    norm_back, token = call(
        image_body,
        [((rows, width), F32), TOKEN],
        [half, ((rows, width), F32)],
        smem=1,
        flops=1000,
        moved=1000,
    )(
        scale, proj_kept, text_near, t2, t3, weights_near, weights_third, weights_fourth,
        unit_near, factors,
    )

    across_later, token = lax.optimization_barrier((across_later, token))
    come_later = send(across_later, "rep", lambda p: p ^ 1)
    (three_sum,) = call(functools.partial(one_sum_body, 3), [(packet, BF16)], flops=1000, moved=1000)(
        token, keep, come_three
    )
    three_on = send(three_sum, "rep", lambda p: p ^ 6)
    (two_sum,) = call(functools.partial(one_sum_body, 2), [(packet, BF16)], flops=3000000000, moved=1000)(
        three_sum, keep, come_two
    )
    two_on = send(two_sum, "rep", lambda p: p ^ 4)
    own_sum, next_one = call(pair_sum_body, [(packet, BF16)] * 2, moved=1000)(two_sum, keep, come_later)
    next_one = send(next_one, "rep", lambda p: p ^ 2)
    feature_grad, token = call(feature_body, [half, TOKEN], moved=12 * near * width)(
        f0_kept, gain_row, norm_back, own_sum
    )
    (far_sum,) = call(far_sum_body, [(packet, F32)], moved=1000)(token, two_on, three_on)
    (reduced,) = call(last_sum_body, [(packet, BF16)], [((4, BAND, LANES), F32)], moved=1000)(
        far_sum, own_sum, next_one, two_on, three_on
    )
    far_block = send(reduced, "loop", lambda p: p ^ 2)
    near_block = send(reduced, "loop", lambda p: p ^ 1)
    blocks = [reduced, near_block, far_block, send(far_block, "loop", lambda p: p ^ 1)]

    proj_grad, gain_gradient = call(
        functools.partial(finish_body, members),
        [((each, width), F32), ((width,), F32)],
        [((members, bands * BAND, full), F32)],
        moved=8 * each * width,
    )(*blocks)
    return feature_grad[:, None, :], text_grad[:, None, :], proj_grad, gain_gradient


def four_fits(mesh, rows_shape):
    members, groups = mesh.shape["loop"], mesh.shape["rep"]
    rows, width = rows_shape[0] // members, rows_shape[2]
    if members != 4 or groups != 8 or width % (members * groups) or width % LANES:
        return False
    columns, each = width // members, width // groups
    full = columns // LANES * LANES
    rest = columns - full
    if rest == 0 or full < LANES or full % rest or each % BAND or rows % 64 or width // LANES > BAND:
        return False
    chunks = each // BAND
    used = (chunks - 1) % (full // rest) + 1
    return used * rest <= full - LANES


def solution(mesh):
    def run(features, text, proj, gain, scale, bias):
        body = local_four if four_fits(mesh, features.shape) else local_any_size
        return jax.shard_map(
            body,
            mesh=mesh,
            in_specs=(P("loop", "rep", None), P("loop", "rep", None), P(), P(), P(), P()),
            out_specs=(P("loop", "rep", None), P("loop", "rep", None), P("rep", None), P()),
            check_vma=False,
        )(features, text, proj, gain, scale, bias)

    return run
```

```python
import functools

import jax
import jax.numpy as jnp
from jax import lax
from jax.experimental import pallas as pl
from jax.experimental.pallas import tpu as pltpu
from jax.sharding import PartitionSpec as P

F32 = jnp.float32
BF16 = jnp.bfloat16
LAST = (((1,), (1,)), ((), ()))
FIRST = (((0,), (0,)), ((), ()))


def dot(a, b, dims=(((1,), (0,)), ((), ()))):
    return lax.dot_general(a, b, dims, preferred_element_type=F32)


def unit_rows(values):
    inverse = lax.rsqrt(jnp.sum(values * values, axis=-1, keepdims=True) + 1e-06)
    return values * inverse, inverse


def standardize(rows):
    values = rows.astype(F32)
    centred = values - jnp.mean(values, axis=-1, keepdims=True)
    inverse = lax.rsqrt(jnp.mean(centred * centred, axis=-1, keepdims=True) + 1e-06)
    return centred * inverse, inverse


def send(value, axis, target):
    count = lax.axis_size(axis)
    return lax.ppermute(value, axis, [(p, target(p)) for p in range(count)])


def gather_group(value, count):
    mine = [value]
    for step in range(1, count // 2):
        mine.append(send(value, "loop", lambda p: (p + 2 * step) % count))
    mates = [send(block, "loop", lambda p: p ^ 1) for block in mine]
    return mine + mates


def local_any_size(features, text, proj, gain, scale, bias):
    n = lax.axis_size("loop")
    m = lax.axis_size("rep")
    me = lax.axis_index("loop")
    half = n // 2
    rows, width = features.shape[0], features.shape[2]
    columns = proj.shape[1] // n
    group_rows = rows * n
    logit_scale, logit_bias = scale[0], bias[0]

    own_features = features[:, 0, :]
    own_text = text[:, 0, :]
    text_blocks = gather_group(own_text, n)
    feature_blocks = gather_group(own_features, n)

    xhat, deviation = standardize(own_features)
    normed = (xhat * gain).astype(BF16)
    img_dir, img_inv = unit_rows(dot(normed, proj))
    img_unit = img_dir.astype(BF16)

    txt_dir, txt_inv = unit_rows(own_text.astype(F32))
    own_txt_unit = txt_dir.astype(BF16)
    txt_unit = jnp.concatenate(
        [own_txt_unit] + [unit_rows(block.astype(F32))[0].astype(BF16) for block in text_blocks[1:]]
    )
    row_ids = lax.broadcasted_iota(jnp.int32, (rows, group_rows), 0)
    column_ids = lax.broadcasted_iota(jnp.int32, (rows, group_rows), 1)
    diagonal = (row_ids == column_ids).astype(F32)

    def weights(left, right):
        logits = logit_scale * dot(left, right, LAST) + logit_bias
        return (jax.nn.sigmoid(logits) - diagonal).astype(BF16)

    img_back = logit_scale * dot(weights(img_unit, txt_unit), txt_unit)
    proj_back = (
        (img_back - img_dir * jnp.sum(img_dir * img_back, axis=-1, keepdims=True)) * img_inv
    ).astype(BF16)

    blocks = jnp.transpose(proj_back.reshape(rows, n, columns), (1, 0, 2))
    blocks = lax.all_to_all(blocks, "loop", 0, 0, tiled=True)
    back_columns = blocks.reshape(group_rows, columns)

    norm_back = dot(proj_back, proj, LAST)
    scaled = norm_back * gain
    feature_grad = (
        deviation
        * (
            scaled
            - jnp.mean(scaled, axis=-1, keepdims=True)
            - xhat * jnp.mean(scaled * xhat, axis=-1, keepdims=True)
        )
    ).astype(BF16)
    gain_term = jnp.sum(norm_back * xhat, axis=0) * (1.0 / group_rows)

    other_normed = [(standardize(block)[0] * gain).astype(BF16) for block in feature_blocks[1:]]
    relative = jnp.stack([normed] + other_normed)
    member = jnp.arange(n)
    same_core = (member % 2) == (me % 2)
    chips_back = ((me // 2 - member // 2) % half)
    position = jnp.where(same_core, chips_back, half + chips_back)
    group_normed = relative[position].reshape(group_rows, width)

    partial = (dot(group_normed, back_columns, FIRST) * (1.0 / group_rows)).astype(BF16)
    pieces = lax.all_to_all(partial.reshape(m, width // m, columns), "rep", 0, 0, tiled=True)
    reduced = jnp.sum(pieces.astype(F32), axis=0).astype(BF16)
    gains = lax.all_gather(gain_term, "rep")
    gain_sum = jnp.sum(gains, axis=0)
    proj_rows = lax.all_gather(reduced, "loop")
    proj_grad = jnp.transpose(proj_rows, (1, 0, 2)).reshape(width // m, n * columns).astype(F32)
    gain_gradient = jnp.sum(lax.all_gather(gain_sum, "loop"), axis=0)

    group_unit = jnp.concatenate(
        [img_unit] + [unit_rows(dot(block, proj))[0].astype(BF16) for block in other_normed]
    )
    text_weights = weights(own_txt_unit, group_unit)
    txt_back = logit_scale * dot(text_weights, group_unit)
    text_grad = (
        (txt_back - txt_dir * jnp.sum(txt_dir * txt_back, axis=-1, keepdims=True)) * txt_inv
    ).astype(BF16)
    return feature_grad[:, None, :], text_grad[:, None, :], proj_grad, gain_gradient


VMEM = pl.BlockSpec(memory_space=pltpu.VMEM)
SMEM = pl.BlockSpec(memory_space=pltpu.SMEM)
HBM = pl.BlockSpec(memory_space=pltpu.HBM)
LANES = 128
BAND = 16
TOKEN = ((8, LANES), F32)


def call(body, outs, scratch=(), smem=0, hbm=0, limit=24, flops=0, moved=0):
    def run(*operands):
        specs = [SMEM] * smem + [HBM] * hbm + [VMEM] * (len(operands) - smem - hbm)
        return pl.pallas_call(
            body,
            out_shape=[jax.ShapeDtypeStruct(shape, kind) for shape, kind in outs],
            in_specs=specs,
            out_specs=[VMEM] * len(outs),
            scratch_shapes=[pltpu.VMEM(shape, kind) for shape, kind in scratch]
            + [pltpu.SemaphoreType.DMA((hbm,))] * bool(hbm),
            compiler_params=pltpu.CompilerParams(vmem_limit_bytes=limit * 2**20),
            cost_estimate=pl.CostEstimate(flops=flops, bytes_accessed=moved, transcendentals=0),
        )(*operands)

    return run


def over_rows(count, step, body):
    def turn(index, _):
        body(pl.ds(pl.multiple_of(index * step, step), step))
        return 0

    lax.fori_loop(0, count // step, turn, 0, unroll=min(4, count // step))


def sums(values):
    return jnp.sum(values, axis=-1, keepdims=True)


def normalize_into(source, gain, target, at):
    rows, width = source.shape

    def chunk(where):
        values = source[where, :].astype(F32)
        centred = values - sums(values) * (1.0 / width)
        inverse = lax.rsqrt(sums(centred * centred) * (1.0 / width) + 1e-06)
        target[pl.ds(at + where.start, where.size), :] = (centred * inverse * gain[...]).astype(BF16)

    over_rows(rows, 32, chunk)


def unit_into(source, target, at, inverses=None):
    rows = source.shape[0]

    def chunk(where):
        values = source[where, :].astype(F32)
        inverse = lax.rsqrt(sums(values * values) + 1e-06)
        place = pl.ds(at + where.start, where.size)
        target[place, :] = (values * inverse).astype(BF16)
        if inverses is not None:
            inverses[place, :] = jnp.broadcast_to(inverse, (where.size, LANES))

    over_rows(rows, 32, chunk)


def weigh(dots, scale, bias, diagonal, weights):
    texts, images = dots.shape

    def chunk(index, total):
        where = pl.ds(pl.multiple_of(index * BAND, BAND), BAND)
        product = dots[where, :]
        weight = jnp.tanh((0.5 * scale) * product + 0.5 * bias)
        offset = 0.5
        if diagonal is not None:
            text = index * BAND + diagonal + lax.broadcasted_iota(jnp.int32, product.shape, 0)
            image = lax.broadcasted_iota(jnp.int32, product.shape, 1)
            offset = jnp.where(text == image, -0.5, 0.5)
        weight = (0.5 * weight + offset).astype(BF16)
        weights[where, :] = weight
        both = weight.astype(F32) * product
        return total + both[:8, :] + both[8:, :]

    total = lax.fori_loop(0, texts // BAND, chunk, jnp.zeros((8, images), F32), unroll=4)
    return jnp.sum(total, axis=0, keepdims=True)


def take_columns(source, target):
    members = source.shape[1] // target.shape[1]
    full = target.shape[1] // LANES * LANES
    rest = target.shape[1] - full
    target[:, :full] = source[:, pl.ds(pl.multiple_of(lax.axis_index("loop") * full, LANES), full)]
    for member in range(members):

        @pl.when(lax.axis_index("loop") == member)
        def _():
            target[:, full:] = source[:, members * full + member * rest : members * full + (member + 1) * rest]


def near_body(
    scale, bias, f0_far, proj_far, t0_far, f1, gain_line,
    f0, proj, t0, gain, normed, unit, factors, text_unit, token, projected, semaphores,
):
    rows = f0.shape[0]
    copies = [
        pltpu.make_async_copy(source, target, semaphores.at[at])
        for at, (source, target) in enumerate(((f0_far, f0), (proj_far, proj), (t0_far, t0)))
    ]
    for copy in copies:
        copy.start()
    for at in range(0, gain.shape[1], LANES):
        gain[:, at : at + LANES] = gain_line[at : at + LANES].reshape(1, LANES)
    normalize_into(f1, gain, normed, rows)
    copies[0].wait()
    normalize_into(f0, gain, normed, 0)
    copies[1].wait()
    projected[...] = dot(normed[...], proj[...])
    copies[2].wait()
    unit_into(t0, text_unit, 0)
    unit_into(projected, unit, 0, factors)
    token[...] = jnp.zeros_like(token)


def near_pairs_body(
    scale, bias, normed, unit, factors, text_own, t1, proj, before,
    text_unit, normed_turned, turned, unit_turned, inverse, text_columns, weights, totals, proj_columns, token, dots,
):
    token[...] = jnp.zeros_like(token)
    rows = t1.shape[0]
    text_unit[:rows, :] = text_own[...]
    text_unit[rows:, :] = t1[...]
    dots[...] = dot(text_unit[...], unit[...], LAST)
    totals[...] = weigh(dots, scale[0], bias[0], 0, weights)
    take_columns(text_unit, text_columns)
    take_columns(proj, proj_columns)
    turn_own(unit, factors, turned, unit_turned, inverse)
    normed_turned[...] = normed[...].T


def turn_own(unit, factors, turned, unit_turned, inverse):
    columns = unit_turned.shape[0]
    full = columns // LANES * LANES
    rest = columns - full
    turned[...] = unit[...].T
    unit_turned[:full, :] = turned[pl.ds(pl.multiple_of(lax.axis_index("loop") * full, LANES), full), :]
    begin = turned.shape[0] // columns * full
    unit_turned[full:, :] = turned[pl.ds(pl.multiple_of(begin + lax.axis_index("loop") * rest, BAND), rest), :]
    inverse[...] = factors[...].T[:1, :]


def split_body(f2, before, head, tail):
    head[...] = f2[: head.shape[0], :]
    tail[...] = f2[head.shape[0] :, :]


def far_body(
    scale, bias, f2, f3_head, f3_tail, proj, gain, text_near, text_columns, weights_near,
    normed_turned, unit, turned, unit_turned, inverse, weights, totals, early_near, early_far, token,
    normed, projected, dots, factors,
):
    rows = f2.shape[0]
    normalize_into(f2, gain, normed, 0)
    normalize_into(f3_head, gain, normed, rows)
    normalize_into(f3_tail, gain, normed, rows + f3_head.shape[0])
    projected[...] = dot(normed[...], proj[...])
    unit_into(projected, unit, 0, factors)
    dots[...] = dot(text_near[...], unit[...], LAST)
    totals[...] = weigh(dots, scale[0], bias[0], None, weights)
    turn_own(unit, factors, turned, unit_turned, inverse)
    normed_turned[...] = normed[...].T
    early_near[...] = dot(text_columns[...], weights_near[...], FIRST)
    early_far[...] = dot(text_columns[...], weights[...], FIRST)
    token[...] = jnp.zeros_like(token)


def third_body(
    scale, bias, text_unit, flat_near, flat_far, totals_near, totals_far, early_near, early_far,
    before, weights, back_near, back_far, totals,
    text_columns, dots,
):
    rows = text_unit.shape[0]
    near = 2 * rows
    take_columns(text_unit, text_columns)
    dots[:, :near] = dot(text_unit[...], flat_near[...])
    dots[:, near:] = dot(text_unit[...], flat_far[...])
    added = weigh(dots, scale[0], bias[0], near, weights)
    totals[:, :near] = totals_near[...] + added[:, :near]
    totals[:, near:] = totals_far[...] + added[:, near:]
    added = dot(text_columns[...], weights[...], FIRST)
    back_near[...] = early_near[...] + added[:, :near]
    back_far[...] = early_far[...] + added[:, near:]


def pack_into(target, block, full):
    rows, columns = block.shape
    rest = columns - full
    target[:rows, :] = block[:, :full].astype(BF16)
    per_band = full // rest
    tail = block[:, full:]
    chunks = [tail[at : at + BAND, :] for at in range(0, rows, BAND)]
    for band in range(0, len(chunks), per_band):
        part = chunks[band : band + per_band]
        if len(part) < per_band:
            part.append(jnp.zeros((BAND, full - rest * len(part)), block.dtype))
        at = rows + (band // per_band) * BAND
        target[at : at + BAND, :] = jnp.concatenate(part, axis=1).astype(BF16)


def partial_body(
    members, groups, scale, bias, text_unit, flat_near, flat_far, totals, back_near, back_far, unit_turned_near,
    unit_turned_far, inverse_near, inverse_far, turned_near, turned_far, proj_columns, gain,
    across_three, across_two, across_next, across_own, keep, weights, text_columns, dots, packed,
):
    rows = text_unit.shape[0]
    near = 2 * rows
    every = members * rows
    width = text_unit.shape[1]
    columns = width // members
    count, full = packed.shape[1:]
    scale, bias = scale[0], bias[0]
    take_columns(text_unit, text_columns)
    dots[:, :near] = dot(text_unit[...], flat_near[...])
    dots[:, near:] = dot(text_unit[...], flat_far[...])
    total = totals[...] + weigh(dots, scale, bias, near + rows, weights)
    added = dot(text_columns[...], weights[...], FIRST)
    back = []
    for where, earlier, unit_turned, inverse in (
        (slice(0, near), back_near, unit_turned_near, inverse_near),
        (slice(near, every), back_far, unit_turned_far, inverse_far),
    ):
        whole = earlier[...] + added[:, where]
        part = (whole - unit_turned[...].astype(F32) * total[:, where]) * (inverse[...] * scale)
        back.append(part.astype(BF16))
    turned = jnp.concatenate([turned_near[...], turned_far[...]], axis=1)
    product = dot(turned, jnp.concatenate(back, axis=1), LAST)
    each = width // groups
    product = product * (1.0 / every)
    for group in range(groups):
        pack_into(packed.at[group], product[group * each : (group + 1) * each, :], full)

    terms = product * proj_columns[...].astype(F32)
    folded = jnp.concatenate([terms[:, full:], jnp.zeros((width, full + LANES - columns), F32)], axis=1)
    for at in range(0, full, LANES):
        folded = folded + terms[:, at : at + LANES]
    high = folded.astype(BF16)
    low = (folded - high.astype(F32)).astype(BF16)
    ones = jnp.ones((BAND, 2 * LANES), BF16)
    gain_row = dot(ones, jnp.concatenate([high, low], axis=1), LAST)[:1, :] / gain[...]
    pieces = [gain_row[:, at : at + LANES] for at in range(0, width, LANES)]
    pieces.append(jnp.zeros((BAND - len(pieces), LANES), F32))
    gain_tile = jnp.concatenate(pieces, axis=0).astype(BF16)
    for group in range(groups):
        packed[group, count - BAND :, full - LANES :] = gain_tile

    own = lax.axis_index("rep")
    across_three[...] = packed[own ^ 7]
    across_two[...] = packed[own ^ 5]
    across_next[...] = packed[own ^ 3]
    across_own[...] = packed[own ^ 1]
    for at in range(4):
        keep[at] = packed[own ^ (2 * at)]


def image_body(
    scale, proj, text_near, text_third, text_fourth, weights_near, weights_third, weights_fourth,
    unit, factors, before, norm_back, token, back, product,
):
    rows = back.shape[0]
    scale = scale[0]
    product[...] = (
        dot(weights_near[:, :rows], text_near[...], FIRST)
        + dot(weights_third[:, :rows], text_third[...], FIRST)
        + dot(weights_fourth[:, :rows], text_fourth[...], FIRST)
    )

    def image_chunk(where):
        values = product[where, :] * scale
        direction = unit[where, :].astype(F32)
        back[where, :] = (
            (values - direction * sums(direction * values)) * factors[where, :1]
        ).astype(BF16)

    over_rows(rows, 32, image_chunk)
    norm_back[...] = dot(back[...], proj[...], LAST)
    token[...] = jnp.zeros_like(token)


def feature_body(features, gain, norm_back, before, feature_grad, token):
    rows, width = features.shape

    def feature_chunk(where):
        values = features[where, :].astype(F32)
        centred = values - sums(values) * (1.0 / width)
        deviation = lax.rsqrt(sums(centred * centred) * (1.0 / width) + 1e-06)
        xhat = centred * deviation
        scaled = norm_back[where, :] * gain[...]
        feature_grad[where, :] = (
            deviation
            * (scaled - sums(scaled) * (1.0 / width) - xhat * (sums(scaled * xhat) * (1.0 / width)))
        ).astype(BF16)

    over_rows(rows, 32, feature_chunk)
    token[...] = jnp.zeros_like(token)


def text_body(
    scale, text, weights_near, weights_far, unit_near, unit_far, before, text_grad, token, product,
):
    rows = text_grad.shape[0]
    scale = scale[0]
    product[...] = dot(weights_near[:rows, :], unit_near[...]) + dot(weights_far[:rows, :], unit_far[...])

    def text_chunk(where):
        values = product[where, :] * scale
        own = text[where, :].astype(F32)
        own_inverse = lax.rsqrt(sums(own * own) + 1e-06)
        direction = own * own_inverse
        text_grad[where, :] = (
            (values - direction * sums(direction * values)) * own_inverse
        ).astype(BF16)

    over_rows(rows, 32, text_chunk)
    token[...] = jnp.zeros_like(token)


def one_sum_body(place, before, keep, come, total):
    total[...] = (keep[place].astype(F32) + come[...].astype(F32)).astype(BF16)


def far_sum_body(before, two_on, three_on, total):
    total[...] = two_on[...].astype(F32) + three_on[...].astype(F32)


def last_sum_body(far, keep, come, next_one, two_on, three_on, total, ordered, own):
    own[...] = (keep[0].astype(F32) + come[...].astype(F32)).astype(BF16)
    parts = (own, next_one, two_on, three_on)
    total[...] = (own[...].astype(F32) + next_one[...].astype(F32) + far[...]).astype(BF16)
    count, full = total.shape
    z = lax.axis_index("rep") // 2
    for step, part in enumerate(parts):
        ordered[z ^ step] = part[count - BAND :, full - LANES :].astype(F32)
    value = ordered[0]
    for at in range(1, len(parts)):
        value = value + ordered[at]
    total[count - BAND :, full - LANES :] = value.astype(BF16)


def finish_body(members, *refs):
    packets, (proj_grad, gain_gradient, ordered) = refs[:members], refs[members:]
    count, full = packets[0].shape
    rows, width = proj_grad.shape
    rest = width // members - full
    per_band = full // rest
    for k in range(members):
        member = lax.axis_index("loop") ^ k
        proj_grad[:, pl.ds(pl.multiple_of(member * full, LANES), full)] = packets[k][:rows, :].astype(F32)
        ordered[member] = packets[k][rows:, :].astype(F32)
    tails = []
    for index in range(rows // BAND):
        at, lane = (index // per_band) * BAND, (index % per_band) * rest
        tails.append(
            jnp.concatenate([ordered[member][at : at + BAND, lane : lane + rest] for member in range(members)], axis=1)
        )
    proj_grad[:, members * full :] = jnp.concatenate(tails, axis=0)
    value = ordered[0][count - rows - BAND :, full - LANES :]
    for member in range(1, members):
        value = value + ordered[member][count - rows - BAND :, full - LANES :]
    for at in range(width // LANES):
        gain_gradient[at * LANES : (at + 1) * LANES] = value[at]


def local_four(features, text, proj, gain, scale, bias):
    members = lax.axis_size("loop")
    groups = lax.axis_size("rep")
    rows, width = features.shape[0], features.shape[2]
    near, every = 2 * rows, 4 * rows
    columns = width // members
    full = columns // LANES * LANES
    each = width // groups
    bands = -(-(each // BAND) // (full // (columns - full)))
    packet = (each + bands * BAND, full)


    f0, t0 = features[:, 0, :], text[:, 0, :]
    f2 = send(f0, "loop", lambda p: p ^ 2)
    f1 = send(f0, "loop", lambda p: p ^ 1)

    wide, half = ((near, width), BF16), ((rows, width), BF16)
    square, part, turned = ((near, near), BF16), ((near, columns), BF16), ((width, near), BF16)

    line, mine = ((1, near), F32), ((columns, near), BF16)
    kept = ((width, width), BF16)
    f0_kept, proj_kept, t0_kept, gain_row, normed_near, unit_near, factors, text_own, token = call(
        near_body,
        [half, kept, half, ((1, width), F32), wide, wide, ((near, LANES), F32), half, TOKEN],
        [((near, width), F32)],
        smem=2,
        hbm=3,
        limit=46,
        flops=2 * near * width * width,
        moved=8 * near * width,
    )(scale, bias, f0, proj, t0, f1, gain)

    t2 = send(text_own, "loop", lambda p: p ^ 2)
    t1 = send(text_own, "loop", lambda p: p ^ 1)
    head = rows // 6 * 5
    f3_head, f3_tail = call(split_body, [((head, width), BF16), ((rows - head, width), BF16)], moved=1000)(f2, token)
    f3_head = send(f3_head, "loop", lambda p: p ^ 1)
    f3_tail = send(f3_tail, "loop", lambda p: p ^ 1)

    (
        text_near, turned_near, flat_near, unit_turned_near, inverse_near, text_columns_near, weights_near, totals_near, proj_columns,
        token,
    ) = call(
        near_pairs_body,
        [wide, turned, turned, mine, line, part, square, line, ((width, columns), BF16), TOKEN],
        [((near, near), F32)],
        smem=2,
        flops=1000,
        moved=1000,
    )(scale, bias, normed_near, unit_near, factors, text_own, t1, proj_kept, token)

    back_kind = ((columns, near), F32)
    (
        turned_far, unit_far, flat_far, unit_turned_far, inverse_far, weights_far, totals_far, early_near, early_far,
        token,
    ) = call(
        far_body,
        [turned, wide, turned, mine, line, square, line, back_kind, back_kind, TOKEN],
        [wide, ((near, width), F32), ((near, near), F32), ((near, LANES), F32)],
        smem=2,
        flops=1000,
        moved=1000,
    )(
        scale, bias, f2, f3_head, f3_tail, proj_kept, gain_row, text_near, text_columns_near, weights_near,
    )

    text_grad, token = call(
        text_body,
        [half, TOKEN],
        [((rows, width), F32)],
        smem=1,
        flops=1000,
        moved=1000,
    )(scale, t0_kept, weights_near, weights_far, unit_near, unit_far, token)

    t2_after, token = lax.optimization_barrier((t2, token))
    t3 = send(t2_after, "loop", lambda p: p ^ 1)

    narrow = ((rows, every), BF16)
    weights_third, back_near, back_far, totals = call(
        third_body,
        [narrow, back_kind, back_kind, ((1, every), F32)],
        [((rows, columns), BF16), ((rows, every), F32)],
        smem=2,
        flops=2 * near * width * width,
        moved=8 * near * width,
    )(
        scale, bias, t2, flat_near, flat_far, totals_near, totals_far, early_near, early_far, token,
    )

    outs = call(
        functools.partial(partial_body, members, groups),
        [(packet, BF16)] * 4 + [((4,) + packet, BF16), narrow],
        [((rows, columns), BF16), ((rows, every), F32), ((groups,) + packet, BF16)],
        smem=2,
        flops=4 * near * width * width,
        moved=16 * near * width,
    )(
        scale, bias, t3, flat_near, flat_far, totals, back_near, back_far, unit_turned_near, unit_turned_far,
        inverse_near, inverse_far, turned_near, turned_far, proj_columns, gain_row,
    )
    across_three, across_two, across_next, across_own, keep, weights_fourth = outs
    come_three = send(across_three, "rep", lambda p: p ^ 1)
    come_two = send(across_two, "rep", lambda p: p ^ 1)
    come_next = send(across_next, "rep", lambda p: p ^ 1)
    come_own = send(across_own, "rep", lambda p: p ^ 1)
    (three_sum,) = call(functools.partial(one_sum_body, 3), [(packet, BF16)], flops=1000, moved=1000)(
        keep, keep, come_three
    )
    three_on = send(three_sum, "rep", lambda p: p ^ 6)
    (two_sum,) = call(functools.partial(one_sum_body, 2), [(packet, BF16)], flops=1000, moved=1000)(
        three_sum, keep, come_two
    )
    two_on = send(two_sum, "rep", lambda p: p ^ 4)
    (next_sum,) = call(functools.partial(one_sum_body, 1), [(packet, BF16)], flops=1000, moved=1000)(
        two_sum, keep, come_next
    )
    next_one = send(next_sum, "rep", lambda p: p ^ 2)
    norm_back, token = call(
        image_body,
        [((rows, width), F32), TOKEN],
        [half, ((rows, width), F32)],
        smem=1,
        flops=1000,
        moved=1000,
    )(
        scale, proj_kept, text_near, t2, t3, weights_near, weights_third, weights_fourth,
        unit_near, factors, next_sum,
    )
    feature_grad, token = call(feature_body, [half, TOKEN], moved=1000)(f0_kept, gain_row, norm_back, token)
    (far_sum,) = call(far_sum_body, [(packet, F32)], moved=1000)(token, two_on, three_on)
    (reduced,) = call(last_sum_body, [(packet, BF16)], [((4, BAND, LANES), F32), (packet, BF16)], moved=1000)(
        far_sum, keep, come_own, next_one, two_on, three_on
    )
    far_block = send(reduced, "loop", lambda p: p ^ 2)
    near_block = send(reduced, "loop", lambda p: p ^ 1)
    blocks = [reduced, near_block, far_block, send(far_block, "loop", lambda p: p ^ 1)]

    proj_grad, gain_gradient = call(
        functools.partial(finish_body, members),
        [((each, width), F32), ((width,), F32)],
        [((members, bands * BAND, full), F32)],
        moved=8 * each * width,
    )(*blocks)
    return feature_grad[:, None, :], text_grad[:, None, :], proj_grad, gain_gradient


def four_fits(mesh, rows_shape):
    members, groups = mesh.shape["loop"], mesh.shape["rep"]
    rows, width = rows_shape[0] // members, rows_shape[2]
    if members != 4 or groups != 8 or width % (members * groups) or width % LANES:
        return False
    columns, each = width // members, width // groups
    full = columns // LANES * LANES
    rest = columns - full
    if rest == 0 or full < LANES or full % rest or each % BAND or rows % 64 or width // LANES > BAND:
        return False
    chunks = each // BAND
    used = (chunks - 1) % (full // rest) + 1
    return used * rest <= full - LANES


def solution(mesh):
    def run(features, text, proj, gain, scale, bias):
        body = local_four if four_fits(mesh, features.shape) else local_any_size
        return jax.shard_map(
            body,
            mesh=mesh,
            in_specs=(P("loop", "rep", None), P("loop", "rep", None), P(), P(), P(), P()),
            out_specs=(P("loop", "rep", None), P("loop", "rep", None), P("rep", None), P()),
            check_vma=False,
        )(features, text, proj, gain, scale, bias)

    return run
```

```python
import functools

import jax
import jax.numpy as jnp
from jax import lax
from jax.experimental import pallas as pl
from jax.experimental.pallas import tpu as pltpu
from jax.sharding import PartitionSpec as P

F32 = jnp.float32
BF16 = jnp.bfloat16
LAST = (((1,), (1,)), ((), ()))
FIRST = (((0,), (0,)), ((), ()))


def dot(a, b, dims=(((1,), (0,)), ((), ()))):
    return lax.dot_general(a, b, dims, preferred_element_type=F32)


def unit_rows(values):
    inverse = lax.rsqrt(jnp.sum(values * values, axis=-1, keepdims=True) + 1e-06)
    return values * inverse, inverse


def standardize(rows):
    values = rows.astype(F32)
    centred = values - jnp.mean(values, axis=-1, keepdims=True)
    inverse = lax.rsqrt(jnp.mean(centred * centred, axis=-1, keepdims=True) + 1e-06)
    return centred * inverse, inverse


def send(value, axis, target):
    count = lax.axis_size(axis)
    return lax.ppermute(value, axis, [(p, target(p)) for p in range(count)])


def gather_group(value, count):
    mine = [value]
    for step in range(1, count // 2):
        mine.append(send(value, "loop", lambda p: (p + 2 * step) % count))
    mates = [send(block, "loop", lambda p: p ^ 1) for block in mine]
    return mine + mates


def local_any_size(features, text, proj, gain, scale, bias):
    n = lax.axis_size("loop")
    m = lax.axis_size("rep")
    me = lax.axis_index("loop")
    half = n // 2
    rows, width = features.shape[0], features.shape[2]
    columns = proj.shape[1] // n
    group_rows = rows * n
    logit_scale, logit_bias = scale[0], bias[0]

    own_features = features[:, 0, :]
    own_text = text[:, 0, :]
    text_blocks = gather_group(own_text, n)
    feature_blocks = gather_group(own_features, n)

    xhat, deviation = standardize(own_features)
    normed = (xhat * gain).astype(BF16)
    img_dir, img_inv = unit_rows(dot(normed, proj))
    img_unit = img_dir.astype(BF16)

    txt_dir, txt_inv = unit_rows(own_text.astype(F32))
    own_txt_unit = txt_dir.astype(BF16)
    txt_unit = jnp.concatenate(
        [own_txt_unit] + [unit_rows(block.astype(F32))[0].astype(BF16) for block in text_blocks[1:]]
    )
    row_ids = lax.broadcasted_iota(jnp.int32, (rows, group_rows), 0)
    column_ids = lax.broadcasted_iota(jnp.int32, (rows, group_rows), 1)
    diagonal = (row_ids == column_ids).astype(F32)

    def weights(left, right):
        logits = logit_scale * dot(left, right, LAST) + logit_bias
        return (jax.nn.sigmoid(logits) - diagonal).astype(BF16)

    img_back = logit_scale * dot(weights(img_unit, txt_unit), txt_unit)
    proj_back = (
        (img_back - img_dir * jnp.sum(img_dir * img_back, axis=-1, keepdims=True)) * img_inv
    ).astype(BF16)

    blocks = jnp.transpose(proj_back.reshape(rows, n, columns), (1, 0, 2))
    blocks = lax.all_to_all(blocks, "loop", 0, 0, tiled=True)
    back_columns = blocks.reshape(group_rows, columns)

    norm_back = dot(proj_back, proj, LAST)
    scaled = norm_back * gain
    feature_grad = (
        deviation
        * (
            scaled
            - jnp.mean(scaled, axis=-1, keepdims=True)
            - xhat * jnp.mean(scaled * xhat, axis=-1, keepdims=True)
        )
    ).astype(BF16)
    gain_term = jnp.sum(norm_back * xhat, axis=0) * (1.0 / group_rows)

    other_normed = [(standardize(block)[0] * gain).astype(BF16) for block in feature_blocks[1:]]
    relative = jnp.stack([normed] + other_normed)
    member = jnp.arange(n)
    same_core = (member % 2) == (me % 2)
    chips_back = ((me // 2 - member // 2) % half)
    position = jnp.where(same_core, chips_back, half + chips_back)
    group_normed = relative[position].reshape(group_rows, width)

    partial = (dot(group_normed, back_columns, FIRST) * (1.0 / group_rows)).astype(BF16)
    pieces = lax.all_to_all(partial.reshape(m, width // m, columns), "rep", 0, 0, tiled=True)
    reduced = jnp.sum(pieces.astype(F32), axis=0).astype(BF16)
    gains = lax.all_gather(gain_term, "rep")
    gain_sum = jnp.sum(gains, axis=0)
    proj_rows = lax.all_gather(reduced, "loop")
    proj_grad = jnp.transpose(proj_rows, (1, 0, 2)).reshape(width // m, n * columns).astype(F32)
    gain_gradient = jnp.sum(lax.all_gather(gain_sum, "loop"), axis=0)

    group_unit = jnp.concatenate(
        [img_unit] + [unit_rows(dot(block, proj))[0].astype(BF16) for block in other_normed]
    )
    text_weights = weights(own_txt_unit, group_unit)
    txt_back = logit_scale * dot(text_weights, group_unit)
    text_grad = (
        (txt_back - txt_dir * jnp.sum(txt_dir * txt_back, axis=-1, keepdims=True)) * txt_inv
    ).astype(BF16)
    return feature_grad[:, None, :], text_grad[:, None, :], proj_grad, gain_gradient


VMEM = pl.BlockSpec(memory_space=pltpu.VMEM)
SMEM = pl.BlockSpec(memory_space=pltpu.SMEM)
HBM = pl.BlockSpec(memory_space=pltpu.HBM)
LANES = 128
BAND = 16
TOKEN = ((8, LANES), F32)


def call(body, outs, scratch=(), smem=0, hbm=0, limit=24, flops=0, moved=0):
    def run(*operands):
        specs = [SMEM] * smem + [HBM] * hbm + [VMEM] * (len(operands) - smem - hbm)
        return pl.pallas_call(
            body,
            out_shape=[jax.ShapeDtypeStruct(shape, kind) for shape, kind in outs],
            in_specs=specs,
            out_specs=[VMEM] * len(outs),
            scratch_shapes=[pltpu.VMEM(shape, kind) for shape, kind in scratch]
            + [pltpu.SemaphoreType.DMA((hbm,))] * bool(hbm),
            compiler_params=pltpu.CompilerParams(vmem_limit_bytes=limit * 2**20),
            cost_estimate=pl.CostEstimate(flops=flops, bytes_accessed=moved, transcendentals=0),
        )(*operands)

    return run


def over_rows(count, step, body):
    def turn(index, _):
        body(pl.ds(pl.multiple_of(index * step, step), step))
        return 0

    lax.fori_loop(0, count // step, turn, 0, unroll=min(4, count // step))


def sums(values):
    return jnp.sum(values, axis=-1, keepdims=True)


def normalize_into(source, gain, target, at):
    rows, width = source.shape

    def chunk(where):
        values = source[where, :].astype(F32)
        centred = values - sums(values) * (1.0 / width)
        inverse = lax.rsqrt(sums(centred * centred) * (1.0 / width) + 1e-06)
        target[pl.ds(at + where.start, where.size), :] = (centred * inverse * gain[...]).astype(BF16)

    over_rows(rows, 32, chunk)


def unit_into(source, target, at, inverses=None):
    rows = source.shape[0]

    def chunk(where):
        values = source[where, :].astype(F32)
        inverse = lax.rsqrt(sums(values * values) + 1e-06)
        place = pl.ds(at + where.start, where.size)
        target[place, :] = (values * inverse).astype(BF16)
        if inverses is not None:
            inverses[place, :] = jnp.broadcast_to(inverse, (where.size, LANES))

    over_rows(rows, 32, chunk)


def weigh(dots, scale, bias, diagonal, weights):
    texts, images = dots.shape

    def chunk(index, total):
        where = pl.ds(pl.multiple_of(index * BAND, BAND), BAND)
        product = dots[where, :]
        weight = jnp.tanh((0.5 * scale) * product + 0.5 * bias)
        offset = 0.5
        if diagonal is not None:
            text = index * BAND + diagonal + lax.broadcasted_iota(jnp.int32, product.shape, 0)
            image = lax.broadcasted_iota(jnp.int32, product.shape, 1)
            offset = jnp.where(text == image, -0.5, 0.5)
        weight = (0.5 * weight + offset).astype(BF16)
        weights[where, :] = weight
        both = weight.astype(F32) * product
        return total + both[:8, :] + both[8:, :]

    total = lax.fori_loop(0, texts // BAND, chunk, jnp.zeros((8, images), F32), unroll=4)
    return jnp.sum(total, axis=0, keepdims=True)


def take_columns(source, target):
    members = source.shape[1] // target.shape[1]
    full = target.shape[1] // LANES * LANES
    rest = target.shape[1] - full
    target[:, :full] = source[:, pl.ds(pl.multiple_of(lax.axis_index("loop") * full, LANES), full)]
    for member in range(members):

        @pl.when(lax.axis_index("loop") == member)
        def _():
            target[:, full:] = source[:, members * full + member * rest : members * full + (member + 1) * rest]


def near_body(
    scale, bias, f0_far, proj_far, t0_far, f1, gain_line,
    f0, proj, t0, gain, normed, unit, factors, text_unit, token, projected, semaphores,
):
    rows = f0.shape[0]
    copies = [
        pltpu.make_async_copy(source, target, semaphores.at[at])
        for at, (source, target) in enumerate(((f0_far, f0), (proj_far, proj), (t0_far, t0)))
    ]
    for copy in copies:
        copy.start()
    for at in range(0, gain.shape[1], LANES):
        gain[:, at : at + LANES] = gain_line[at : at + LANES].reshape(1, LANES)
    normalize_into(f1, gain, normed, rows)
    copies[0].wait()
    normalize_into(f0, gain, normed, 0)
    copies[1].wait()
    projected[...] = dot(normed[...], proj[...])
    copies[2].wait()
    unit_into(t0, text_unit, 0)
    unit_into(projected, unit, 0, factors)
    token[...] = jnp.zeros_like(token)


def near_pairs_body(
    scale, bias, normed, unit, factors, text_own, t1, proj, before,
    text_unit, normed_turned, turned, unit_turned, inverse, text_columns, weights, totals, proj_columns, token, dots,
):
    token[...] = jnp.zeros_like(token)
    rows = t1.shape[0]
    text_unit[:rows, :] = text_own[...]
    text_unit[rows:, :] = t1[...]
    dots[...] = dot(text_unit[...], unit[...], LAST)
    totals[...] = weigh(dots, scale[0], bias[0], 0, weights)
    take_columns(text_unit, text_columns)
    take_columns(proj, proj_columns)
    turn_own(unit, factors, turned, unit_turned, inverse)
    normed_turned[...] = normed[...].T


def turn_own(unit, factors, turned, unit_turned, inverse):
    columns = unit_turned.shape[0]
    full = columns // LANES * LANES
    rest = columns - full
    turned[...] = unit[...].T
    unit_turned[:full, :] = turned[pl.ds(pl.multiple_of(lax.axis_index("loop") * full, LANES), full), :]
    begin = turned.shape[0] // columns * full
    unit_turned[full:, :] = turned[pl.ds(pl.multiple_of(begin + lax.axis_index("loop") * rest, BAND), rest), :]
    inverse[...] = factors[...].T[:1, :]


def split_body(f2, before, head, tail):
    head[...] = f2[: head.shape[0], :]
    tail[...] = f2[head.shape[0] :, :]


def far_body(
    scale, bias, f2, f3_head, f3_tail, proj, gain, text_near, text_columns, weights_near,
    normed_turned, unit, turned, unit_turned, inverse, weights, totals, early_near, early_far, token,
    normed, projected, dots, factors,
):
    rows = f2.shape[0]
    normalize_into(f2, gain, normed, 0)
    normalize_into(f3_head, gain, normed, rows)
    normalize_into(f3_tail, gain, normed, rows + f3_head.shape[0])
    projected[...] = dot(normed[...], proj[...])
    unit_into(projected, unit, 0, factors)
    dots[...] = dot(text_near[...], unit[...], LAST)
    totals[...] = weigh(dots, scale[0], bias[0], None, weights)
    turn_own(unit, factors, turned, unit_turned, inverse)
    normed_turned[...] = normed[...].T
    early_near[...] = dot(text_columns[...], weights_near[...], FIRST)
    early_far[...] = dot(text_columns[...], weights[...], FIRST)
    token[...] = jnp.zeros_like(token)


def third_body(
    scale, bias, text_unit, flat_near, flat_far, totals_near, totals_far, early_near, early_far,
    before, weights, back_near, back_far, totals,
    text_columns, dots,
):
    rows = text_unit.shape[0]
    near = 2 * rows
    take_columns(text_unit, text_columns)
    dots[:, :near] = dot(text_unit[...], flat_near[...])
    dots[:, near:] = dot(text_unit[...], flat_far[...])
    added = weigh(dots, scale[0], bias[0], near, weights)
    totals[:, :near] = totals_near[...] + added[:, :near]
    totals[:, near:] = totals_far[...] + added[:, near:]
    added = dot(text_columns[...], weights[...], FIRST)
    back_near[...] = early_near[...] + added[:, :near]
    back_far[...] = early_far[...] + added[:, near:]


def pack_into(target, block, full):
    rows, columns = block.shape
    rest = columns - full
    target[:rows, :] = block[:, :full].astype(BF16)
    per_band = full // rest
    tail = block[:, full:]
    chunks = [tail[at : at + BAND, :] for at in range(0, rows, BAND)]
    for band in range(0, len(chunks), per_band):
        part = chunks[band : band + per_band]
        if len(part) < per_band:
            part.append(jnp.zeros((BAND, full - rest * len(part)), block.dtype))
        at = rows + (band // per_band) * BAND
        target[at : at + BAND, :] = jnp.concatenate(part, axis=1).astype(BF16)


def partial_body(
    members, groups, scale, bias, text_unit, flat_near, flat_far, totals, back_near, back_far, unit_turned_near,
    unit_turned_far, inverse_near, inverse_far, turned_near, turned_far, proj_columns, gain,
    across_three, across_two, across_next, across_own, keep, weights, text_columns, dots, packed,
):
    rows = text_unit.shape[0]
    near = 2 * rows
    every = members * rows
    width = text_unit.shape[1]
    columns = width // members
    count, full = packed.shape[1:]
    scale, bias = scale[0], bias[0]
    take_columns(text_unit, text_columns)
    dots[:, :near] = dot(text_unit[...], flat_near[...])
    dots[:, near:] = dot(text_unit[...], flat_far[...])
    total = totals[...] + weigh(dots, scale, bias, near + rows, weights)
    added = dot(text_columns[...], weights[...], FIRST)
    back = []
    for where, earlier, unit_turned, inverse in (
        (slice(0, near), back_near, unit_turned_near, inverse_near),
        (slice(near, every), back_far, unit_turned_far, inverse_far),
    ):
        whole = earlier[...] + added[:, where]
        part = (whole - unit_turned[...].astype(F32) * total[:, where]) * (inverse[...] * scale)
        back.append(part.astype(BF16))
    turned = jnp.concatenate([turned_near[...], turned_far[...]], axis=1)
    product = dot(turned, jnp.concatenate(back, axis=1), LAST)
    each = width // groups
    product = product * (1.0 / every)
    for group in range(groups):
        pack_into(packed.at[group], product[group * each : (group + 1) * each, :], full)

    terms = product * proj_columns[...].astype(F32)
    folded = jnp.concatenate([terms[:, full:], jnp.zeros((width, full + LANES - columns), F32)], axis=1)
    for at in range(0, full, LANES):
        folded = folded + terms[:, at : at + LANES]
    high = folded.astype(BF16)
    low = (folded - high.astype(F32)).astype(BF16)
    ones = jnp.ones((BAND, 2 * LANES), BF16)
    gain_row = dot(ones, jnp.concatenate([high, low], axis=1), LAST)[:1, :] / gain[...]
    pieces = [gain_row[:, at : at + LANES] for at in range(0, width, LANES)]
    pieces.append(jnp.zeros((BAND - len(pieces), LANES), F32))
    gain_tile = jnp.concatenate(pieces, axis=0).astype(BF16)
    for group in range(groups):
        packed[group, count - BAND :, full - LANES :] = gain_tile

    own = lax.axis_index("rep")
    across_three[...] = packed[own ^ 7]
    across_two[...] = packed[own ^ 5]
    across_next[...] = packed[own ^ 3]
    across_own[...] = packed[own ^ 1]
    for at in range(4):
        keep[at] = packed[own ^ (2 * at)]


def image_body(
    scale, proj, text_near, text_third, text_fourth, weights_near, weights_third, weights_fourth,
    unit, factors, before, norm_back, token, back, product,
):
    rows = back.shape[0]
    scale = scale[0]
    product[...] = (
        dot(weights_near[:, :rows], text_near[...], FIRST)
        + dot(weights_third[:, :rows], text_third[...], FIRST)
        + dot(weights_fourth[:, :rows], text_fourth[...], FIRST)
    )

    def image_chunk(where):
        values = product[where, :] * scale
        direction = unit[where, :].astype(F32)
        back[where, :] = (
            (values - direction * sums(direction * values)) * factors[where, :1]
        ).astype(BF16)

    over_rows(rows, 32, image_chunk)
    norm_back[...] = dot(back[...], proj[...], LAST)
    token[...] = jnp.zeros_like(token)


def feature_body(features, gain, norm_back, before, feature_grad, token):
    rows, width = features.shape

    def feature_chunk(where):
        values = features[where, :].astype(F32)
        centred = values - sums(values) * (1.0 / width)
        deviation = lax.rsqrt(sums(centred * centred) * (1.0 / width) + 1e-06)
        xhat = centred * deviation
        scaled = norm_back[where, :] * gain[...]
        feature_grad[where, :] = (
            deviation
            * (scaled - sums(scaled) * (1.0 / width) - xhat * (sums(scaled * xhat) * (1.0 / width)))
        ).astype(BF16)

    over_rows(rows, 32, feature_chunk)
    token[...] = jnp.zeros_like(token)


def text_body(
    scale, text, weights_near, weights_far, unit_near, unit_far, before, text_grad, token, product,
):
    rows = text_grad.shape[0]
    scale = scale[0]
    product[...] = dot(weights_near[:rows, :], unit_near[...]) + dot(weights_far[:rows, :], unit_far[...])

    def text_chunk(where):
        values = product[where, :] * scale
        own = text[where, :].astype(F32)
        own_inverse = lax.rsqrt(sums(own * own) + 1e-06)
        direction = own * own_inverse
        text_grad[where, :] = (
            (values - direction * sums(direction * values)) * own_inverse
        ).astype(BF16)

    over_rows(rows, 32, text_chunk)
    token[...] = jnp.zeros_like(token)


def one_sum_body(place, before, keep, come, total):
    total[...] = (keep[place].astype(F32) + come[...].astype(F32)).astype(BF16)


def far_sum_body(before, two_on, three_on, total):
    total[...] = two_on[...].astype(F32) + three_on[...].astype(F32)


def last_sum_body(far, keep, come, next_one, two_on, three_on, total, ordered, own):
    own[...] = (keep[0].astype(F32) + come[...].astype(F32)).astype(BF16)
    parts = (own, next_one, two_on, three_on)
    total[...] = (own[...].astype(F32) + next_one[...].astype(F32) + far[...]).astype(BF16)
    count, full = total.shape
    z = lax.axis_index("rep") // 2
    for step, part in enumerate(parts):
        ordered[z ^ step] = part[count - BAND :, full - LANES :].astype(F32)
    value = ordered[0]
    for at in range(1, len(parts)):
        value = value + ordered[at]
    total[count - BAND :, full - LANES :] = value.astype(BF16)


def finish_body(members, before, *refs):
    packets, (proj_grad, gain_gradient, ordered) = refs[:members], refs[members:]
    count, full = packets[0].shape
    rows, width = proj_grad.shape
    rest = width // members - full
    per_band = full // rest
    for k in range(members):
        member = lax.axis_index("loop") ^ k
        proj_grad[:, pl.ds(pl.multiple_of(member * full, LANES), full)] = packets[k][:rows, :].astype(F32)
        ordered[member] = packets[k][rows:, :].astype(F32)
    tails = []
    for index in range(rows // BAND):
        at, lane = (index // per_band) * BAND, (index % per_band) * rest
        tails.append(
            jnp.concatenate([ordered[member][at : at + BAND, lane : lane + rest] for member in range(members)], axis=1)
        )
    proj_grad[:, members * full :] = jnp.concatenate(tails, axis=0)
    value = ordered[0][count - rows - BAND :, full - LANES :]
    for member in range(1, members):
        value = value + ordered[member][count - rows - BAND :, full - LANES :]
    for at in range(width // LANES):
        gain_gradient[at * LANES : (at + 1) * LANES] = value[at]


def local_four(features, text, proj, gain, scale, bias):
    members = lax.axis_size("loop")
    groups = lax.axis_size("rep")
    rows, width = features.shape[0], features.shape[2]
    near, every = 2 * rows, 4 * rows
    columns = width // members
    full = columns // LANES * LANES
    each = width // groups
    bands = -(-(each // BAND) // (full // (columns - full)))
    packet = (each + bands * BAND, full)


    f0, t0 = features[:, 0, :], text[:, 0, :]
    f2 = send(f0, "loop", lambda p: p ^ 2)
    f1 = send(f0, "loop", lambda p: p ^ 1)

    wide, half = ((near, width), BF16), ((rows, width), BF16)
    square, part, turned = ((near, near), BF16), ((near, columns), BF16), ((width, near), BF16)

    line, mine = ((1, near), F32), ((columns, near), BF16)
    kept = ((width, width), BF16)
    f0_kept, proj_kept, t0_kept, gain_row, normed_near, unit_near, factors, text_own, token = call(
        near_body,
        [half, kept, half, ((1, width), F32), wide, wide, ((near, LANES), F32), half, TOKEN],
        [((near, width), F32)],
        smem=2,
        hbm=3,
        limit=46,
        flops=2 * near * width * width,
        moved=8 * near * width,
    )(scale, bias, f0, proj, t0, f1, gain)

    t2 = send(text_own, "loop", lambda p: p ^ 2)
    t1 = send(text_own, "loop", lambda p: p ^ 1)
    head = rows // 6 * 5
    f3_head, f3_tail = call(split_body, [((head, width), BF16), ((rows - head, width), BF16)], moved=1000)(f2, token)
    f3_head = send(f3_head, "loop", lambda p: p ^ 1)
    f3_tail = send(f3_tail, "loop", lambda p: p ^ 1)

    (
        text_near, turned_near, flat_near, unit_turned_near, inverse_near, text_columns_near, weights_near, totals_near, proj_columns,
        token,
    ) = call(
        near_pairs_body,
        [wide, turned, turned, mine, line, part, square, line, ((width, columns), BF16), TOKEN],
        [((near, near), F32)],
        smem=2,
        flops=1000,
        moved=1000,
    )(scale, bias, normed_near, unit_near, factors, text_own, t1, proj_kept, token)

    back_kind = ((columns, near), F32)
    (
        turned_far, unit_far, flat_far, unit_turned_far, inverse_far, weights_far, totals_far, early_near, early_far,
        token,
    ) = call(
        far_body,
        [turned, wide, turned, mine, line, square, line, back_kind, back_kind, TOKEN],
        [wide, ((near, width), F32), ((near, near), F32), ((near, LANES), F32)],
        smem=2,
        flops=1000,
        moved=1000,
    )(
        scale, bias, f2, f3_head, f3_tail, proj_kept, gain_row, text_near, text_columns_near, weights_near,
    )

    text_grad, token = call(
        text_body,
        [half, TOKEN],
        [((rows, width), F32)],
        smem=1,
        flops=1000,
        moved=1000,
    )(scale, t0_kept, weights_near, weights_far, unit_near, unit_far, token)

    t2_after, token = lax.optimization_barrier((t2, token))
    t3 = send(t2_after, "loop", lambda p: p ^ 1)

    narrow = ((rows, every), BF16)
    weights_third, back_near, back_far, totals = call(
        third_body,
        [narrow, back_kind, back_kind, ((1, every), F32)],
        [((rows, columns), BF16), ((rows, every), F32)],
        smem=2,
        flops=2 * near * width * width,
        moved=8 * near * width,
    )(
        scale, bias, t2, flat_near, flat_far, totals_near, totals_far, early_near, early_far, token,
    )

    outs = call(
        functools.partial(partial_body, members, groups),
        [(packet, BF16)] * 4 + [((4,) + packet, BF16), narrow],
        [((rows, columns), BF16), ((rows, every), F32), ((groups,) + packet, BF16)],
        smem=2,
        flops=4 * near * width * width,
        moved=16 * near * width,
    )(
        scale, bias, t3, flat_near, flat_far, totals, back_near, back_far, unit_turned_near, unit_turned_far,
        inverse_near, inverse_far, turned_near, turned_far, proj_columns, gain_row,
    )
    across_three, across_two, across_next, across_own, keep, weights_fourth = outs
    come_three = send(across_three, "rep", lambda p: p ^ 1)
    come_two = send(across_two, "rep", lambda p: p ^ 1)
    come_next = send(across_next, "rep", lambda p: p ^ 1)
    come_own = send(across_own, "rep", lambda p: p ^ 1)
    (three_sum,) = call(functools.partial(one_sum_body, 3), [(packet, BF16)], flops=1000, moved=1000)(
        keep, keep, come_three
    )
    three_on = send(three_sum, "rep", lambda p: p ^ 6)
    (two_sum,) = call(functools.partial(one_sum_body, 2), [(packet, BF16)], flops=1000, moved=1000)(
        three_sum, keep, come_two
    )
    two_on = send(two_sum, "rep", lambda p: p ^ 4)
    (next_sum,) = call(functools.partial(one_sum_body, 1), [(packet, BF16)], flops=1000, moved=1000)(
        two_sum, keep, come_next
    )
    next_one = send(next_sum, "rep", lambda p: p ^ 2)
    norm_back, token = call(
        image_body,
        [((rows, width), F32), TOKEN],
        [half, ((rows, width), F32)],
        smem=1,
        flops=1000,
        moved=1000,
    )(
        scale, proj_kept, text_near, t2, t3, weights_near, weights_third, weights_fourth,
        unit_near, factors, next_sum,
    )
    (far_sum,) = call(far_sum_body, [(packet, F32)], moved=1000)(token, two_on, three_on)
    (reduced,) = call(last_sum_body, [(packet, BF16)], [((4, BAND, LANES), F32), (packet, BF16)], moved=1000)(
        far_sum, keep, come_own, next_one, two_on, three_on
    )
    far_block = send(reduced, "loop", lambda p: p ^ 2)
    near_block = send(reduced, "loop", lambda p: p ^ 1)
    feature_grad, token = call(feature_body, [half, TOKEN], moved=12 * near * width)(
        f0_kept, gain_row, norm_back, reduced
    )
    far_block, token = lax.optimization_barrier((far_block, token))
    blocks = [reduced, near_block, far_block, send(far_block, "loop", lambda p: p ^ 1)]

    proj_grad, gain_gradient = call(
        functools.partial(finish_body, members),
        [((each, width), F32), ((width,), F32)],
        [((members, bands * BAND, full), F32)],
        moved=8 * each * width,
    )(token, *blocks)
    return feature_grad[:, None, :], text_grad[:, None, :], proj_grad, gain_gradient


def four_fits(mesh, rows_shape):
    members, groups = mesh.shape["loop"], mesh.shape["rep"]
    rows, width = rows_shape[0] // members, rows_shape[2]
    if members != 4 or groups != 8 or width % (members * groups) or width % LANES:
        return False
    columns, each = width // members, width // groups
    full = columns // LANES * LANES
    rest = columns - full
    if rest == 0 or full < LANES or full % rest or each % BAND or rows % 64 or width // LANES > BAND:
        return False
    chunks = each // BAND
    used = (chunks - 1) % (full // rest) + 1
    return used * rest <= full - LANES


def solution(mesh):
    def run(features, text, proj, gain, scale, bias):
        body = local_four if four_fits(mesh, features.shape) else local_any_size
        return jax.shard_map(
            body,
            mesh=mesh,
            in_specs=(P("loop", "rep", None), P("loop", "rep", None), P(), P(), P(), P()),
            out_specs=(P("loop", "rep", None), P("loop", "rep", None), P("rep", None), P()),
            check_vma=False,
        )(features, text, proj, gain, scale, bias)

    return run
```

```python
import functools

import jax
import jax.numpy as jnp
from jax import lax
from jax.experimental import pallas as pl
from jax.experimental.pallas import tpu as pltpu
from jax.sharding import PartitionSpec as P

F32 = jnp.float32
BF16 = jnp.bfloat16
LAST = (((1,), (1,)), ((), ()))
FIRST = (((0,), (0,)), ((), ()))


def dot(a, b, dims=(((1,), (0,)), ((), ()))):
    return lax.dot_general(a, b, dims, preferred_element_type=F32)


def unit_rows(values):
    inverse = lax.rsqrt(jnp.sum(values * values, axis=-1, keepdims=True) + 1e-06)
    return values * inverse, inverse


def standardize(rows):
    values = rows.astype(F32)
    centred = values - jnp.mean(values, axis=-1, keepdims=True)
    inverse = lax.rsqrt(jnp.mean(centred * centred, axis=-1, keepdims=True) + 1e-06)
    return centred * inverse, inverse


def send(value, axis, target):
    count = lax.axis_size(axis)
    return lax.ppermute(value, axis, [(p, target(p)) for p in range(count)])


def gather_group(value, count):
    mine = [value]
    for step in range(1, count // 2):
        mine.append(send(value, "loop", lambda p: (p + 2 * step) % count))
    mates = [send(block, "loop", lambda p: p ^ 1) for block in mine]
    return mine + mates


def local_any_size(features, text, proj, gain, scale, bias):
    n = lax.axis_size("loop")
    m = lax.axis_size("rep")
    me = lax.axis_index("loop")
    half = n // 2
    rows, width = features.shape[0], features.shape[2]
    columns = proj.shape[1] // n
    group_rows = rows * n
    logit_scale, logit_bias = scale[0], bias[0]

    own_features = features[:, 0, :]
    own_text = text[:, 0, :]
    text_blocks = gather_group(own_text, n)
    feature_blocks = gather_group(own_features, n)

    xhat, deviation = standardize(own_features)
    normed = (xhat * gain).astype(BF16)
    img_dir, img_inv = unit_rows(dot(normed, proj))
    img_unit = img_dir.astype(BF16)

    txt_dir, txt_inv = unit_rows(own_text.astype(F32))
    own_txt_unit = txt_dir.astype(BF16)
    txt_unit = jnp.concatenate(
        [own_txt_unit] + [unit_rows(block.astype(F32))[0].astype(BF16) for block in text_blocks[1:]]
    )
    row_ids = lax.broadcasted_iota(jnp.int32, (rows, group_rows), 0)
    column_ids = lax.broadcasted_iota(jnp.int32, (rows, group_rows), 1)
    diagonal = (row_ids == column_ids).astype(F32)

    def weights(left, right):
        logits = logit_scale * dot(left, right, LAST) + logit_bias
        return (jax.nn.sigmoid(logits) - diagonal).astype(BF16)

    img_back = logit_scale * dot(weights(img_unit, txt_unit), txt_unit)
    proj_back = (
        (img_back - img_dir * jnp.sum(img_dir * img_back, axis=-1, keepdims=True)) * img_inv
    ).astype(BF16)

    blocks = jnp.transpose(proj_back.reshape(rows, n, columns), (1, 0, 2))
    blocks = lax.all_to_all(blocks, "loop", 0, 0, tiled=True)
    back_columns = blocks.reshape(group_rows, columns)

    norm_back = dot(proj_back, proj, LAST)
    scaled = norm_back * gain
    feature_grad = (
        deviation
        * (
            scaled
            - jnp.mean(scaled, axis=-1, keepdims=True)
            - xhat * jnp.mean(scaled * xhat, axis=-1, keepdims=True)
        )
    ).astype(BF16)
    gain_term = jnp.sum(norm_back * xhat, axis=0) * (1.0 / group_rows)

    other_normed = [(standardize(block)[0] * gain).astype(BF16) for block in feature_blocks[1:]]
    relative = jnp.stack([normed] + other_normed)
    member = jnp.arange(n)
    same_core = (member % 2) == (me % 2)
    chips_back = ((me // 2 - member // 2) % half)
    position = jnp.where(same_core, chips_back, half + chips_back)
    group_normed = relative[position].reshape(group_rows, width)

    partial = (dot(group_normed, back_columns, FIRST) * (1.0 / group_rows)).astype(BF16)
    pieces = lax.all_to_all(partial.reshape(m, width // m, columns), "rep", 0, 0, tiled=True)
    reduced = jnp.sum(pieces.astype(F32), axis=0).astype(BF16)
    gains = lax.all_gather(gain_term, "rep")
    gain_sum = jnp.sum(gains, axis=0)
    proj_rows = lax.all_gather(reduced, "loop")
    proj_grad = jnp.transpose(proj_rows, (1, 0, 2)).reshape(width // m, n * columns).astype(F32)
    gain_gradient = jnp.sum(lax.all_gather(gain_sum, "loop"), axis=0)

    group_unit = jnp.concatenate(
        [img_unit] + [unit_rows(dot(block, proj))[0].astype(BF16) for block in other_normed]
    )
    text_weights = weights(own_txt_unit, group_unit)
    txt_back = logit_scale * dot(text_weights, group_unit)
    text_grad = (
        (txt_back - txt_dir * jnp.sum(txt_dir * txt_back, axis=-1, keepdims=True)) * txt_inv
    ).astype(BF16)
    return feature_grad[:, None, :], text_grad[:, None, :], proj_grad, gain_gradient


VMEM = pl.BlockSpec(memory_space=pltpu.VMEM)
SMEM = pl.BlockSpec(memory_space=pltpu.SMEM)
HBM = pl.BlockSpec(memory_space=pltpu.HBM)
LANES = 128
BAND = 16
TOKEN = ((8, LANES), F32)


def call(body, outs, scratch=(), smem=0, hbm=0, limit=24, flops=0, moved=0):
    def run(*operands):
        specs = [SMEM] * smem + [HBM] * hbm + [VMEM] * (len(operands) - smem - hbm)
        return pl.pallas_call(
            body,
            out_shape=[jax.ShapeDtypeStruct(shape, kind) for shape, kind in outs],
            in_specs=specs,
            out_specs=[VMEM] * len(outs),
            scratch_shapes=[pltpu.VMEM(shape, kind) for shape, kind in scratch]
            + [pltpu.SemaphoreType.DMA((hbm,))] * bool(hbm),
            compiler_params=pltpu.CompilerParams(vmem_limit_bytes=limit * 2**20),
            cost_estimate=pl.CostEstimate(flops=flops, bytes_accessed=moved, transcendentals=0),
        )(*operands)

    return run


def over_rows(count, step, body):
    def turn(index, _):
        body(pl.ds(pl.multiple_of(index * step, step), step))
        return 0

    lax.fori_loop(0, count // step, turn, 0, unroll=min(4, count // step))


def sums(values):
    return jnp.sum(values, axis=-1, keepdims=True)


def normalize_into(source, gain, target, at):
    rows, width = source.shape

    def chunk(where):
        values = source[where, :].astype(F32)
        centred = values - sums(values) * (1.0 / width)
        inverse = lax.rsqrt(sums(centred * centred) * (1.0 / width) + 1e-06)
        target[pl.ds(at + where.start, where.size), :] = (centred * inverse * gain[...]).astype(BF16)

    over_rows(rows, 32, chunk)


def unit_into(source, target, at, inverses=None):
    rows = source.shape[0]

    def chunk(where):
        values = source[where, :].astype(F32)
        inverse = lax.rsqrt(sums(values * values) + 1e-06)
        place = pl.ds(at + where.start, where.size)
        target[place, :] = (values * inverse).astype(BF16)
        if inverses is not None:
            inverses[place, :] = jnp.broadcast_to(inverse, (where.size, LANES))

    over_rows(rows, 32, chunk)


def weigh(dots, scale, bias, diagonal, weights):
    texts, images = dots.shape

    def chunk(index, total):
        where = pl.ds(pl.multiple_of(index * BAND, BAND), BAND)
        product = dots[where, :]
        weight = jnp.tanh((0.5 * scale) * product + 0.5 * bias)
        offset = 0.5
        if diagonal is not None:
            text = index * BAND + diagonal + lax.broadcasted_iota(jnp.int32, product.shape, 0)
            image = lax.broadcasted_iota(jnp.int32, product.shape, 1)
            offset = jnp.where(text == image, -0.5, 0.5)
        weight = (0.5 * weight + offset).astype(BF16)
        weights[where, :] = weight
        both = weight.astype(F32) * product
        return total + both[:8, :] + both[8:, :]

    total = lax.fori_loop(0, texts // BAND, chunk, jnp.zeros((8, images), F32), unroll=4)
    return jnp.sum(total, axis=0, keepdims=True)


def take_columns(source, target):
    members = source.shape[1] // target.shape[1]
    full = target.shape[1] // LANES * LANES
    rest = target.shape[1] - full
    target[:, :full] = source[:, pl.ds(pl.multiple_of(lax.axis_index("loop") * full, LANES), full)]
    for member in range(members):

        @pl.when(lax.axis_index("loop") == member)
        def _():
            target[:, full:] = source[:, members * full + member * rest : members * full + (member + 1) * rest]


def near_body(
    scale, bias, f0_far, proj_far, t0_far, f1, gain_line,
    f0, proj, t0, gain, normed, unit, factors, text_unit, token, projected, semaphores,
):
    rows = f0.shape[0]
    copies = [
        pltpu.make_async_copy(source, target, semaphores.at[at])
        for at, (source, target) in enumerate(((f0_far, f0), (proj_far, proj), (t0_far, t0)))
    ]
    for copy in copies:
        copy.start()
    for at in range(0, gain.shape[1], LANES):
        gain[:, at : at + LANES] = gain_line[at : at + LANES].reshape(1, LANES)
    normalize_into(f1, gain, normed, rows)
    copies[0].wait()
    normalize_into(f0, gain, normed, 0)
    copies[1].wait()
    projected[...] = dot(normed[...], proj[...])
    copies[2].wait()
    unit_into(t0, text_unit, 0)
    unit_into(projected, unit, 0, factors)
    token[...] = jnp.zeros_like(token)


def near_pairs_body(
    scale, bias, normed, unit, factors, text_own, t1, proj, before,
    text_unit, normed_turned, turned, unit_turned, inverse, text_columns, weights, totals, proj_columns, token, dots,
):
    token[...] = jnp.zeros_like(token)
    rows = t1.shape[0]
    text_unit[:rows, :] = text_own[...]
    text_unit[rows:, :] = t1[...]
    dots[...] = dot(text_unit[...], unit[...], LAST)
    totals[...] = weigh(dots, scale[0], bias[0], 0, weights)
    take_columns(text_unit, text_columns)
    take_columns(proj, proj_columns)
    turn_own(unit, factors, turned, unit_turned, inverse)
    normed_turned[...] = normed[...].T


def turn_own(unit, factors, turned, unit_turned, inverse):
    columns = unit_turned.shape[0]
    full = columns // LANES * LANES
    rest = columns - full
    turned[...] = unit[...].T
    unit_turned[:full, :] = turned[pl.ds(pl.multiple_of(lax.axis_index("loop") * full, LANES), full), :]
    begin = turned.shape[0] // columns * full
    unit_turned[full:, :] = turned[pl.ds(pl.multiple_of(begin + lax.axis_index("loop") * rest, BAND), rest), :]
    inverse[...] = factors[...].T[:1, :]


def split_body(f2, before, head, tail):
    head[...] = f2[: head.shape[0], :]
    tail[...] = f2[head.shape[0] :, :]


def far_body(
    scale, bias, f2, f3_head, f3_tail, proj, gain, text_near, text_columns, weights_near,
    normed_turned, unit, turned, unit_turned, inverse, weights, totals, early_near, early_far, token,
    normed, projected, dots, factors,
):
    rows = f2.shape[0]
    normalize_into(f2, gain, normed, 0)
    normalize_into(f3_head, gain, normed, rows)
    normalize_into(f3_tail, gain, normed, rows + f3_head.shape[0])
    projected[...] = dot(normed[...], proj[...])
    unit_into(projected, unit, 0, factors)
    dots[...] = dot(text_near[...], unit[...], LAST)
    totals[...] = weigh(dots, scale[0], bias[0], None, weights)
    turn_own(unit, factors, turned, unit_turned, inverse)
    normed_turned[...] = normed[...].T
    early_near[...] = dot(text_columns[...], weights_near[...], FIRST)
    early_far[...] = dot(text_columns[...], weights[...], FIRST)
    token[...] = jnp.zeros_like(token)


def third_body(
    scale, bias, text_unit, flat_near, flat_far, totals_near, totals_far, early_near, early_far,
    before, weights, back_near, back_far, totals,
    text_columns, dots,
):
    rows = text_unit.shape[0]
    near = 2 * rows
    take_columns(text_unit, text_columns)
    dots[:, :near] = dot(text_unit[...], flat_near[...])
    dots[:, near:] = dot(text_unit[...], flat_far[...])
    added = weigh(dots, scale[0], bias[0], near, weights)
    totals[:, :near] = totals_near[...] + added[:, :near]
    totals[:, near:] = totals_far[...] + added[:, near:]
    added = dot(text_columns[...], weights[...], FIRST)
    back_near[...] = early_near[...] + added[:, :near]
    back_far[...] = early_far[...] + added[:, near:]


def pack_into(target, block, full):
    rows, columns = block.shape
    rest = columns - full
    target[:rows, :] = block[:, :full].astype(BF16)
    per_band = full // rest
    tail = block[:, full:]
    chunks = [tail[at : at + BAND, :] for at in range(0, rows, BAND)]
    for band in range(0, len(chunks), per_band):
        part = chunks[band : band + per_band]
        if len(part) < per_band:
            part.append(jnp.zeros((BAND, full - rest * len(part)), block.dtype))
        at = rows + (band // per_band) * BAND
        target[at : at + BAND, :] = jnp.concatenate(part, axis=1).astype(BF16)


def partial_body(
    members, groups, scale, bias, text_unit, flat_near, flat_far, totals, back_near, back_far, unit_turned_near,
    unit_turned_far, inverse_near, inverse_far, turned_near, turned_far, proj_columns, gain,
    across_three, across_two, across_next, across_own, keep, weights, text_columns, dots, packed,
):
    rows = text_unit.shape[0]
    near = 2 * rows
    every = members * rows
    width = text_unit.shape[1]
    columns = width // members
    count, full = packed.shape[1:]
    scale, bias = scale[0], bias[0]
    take_columns(text_unit, text_columns)
    dots[:, :near] = dot(text_unit[...], flat_near[...])
    dots[:, near:] = dot(text_unit[...], flat_far[...])
    total = totals[...] + weigh(dots, scale, bias, near + rows, weights)
    added = dot(text_columns[...], weights[...], FIRST)
    back = []
    for where, earlier, unit_turned, inverse in (
        (slice(0, near), back_near, unit_turned_near, inverse_near),
        (slice(near, every), back_far, unit_turned_far, inverse_far),
    ):
        whole = earlier[...] + added[:, where]
        part = (whole - unit_turned[...].astype(F32) * total[:, where]) * (inverse[...] * scale)
        back.append(part.astype(BF16))
    turned = jnp.concatenate([turned_near[...], turned_far[...]], axis=1)
    product = dot(turned, jnp.concatenate(back, axis=1), LAST)
    each = width // groups
    product = product * (1.0 / every)
    for group in range(groups):
        pack_into(packed.at[group], product[group * each : (group + 1) * each, :], full)

    terms = product * proj_columns[...].astype(F32)
    folded = jnp.concatenate([terms[:, full:], jnp.zeros((width, full + LANES - columns), F32)], axis=1)
    for at in range(0, full, LANES):
        folded = folded + terms[:, at : at + LANES]
    high = folded.astype(BF16)
    low = (folded - high.astype(F32)).astype(BF16)
    ones = jnp.ones((BAND, 2 * LANES), BF16)
    gain_row = dot(ones, jnp.concatenate([high, low], axis=1), LAST)[:1, :] / gain[...]
    pieces = [gain_row[:, at : at + LANES] for at in range(0, width, LANES)]
    pieces.append(jnp.zeros((BAND - len(pieces), LANES), F32))
    gain_tile = jnp.concatenate(pieces, axis=0).astype(BF16)
    for group in range(groups):
        packed[group, count - BAND :, full - LANES :] = gain_tile

    own = lax.axis_index("rep")
    across_three[...] = packed[own ^ 7]
    across_two[...] = packed[own ^ 5]
    across_next[...] = packed[own ^ 3]
    across_own[...] = packed[own ^ 1]
    for at in range(4):
        keep[at] = packed[own ^ (2 * at)]


def image_body(
    scale, proj, text_near, text_third, text_fourth, weights_near, weights_third, weights_fourth,
    unit, factors, before, norm_back, token, back, product,
):
    rows = back.shape[0]
    scale = scale[0]
    product[...] = (
        dot(weights_near[:, :rows], text_near[...], FIRST)
        + dot(weights_third[:, :rows], text_third[...], FIRST)
        + dot(weights_fourth[:, :rows], text_fourth[...], FIRST)
    )

    def image_chunk(where):
        values = product[where, :] * scale
        direction = unit[where, :].astype(F32)
        back[where, :] = (
            (values - direction * sums(direction * values)) * factors[where, :1]
        ).astype(BF16)

    over_rows(rows, 32, image_chunk)
    norm_back[...] = dot(back[...], proj[...], LAST)
    token[...] = jnp.zeros_like(token)


def feature_body(features, gain, norm_back, before, feature_grad, token):
    rows, width = features.shape

    def feature_chunk(where):
        values = features[where, :].astype(F32)
        centred = values - sums(values) * (1.0 / width)
        deviation = lax.rsqrt(sums(centred * centred) * (1.0 / width) + 1e-06)
        xhat = centred * deviation
        scaled = norm_back[where, :] * gain[...]
        feature_grad[where, :] = (
            deviation
            * (scaled - sums(scaled) * (1.0 / width) - xhat * (sums(scaled * xhat) * (1.0 / width)))
        ).astype(BF16)

    over_rows(rows, 32, feature_chunk)
    token[...] = jnp.zeros_like(token)


def text_body(
    scale, text, weights_near, weights_far, unit_near, unit_far, before, text_grad, token, product,
):
    rows = text_grad.shape[0]
    scale = scale[0]
    product[...] = dot(weights_near[:rows, :], unit_near[...]) + dot(weights_far[:rows, :], unit_far[...])

    def text_chunk(where):
        values = product[where, :] * scale
        own = text[where, :].astype(F32)
        own_inverse = lax.rsqrt(sums(own * own) + 1e-06)
        direction = own * own_inverse
        text_grad[where, :] = (
            (values - direction * sums(direction * values)) * own_inverse
        ).astype(BF16)

    over_rows(rows, 32, text_chunk)
    token[...] = jnp.zeros_like(token)


def one_sum_body(place, before, keep, come, total):
    total[...] = (keep[place].astype(F32) + come[...].astype(F32)).astype(BF16)


def far_sum_body(before, two_on, three_on, total):
    total[...] = two_on[...].astype(F32) + three_on[...].astype(F32)


def others_sum_body(far, next_one, total):
    total[...] = far[...] + next_one[...].astype(F32)


def last_sum_body(others, keep, come, next_one, two_on, three_on, total, ordered, own):
    own[...] = (keep[0].astype(F32) + come[...].astype(F32)).astype(BF16)
    parts = (own, next_one, two_on, three_on)
    total[...] = (own[...].astype(F32) + others[...]).astype(BF16)
    count, full = total.shape
    z = lax.axis_index("rep") // 2
    for step, part in enumerate(parts):
        ordered[z ^ step] = part[count - BAND :, full - LANES :].astype(F32)
    value = ordered[0]
    for at in range(1, len(parts)):
        value = value + ordered[at]
    total[count - BAND :, full - LANES :] = value.astype(BF16)


def finish_body(members, before, *refs):
    packets, (proj_grad, gain_gradient, ordered) = refs[:members], refs[members:]
    count, full = packets[0].shape
    rows, width = proj_grad.shape
    rest = width // members - full
    per_band = full // rest
    for k in range(members):
        member = lax.axis_index("loop") ^ k
        proj_grad[:, pl.ds(pl.multiple_of(member * full, LANES), full)] = packets[k][:rows, :].astype(F32)
        ordered[member] = packets[k][rows:, :].astype(F32)
    tails = []
    for index in range(rows // BAND):
        at, lane = (index // per_band) * BAND, (index % per_band) * rest
        tails.append(
            jnp.concatenate([ordered[member][at : at + BAND, lane : lane + rest] for member in range(members)], axis=1)
        )
    proj_grad[:, members * full :] = jnp.concatenate(tails, axis=0)
    value = ordered[0][count - rows - BAND :, full - LANES :]
    for member in range(1, members):
        value = value + ordered[member][count - rows - BAND :, full - LANES :]
    for at in range(width // LANES):
        gain_gradient[at * LANES : (at + 1) * LANES] = value[at]


def local_four(features, text, proj, gain, scale, bias):
    members = lax.axis_size("loop")
    groups = lax.axis_size("rep")
    rows, width = features.shape[0], features.shape[2]
    near, every = 2 * rows, 4 * rows
    columns = width // members
    full = columns // LANES * LANES
    each = width // groups
    bands = -(-(each // BAND) // (full // (columns - full)))
    packet = (each + bands * BAND, full)


    f0, t0 = features[:, 0, :], text[:, 0, :]
    f2 = send(f0, "loop", lambda p: p ^ 2)
    f1 = send(f0, "loop", lambda p: p ^ 1)

    wide, half = ((near, width), BF16), ((rows, width), BF16)
    square, part, turned = ((near, near), BF16), ((near, columns), BF16), ((width, near), BF16)

    line, mine = ((1, near), F32), ((columns, near), BF16)
    kept = ((width, width), BF16)
    f0_kept, proj_kept, t0_kept, gain_row, normed_near, unit_near, factors, text_own, token = call(
        near_body,
        [half, kept, half, ((1, width), F32), wide, wide, ((near, LANES), F32), half, TOKEN],
        [((near, width), F32)],
        smem=2,
        hbm=3,
        limit=46,
        flops=2 * near * width * width,
        moved=8 * near * width,
    )(scale, bias, f0, proj, t0, f1, gain)

    t2 = send(text_own, "loop", lambda p: p ^ 2)
    t1 = send(text_own, "loop", lambda p: p ^ 1)
    head = rows // 6 * 5
    f3_head, f3_tail = call(split_body, [((head, width), BF16), ((rows - head, width), BF16)], moved=1000)(f2, token)
    f3_head = send(f3_head, "loop", lambda p: p ^ 1)
    f3_tail = send(f3_tail, "loop", lambda p: p ^ 1)

    (
        text_near, turned_near, flat_near, unit_turned_near, inverse_near, text_columns_near, weights_near, totals_near, proj_columns,
        token,
    ) = call(
        near_pairs_body,
        [wide, turned, turned, mine, line, part, square, line, ((width, columns), BF16), TOKEN],
        [((near, near), F32)],
        smem=2,
        flops=1000,
        moved=1000,
    )(scale, bias, normed_near, unit_near, factors, text_own, t1, proj_kept, token)

    back_kind = ((columns, near), F32)
    (
        turned_far, unit_far, flat_far, unit_turned_far, inverse_far, weights_far, totals_far, early_near, early_far,
        token,
    ) = call(
        far_body,
        [turned, wide, turned, mine, line, square, line, back_kind, back_kind, TOKEN],
        [wide, ((near, width), F32), ((near, near), F32), ((near, LANES), F32)],
        smem=2,
        flops=1000,
        moved=1000,
    )(
        scale, bias, f2, f3_head, f3_tail, proj_kept, gain_row, text_near, text_columns_near, weights_near,
    )

    text_grad, token = call(
        text_body,
        [half, TOKEN],
        [((rows, width), F32)],
        smem=1,
        flops=1000,
        moved=1000,
    )(scale, t0_kept, weights_near, weights_far, unit_near, unit_far, token)

    t2_after, token = lax.optimization_barrier((t2, token))
    t3 = send(t2_after, "loop", lambda p: p ^ 1)

    narrow = ((rows, every), BF16)
    weights_third, back_near, back_far, totals = call(
        third_body,
        [narrow, back_kind, back_kind, ((1, every), F32)],
        [((rows, columns), BF16), ((rows, every), F32)],
        smem=2,
        flops=2 * near * width * width,
        moved=8 * near * width,
    )(
        scale, bias, t2, flat_near, flat_far, totals_near, totals_far, early_near, early_far, token,
    )

    outs = call(
        functools.partial(partial_body, members, groups),
        [(packet, BF16)] * 4 + [((4,) + packet, BF16), narrow],
        [((rows, columns), BF16), ((rows, every), F32), ((groups,) + packet, BF16)],
        smem=2,
        flops=4 * near * width * width,
        moved=16 * near * width,
    )(
        scale, bias, t3, flat_near, flat_far, totals, back_near, back_far, unit_turned_near, unit_turned_far,
        inverse_near, inverse_far, turned_near, turned_far, proj_columns, gain_row,
    )
    across_three, across_two, across_next, across_own, keep, weights_fourth = outs
    come_three = send(across_three, "rep", lambda p: p ^ 1)
    come_two = send(across_two, "rep", lambda p: p ^ 1)
    come_next = send(across_next, "rep", lambda p: p ^ 1)
    come_own = send(across_own, "rep", lambda p: p ^ 1)
    (three_sum,) = call(functools.partial(one_sum_body, 3), [(packet, BF16)], flops=1000, moved=1000)(
        keep, keep, come_three
    )
    three_on = send(three_sum, "rep", lambda p: p ^ 6)
    (two_sum,) = call(functools.partial(one_sum_body, 2), [(packet, BF16)], flops=1000, moved=1000)(
        three_sum, keep, come_two
    )
    two_on = send(two_sum, "rep", lambda p: p ^ 4)
    (next_sum,) = call(functools.partial(one_sum_body, 1), [(packet, BF16)], flops=1000, moved=1000)(
        two_sum, keep, come_next
    )
    next_one = send(next_sum, "rep", lambda p: p ^ 2)
    norm_back, token = call(
        image_body,
        [((rows, width), F32), TOKEN],
        [half, ((rows, width), F32)],
        smem=1,
        flops=1000,
        moved=1000,
    )(
        scale, proj_kept, text_near, t2, t3, weights_near, weights_third, weights_fourth,
        unit_near, factors, next_sum,
    )
    (far_sum,) = call(far_sum_body, [(packet, F32)], moved=1000)(token, two_on, three_on)
    (others,) = call(others_sum_body, [(packet, F32)], moved=1000)(far_sum, next_one)
    (reduced,) = call(last_sum_body, [(packet, BF16)], [((4, BAND, LANES), F32), (packet, BF16)], moved=1000)(
        others, keep, come_own, next_one, two_on, three_on
    )
    far_block = send(reduced, "loop", lambda p: p ^ 2)
    near_block = send(reduced, "loop", lambda p: p ^ 1)
    feature_grad, token = call(feature_body, [half, TOKEN], moved=12 * near * width)(
        f0_kept, gain_row, norm_back, reduced
    )
    far_block, token = lax.optimization_barrier((far_block, token))
    blocks = [reduced, near_block, far_block, send(far_block, "loop", lambda p: p ^ 1)]

    proj_grad, gain_gradient = call(
        functools.partial(finish_body, members),
        [((each, width), F32), ((width,), F32)],
        [((members, bands * BAND, full), F32)],
        moved=8 * each * width,
    )(token, *blocks)
    return feature_grad[:, None, :], text_grad[:, None, :], proj_grad, gain_gradient


def four_fits(mesh, rows_shape):
    members, groups = mesh.shape["loop"], mesh.shape["rep"]
    rows, width = rows_shape[0] // members, rows_shape[2]
    if members != 4 or groups != 8 or width % (members * groups) or width % LANES:
        return False
    columns, each = width // members, width // groups
    full = columns // LANES * LANES
    rest = columns - full
    if rest == 0 or full < LANES or full % rest or each % BAND or rows % 64 or width // LANES > BAND:
        return False
    chunks = each // BAND
    used = (chunks - 1) % (full // rest) + 1
    return used * rest <= full - LANES


def solution(mesh):
    def run(features, text, proj, gain, scale, bias):
        body = local_four if four_fits(mesh, features.shape) else local_any_size
        return jax.shard_map(
            body,
            mesh=mesh,
            in_specs=(P("loop", "rep", None), P("loop", "rep", None), P(), P(), P(), P()),
            out_specs=(P("loop", "rep", None), P("loop", "rep", None), P("rep", None), P()),
            check_vma=False,
        )(features, text, proj, gain, scale, bias)

    return run
```

```python
import functools

import jax
import jax.numpy as jnp
from jax import lax
from jax.experimental import pallas as pl
from jax.experimental.pallas import tpu as pltpu
from jax.sharding import PartitionSpec as P

F32 = jnp.float32
BF16 = jnp.bfloat16
LAST = (((1,), (1,)), ((), ()))
FIRST = (((0,), (0,)), ((), ()))


def dot(a, b, dims=(((1,), (0,)), ((), ()))):
    return lax.dot_general(a, b, dims, preferred_element_type=F32)


def unit_rows(values):
    inverse = lax.rsqrt(jnp.sum(values * values, axis=-1, keepdims=True) + 1e-06)
    return values * inverse, inverse


def standardize(rows):
    values = rows.astype(F32)
    centred = values - jnp.mean(values, axis=-1, keepdims=True)
    inverse = lax.rsqrt(jnp.mean(centred * centred, axis=-1, keepdims=True) + 1e-06)
    return centred * inverse, inverse


def send(value, axis, target):
    count = lax.axis_size(axis)
    return lax.ppermute(value, axis, [(p, target(p)) for p in range(count)])


def gather_group(value, count):
    mine = [value]
    for step in range(1, count // 2):
        mine.append(send(value, "loop", lambda p: (p + 2 * step) % count))
    mates = [send(block, "loop", lambda p: p ^ 1) for block in mine]
    return mine + mates


def local_any_size(features, text, proj, gain, scale, bias):
    n = lax.axis_size("loop")
    m = lax.axis_size("rep")
    me = lax.axis_index("loop")
    half = n // 2
    rows, width = features.shape[0], features.shape[2]
    columns = proj.shape[1] // n
    group_rows = rows * n
    logit_scale, logit_bias = scale[0], bias[0]

    own_features = features[:, 0, :]
    own_text = text[:, 0, :]
    text_blocks = gather_group(own_text, n)
    feature_blocks = gather_group(own_features, n)

    xhat, deviation = standardize(own_features)
    normed = (xhat * gain).astype(BF16)
    img_dir, img_inv = unit_rows(dot(normed, proj))
    img_unit = img_dir.astype(BF16)

    txt_dir, txt_inv = unit_rows(own_text.astype(F32))
    own_txt_unit = txt_dir.astype(BF16)
    txt_unit = jnp.concatenate(
        [own_txt_unit] + [unit_rows(block.astype(F32))[0].astype(BF16) for block in text_blocks[1:]]
    )
    row_ids = lax.broadcasted_iota(jnp.int32, (rows, group_rows), 0)
    column_ids = lax.broadcasted_iota(jnp.int32, (rows, group_rows), 1)
    diagonal = (row_ids == column_ids).astype(F32)

    def weights(left, right):
        logits = logit_scale * dot(left, right, LAST) + logit_bias
        return (jax.nn.sigmoid(logits) - diagonal).astype(BF16)

    img_back = logit_scale * dot(weights(img_unit, txt_unit), txt_unit)
    proj_back = (
        (img_back - img_dir * jnp.sum(img_dir * img_back, axis=-1, keepdims=True)) * img_inv
    ).astype(BF16)

    blocks = jnp.transpose(proj_back.reshape(rows, n, columns), (1, 0, 2))
    blocks = lax.all_to_all(blocks, "loop", 0, 0, tiled=True)
    back_columns = blocks.reshape(group_rows, columns)

    norm_back = dot(proj_back, proj, LAST)
    scaled = norm_back * gain
    feature_grad = (
        deviation
        * (
            scaled
            - jnp.mean(scaled, axis=-1, keepdims=True)
            - xhat * jnp.mean(scaled * xhat, axis=-1, keepdims=True)
        )
    ).astype(BF16)
    gain_term = jnp.sum(norm_back * xhat, axis=0) * (1.0 / group_rows)

    other_normed = [(standardize(block)[0] * gain).astype(BF16) for block in feature_blocks[1:]]
    relative = jnp.stack([normed] + other_normed)
    member = jnp.arange(n)
    same_core = (member % 2) == (me % 2)
    chips_back = ((me // 2 - member // 2) % half)
    position = jnp.where(same_core, chips_back, half + chips_back)
    group_normed = relative[position].reshape(group_rows, width)

    partial = (dot(group_normed, back_columns, FIRST) * (1.0 / group_rows)).astype(BF16)
    pieces = lax.all_to_all(partial.reshape(m, width // m, columns), "rep", 0, 0, tiled=True)
    reduced = jnp.sum(pieces.astype(F32), axis=0).astype(BF16)
    gains = lax.all_gather(gain_term, "rep")
    gain_sum = jnp.sum(gains, axis=0)
    proj_rows = lax.all_gather(reduced, "loop")
    proj_grad = jnp.transpose(proj_rows, (1, 0, 2)).reshape(width // m, n * columns).astype(F32)
    gain_gradient = jnp.sum(lax.all_gather(gain_sum, "loop"), axis=0)

    group_unit = jnp.concatenate(
        [img_unit] + [unit_rows(dot(block, proj))[0].astype(BF16) for block in other_normed]
    )
    text_weights = weights(own_txt_unit, group_unit)
    txt_back = logit_scale * dot(text_weights, group_unit)
    text_grad = (
        (txt_back - txt_dir * jnp.sum(txt_dir * txt_back, axis=-1, keepdims=True)) * txt_inv
    ).astype(BF16)
    return feature_grad[:, None, :], text_grad[:, None, :], proj_grad, gain_gradient


VMEM = pl.BlockSpec(memory_space=pltpu.VMEM)
SMEM = pl.BlockSpec(memory_space=pltpu.SMEM)
HBM = pl.BlockSpec(memory_space=pltpu.HBM)
LANES = 128
BAND = 16
TOKEN = ((8, LANES), F32)


def call(body, outs, scratch=(), smem=0, hbm=0, limit=24, flops=0, moved=0):
    def run(*operands):
        specs = [SMEM] * smem + [HBM] * hbm + [VMEM] * (len(operands) - smem - hbm)
        return pl.pallas_call(
            body,
            out_shape=[jax.ShapeDtypeStruct(shape, kind) for shape, kind in outs],
            in_specs=specs,
            out_specs=[VMEM] * len(outs),
            scratch_shapes=[pltpu.VMEM(shape, kind) for shape, kind in scratch]
            + [pltpu.SemaphoreType.DMA((hbm,))] * bool(hbm),
            compiler_params=pltpu.CompilerParams(vmem_limit_bytes=limit * 2**20),
            cost_estimate=pl.CostEstimate(flops=flops, bytes_accessed=moved, transcendentals=0),
        )(*operands)

    return run


def over_rows(count, step, body):
    def turn(index, _):
        body(pl.ds(pl.multiple_of(index * step, step), step))
        return 0

    lax.fori_loop(0, count // step, turn, 0, unroll=min(4, count // step))


def sums(values):
    return jnp.sum(values, axis=-1, keepdims=True)


def normalize_into(source, gain, target, at):
    rows, width = source.shape

    def chunk(where):
        values = source[where, :].astype(F32)
        centred = values - sums(values) * (1.0 / width)
        inverse = lax.rsqrt(sums(centred * centred) * (1.0 / width) + 1e-06)
        target[pl.ds(at + where.start, where.size), :] = (centred * inverse * gain[...]).astype(BF16)

    over_rows(rows, 32, chunk)


def unit_into(source, target, at, inverses=None):
    rows = source.shape[0]

    def chunk(where):
        values = source[where, :].astype(F32)
        inverse = lax.rsqrt(sums(values * values) + 1e-06)
        place = pl.ds(at + where.start, where.size)
        target[place, :] = (values * inverse).astype(BF16)
        if inverses is not None:
            inverses[place, :] = jnp.broadcast_to(inverse, (where.size, LANES))

    over_rows(rows, 32, chunk)


def weigh(dots, scale, bias, diagonal, weights):
    texts, images = dots.shape

    def chunk(index, total):
        where = pl.ds(pl.multiple_of(index * BAND, BAND), BAND)
        product = dots[where, :]
        weight = jnp.tanh((0.5 * scale) * product + 0.5 * bias)
        offset = 0.5
        if diagonal is not None:
            text = index * BAND + diagonal + lax.broadcasted_iota(jnp.int32, product.shape, 0)
            image = lax.broadcasted_iota(jnp.int32, product.shape, 1)
            offset = jnp.where(text == image, -0.5, 0.5)
        weight = (0.5 * weight + offset).astype(BF16)
        weights[where, :] = weight
        both = weight.astype(F32) * product
        return total + both[:8, :] + both[8:, :]

    total = lax.fori_loop(0, texts // BAND, chunk, jnp.zeros((8, images), F32), unroll=4)
    return jnp.sum(total, axis=0, keepdims=True)


def take_columns(source, target):
    members = source.shape[1] // target.shape[1]
    full = target.shape[1] // LANES * LANES
    rest = target.shape[1] - full
    target[:, :full] = source[:, pl.ds(pl.multiple_of(lax.axis_index("loop") * full, LANES), full)]
    for member in range(members):

        @pl.when(lax.axis_index("loop") == member)
        def _():
            target[:, full:] = source[:, members * full + member * rest : members * full + (member + 1) * rest]


def near_body(
    scale, bias, f0_far, proj_far, t0_far, f1, gain_line,
    f0, proj, t0, gain, normed, unit, factors, text_unit, token, projected, semaphores,
):
    rows = f0.shape[0]
    copies = [
        pltpu.make_async_copy(source, target, semaphores.at[at])
        for at, (source, target) in enumerate(((f0_far, f0), (proj_far, proj), (t0_far, t0)))
    ]
    for copy in copies:
        copy.start()
    for at in range(0, gain.shape[1], LANES):
        gain[:, at : at + LANES] = gain_line[at : at + LANES].reshape(1, LANES)
    normalize_into(f1, gain, normed, rows)
    copies[0].wait()
    normalize_into(f0, gain, normed, 0)
    copies[1].wait()
    projected[...] = dot(normed[...], proj[...])
    copies[2].wait()
    unit_into(t0, text_unit, 0)
    unit_into(projected, unit, 0, factors)
    token[...] = jnp.zeros_like(token)


def near_pairs_body(
    scale, bias, normed, unit, factors, text_own, t1, proj, before,
    text_unit, normed_turned, turned, unit_turned, inverse, text_columns, weights, totals, proj_columns, token, dots,
):
    token[...] = jnp.zeros_like(token)
    rows = t1.shape[0]
    text_unit[:rows, :] = text_own[...]
    text_unit[rows:, :] = t1[...]
    dots[...] = dot(text_unit[...], unit[...], LAST)
    totals[...] = weigh(dots, scale[0], bias[0], 0, weights)
    take_columns(text_unit, text_columns)
    take_columns(proj, proj_columns)
    turn_own(unit, factors, turned, unit_turned, inverse)
    normed_turned[...] = normed[...].T


def turn_own(unit, factors, turned, unit_turned, inverse):
    columns = unit_turned.shape[0]
    full = columns // LANES * LANES
    rest = columns - full
    turned[...] = unit[...].T
    unit_turned[:full, :] = turned[pl.ds(pl.multiple_of(lax.axis_index("loop") * full, LANES), full), :]
    begin = turned.shape[0] // columns * full
    unit_turned[full:, :] = turned[pl.ds(pl.multiple_of(begin + lax.axis_index("loop") * rest, BAND), rest), :]
    inverse[...] = factors[...].T[:1, :]


def split_body(f2, before, head, tail):
    head[...] = f2[: head.shape[0], :]
    tail[...] = f2[head.shape[0] :, :]


def far_body(
    scale, bias, f2, f3_head, f3_tail, proj, gain, text_near, text_columns, weights_near,
    normed_turned, unit, turned, unit_turned, inverse, weights, totals, early_near, early_far, token,
    normed, projected, dots, factors,
):
    rows = f2.shape[0]
    normalize_into(f2, gain, normed, 0)
    normalize_into(f3_head, gain, normed, rows)
    normalize_into(f3_tail, gain, normed, rows + f3_head.shape[0])
    projected[...] = dot(normed[...], proj[...])
    unit_into(projected, unit, 0, factors)
    dots[...] = dot(text_near[...], unit[...], LAST)
    totals[...] = weigh(dots, scale[0], bias[0], None, weights)
    turn_own(unit, factors, turned, unit_turned, inverse)
    normed_turned[...] = normed[...].T
    early_near[...] = dot(text_columns[...], weights_near[...], FIRST)
    early_far[...] = dot(text_columns[...], weights[...], FIRST)
    token[...] = jnp.zeros_like(token)


def third_body(
    scale, bias, text_unit, flat_near, flat_far, totals_near, totals_far, early_near, early_far,
    before, weights, back_near, back_far, totals,
    text_columns, dots,
):
    rows = text_unit.shape[0]
    near = 2 * rows
    take_columns(text_unit, text_columns)
    dots[:, :near] = dot(text_unit[...], flat_near[...])
    dots[:, near:] = dot(text_unit[...], flat_far[...])
    added = weigh(dots, scale[0], bias[0], near, weights)
    totals[:, :near] = totals_near[...] + added[:, :near]
    totals[:, near:] = totals_far[...] + added[:, near:]
    added = dot(text_columns[...], weights[...], FIRST)
    back_near[...] = early_near[...] + added[:, :near]
    back_far[...] = early_far[...] + added[:, near:]


def pack_into(target, block, full):
    rows, columns = block.shape
    rest = columns - full
    target[:rows, :] = block[:, :full].astype(BF16)
    per_band = full // rest
    tail = block[:, full:]
    chunks = [tail[at : at + BAND, :] for at in range(0, rows, BAND)]
    for band in range(0, len(chunks), per_band):
        part = chunks[band : band + per_band]
        if len(part) < per_band:
            part.append(jnp.zeros((BAND, full - rest * len(part)), block.dtype))
        at = rows + (band // per_band) * BAND
        target[at : at + BAND, :] = jnp.concatenate(part, axis=1).astype(BF16)


def partial_body(
    members, groups, scale, bias, text_unit, flat_near, flat_far, totals, back_near, back_far, unit_turned_near,
    unit_turned_far, inverse_near, inverse_far, turned_near, turned_far, proj_columns, gain,
    across_three, across_two, across_next, across_own, keep, weights, text_columns, dots, packed,
):
    rows = text_unit.shape[0]
    near = 2 * rows
    every = members * rows
    width = text_unit.shape[1]
    columns = width // members
    count, full = packed.shape[1:]
    scale, bias = scale[0], bias[0]
    take_columns(text_unit, text_columns)
    dots[:, :near] = dot(text_unit[...], flat_near[...])
    dots[:, near:] = dot(text_unit[...], flat_far[...])
    total = totals[...] + weigh(dots, scale, bias, near + rows, weights)
    added = dot(text_columns[...], weights[...], FIRST)
    back = []
    for where, earlier, unit_turned, inverse in (
        (slice(0, near), back_near, unit_turned_near, inverse_near),
        (slice(near, every), back_far, unit_turned_far, inverse_far),
    ):
        whole = earlier[...] + added[:, where]
        part = (whole - unit_turned[...].astype(F32) * total[:, where]) * (inverse[...] * scale)
        back.append(part.astype(BF16))
    turned = jnp.concatenate([turned_near[...], turned_far[...]], axis=1)
    product = dot(turned, jnp.concatenate(back, axis=1), LAST)
    each = width // groups
    product = product * (1.0 / every)
    for group in range(groups):
        pack_into(packed.at[group], product[group * each : (group + 1) * each, :], full)

    terms = product * proj_columns[...].astype(F32)
    folded = jnp.concatenate([terms[:, full:], jnp.zeros((width, full + LANES - columns), F32)], axis=1)
    for at in range(0, full, LANES):
        folded = folded + terms[:, at : at + LANES]
    high = folded.astype(BF16)
    low = (folded - high.astype(F32)).astype(BF16)
    ones = jnp.ones((BAND, 2 * LANES), BF16)
    gain_row = dot(ones, jnp.concatenate([high, low], axis=1), LAST)[:1, :] / gain[...]
    pieces = [gain_row[:, at : at + LANES] for at in range(0, width, LANES)]
    pieces.append(jnp.zeros((BAND - len(pieces), LANES), F32))
    gain_tile = jnp.concatenate(pieces, axis=0).astype(BF16)
    for group in range(groups):
        packed[group, count - BAND :, full - LANES :] = gain_tile

    own = lax.axis_index("rep")
    across_three[...] = packed[own ^ 7]
    across_two[...] = packed[own ^ 5]
    across_next[...] = packed[own ^ 3]
    across_own[...] = packed[own ^ 1]
    for at in range(4):
        keep[at] = packed[own ^ (2 * at)]


def image_body(
    scale, proj, text_near, text_third, text_fourth, weights_near, weights_third, weights_fourth,
    unit, factors, before, norm_back, token, back, product,
):
    rows = back.shape[0]
    scale = scale[0]
    product[...] = (
        dot(weights_near[:, :rows], text_near[...], FIRST)
        + dot(weights_third[:, :rows], text_third[...], FIRST)
        + dot(weights_fourth[:, :rows], text_fourth[...], FIRST)
    )

    def image_chunk(where):
        values = product[where, :] * scale
        direction = unit[where, :].astype(F32)
        back[where, :] = (
            (values - direction * sums(direction * values)) * factors[where, :1]
        ).astype(BF16)

    over_rows(rows, 32, image_chunk)
    norm_back[...] = dot(back[...], proj[...], LAST)
    token[...] = jnp.zeros_like(token)


def feature_body(features, gain, norm_back, before, feature_grad, token):
    rows, width = features.shape

    def feature_chunk(where):
        values = features[where, :].astype(F32)
        centred = values - sums(values) * (1.0 / width)
        deviation = lax.rsqrt(sums(centred * centred) * (1.0 / width) + 1e-06)
        xhat = centred * deviation
        scaled = norm_back[where, :] * gain[...]
        feature_grad[where, :] = (
            deviation
            * (scaled - sums(scaled) * (1.0 / width) - xhat * (sums(scaled * xhat) * (1.0 / width)))
        ).astype(BF16)

    over_rows(rows, 32, feature_chunk)
    token[...] = jnp.zeros_like(token)


def text_body(
    scale, text, weights_near, weights_far, unit_near, unit_far, before, text_grad, token, product,
):
    rows = text_grad.shape[0]
    scale = scale[0]
    product[...] = dot(weights_near[:rows, :], unit_near[...]) + dot(weights_far[:rows, :], unit_far[...])

    def text_chunk(where):
        values = product[where, :] * scale
        own = text[where, :].astype(F32)
        own_inverse = lax.rsqrt(sums(own * own) + 1e-06)
        direction = own * own_inverse
        text_grad[where, :] = (
            (values - direction * sums(direction * values)) * own_inverse
        ).astype(BF16)

    over_rows(rows, 32, text_chunk)
    token[...] = jnp.zeros_like(token)


def one_sum_body(place, before, keep, come, total):
    total[...] = (keep[place].astype(F32) + come[...].astype(F32)).astype(BF16)


def far_sum_body(before, two_on, three_on, total):
    total[...] = two_on[...].astype(F32) + three_on[...].astype(F32)


def others_sum_body(far, next_one, total):
    total[...] = far[...] + next_one[...].astype(F32)


def last_sum_body(others, keep, come, next_one, two_on, three_on, total, ordered, own):
    own[...] = (keep[0].astype(F32) + come[...].astype(F32)).astype(BF16)
    parts = (own, next_one, two_on, three_on)
    total[...] = (own[...].astype(F32) + others[...]).astype(BF16)
    count, full = total.shape
    z = lax.axis_index("rep") // 2
    for step, part in enumerate(parts):
        ordered[z ^ step] = part[count - BAND :, full - LANES :].astype(F32)
    value = ordered[0]
    for at in range(1, len(parts)):
        value = value + ordered[at]
    total[count - BAND :, full - LANES :] = value.astype(BF16)


def finish_body(members, before, *refs):
    packets, (proj_grad, gain_gradient, ordered) = refs[:members], refs[members:]
    count, full = packets[0].shape
    rows, width = proj_grad.shape
    rest = width // members - full
    per_band = full // rest
    for k in range(members):
        member = lax.axis_index("loop") ^ k
        proj_grad[:, pl.ds(pl.multiple_of(member * full, LANES), full)] = packets[k][:rows, :].astype(F32)
        ordered[member] = packets[k][rows:, :].astype(F32)
    tails = []
    for index in range(rows // BAND):
        at, lane = (index // per_band) * BAND, (index % per_band) * rest
        tails.append(
            jnp.concatenate([ordered[member][at : at + BAND, lane : lane + rest] for member in range(members)], axis=1)
        )
    proj_grad[:, members * full :] = jnp.concatenate(tails, axis=0)
    value = ordered[0][count - rows - BAND :, full - LANES :]
    for member in range(1, members):
        value = value + ordered[member][count - rows - BAND :, full - LANES :]
    for at in range(width // LANES):
        gain_gradient[at * LANES : (at + 1) * LANES] = value[at]


def local_four(features, text, proj, gain, scale, bias):
    members = lax.axis_size("loop")
    groups = lax.axis_size("rep")
    rows, width = features.shape[0], features.shape[2]
    near, every = 2 * rows, 4 * rows
    columns = width // members
    full = columns // LANES * LANES
    each = width // groups
    bands = -(-(each // BAND) // (full // (columns - full)))
    packet = (each + bands * BAND, full)


    f0, t0 = features[:, 0, :], text[:, 0, :]
    f2 = send(f0, "loop", lambda p: p ^ 2)
    f1 = send(f0, "loop", lambda p: p ^ 1)

    wide, half = ((near, width), BF16), ((rows, width), BF16)
    square, part, turned = ((near, near), BF16), ((near, columns), BF16), ((width, near), BF16)

    line, mine = ((1, near), F32), ((columns, near), BF16)
    kept = ((width, width), BF16)
    f0_kept, proj_kept, t0_kept, gain_row, normed_near, unit_near, factors, text_own, token = call(
        near_body,
        [half, kept, half, ((1, width), F32), wide, wide, ((near, LANES), F32), half, TOKEN],
        [((near, width), F32)],
        smem=2,
        hbm=3,
        limit=46,
        flops=2 * near * width * width,
        moved=8 * near * width,
    )(scale, bias, f0, proj, t0, f1, gain)

    t2 = send(text_own, "loop", lambda p: p ^ 2)
    t1 = send(text_own, "loop", lambda p: p ^ 1)
    head = rows // 6 * 5
    f3_head, f3_tail = call(split_body, [((head, width), BF16), ((rows - head, width), BF16)], moved=1000)(f2, token)
    f3_head = send(f3_head, "loop", lambda p: p ^ 1)
    f3_tail = send(f3_tail, "loop", lambda p: p ^ 1)

    (
        text_near, turned_near, flat_near, unit_turned_near, inverse_near, text_columns_near, weights_near, totals_near, proj_columns,
        token,
    ) = call(
        near_pairs_body,
        [wide, turned, turned, mine, line, part, square, line, ((width, columns), BF16), TOKEN],
        [((near, near), F32)],
        smem=2,
        flops=1000,
        moved=1000,
    )(scale, bias, normed_near, unit_near, factors, text_own, t1, proj_kept, token)

    back_kind = ((columns, near), F32)
    (
        turned_far, unit_far, flat_far, unit_turned_far, inverse_far, weights_far, totals_far, early_near, early_far,
        token,
    ) = call(
        far_body,
        [turned, wide, turned, mine, line, square, line, back_kind, back_kind, TOKEN],
        [wide, ((near, width), F32), ((near, near), F32), ((near, LANES), F32)],
        smem=2,
        flops=1000,
        moved=1000,
    )(
        scale, bias, f2, f3_head, f3_tail, proj_kept, gain_row, text_near, text_columns_near, weights_near,
    )

    text_grad, token = call(
        text_body,
        [half, TOKEN],
        [((rows, width), F32)],
        smem=1,
        flops=1000,
        moved=1000,
    )(scale, t0_kept, weights_near, weights_far, unit_near, unit_far, token)

    t2_after, token = lax.optimization_barrier((t2, token))
    t3 = send(t2_after, "loop", lambda p: p ^ 1)

    narrow = ((rows, every), BF16)
    weights_third, back_near, back_far, totals = call(
        third_body,
        [narrow, back_kind, back_kind, ((1, every), F32)],
        [((rows, columns), BF16), ((rows, every), F32)],
        smem=2,
        flops=2 * near * width * width,
        moved=8 * near * width,
    )(
        scale, bias, t2, flat_near, flat_far, totals_near, totals_far, early_near, early_far, token,
    )

    outs = call(
        functools.partial(partial_body, members, groups),
        [(packet, BF16)] * 4 + [((4,) + packet, BF16), narrow],
        [((rows, columns), BF16), ((rows, every), F32), ((groups,) + packet, BF16)],
        smem=2,
        flops=4 * near * width * width,
        moved=16 * near * width,
    )(
        scale, bias, t3, flat_near, flat_far, totals, back_near, back_far, unit_turned_near, unit_turned_far,
        inverse_near, inverse_far, turned_near, turned_far, proj_columns, gain_row,
    )
    across_three, across_two, across_next, across_own, keep, weights_fourth = outs
    come_three = send(across_three, "rep", lambda p: p ^ 1)
    come_two = send(across_two, "rep", lambda p: p ^ 1)
    come_own = send(across_own, "rep", lambda p: p ^ 1)
    (three_sum,) = call(functools.partial(one_sum_body, 3), [(packet, BF16)], flops=1000, moved=1000)(
        keep, keep, come_three
    )
    three_on = send(three_sum, "rep", lambda p: p ^ 6)
    across_next, three_sum = lax.optimization_barrier((across_next, three_sum))
    come_next = send(across_next, "rep", lambda p: p ^ 1)
    (two_sum,) = call(functools.partial(one_sum_body, 2), [(packet, BF16)], flops=1000, moved=1000)(
        three_sum, keep, come_two
    )
    two_on = send(two_sum, "rep", lambda p: p ^ 4)
    (next_sum,) = call(functools.partial(one_sum_body, 1), [(packet, BF16)], flops=1000, moved=1000)(
        two_sum, keep, come_next
    )
    next_one = send(next_sum, "rep", lambda p: p ^ 2)
    norm_back, token = call(
        image_body,
        [((rows, width), F32), TOKEN],
        [half, ((rows, width), F32)],
        smem=1,
        flops=1000,
        moved=1000,
    )(
        scale, proj_kept, text_near, t2, t3, weights_near, weights_third, weights_fourth,
        unit_near, factors, next_sum,
    )
    (far_sum,) = call(far_sum_body, [(packet, F32)], moved=1000)(token, two_on, three_on)
    (others,) = call(others_sum_body, [(packet, F32)], moved=1000)(far_sum, next_one)
    (reduced,) = call(last_sum_body, [(packet, BF16)], [((4, BAND, LANES), F32), (packet, BF16)], moved=1000)(
        others, keep, come_own, next_one, two_on, three_on
    )
    far_block = send(reduced, "loop", lambda p: p ^ 2)
    near_block = send(reduced, "loop", lambda p: p ^ 1)
    feature_grad, token = call(feature_body, [half, TOKEN], moved=12 * near * width)(
        f0_kept, gain_row, norm_back, reduced
    )
    far_block, token = lax.optimization_barrier((far_block, token))
    blocks = [reduced, near_block, far_block, send(far_block, "loop", lambda p: p ^ 1)]

    proj_grad, gain_gradient = call(
        functools.partial(finish_body, members),
        [((each, width), F32), ((width,), F32)],
        [((members, bands * BAND, full), F32)],
        moved=8 * each * width,
    )(token, *blocks)
    return feature_grad[:, None, :], text_grad[:, None, :], proj_grad, gain_gradient


def four_fits(mesh, rows_shape):
    members, groups = mesh.shape["loop"], mesh.shape["rep"]
    rows, width = rows_shape[0] // members, rows_shape[2]
    if members != 4 or groups != 8 or width % (members * groups) or width % LANES:
        return False
    columns, each = width // members, width // groups
    full = columns // LANES * LANES
    rest = columns - full
    if rest == 0 or full < LANES or full % rest or each % BAND or rows % 64 or width // LANES > BAND:
        return False
    chunks = each // BAND
    used = (chunks - 1) % (full // rest) + 1
    return used * rest <= full - LANES


def solution(mesh):
    def run(features, text, proj, gain, scale, bias):
        body = local_four if four_fits(mesh, features.shape) else local_any_size
        return jax.shard_map(
            body,
            mesh=mesh,
            in_specs=(P("loop", "rep", None), P("loop", "rep", None), P(), P(), P(), P()),
            out_specs=(P("loop", "rep", None), P("loop", "rep", None), P("rep", None), P()),
            check_vma=False,
        )(features, text, proj, gain, scale, bias)

    return run
```

```python
import functools

import jax
import jax.numpy as jnp
from jax import lax
from jax.experimental import pallas as pl
from jax.experimental.pallas import tpu as pltpu
from jax.sharding import PartitionSpec as P

F32 = jnp.float32
BF16 = jnp.bfloat16
LAST = (((1,), (1,)), ((), ()))
FIRST = (((0,), (0,)), ((), ()))


def dot(a, b, dims=(((1,), (0,)), ((), ()))):
    return lax.dot_general(a, b, dims, preferred_element_type=F32)


def unit_rows(values):
    inverse = lax.rsqrt(jnp.sum(values * values, axis=-1, keepdims=True) + 1e-06)
    return values * inverse, inverse


def standardize(rows):
    values = rows.astype(F32)
    centred = values - jnp.mean(values, axis=-1, keepdims=True)
    inverse = lax.rsqrt(jnp.mean(centred * centred, axis=-1, keepdims=True) + 1e-06)
    return centred * inverse, inverse


def send(value, axis, target):
    count = lax.axis_size(axis)
    return lax.ppermute(value, axis, [(p, target(p)) for p in range(count)])


def gather_group(value, count):
    mine = [value]
    for step in range(1, count // 2):
        mine.append(send(value, "loop", lambda p: (p + 2 * step) % count))
    mates = [send(block, "loop", lambda p: p ^ 1) for block in mine]
    return mine + mates


def local_any_size(features, text, proj, gain, scale, bias):
    n = lax.axis_size("loop")
    m = lax.axis_size("rep")
    me = lax.axis_index("loop")
    half = n // 2
    rows, width = features.shape[0], features.shape[2]
    columns = proj.shape[1] // n
    group_rows = rows * n
    logit_scale, logit_bias = scale[0], bias[0]

    own_features = features[:, 0, :]
    own_text = text[:, 0, :]
    text_blocks = gather_group(own_text, n)
    feature_blocks = gather_group(own_features, n)

    xhat, deviation = standardize(own_features)
    normed = (xhat * gain).astype(BF16)
    img_dir, img_inv = unit_rows(dot(normed, proj))
    img_unit = img_dir.astype(BF16)

    txt_dir, txt_inv = unit_rows(own_text.astype(F32))
    own_txt_unit = txt_dir.astype(BF16)
    txt_unit = jnp.concatenate(
        [own_txt_unit] + [unit_rows(block.astype(F32))[0].astype(BF16) for block in text_blocks[1:]]
    )
    row_ids = lax.broadcasted_iota(jnp.int32, (rows, group_rows), 0)
    column_ids = lax.broadcasted_iota(jnp.int32, (rows, group_rows), 1)
    diagonal = (row_ids == column_ids).astype(F32)

    def weights(left, right):
        logits = logit_scale * dot(left, right, LAST) + logit_bias
        return (jax.nn.sigmoid(logits) - diagonal).astype(BF16)

    img_back = logit_scale * dot(weights(img_unit, txt_unit), txt_unit)
    proj_back = (
        (img_back - img_dir * jnp.sum(img_dir * img_back, axis=-1, keepdims=True)) * img_inv
    ).astype(BF16)

    blocks = jnp.transpose(proj_back.reshape(rows, n, columns), (1, 0, 2))
    blocks = lax.all_to_all(blocks, "loop", 0, 0, tiled=True)
    back_columns = blocks.reshape(group_rows, columns)

    norm_back = dot(proj_back, proj, LAST)
    scaled = norm_back * gain
    feature_grad = (
        deviation
        * (
            scaled
            - jnp.mean(scaled, axis=-1, keepdims=True)
            - xhat * jnp.mean(scaled * xhat, axis=-1, keepdims=True)
        )
    ).astype(BF16)
    gain_term = jnp.sum(norm_back * xhat, axis=0) * (1.0 / group_rows)

    other_normed = [(standardize(block)[0] * gain).astype(BF16) for block in feature_blocks[1:]]
    relative = jnp.stack([normed] + other_normed)
    member = jnp.arange(n)
    same_core = (member % 2) == (me % 2)
    chips_back = ((me // 2 - member // 2) % half)
    position = jnp.where(same_core, chips_back, half + chips_back)
    group_normed = relative[position].reshape(group_rows, width)

    partial = (dot(group_normed, back_columns, FIRST) * (1.0 / group_rows)).astype(BF16)
    pieces = lax.all_to_all(partial.reshape(m, width // m, columns), "rep", 0, 0, tiled=True)
    reduced = jnp.sum(pieces.astype(F32), axis=0).astype(BF16)
    gains = lax.all_gather(gain_term, "rep")
    gain_sum = jnp.sum(gains, axis=0)
    proj_rows = lax.all_gather(reduced, "loop")
    proj_grad = jnp.transpose(proj_rows, (1, 0, 2)).reshape(width // m, n * columns).astype(F32)
    gain_gradient = jnp.sum(lax.all_gather(gain_sum, "loop"), axis=0)

    group_unit = jnp.concatenate(
        [img_unit] + [unit_rows(dot(block, proj))[0].astype(BF16) for block in other_normed]
    )
    text_weights = weights(own_txt_unit, group_unit)
    txt_back = logit_scale * dot(text_weights, group_unit)
    text_grad = (
        (txt_back - txt_dir * jnp.sum(txt_dir * txt_back, axis=-1, keepdims=True)) * txt_inv
    ).astype(BF16)
    return feature_grad[:, None, :], text_grad[:, None, :], proj_grad, gain_gradient


VMEM = pl.BlockSpec(memory_space=pltpu.VMEM)
SMEM = pl.BlockSpec(memory_space=pltpu.SMEM)
HBM = pl.BlockSpec(memory_space=pltpu.HBM)
LANES = 128
BAND = 16
TOKEN = ((8, LANES), F32)


def call(body, outs, scratch=(), smem=0, hbm=0, limit=24, flops=0, moved=0):
    def run(*operands):
        specs = [SMEM] * smem + [HBM] * hbm + [VMEM] * (len(operands) - smem - hbm)
        return pl.pallas_call(
            body,
            out_shape=[jax.ShapeDtypeStruct(shape, kind) for shape, kind in outs],
            in_specs=specs,
            out_specs=[VMEM] * len(outs),
            scratch_shapes=[pltpu.VMEM(shape, kind) for shape, kind in scratch]
            + [pltpu.SemaphoreType.DMA((hbm,))] * bool(hbm),
            compiler_params=pltpu.CompilerParams(vmem_limit_bytes=limit * 2**20),
            cost_estimate=pl.CostEstimate(flops=flops, bytes_accessed=moved, transcendentals=0),
        )(*operands)

    return run


def over_rows(count, step, body):
    def turn(index, _):
        body(pl.ds(pl.multiple_of(index * step, step), step))
        return 0

    lax.fori_loop(0, count // step, turn, 0, unroll=min(4, count // step))


def sums(values):
    return jnp.sum(values, axis=-1, keepdims=True)


def normalize_into(source, gain, target, at):
    rows, width = source.shape

    def chunk(where):
        values = source[where, :].astype(F32)
        centred = values - sums(values) * (1.0 / width)
        inverse = lax.rsqrt(sums(centred * centred) * (1.0 / width) + 1e-06)
        target[pl.ds(at + where.start, where.size), :] = (centred * inverse * gain[...]).astype(BF16)

    over_rows(rows, 32, chunk)


def unit_into(source, target, at, inverses=None):
    rows = source.shape[0]

    def chunk(where):
        values = source[where, :].astype(F32)
        inverse = lax.rsqrt(sums(values * values) + 1e-06)
        place = pl.ds(at + where.start, where.size)
        target[place, :] = (values * inverse).astype(BF16)
        if inverses is not None:
            inverses[place, :] = jnp.broadcast_to(inverse, (where.size, LANES))

    over_rows(rows, 32, chunk)


def weigh(dots, scale, bias, diagonal, weights):
    texts, images = dots.shape

    def chunk(index, total):
        where = pl.ds(pl.multiple_of(index * BAND, BAND), BAND)
        product = dots[where, :]
        weight = jnp.tanh((0.5 * scale) * product + 0.5 * bias)
        offset = 0.5
        if diagonal is not None:
            text = index * BAND + diagonal + lax.broadcasted_iota(jnp.int32, product.shape, 0)
            image = lax.broadcasted_iota(jnp.int32, product.shape, 1)
            offset = jnp.where(text == image, -0.5, 0.5)
        weight = (0.5 * weight + offset).astype(BF16)
        weights[where, :] = weight
        both = weight.astype(F32) * product
        return total + both[:8, :] + both[8:, :]

    total = lax.fori_loop(0, texts // BAND, chunk, jnp.zeros((8, images), F32), unroll=4)
    return jnp.sum(total, axis=0, keepdims=True)


def take_columns(source, target):
    members = source.shape[1] // target.shape[1]
    full = target.shape[1] // LANES * LANES
    rest = target.shape[1] - full
    target[:, :full] = source[:, pl.ds(pl.multiple_of(lax.axis_index("loop") * full, LANES), full)]
    for member in range(members):

        @pl.when(lax.axis_index("loop") == member)
        def _():
            target[:, full:] = source[:, members * full + member * rest : members * full + (member + 1) * rest]


def near_body(
    scale, bias, f0_far, proj_far, t0_far, f1, gain_line,
    f0, proj, t0, gain, normed, unit, factors, text_unit, token, projected, semaphores,
):
    rows = f0.shape[0]
    copies = [
        pltpu.make_async_copy(source, target, semaphores.at[at])
        for at, (source, target) in enumerate(((f0_far, f0), (proj_far, proj), (t0_far, t0)))
    ]
    for copy in copies:
        copy.start()
    for at in range(0, gain.shape[1], LANES):
        gain[:, at : at + LANES] = gain_line[at : at + LANES].reshape(1, LANES)
    normalize_into(f1, gain, normed, rows)
    copies[0].wait()
    normalize_into(f0, gain, normed, 0)
    copies[1].wait()
    projected[...] = dot(normed[...], proj[...])
    copies[2].wait()
    unit_into(t0, text_unit, 0)
    unit_into(projected, unit, 0, factors)
    token[...] = jnp.zeros_like(token)


def near_pairs_body(
    scale, bias, normed, unit, factors, text_own, t1, proj, before,
    text_unit, normed_turned, turned, unit_turned, inverse, text_columns, weights, totals, proj_columns, token, dots,
):
    token[...] = jnp.zeros_like(token)
    rows = t1.shape[0]
    text_unit[:rows, :] = text_own[...]
    text_unit[rows:, :] = t1[...]
    dots[...] = dot(text_unit[...], unit[...], LAST)
    totals[...] = weigh(dots, scale[0], bias[0], 0, weights)
    take_columns(text_unit, text_columns)
    take_columns(proj, proj_columns)
    turn_own(unit, factors, turned, unit_turned, inverse)
    normed_turned[...] = normed[...].T


def turn_own(unit, factors, turned, unit_turned, inverse):
    columns = unit_turned.shape[0]
    full = columns // LANES * LANES
    rest = columns - full
    turned[...] = unit[...].T
    unit_turned[:full, :] = turned[pl.ds(pl.multiple_of(lax.axis_index("loop") * full, LANES), full), :]
    begin = turned.shape[0] // columns * full
    unit_turned[full:, :] = turned[pl.ds(pl.multiple_of(begin + lax.axis_index("loop") * rest, BAND), rest), :]
    inverse[...] = factors[...].T[:1, :]


def split_body(f2, before, head, tail):
    head[...] = f2[: head.shape[0], :]
    tail[...] = f2[head.shape[0] :, :]


def far_body(
    scale, bias, f2, f3_head, f3_tail, proj, gain, text_near, text_columns, weights_near,
    normed_turned, unit, turned, unit_turned, inverse, weights, totals, early_near, early_far, token,
    normed, projected, dots, factors,
):
    rows = f2.shape[0]
    normalize_into(f2, gain, normed, 0)
    normalize_into(f3_head, gain, normed, rows)
    normalize_into(f3_tail, gain, normed, rows + f3_head.shape[0])
    projected[...] = dot(normed[...], proj[...])
    unit_into(projected, unit, 0, factors)
    dots[...] = dot(text_near[...], unit[...], LAST)
    totals[...] = weigh(dots, scale[0], bias[0], None, weights)
    turn_own(unit, factors, turned, unit_turned, inverse)
    normed_turned[...] = normed[...].T
    early_near[...] = dot(text_columns[...], weights_near[...], FIRST)
    early_far[...] = dot(text_columns[...], weights[...], FIRST)
    token[...] = jnp.zeros_like(token)


def third_body(
    scale, bias, text_unit, flat_near, flat_far, totals_near, totals_far, early_near, early_far,
    before, weights, back_near, back_far, totals,
    text_columns, dots,
):
    rows = text_unit.shape[0]
    near = 2 * rows
    take_columns(text_unit, text_columns)
    dots[:, :near] = dot(text_unit[...], flat_near[...])
    dots[:, near:] = dot(text_unit[...], flat_far[...])
    added = weigh(dots, scale[0], bias[0], near, weights)
    totals[:, :near] = totals_near[...] + added[:, :near]
    totals[:, near:] = totals_far[...] + added[:, near:]
    added = dot(text_columns[...], weights[...], FIRST)
    back_near[...] = early_near[...] + added[:, :near]
    back_far[...] = early_far[...] + added[:, near:]


def pack_into(target, block, full):
    rows, columns = block.shape
    rest = columns - full
    target[:rows, :] = block[:, :full].astype(BF16)
    per_band = full // rest
    tail = block[:, full:]
    chunks = [tail[at : at + BAND, :] for at in range(0, rows, BAND)]
    for band in range(0, len(chunks), per_band):
        part = chunks[band : band + per_band]
        if len(part) < per_band:
            part.append(jnp.zeros((BAND, full - rest * len(part)), block.dtype))
        at = rows + (band // per_band) * BAND
        target[at : at + BAND, :] = jnp.concatenate(part, axis=1).astype(BF16)


def partial_body(
    members, groups, scale, bias, text_unit, flat_near, flat_far, totals, back_near, back_far, unit_turned_near,
    unit_turned_far, inverse_near, inverse_far, turned_near, turned_far, proj_columns, gain,
    across_three, across_two, across_next, across_own, keep, weights, text_columns, dots, packed,
):
    rows = text_unit.shape[0]
    near = 2 * rows
    every = members * rows
    width = text_unit.shape[1]
    columns = width // members
    count, full = packed.shape[1:]
    scale, bias = scale[0], bias[0]
    take_columns(text_unit, text_columns)
    dots[:, :near] = dot(text_unit[...], flat_near[...])
    dots[:, near:] = dot(text_unit[...], flat_far[...])
    total = totals[...] + weigh(dots, scale, bias, near + rows, weights)
    added = dot(text_columns[...], weights[...], FIRST)
    back = []
    for where, earlier, unit_turned, inverse in (
        (slice(0, near), back_near, unit_turned_near, inverse_near),
        (slice(near, every), back_far, unit_turned_far, inverse_far),
    ):
        whole = earlier[...] + added[:, where]
        part = (whole - unit_turned[...].astype(F32) * total[:, where]) * (inverse[...] * scale)
        back.append(part.astype(BF16))
    turned = jnp.concatenate([turned_near[...], turned_far[...]], axis=1)
    product = dot(turned, jnp.concatenate(back, axis=1), LAST)
    each = width // groups
    product = product * (1.0 / every)
    for group in range(groups):
        pack_into(packed.at[group], product[group * each : (group + 1) * each, :], full)

    terms = product * proj_columns[...].astype(F32)
    folded = jnp.concatenate([terms[:, full:], jnp.zeros((width, full + LANES - columns), F32)], axis=1)
    for at in range(0, full, LANES):
        folded = folded + terms[:, at : at + LANES]
    high = folded.astype(BF16)
    low = (folded - high.astype(F32)).astype(BF16)
    ones = jnp.ones((BAND, 2 * LANES), BF16)
    gain_row = dot(ones, jnp.concatenate([high, low], axis=1), LAST)[:1, :] / gain[...]
    pieces = [gain_row[:, at : at + LANES] for at in range(0, width, LANES)]
    pieces.append(jnp.zeros((BAND - len(pieces), LANES), F32))
    gain_tile = jnp.concatenate(pieces, axis=0).astype(BF16)
    for group in range(groups):
        packed[group, count - BAND :, full - LANES :] = gain_tile

    own = lax.axis_index("rep")
    across_three[...] = packed[own ^ 7]
    across_two[...] = packed[own ^ 5]
    across_next[...] = packed[own ^ 3]
    across_own[...] = packed[own ^ 1]
    for at in range(4):
        keep[at] = packed[own ^ (2 * at)]


def image_body(
    scale, proj, text_near, text_third, text_fourth, weights_near, weights_third, weights_fourth,
    unit, factors, before, norm_back, token, back, product,
):
    rows = back.shape[0]
    scale = scale[0]
    product[...] = (
        dot(weights_near[:, :rows], text_near[...], FIRST)
        + dot(weights_third[:, :rows], text_third[...], FIRST)
        + dot(weights_fourth[:, :rows], text_fourth[...], FIRST)
    )

    def image_chunk(where):
        values = product[where, :] * scale
        direction = unit[where, :].astype(F32)
        back[where, :] = (
            (values - direction * sums(direction * values)) * factors[where, :1]
        ).astype(BF16)

    over_rows(rows, 32, image_chunk)
    norm_back[...] = dot(back[...], proj[...], LAST)
    token[...] = jnp.zeros_like(token)


def feature_body(features, gain, norm_back, before, feature_grad, token):
    rows, width = features.shape

    def feature_chunk(where):
        values = features[where, :].astype(F32)
        centred = values - sums(values) * (1.0 / width)
        deviation = lax.rsqrt(sums(centred * centred) * (1.0 / width) + 1e-06)
        xhat = centred * deviation
        scaled = norm_back[where, :] * gain[...]
        feature_grad[where, :] = (
            deviation
            * (scaled - sums(scaled) * (1.0 / width) - xhat * (sums(scaled * xhat) * (1.0 / width)))
        ).astype(BF16)

    over_rows(rows, 32, feature_chunk)
    token[...] = jnp.zeros_like(token)


def text_body(
    scale, text, weights_near, weights_far, unit_near, unit_far, before, text_grad, token, product,
):
    rows = text_grad.shape[0]
    scale = scale[0]
    product[...] = dot(weights_near[:rows, :], unit_near[...]) + dot(weights_far[:rows, :], unit_far[...])

    def text_chunk(where):
        values = product[where, :] * scale
        own = text[where, :].astype(F32)
        own_inverse = lax.rsqrt(sums(own * own) + 1e-06)
        direction = own * own_inverse
        text_grad[where, :] = (
            (values - direction * sums(direction * values)) * own_inverse
        ).astype(BF16)

    over_rows(rows, 32, text_chunk)
    token[...] = jnp.zeros_like(token)


def one_sum_body(place, before, keep, come, total):
    total[...] = (keep[place].astype(F32) + come[...].astype(F32)).astype(BF16)


def far_sum_body(before, two_on, three_on, total):
    total[...] = two_on[...].astype(F32) + three_on[...].astype(F32)


def others_sum_body(far, next_one, total):
    total[...] = far[...] + next_one[...].astype(F32)


def last_sum_body(others, keep, come, next_one, two_on, three_on, total, ordered, own):
    own[...] = (keep[0].astype(F32) + come[...].astype(F32)).astype(BF16)
    parts = (own, next_one, two_on, three_on)
    total[...] = (own[...].astype(F32) + others[...]).astype(BF16)
    count, full = total.shape
    z = lax.axis_index("rep") // 2
    for step, part in enumerate(parts):
        ordered[z ^ step] = part[count - BAND :, full - LANES :].astype(F32)
    value = ordered[0]
    for at in range(1, len(parts)):
        value = value + ordered[at]
    total[count - BAND :, full - LANES :] = value.astype(BF16)


def place_main(packet, member, buffer, out, semaphore):
    rows, full = buffer.shape
    buffer[...] = packet[:rows, :].astype(F32)
    where = pl.ds(pl.multiple_of(member * full, LANES), full)
    copy = pltpu.make_async_copy(buffer, out.at[:, where], semaphore)
    copy.start()
    return copy


def finish_most_body(before, own, near, far, out, first, second, third, semaphores):
    copies = [
        place_main(packet, lax.axis_index("loop") ^ k, buffer, out, semaphores.at[k])
        for k, (packet, buffer) in enumerate(((own, first), (near, second), (far, third)))
    ]
    for copy in copies:
        copy.wait()


def finish_body(members, begun, *refs):
    packets, (out, gain_gradient, ordered, main, last, semaphores) = refs[:members], refs[members:]
    count, full = packets[0].shape
    rows, width = out.shape
    rest = width // members - full
    per_band = full // rest
    main_out = place_main(packets[-1], lax.axis_index("loop") ^ (members - 1), main, out, semaphores.at[0])
    for k in range(members):
        ordered[lax.axis_index("loop") ^ k] = packets[k][rows:, :].astype(F32)
    tails = []
    for index in range(rows // BAND):
        at, lane = (index // per_band) * BAND, (index % per_band) * rest
        tails.append(
            jnp.concatenate([ordered[member][at : at + BAND, lane : lane + rest] for member in range(members)], axis=1)
        )
    last[...] = jnp.concatenate(tails, axis=0)
    last_out = pltpu.make_async_copy(last, out.at[:, members * full :], semaphores.at[1])
    last_out.start()
    value = ordered[0][count - rows - BAND :, full - LANES :]
    for member in range(1, members):
        value = value + ordered[member][count - rows - BAND :, full - LANES :]
    for at in range(width // LANES):
        gain_gradient[at * LANES : (at + 1) * LANES] = value[at]
    main_out.wait()
    last_out.wait()


def local_four(features, text, proj, gain, scale, bias):
    members = lax.axis_size("loop")
    groups = lax.axis_size("rep")
    rows, width = features.shape[0], features.shape[2]
    near, every = 2 * rows, 4 * rows
    columns = width // members
    full = columns // LANES * LANES
    each = width // groups
    bands = -(-(each // BAND) // (full // (columns - full)))
    packet = (each + bands * BAND, full)


    f0, t0 = features[:, 0, :], text[:, 0, :]
    f2 = send(f0, "loop", lambda p: p ^ 2)
    f1 = send(f0, "loop", lambda p: p ^ 1)

    wide, half = ((near, width), BF16), ((rows, width), BF16)
    square, part, turned = ((near, near), BF16), ((near, columns), BF16), ((width, near), BF16)

    line, mine = ((1, near), F32), ((columns, near), BF16)
    kept = ((width, width), BF16)
    f0_kept, proj_kept, t0_kept, gain_row, normed_near, unit_near, factors, text_own, token = call(
        near_body,
        [half, kept, half, ((1, width), F32), wide, wide, ((near, LANES), F32), half, TOKEN],
        [((near, width), F32)],
        smem=2,
        hbm=3,
        limit=46,
        flops=2 * near * width * width,
        moved=8 * near * width,
    )(scale, bias, f0, proj, t0, f1, gain)

    t2 = send(text_own, "loop", lambda p: p ^ 2)
    t1 = send(text_own, "loop", lambda p: p ^ 1)
    head = rows // 6 * 5
    f3_head, f3_tail = call(split_body, [((head, width), BF16), ((rows - head, width), BF16)], moved=1000)(f2, token)
    f3_head = send(f3_head, "loop", lambda p: p ^ 1)
    f3_tail = send(f3_tail, "loop", lambda p: p ^ 1)

    (
        text_near, turned_near, flat_near, unit_turned_near, inverse_near, text_columns_near, weights_near, totals_near, proj_columns,
        token,
    ) = call(
        near_pairs_body,
        [wide, turned, turned, mine, line, part, square, line, ((width, columns), BF16), TOKEN],
        [((near, near), F32)],
        smem=2,
        flops=1000,
        moved=1000,
    )(scale, bias, normed_near, unit_near, factors, text_own, t1, proj_kept, token)

    back_kind = ((columns, near), F32)
    (
        turned_far, unit_far, flat_far, unit_turned_far, inverse_far, weights_far, totals_far, early_near, early_far,
        token,
    ) = call(
        far_body,
        [turned, wide, turned, mine, line, square, line, back_kind, back_kind, TOKEN],
        [wide, ((near, width), F32), ((near, near), F32), ((near, LANES), F32)],
        smem=2,
        flops=1000,
        moved=1000,
    )(
        scale, bias, f2, f3_head, f3_tail, proj_kept, gain_row, text_near, text_columns_near, weights_near,
    )

    text_grad, token = call(
        text_body,
        [half, TOKEN],
        [((rows, width), F32)],
        smem=1,
        flops=1000,
        moved=1000,
    )(scale, t0_kept, weights_near, weights_far, unit_near, unit_far, token)

    t2_after, token = lax.optimization_barrier((t2, token))
    t3 = send(t2_after, "loop", lambda p: p ^ 1)

    narrow = ((rows, every), BF16)
    weights_third, back_near, back_far, totals = call(
        third_body,
        [narrow, back_kind, back_kind, ((1, every), F32)],
        [((rows, columns), BF16), ((rows, every), F32)],
        smem=2,
        flops=2 * near * width * width,
        moved=8 * near * width,
    )(
        scale, bias, t2, flat_near, flat_far, totals_near, totals_far, early_near, early_far, token,
    )

    outs = call(
        functools.partial(partial_body, members, groups),
        [(packet, BF16)] * 4 + [((4,) + packet, BF16), narrow],
        [((rows, columns), BF16), ((rows, every), F32), ((groups,) + packet, BF16)],
        smem=2,
        flops=4 * near * width * width,
        moved=16 * near * width,
    )(
        scale, bias, t3, flat_near, flat_far, totals, back_near, back_far, unit_turned_near, unit_turned_far,
        inverse_near, inverse_far, turned_near, turned_far, proj_columns, gain_row,
    )
    across_three, across_two, across_next, across_own, keep, weights_fourth = outs
    come_three = send(across_three, "rep", lambda p: p ^ 1)
    come_two = send(across_two, "rep", lambda p: p ^ 1)
    come_next = send(across_next, "rep", lambda p: p ^ 1)
    come_own = send(across_own, "rep", lambda p: p ^ 1)
    (three_sum,) = call(functools.partial(one_sum_body, 3), [(packet, BF16)], flops=1000, moved=1000)(
        keep, keep, come_three
    )
    three_on = send(three_sum, "rep", lambda p: p ^ 6)
    (two_sum,) = call(functools.partial(one_sum_body, 2), [(packet, BF16)], flops=1000, moved=1000)(
        three_sum, keep, come_two
    )
    two_on = send(two_sum, "rep", lambda p: p ^ 4)
    (next_sum,) = call(functools.partial(one_sum_body, 1), [(packet, BF16)], flops=1000, moved=1000)(
        two_sum, keep, come_next
    )
    next_one = send(next_sum, "rep", lambda p: p ^ 2)
    norm_back, token = call(
        image_body,
        [((rows, width), F32), TOKEN],
        [half, ((rows, width), F32)],
        smem=1,
        flops=1000,
        moved=1000,
    )(
        scale, proj_kept, text_near, t2, t3, weights_near, weights_third, weights_fourth,
        unit_near, factors, next_sum,
    )
    (far_sum,) = call(far_sum_body, [(packet, F32)], moved=1000)(token, two_on, three_on)
    (others,) = call(others_sum_body, [(packet, F32)], moved=1000)(far_sum, next_one)
    (reduced,) = call(last_sum_body, [(packet, BF16)], [((4, BAND, LANES), F32), (packet, BF16)], moved=1000)(
        others, keep, come_own, next_one, two_on, three_on
    )
    far_block = send(reduced, "loop", lambda p: p ^ 2)
    near_block = send(reduced, "loop", lambda p: p ^ 1)
    feature_grad, token = call(feature_body, [half, TOKEN], moved=12 * near * width)(
        f0_kept, gain_row, norm_back, reduced
    )
    far_block, token = lax.optimization_barrier((far_block, token))
    last_block = send(far_block, "loop", lambda p: p ^ 1)
    out_kind = jax.ShapeDtypeStruct((each, width), F32)
    main_room = pltpu.VMEM((each, full), F32)
    begun = pl.pallas_call(
        finish_most_body,
        out_shape=out_kind,
        in_specs=[VMEM] * 4,
        out_specs=HBM,
        scratch_shapes=[main_room] * 3 + [pltpu.SemaphoreType.DMA((3,))],
        compiler_params=pltpu.CompilerParams(vmem_limit_bytes=24 * 2**20),
        cost_estimate=pl.CostEstimate(flops=0, bytes_accessed=8 * each * width, transcendentals=0),
    )(token, reduced, near_block, far_block)
    proj_grad, gain_gradient = pl.pallas_call(
        functools.partial(finish_body, members),
        out_shape=[out_kind, jax.ShapeDtypeStruct((width,), F32)],
        in_specs=[HBM] + [VMEM] * members,
        out_specs=[HBM, VMEM],
        input_output_aliases={0: 0},
        scratch_shapes=[
            pltpu.VMEM((members, bands * BAND, full), F32),
            main_room,
            pltpu.VMEM((each, width - members * full), F32),
            pltpu.SemaphoreType.DMA((2,)),
        ],
        compiler_params=pltpu.CompilerParams(vmem_limit_bytes=24 * 2**20),
        cost_estimate=pl.CostEstimate(flops=0, bytes_accessed=2 * each * width, transcendentals=0),
    )(begun, reduced, near_block, far_block, last_block)
    return feature_grad[:, None, :], text_grad[:, None, :], proj_grad, gain_gradient


def four_fits(mesh, rows_shape):
    members, groups = mesh.shape["loop"], mesh.shape["rep"]
    rows, width = rows_shape[0] // members, rows_shape[2]
    if members != 4 or groups != 8 or width % (members * groups) or width % LANES:
        return False
    columns, each = width // members, width // groups
    full = columns // LANES * LANES
    rest = columns - full
    if rest == 0 or full < LANES or full % rest or each % BAND or rows % 64 or width // LANES > BAND:
        return False
    chunks = each // BAND
    used = (chunks - 1) % (full // rest) + 1
    return used * rest <= full - LANES


def solution(mesh):
    def run(features, text, proj, gain, scale, bias):
        body = local_four if four_fits(mesh, features.shape) else local_any_size
        return jax.shard_map(
            body,
            mesh=mesh,
            in_specs=(P("loop", "rep", None), P("loop", "rep", None), P(), P(), P(), P()),
            out_specs=(P("loop", "rep", None), P("loop", "rep", None), P("rep", None), P()),
            check_vma=False,
        )(features, text, proj, gain, scale, bias)

    return run
```

```python
import functools

import jax
import jax.numpy as jnp
from jax import lax
from jax.experimental import pallas as pl
from jax.experimental.pallas import tpu as pltpu
from jax.sharding import PartitionSpec as P

F32 = jnp.float32
BF16 = jnp.bfloat16
LAST = (((1,), (1,)), ((), ()))
FIRST = (((0,), (0,)), ((), ()))


def dot(a, b, dims=(((1,), (0,)), ((), ()))):
    return lax.dot_general(a, b, dims, preferred_element_type=F32)


def unit_rows(values):
    inverse = lax.rsqrt(jnp.sum(values * values, axis=-1, keepdims=True) + 1e-06)
    return values * inverse, inverse


def standardize(rows):
    values = rows.astype(F32)
    centred = values - jnp.mean(values, axis=-1, keepdims=True)
    inverse = lax.rsqrt(jnp.mean(centred * centred, axis=-1, keepdims=True) + 1e-06)
    return centred * inverse, inverse


def send(value, axis, target):
    count = lax.axis_size(axis)
    return lax.ppermute(value, axis, [(p, target(p)) for p in range(count)])


def gather_group(value, count):
    mine = [value]
    for step in range(1, count // 2):
        mine.append(send(value, "loop", lambda p: (p + 2 * step) % count))
    mates = [send(block, "loop", lambda p: p ^ 1) for block in mine]
    return mine + mates


def local_any_size(features, text, proj, gain, scale, bias):
    n = lax.axis_size("loop")
    m = lax.axis_size("rep")
    me = lax.axis_index("loop")
    half = n // 2
    rows, width = features.shape[0], features.shape[2]
    columns = proj.shape[1] // n
    group_rows = rows * n
    logit_scale, logit_bias = scale[0], bias[0]

    own_features = features[:, 0, :]
    own_text = text[:, 0, :]
    text_blocks = gather_group(own_text, n)
    feature_blocks = gather_group(own_features, n)

    xhat, deviation = standardize(own_features)
    normed = (xhat * gain).astype(BF16)
    img_dir, img_inv = unit_rows(dot(normed, proj))
    img_unit = img_dir.astype(BF16)

    txt_dir, txt_inv = unit_rows(own_text.astype(F32))
    own_txt_unit = txt_dir.astype(BF16)
    txt_unit = jnp.concatenate(
        [own_txt_unit] + [unit_rows(block.astype(F32))[0].astype(BF16) for block in text_blocks[1:]]
    )
    row_ids = lax.broadcasted_iota(jnp.int32, (rows, group_rows), 0)
    column_ids = lax.broadcasted_iota(jnp.int32, (rows, group_rows), 1)
    diagonal = (row_ids == column_ids).astype(F32)

    def weights(left, right):
        logits = logit_scale * dot(left, right, LAST) + logit_bias
        return (jax.nn.sigmoid(logits) - diagonal).astype(BF16)

    img_back = logit_scale * dot(weights(img_unit, txt_unit), txt_unit)
    proj_back = (
        (img_back - img_dir * jnp.sum(img_dir * img_back, axis=-1, keepdims=True)) * img_inv
    ).astype(BF16)

    blocks = jnp.transpose(proj_back.reshape(rows, n, columns), (1, 0, 2))
    blocks = lax.all_to_all(blocks, "loop", 0, 0, tiled=True)
    back_columns = blocks.reshape(group_rows, columns)

    norm_back = dot(proj_back, proj, LAST)
    scaled = norm_back * gain
    feature_grad = (
        deviation
        * (
            scaled
            - jnp.mean(scaled, axis=-1, keepdims=True)
            - xhat * jnp.mean(scaled * xhat, axis=-1, keepdims=True)
        )
    ).astype(BF16)
    gain_term = jnp.sum(norm_back * xhat, axis=0) * (1.0 / group_rows)

    other_normed = [(standardize(block)[0] * gain).astype(BF16) for block in feature_blocks[1:]]
    relative = jnp.stack([normed] + other_normed)
    member = jnp.arange(n)
    same_core = (member % 2) == (me % 2)
    chips_back = ((me // 2 - member // 2) % half)
    position = jnp.where(same_core, chips_back, half + chips_back)
    group_normed = relative[position].reshape(group_rows, width)

    partial = (dot(group_normed, back_columns, FIRST) * (1.0 / group_rows)).astype(BF16)
    pieces = lax.all_to_all(partial.reshape(m, width // m, columns), "rep", 0, 0, tiled=True)
    reduced = jnp.sum(pieces.astype(F32), axis=0).astype(BF16)
    gains = lax.all_gather(gain_term, "rep")
    gain_sum = jnp.sum(gains, axis=0)
    proj_rows = lax.all_gather(reduced, "loop")
    proj_grad = jnp.transpose(proj_rows, (1, 0, 2)).reshape(width // m, n * columns).astype(F32)
    gain_gradient = jnp.sum(lax.all_gather(gain_sum, "loop"), axis=0)

    group_unit = jnp.concatenate(
        [img_unit] + [unit_rows(dot(block, proj))[0].astype(BF16) for block in other_normed]
    )
    text_weights = weights(own_txt_unit, group_unit)
    txt_back = logit_scale * dot(text_weights, group_unit)
    text_grad = (
        (txt_back - txt_dir * jnp.sum(txt_dir * txt_back, axis=-1, keepdims=True)) * txt_inv
    ).astype(BF16)
    return feature_grad[:, None, :], text_grad[:, None, :], proj_grad, gain_gradient


VMEM = pl.BlockSpec(memory_space=pltpu.VMEM)
SMEM = pl.BlockSpec(memory_space=pltpu.SMEM)
HBM = pl.BlockSpec(memory_space=pltpu.HBM)
LANES = 128
BAND = 16
TOKEN = ((8, LANES), F32)


def call(body, outs, scratch=(), smem=0, hbm=0, limit=24, flops=0, moved=0):
    def run(*operands):
        specs = [SMEM] * smem + [HBM] * hbm + [VMEM] * (len(operands) - smem - hbm)
        return pl.pallas_call(
            body,
            out_shape=[jax.ShapeDtypeStruct(shape, kind) for shape, kind in outs],
            in_specs=specs,
            out_specs=[VMEM] * len(outs),
            scratch_shapes=[pltpu.VMEM(shape, kind) for shape, kind in scratch]
            + [pltpu.SemaphoreType.DMA((hbm,))] * bool(hbm),
            compiler_params=pltpu.CompilerParams(vmem_limit_bytes=limit * 2**20),
            cost_estimate=pl.CostEstimate(flops=flops, bytes_accessed=moved, transcendentals=0),
        )(*operands)

    return run


def over_rows(count, step, body):
    def turn(index, _):
        body(pl.ds(pl.multiple_of(index * step, step), step))
        return 0

    lax.fori_loop(0, count // step, turn, 0, unroll=min(4, count // step))


def sums(values):
    return jnp.sum(values, axis=-1, keepdims=True)


def normalize_into(source, gain, target, at):
    rows, width = source.shape

    def chunk(where):
        values = source[where, :].astype(F32)
        centred = values - sums(values) * (1.0 / width)
        inverse = lax.rsqrt(sums(centred * centred) * (1.0 / width) + 1e-06)
        target[pl.ds(at + where.start, where.size), :] = (centred * inverse * gain[...]).astype(BF16)

    over_rows(rows, 32, chunk)


def unit_into(source, target, at, inverses=None):
    rows = source.shape[0]

    def chunk(where):
        values = source[where, :].astype(F32)
        inverse = lax.rsqrt(sums(values * values) + 1e-06)
        place = pl.ds(at + where.start, where.size)
        target[place, :] = (values * inverse).astype(BF16)
        if inverses is not None:
            inverses[place, :] = jnp.broadcast_to(inverse, (where.size, LANES))

    over_rows(rows, 32, chunk)


def weigh(dots, scale, bias, diagonal, weights):
    texts, images = dots.shape

    def chunk(index, total):
        where = pl.ds(pl.multiple_of(index * BAND, BAND), BAND)
        product = dots[where, :]
        weight = jnp.tanh((0.5 * scale) * product + 0.5 * bias)
        offset = 0.5
        if diagonal is not None:
            text = index * BAND + diagonal + lax.broadcasted_iota(jnp.int32, product.shape, 0)
            image = lax.broadcasted_iota(jnp.int32, product.shape, 1)
            offset = jnp.where(text == image, -0.5, 0.5)
        weight = (0.5 * weight + offset).astype(BF16)
        weights[where, :] = weight
        both = weight.astype(F32) * product
        return total + both[:8, :] + both[8:, :]

    total = lax.fori_loop(0, texts // BAND, chunk, jnp.zeros((8, images), F32), unroll=4)
    return jnp.sum(total, axis=0, keepdims=True)


def take_columns(source, target):
    members = source.shape[1] // target.shape[1]
    full = target.shape[1] // LANES * LANES
    rest = target.shape[1] - full
    target[:, :full] = source[:, pl.ds(pl.multiple_of(lax.axis_index("loop") * full, LANES), full)]
    for member in range(members):

        @pl.when(lax.axis_index("loop") == member)
        def _():
            target[:, full:] = source[:, members * full + member * rest : members * full + (member + 1) * rest]


def near_body(
    scale, bias, f0_far, proj_far, t0_far, f1, gain_line,
    f0, proj, t0, gain, normed, unit, factors, text_unit, token, projected, semaphores,
):
    rows = f0.shape[0]
    copies = [
        pltpu.make_async_copy(source, target, semaphores.at[at])
        for at, (source, target) in enumerate(((f0_far, f0), (proj_far, proj), (t0_far, t0)))
    ]
    for copy in copies:
        copy.start()
    for at in range(0, gain.shape[1], LANES):
        gain[:, at : at + LANES] = gain_line[at : at + LANES].reshape(1, LANES)
    normalize_into(f1, gain, normed, rows)
    copies[0].wait()
    normalize_into(f0, gain, normed, 0)
    copies[1].wait()
    projected[...] = dot(normed[...], proj[...])
    copies[2].wait()
    unit_into(t0, text_unit, 0)
    unit_into(projected, unit, 0, factors)
    token[...] = jnp.zeros_like(token)


def near_pairs_body(
    scale, bias, normed, unit, factors, text_own, t1, proj, before,
    text_unit, normed_turned, turned, unit_turned, inverse, text_columns, weights, totals, proj_columns, token, dots,
):
    token[...] = jnp.zeros_like(token)
    rows = t1.shape[0]
    text_unit[:rows, :] = text_own[...]
    text_unit[rows:, :] = t1[...]
    dots[...] = dot(text_unit[...], unit[...], LAST)
    totals[...] = weigh(dots, scale[0], bias[0], 0, weights)
    take_columns(text_unit, text_columns)
    take_columns(proj, proj_columns)
    turn_own(unit, factors, turned, unit_turned, inverse)
    normed_turned[...] = normed[...].T


def turn_own(unit, factors, turned, unit_turned, inverse):
    columns = unit_turned.shape[0]
    full = columns // LANES * LANES
    rest = columns - full
    turned[...] = unit[...].T
    unit_turned[:full, :] = turned[pl.ds(pl.multiple_of(lax.axis_index("loop") * full, LANES), full), :]
    begin = turned.shape[0] // columns * full
    unit_turned[full:, :] = turned[pl.ds(pl.multiple_of(begin + lax.axis_index("loop") * rest, BAND), rest), :]
    inverse[...] = factors[...].T[:1, :]


def split_body(f2, before, head, tail):
    head[...] = f2[: head.shape[0], :]
    tail[...] = f2[head.shape[0] :, :]


def far_body(
    scale, bias, f2, f3_head, f3_tail, proj, gain, text_near, text_columns, weights_near,
    normed_turned, unit, turned, unit_turned, inverse, weights, totals, early_near, early_far, token,
    normed, projected, dots, factors,
):
    rows = f2.shape[0]
    normalize_into(f2, gain, normed, 0)
    normalize_into(f3_head, gain, normed, rows)
    normalize_into(f3_tail, gain, normed, rows + f3_head.shape[0])
    projected[...] = dot(normed[...], proj[...])
    unit_into(projected, unit, 0, factors)
    dots[...] = dot(text_near[...], unit[...], LAST)
    totals[...] = weigh(dots, scale[0], bias[0], None, weights)
    turn_own(unit, factors, turned, unit_turned, inverse)
    normed_turned[...] = normed[...].T
    early_near[...] = dot(text_columns[...], weights_near[...], FIRST)
    early_far[...] = dot(text_columns[...], weights[...], FIRST)
    token[...] = jnp.zeros_like(token)


def third_body(
    scale, bias, text_unit, flat_near, flat_far, totals_near, totals_far, early_near, early_far,
    before, weights, back_near, back_far, totals,
    text_columns, dots,
):
    rows = text_unit.shape[0]
    near = 2 * rows
    take_columns(text_unit, text_columns)
    dots[:, :near] = dot(text_unit[...], flat_near[...])
    dots[:, near:] = dot(text_unit[...], flat_far[...])
    added = weigh(dots, scale[0], bias[0], near, weights)
    totals[:, :near] = totals_near[...] + added[:, :near]
    totals[:, near:] = totals_far[...] + added[:, near:]
    added = dot(text_columns[...], weights[...], FIRST)
    back_near[...] = early_near[...] + added[:, :near]
    back_far[...] = early_far[...] + added[:, near:]


def pack_into(target, block, full):
    rows, columns = block.shape
    rest = columns - full
    target[:rows, :] = block[:, :full].astype(BF16)
    per_band = full // rest
    tail = block[:, full:]
    chunks = [tail[at : at + BAND, :] for at in range(0, rows, BAND)]
    for band in range(0, len(chunks), per_band):
        part = chunks[band : band + per_band]
        if len(part) < per_band:
            part.append(jnp.zeros((BAND, full - rest * len(part)), block.dtype))
        at = rows + (band // per_band) * BAND
        target[at : at + BAND, :] = jnp.concatenate(part, axis=1).astype(BF16)


def partial_body(
    members, groups, scale, bias, text_unit, flat_near, flat_far, totals, back_near, back_far, unit_turned_near,
    unit_turned_far, inverse_near, inverse_far, turned_near, turned_far, proj_columns, gain,
    across_three, across_two, across_next, across_own, keep, weights, text_columns, dots, packed,
):
    rows = text_unit.shape[0]
    near = 2 * rows
    every = members * rows
    width = text_unit.shape[1]
    columns = width // members
    count, full = packed.shape[1:]
    scale, bias = scale[0], bias[0]
    take_columns(text_unit, text_columns)
    dots[:, :near] = dot(text_unit[...], flat_near[...])
    dots[:, near:] = dot(text_unit[...], flat_far[...])
    total = totals[...] + weigh(dots, scale, bias, near + rows, weights)
    added = dot(text_columns[...], weights[...], FIRST)
    back = []
    for where, earlier, unit_turned, inverse in (
        (slice(0, near), back_near, unit_turned_near, inverse_near),
        (slice(near, every), back_far, unit_turned_far, inverse_far),
    ):
        whole = earlier[...] + added[:, where]
        part = (whole - unit_turned[...].astype(F32) * total[:, where]) * (inverse[...] * scale)
        back.append(part.astype(BF16))
    turned = jnp.concatenate([turned_near[...], turned_far[...]], axis=1)
    product = dot(turned, jnp.concatenate(back, axis=1), LAST)
    each = width // groups
    product = product * (1.0 / every)
    for group in range(groups):
        pack_into(packed.at[group], product[group * each : (group + 1) * each, :], full)

    terms = product * proj_columns[...].astype(F32)
    folded = jnp.concatenate([terms[:, full:], jnp.zeros((width, full + LANES - columns), F32)], axis=1)
    for at in range(0, full, LANES):
        folded = folded + terms[:, at : at + LANES]
    high = folded.astype(BF16)
    low = (folded - high.astype(F32)).astype(BF16)
    ones = jnp.ones((BAND, 2 * LANES), BF16)
    gain_row = dot(ones, jnp.concatenate([high, low], axis=1), LAST)[:1, :] / gain[...]
    pieces = [gain_row[:, at : at + LANES] for at in range(0, width, LANES)]
    pieces.append(jnp.zeros((BAND - len(pieces), LANES), F32))
    gain_tile = jnp.concatenate(pieces, axis=0).astype(BF16)
    for group in range(groups):
        packed[group, count - BAND :, full - LANES :] = gain_tile

    own = lax.axis_index("rep")
    across_three[...] = packed[own ^ 7]
    across_two[...] = packed[own ^ 5]
    across_next[...] = packed[own ^ 3]
    across_own[...] = packed[own ^ 1]
    for at in range(4):
        keep[at] = packed[own ^ (2 * at)]


def image_body(
    scale, proj, text_near, text_third, text_fourth, weights_near, weights_third, weights_fourth,
    unit, factors, before, norm_back, token, back, product,
):
    rows = back.shape[0]
    scale = scale[0]
    product[...] = (
        dot(weights_near[:, :rows], text_near[...], FIRST)
        + dot(weights_third[:, :rows], text_third[...], FIRST)
        + dot(weights_fourth[:, :rows], text_fourth[...], FIRST)
    )

    def image_chunk(where):
        values = product[where, :] * scale
        direction = unit[where, :].astype(F32)
        back[where, :] = (
            (values - direction * sums(direction * values)) * factors[where, :1]
        ).astype(BF16)

    over_rows(rows, 32, image_chunk)
    norm_back[...] = dot(back[...], proj[...], LAST)
    token[...] = jnp.zeros_like(token)


def feature_body(features, gain, norm_back, before, feature_grad, token):
    rows, width = features.shape

    def feature_chunk(where):
        values = features[where, :].astype(F32)
        centred = values - sums(values) * (1.0 / width)
        deviation = lax.rsqrt(sums(centred * centred) * (1.0 / width) + 1e-06)
        xhat = centred * deviation
        scaled = norm_back[where, :] * gain[...]
        feature_grad[where, :] = (
            deviation
            * (scaled - sums(scaled) * (1.0 / width) - xhat * (sums(scaled * xhat) * (1.0 / width)))
        ).astype(BF16)

    over_rows(rows, 32, feature_chunk)
    token[...] = jnp.zeros_like(token)


def text_body(
    scale, text, weights_near, weights_far, unit_near, unit_far, before, text_grad, token, product,
):
    rows = text_grad.shape[0]
    scale = scale[0]
    product[...] = dot(weights_near[:rows, :], unit_near[...]) + dot(weights_far[:rows, :], unit_far[...])

    def text_chunk(where):
        values = product[where, :] * scale
        own = text[where, :].astype(F32)
        own_inverse = lax.rsqrt(sums(own * own) + 1e-06)
        direction = own * own_inverse
        text_grad[where, :] = (
            (values - direction * sums(direction * values)) * own_inverse
        ).astype(BF16)

    over_rows(rows, 32, text_chunk)
    token[...] = jnp.zeros_like(token)


def one_sum_body(place, before, keep, come, total):
    total[...] = (keep[place].astype(F32) + come[...].astype(F32)).astype(BF16)


def far_sum_body(before, two_on, three_on, total):
    total[...] = two_on[...].astype(F32) + three_on[...].astype(F32)


def others_sum_body(far, next_one, total):
    total[...] = far[...] + next_one[...].astype(F32)


def last_sum_body(others, keep, come, next_one, two_on, three_on, total, ordered, own):
    own[...] = (keep[0].astype(F32) + come[...].astype(F32)).astype(BF16)
    parts = (own, next_one, two_on, three_on)
    total[...] = (own[...].astype(F32) + others[...]).astype(BF16)
    count, full = total.shape
    z = lax.axis_index("rep") // 2
    for step, part in enumerate(parts):
        ordered[z ^ step] = part[count - BAND :, full - LANES :].astype(F32)
    value = ordered[0]
    for at in range(1, len(parts)):
        value = value + ordered[at]
    total[count - BAND :, full - LANES :] = value.astype(BF16)


def finish_body(members, before, *refs):
    packets, (proj_grad, gain_gradient, ordered) = refs[:members], refs[members:]
    count, full = packets[0].shape
    rows, width = proj_grad.shape
    rest = width // members - full
    per_band = full // rest
    for k in range(members):
        member = lax.axis_index("loop") ^ k
        proj_grad[:, pl.ds(pl.multiple_of(member * full, LANES), full)] = packets[k][:rows, :].astype(F32)
        ordered[member] = packets[k][rows:, :].astype(F32)
    tails = []
    for index in range(rows // BAND):
        at, lane = (index // per_band) * BAND, (index % per_band) * rest
        tails.append(
            jnp.concatenate([ordered[member][at : at + BAND, lane : lane + rest] for member in range(members)], axis=1)
        )
    proj_grad[:, members * full :] = jnp.concatenate(tails, axis=0)
    value = ordered[0][count - rows - BAND :, full - LANES :]
    for member in range(1, members):
        value = value + ordered[member][count - rows - BAND :, full - LANES :]
    for at in range(width // LANES):
        gain_gradient[at * LANES : (at + 1) * LANES] = value[at]


def local_four(features, text, proj, gain, scale, bias):
    members = lax.axis_size("loop")
    groups = lax.axis_size("rep")
    rows, width = features.shape[0], features.shape[2]
    near, every = 2 * rows, 4 * rows
    columns = width // members
    full = columns // LANES * LANES
    each = width // groups
    bands = -(-(each // BAND) // (full // (columns - full)))
    packet = (each + bands * BAND, full)


    f0, t0 = features[:, 0, :], text[:, 0, :]
    f2 = send(f0, "loop", lambda p: p ^ 2)
    f1 = send(f0, "loop", lambda p: p ^ 1)

    wide, half = ((near, width), BF16), ((rows, width), BF16)
    square, part, turned = ((near, near), BF16), ((near, columns), BF16), ((width, near), BF16)

    line, mine = ((1, near), F32), ((columns, near), BF16)
    kept = ((width, width), BF16)
    f0_kept, proj_kept, t0_kept, gain_row, normed_near, unit_near, factors, text_own, token = call(
        near_body,
        [half, kept, half, ((1, width), F32), wide, wide, ((near, LANES), F32), half, TOKEN],
        [((near, width), F32)],
        smem=2,
        hbm=3,
        limit=46,
        flops=2 * near * width * width,
        moved=8 * near * width,
    )(scale, bias, f0, proj, t0, f1, gain)

    t2 = send(text_own, "loop", lambda p: p ^ 2)
    t1 = send(text_own, "loop", lambda p: p ^ 1)
    head = rows // 6 * 5
    f3_head, f3_tail = call(split_body, [((head, width), BF16), ((rows - head, width), BF16)], moved=1000)(f2, token)
    f3_head = send(f3_head, "loop", lambda p: p ^ 1)
    f3_tail = send(f3_tail, "loop", lambda p: p ^ 1)

    (
        text_near, turned_near, flat_near, unit_turned_near, inverse_near, text_columns_near, weights_near, totals_near, proj_columns,
        token,
    ) = call(
        near_pairs_body,
        [wide, turned, turned, mine, line, part, square, line, ((width, columns), BF16), TOKEN],
        [((near, near), F32)],
        smem=2,
        flops=1000,
        moved=1000,
    )(scale, bias, normed_near, unit_near, factors, text_own, t1, proj_kept, token)

    back_kind = ((columns, near), F32)
    (
        turned_far, unit_far, flat_far, unit_turned_far, inverse_far, weights_far, totals_far, early_near, early_far,
        token,
    ) = call(
        far_body,
        [turned, wide, turned, mine, line, square, line, back_kind, back_kind, TOKEN],
        [wide, ((near, width), F32), ((near, near), F32), ((near, LANES), F32)],
        smem=2,
        flops=1000,
        moved=1000,
    )(
        scale, bias, f2, f3_head, f3_tail, proj_kept, gain_row, text_near, text_columns_near, weights_near,
    )

    text_grad, token = call(
        text_body,
        [half, TOKEN],
        [((rows, width), F32)],
        smem=1,
        flops=1000,
        moved=1000,
    )(scale, t0_kept, weights_near, weights_far, unit_near, unit_far, token)

    t2_after, token = lax.optimization_barrier((t2, token))
    t3 = send(t2_after, "loop", lambda p: p ^ 1)

    narrow = ((rows, every), BF16)
    weights_third, back_near, back_far, totals = call(
        third_body,
        [narrow, back_kind, back_kind, ((1, every), F32)],
        [((rows, columns), BF16), ((rows, every), F32)],
        smem=2,
        flops=2 * near * width * width,
        moved=8 * near * width,
    )(
        scale, bias, t2, flat_near, flat_far, totals_near, totals_far, early_near, early_far, token,
    )

    outs = call(
        functools.partial(partial_body, members, groups),
        [(packet, BF16)] * 4 + [((4,) + packet, BF16), narrow],
        [((rows, columns), BF16), ((rows, every), F32), ((groups,) + packet, BF16)],
        smem=2,
        flops=4 * near * width * width,
        moved=16 * near * width,
    )(
        scale, bias, t3, flat_near, flat_far, totals, back_near, back_far, unit_turned_near, unit_turned_far,
        inverse_near, inverse_far, turned_near, turned_far, proj_columns, gain_row,
    )
    across_three, across_two, across_next, across_own, keep, weights_fourth = outs
    come_two = send(across_two, "rep", lambda p: p ^ 1)
    come_three = send(across_three, "rep", lambda p: p ^ 1)
    come_next = send(across_next, "rep", lambda p: p ^ 1)
    come_own = send(across_own, "rep", lambda p: p ^ 1)
    (two_sum,) = call(functools.partial(one_sum_body, 2), [(packet, BF16)], flops=1000, moved=1000)(
        keep, keep, come_two
    )
    two_on = send(two_sum, "rep", lambda p: p ^ 4)
    (three_sum,) = call(functools.partial(one_sum_body, 3), [(packet, BF16)], flops=1000, moved=1000)(
        two_sum, keep, come_three
    )
    three_on = send(three_sum, "rep", lambda p: p ^ 6)
    (next_sum,) = call(functools.partial(one_sum_body, 1), [(packet, BF16)], flops=1000, moved=1000)(
        three_sum, keep, come_next
    )
    next_one = send(next_sum, "rep", lambda p: p ^ 2)
    norm_back, token = call(
        image_body,
        [((rows, width), F32), TOKEN],
        [half, ((rows, width), F32)],
        smem=1,
        flops=1000,
        moved=1000,
    )(
        scale, proj_kept, text_near, t2, t3, weights_near, weights_third, weights_fourth,
        unit_near, factors, next_sum,
    )
    (far_sum,) = call(far_sum_body, [(packet, F32)], moved=1000)(token, two_on, three_on)
    (others,) = call(others_sum_body, [(packet, F32)], moved=1000)(far_sum, next_one)
    (reduced,) = call(last_sum_body, [(packet, BF16)], [((4, BAND, LANES), F32), (packet, BF16)], moved=1000)(
        others, keep, come_own, next_one, two_on, three_on
    )
    far_block = send(reduced, "loop", lambda p: p ^ 2)
    near_block = send(reduced, "loop", lambda p: p ^ 1)
    feature_grad, token = call(feature_body, [half, TOKEN], moved=12 * near * width)(
        f0_kept, gain_row, norm_back, reduced
    )
    far_block, token = lax.optimization_barrier((far_block, token))
    blocks = [reduced, near_block, far_block, send(far_block, "loop", lambda p: p ^ 1)]

    proj_grad, gain_gradient = call(
        functools.partial(finish_body, members),
        [((each, width), F32), ((width,), F32)],
        [((members, bands * BAND, full), F32)],
        moved=8 * each * width,
    )(token, *blocks)
    return feature_grad[:, None, :], text_grad[:, None, :], proj_grad, gain_gradient


def four_fits(mesh, rows_shape):
    members, groups = mesh.shape["loop"], mesh.shape["rep"]
    rows, width = rows_shape[0] // members, rows_shape[2]
    if members != 4 or groups != 8 or width % (members * groups) or width % LANES:
        return False
    columns, each = width // members, width // groups
    full = columns // LANES * LANES
    rest = columns - full
    if rest == 0 or full < LANES or full % rest or each % BAND or rows % 64 or width // LANES > BAND:
        return False
    chunks = each // BAND
    used = (chunks - 1) % (full // rest) + 1
    return used * rest <= full - LANES


def solution(mesh):
    def run(features, text, proj, gain, scale, bias):
        body = local_four if four_fits(mesh, features.shape) else local_any_size
        return jax.shard_map(
            body,
            mesh=mesh,
            in_specs=(P("loop", "rep", None), P("loop", "rep", None), P(), P(), P(), P()),
            out_specs=(P("loop", "rep", None), P("loop", "rep", None), P("rep", None), P()),
            check_vma=False,
        )(features, text, proj, gain, scale, bias)

    return run
```

```python
import functools

import jax
import jax.numpy as jnp
from jax import lax
from jax.experimental import pallas as pl
from jax.experimental.pallas import tpu as pltpu
from jax.sharding import PartitionSpec as P

F32 = jnp.float32
BF16 = jnp.bfloat16
LAST = (((1,), (1,)), ((), ()))
FIRST = (((0,), (0,)), ((), ()))


def dot(a, b, dims=(((1,), (0,)), ((), ()))):
    return lax.dot_general(a, b, dims, preferred_element_type=F32)


def unit_rows(values):
    inverse = lax.rsqrt(jnp.sum(values * values, axis=-1, keepdims=True) + 1e-06)
    return values * inverse, inverse


def standardize(rows):
    values = rows.astype(F32)
    centred = values - jnp.mean(values, axis=-1, keepdims=True)
    inverse = lax.rsqrt(jnp.mean(centred * centred, axis=-1, keepdims=True) + 1e-06)
    return centred * inverse, inverse


def send(value, axis, target):
    count = lax.axis_size(axis)
    return lax.ppermute(value, axis, [(p, target(p)) for p in range(count)])


def gather_group(value, count):
    mine = [value]
    for step in range(1, count // 2):
        mine.append(send(value, "loop", lambda p: (p + 2 * step) % count))
    mates = [send(block, "loop", lambda p: p ^ 1) for block in mine]
    return mine + mates


def local_any_size(features, text, proj, gain, scale, bias):
    n = lax.axis_size("loop")
    m = lax.axis_size("rep")
    me = lax.axis_index("loop")
    half = n // 2
    rows, width = features.shape[0], features.shape[2]
    columns = proj.shape[1] // n
    group_rows = rows * n
    logit_scale, logit_bias = scale[0], bias[0]

    own_features = features[:, 0, :]
    own_text = text[:, 0, :]
    text_blocks = gather_group(own_text, n)
    feature_blocks = gather_group(own_features, n)

    xhat, deviation = standardize(own_features)
    normed = (xhat * gain).astype(BF16)
    img_dir, img_inv = unit_rows(dot(normed, proj))
    img_unit = img_dir.astype(BF16)

    txt_dir, txt_inv = unit_rows(own_text.astype(F32))
    own_txt_unit = txt_dir.astype(BF16)
    txt_unit = jnp.concatenate(
        [own_txt_unit] + [unit_rows(block.astype(F32))[0].astype(BF16) for block in text_blocks[1:]]
    )
    row_ids = lax.broadcasted_iota(jnp.int32, (rows, group_rows), 0)
    column_ids = lax.broadcasted_iota(jnp.int32, (rows, group_rows), 1)
    diagonal = (row_ids == column_ids).astype(F32)

    def weights(left, right):
        logits = logit_scale * dot(left, right, LAST) + logit_bias
        return (jax.nn.sigmoid(logits) - diagonal).astype(BF16)

    img_back = logit_scale * dot(weights(img_unit, txt_unit), txt_unit)
    proj_back = (
        (img_back - img_dir * jnp.sum(img_dir * img_back, axis=-1, keepdims=True)) * img_inv
    ).astype(BF16)

    blocks = jnp.transpose(proj_back.reshape(rows, n, columns), (1, 0, 2))
    blocks = lax.all_to_all(blocks, "loop", 0, 0, tiled=True)
    back_columns = blocks.reshape(group_rows, columns)

    norm_back = dot(proj_back, proj, LAST)
    scaled = norm_back * gain
    feature_grad = (
        deviation
        * (
            scaled
            - jnp.mean(scaled, axis=-1, keepdims=True)
            - xhat * jnp.mean(scaled * xhat, axis=-1, keepdims=True)
        )
    ).astype(BF16)
    gain_term = jnp.sum(norm_back * xhat, axis=0) * (1.0 / group_rows)

    other_normed = [(standardize(block)[0] * gain).astype(BF16) for block in feature_blocks[1:]]
    relative = jnp.stack([normed] + other_normed)
    member = jnp.arange(n)
    same_core = (member % 2) == (me % 2)
    chips_back = ((me // 2 - member // 2) % half)
    position = jnp.where(same_core, chips_back, half + chips_back)
    group_normed = relative[position].reshape(group_rows, width)

    partial = (dot(group_normed, back_columns, FIRST) * (1.0 / group_rows)).astype(BF16)
    pieces = lax.all_to_all(partial.reshape(m, width // m, columns), "rep", 0, 0, tiled=True)
    reduced = jnp.sum(pieces.astype(F32), axis=0).astype(BF16)
    gains = lax.all_gather(gain_term, "rep")
    gain_sum = jnp.sum(gains, axis=0)
    proj_rows = lax.all_gather(reduced, "loop")
    proj_grad = jnp.transpose(proj_rows, (1, 0, 2)).reshape(width // m, n * columns).astype(F32)
    gain_gradient = jnp.sum(lax.all_gather(gain_sum, "loop"), axis=0)

    group_unit = jnp.concatenate(
        [img_unit] + [unit_rows(dot(block, proj))[0].astype(BF16) for block in other_normed]
    )
    text_weights = weights(own_txt_unit, group_unit)
    txt_back = logit_scale * dot(text_weights, group_unit)
    text_grad = (
        (txt_back - txt_dir * jnp.sum(txt_dir * txt_back, axis=-1, keepdims=True)) * txt_inv
    ).astype(BF16)
    return feature_grad[:, None, :], text_grad[:, None, :], proj_grad, gain_gradient


VMEM = pl.BlockSpec(memory_space=pltpu.VMEM)
SMEM = pl.BlockSpec(memory_space=pltpu.SMEM)
HBM = pl.BlockSpec(memory_space=pltpu.HBM)
LANES = 128
BAND = 16
TOKEN = ((8, LANES), F32)


def call(body, outs, scratch=(), smem=0, hbm=0, limit=24, flops=0, moved=0):
    def run(*operands):
        specs = [SMEM] * smem + [HBM] * hbm + [VMEM] * (len(operands) - smem - hbm)
        return pl.pallas_call(
            body,
            out_shape=[jax.ShapeDtypeStruct(shape, kind) for shape, kind in outs],
            in_specs=specs,
            out_specs=[VMEM] * len(outs),
            scratch_shapes=[pltpu.VMEM(shape, kind) for shape, kind in scratch]
            + [pltpu.SemaphoreType.DMA((hbm,))] * bool(hbm),
            compiler_params=pltpu.CompilerParams(vmem_limit_bytes=limit * 2**20),
            cost_estimate=pl.CostEstimate(flops=flops, bytes_accessed=moved, transcendentals=0),
        )(*operands)

    return run


def over_rows(count, step, body):
    def turn(index, _):
        body(pl.ds(pl.multiple_of(index * step, step), step))
        return 0

    lax.fori_loop(0, count // step, turn, 0, unroll=min(4, count // step))


def sums(values):
    return jnp.sum(values, axis=-1, keepdims=True)


def normalize_into(source, gain, target, at):
    rows, width = source.shape

    def chunk(where):
        values = source[where, :].astype(F32)
        centred = values - sums(values) * (1.0 / width)
        inverse = lax.rsqrt(sums(centred * centred) * (1.0 / width) + 1e-06)
        target[pl.ds(at + where.start, where.size), :] = (centred * inverse * gain[...]).astype(BF16)

    over_rows(rows, 32, chunk)


def unit_into(source, target, at, inverses=None):
    rows = source.shape[0]

    def chunk(where):
        values = source[where, :].astype(F32)
        inverse = lax.rsqrt(sums(values * values) + 1e-06)
        place = pl.ds(at + where.start, where.size)
        target[place, :] = (values * inverse).astype(BF16)
        if inverses is not None:
            inverses[place, :] = jnp.broadcast_to(inverse, (where.size, LANES))

    over_rows(rows, 32, chunk)


def weigh(dots, scale, bias, diagonal, weights):
    texts, images = dots.shape

    def chunk(index, total):
        where = pl.ds(pl.multiple_of(index * BAND, BAND), BAND)
        product = dots[where, :]
        weight = jnp.tanh((0.5 * scale) * product + 0.5 * bias)
        offset = 0.5
        if diagonal is not None:
            text = index * BAND + diagonal + lax.broadcasted_iota(jnp.int32, product.shape, 0)
            image = lax.broadcasted_iota(jnp.int32, product.shape, 1)
            offset = jnp.where(text == image, -0.5, 0.5)
        weight = (0.5 * weight + offset).astype(BF16)
        weights[where, :] = weight
        both = weight.astype(F32) * product
        return total + both[:8, :] + both[8:, :]

    total = lax.fori_loop(0, texts // BAND, chunk, jnp.zeros((8, images), F32), unroll=4)
    return jnp.sum(total, axis=0, keepdims=True)


def take_columns(source, target):
    members = source.shape[1] // target.shape[1]
    full = target.shape[1] // LANES * LANES
    rest = target.shape[1] - full
    target[:, :full] = source[:, pl.ds(pl.multiple_of(lax.axis_index("loop") * full, LANES), full)]
    for member in range(members):

        @pl.when(lax.axis_index("loop") == member)
        def _():
            target[:, full:] = source[:, members * full + member * rest : members * full + (member + 1) * rest]


def near_body(
    scale, bias, f0_far, proj_far, t0_far, f1, gain_line,
    f0, proj, t0, gain, normed, unit, factors, text_unit, token, projected, semaphores,
):
    rows = f0.shape[0]
    copies = [
        pltpu.make_async_copy(source, target, semaphores.at[at])
        for at, (source, target) in enumerate(((f0_far, f0), (proj_far, proj), (t0_far, t0)))
    ]
    for copy in copies:
        copy.start()
    for at in range(0, gain.shape[1], LANES):
        gain[:, at : at + LANES] = gain_line[at : at + LANES].reshape(1, LANES)
    normalize_into(f1, gain, normed, rows)
    copies[0].wait()
    normalize_into(f0, gain, normed, 0)
    copies[1].wait()
    projected[...] = dot(normed[...], proj[...])
    copies[2].wait()
    unit_into(t0, text_unit, 0)
    unit_into(projected, unit, 0, factors)
    token[...] = jnp.zeros_like(token)


def near_pairs_body(
    scale, bias, normed, unit, factors, text_own, t1, proj, before,
    text_unit, normed_turned, turned, unit_turned, inverse, text_columns, weights, totals, proj_columns, token, dots,
):
    token[...] = jnp.zeros_like(token)
    rows = t1.shape[0]
    text_unit[:rows, :] = text_own[...]
    text_unit[rows:, :] = t1[...]
    dots[...] = dot(text_unit[...], unit[...], LAST)
    totals[...] = weigh(dots, scale[0], bias[0], 0, weights)
    take_columns(text_unit, text_columns)
    take_columns(proj, proj_columns)
    turn_own(unit, factors, turned, unit_turned, inverse)
    normed_turned[...] = normed[...].T


def turn_own(unit, factors, turned, unit_turned, inverse):
    columns = unit_turned.shape[0]
    full = columns // LANES * LANES
    rest = columns - full
    turned[...] = unit[...].T
    unit_turned[:full, :] = turned[pl.ds(pl.multiple_of(lax.axis_index("loop") * full, LANES), full), :]
    begin = turned.shape[0] // columns * full
    unit_turned[full:, :] = turned[pl.ds(pl.multiple_of(begin + lax.axis_index("loop") * rest, BAND), rest), :]
    inverse[...] = factors[...].T[:1, :]


def split_body(f2, before, head, tail):
    head[...] = f2[: head.shape[0], :]
    tail[...] = f2[head.shape[0] :, :]


def far_body(
    scale, bias, f2, f3_head, f3_tail, proj, gain, text_near, text_columns, weights_near,
    normed_turned, unit, turned, unit_turned, inverse, weights, totals, early_near, early_far, token,
    normed, projected, dots, factors,
):
    rows = f2.shape[0]
    normalize_into(f2, gain, normed, 0)
    normalize_into(f3_head, gain, normed, rows)
    normalize_into(f3_tail, gain, normed, rows + f3_head.shape[0])
    projected[...] = dot(normed[...], proj[...])
    unit_into(projected, unit, 0, factors)
    dots[...] = dot(text_near[...], unit[...], LAST)
    totals[...] = weigh(dots, scale[0], bias[0], None, weights)
    turn_own(unit, factors, turned, unit_turned, inverse)
    normed_turned[...] = normed[...].T
    early_near[...] = dot(text_columns[...], weights_near[...], FIRST)
    early_far[...] = dot(text_columns[...], weights[...], FIRST)
    token[...] = jnp.zeros_like(token)


def third_body(
    scale, bias, text_unit, flat_near, flat_far, totals_near, totals_far, early_near, early_far,
    before, weights, back_near, back_far, totals,
    text_columns, dots,
):
    rows = text_unit.shape[0]
    near = 2 * rows
    take_columns(text_unit, text_columns)
    dots[:, :near] = dot(text_unit[...], flat_near[...])
    dots[:, near:] = dot(text_unit[...], flat_far[...])
    added = weigh(dots, scale[0], bias[0], near, weights)
    totals[:, :near] = totals_near[...] + added[:, :near]
    totals[:, near:] = totals_far[...] + added[:, near:]
    added = dot(text_columns[...], weights[...], FIRST)
    back_near[...] = early_near[...] + added[:, :near]
    back_far[...] = early_far[...] + added[:, near:]


def pack_into(target, block, full):
    rows, columns = block.shape
    rest = columns - full
    target[:rows, :] = block[:, :full].astype(BF16)
    per_band = full // rest
    tail = block[:, full:]
    chunks = [tail[at : at + BAND, :] for at in range(0, rows, BAND)]
    for band in range(0, len(chunks), per_band):
        part = chunks[band : band + per_band]
        if len(part) < per_band:
            part.append(jnp.zeros((BAND, full - rest * len(part)), block.dtype))
        at = rows + (band // per_band) * BAND
        target[at : at + BAND, :] = jnp.concatenate(part, axis=1).astype(BF16)


def partial_body(
    members, groups, scale, bias, text_unit, flat_near, flat_far, totals, back_near, back_far, unit_turned_near,
    unit_turned_far, inverse_near, inverse_far, turned_near, turned_far, proj_columns, gain,
    across_three, across_two, across_next, across_own, keep, weights, text_columns, dots, packed,
):
    rows = text_unit.shape[0]
    near = 2 * rows
    every = members * rows
    width = text_unit.shape[1]
    columns = width // members
    count, full = packed.shape[1:]
    scale, bias = scale[0], bias[0]
    take_columns(text_unit, text_columns)
    dots[:, :near] = dot(text_unit[...], flat_near[...])
    dots[:, near:] = dot(text_unit[...], flat_far[...])
    total = totals[...] + weigh(dots, scale, bias, near + rows, weights)
    added = dot(text_columns[...], weights[...], FIRST)
    back = []
    for where, earlier, unit_turned, inverse in (
        (slice(0, near), back_near, unit_turned_near, inverse_near),
        (slice(near, every), back_far, unit_turned_far, inverse_far),
    ):
        whole = earlier[...] + added[:, where]
        part = (whole - unit_turned[...].astype(F32) * total[:, where]) * (inverse[...] * (scale * (1.0 / every)))
        back.append(part.astype(BF16))
    turned = jnp.concatenate([turned_near[...], turned_far[...]], axis=1)
    product = dot(turned, jnp.concatenate(back, axis=1), LAST)
    each = width // groups
    for group in range(groups):
        pack_into(packed.at[group], product[group * each : (group + 1) * each, :], full)

    terms = product * proj_columns[...].astype(F32)
    folded = jnp.concatenate([terms[:, full:], jnp.zeros((width, full + LANES - columns), F32)], axis=1)
    for at in range(0, full, LANES):
        folded = folded + terms[:, at : at + LANES]
    high = folded.astype(BF16)
    low = (folded - high.astype(F32)).astype(BF16)
    ones = jnp.ones((BAND, 2 * LANES), BF16)
    gain_row = dot(ones, jnp.concatenate([high, low], axis=1), LAST)[:1, :] / gain[...]
    pieces = [gain_row[:, at : at + LANES] for at in range(0, width, LANES)]
    pieces.append(jnp.zeros((BAND - len(pieces), LANES), F32))
    gain_tile = jnp.concatenate(pieces, axis=0).astype(BF16)
    for group in range(groups):
        packed[group, count - BAND :, full - LANES :] = gain_tile

    own = lax.axis_index("rep")
    across_three[...] = packed[own ^ 7]
    across_two[...] = packed[own ^ 5]
    across_next[...] = packed[own ^ 3]
    across_own[...] = packed[own ^ 1]
    for at in range(4):
        keep[at] = packed[own ^ (2 * at)]


def image_body(
    scale, proj, text_near, text_third, text_fourth, weights_near, weights_third, weights_fourth,
    unit, factors, before, norm_back, token, back, product,
):
    rows = back.shape[0]
    scale = scale[0]
    product[...] = (
        dot(weights_near[:, :rows], text_near[...], FIRST)
        + dot(weights_third[:, :rows], text_third[...], FIRST)
        + dot(weights_fourth[:, :rows], text_fourth[...], FIRST)
    )

    def image_chunk(where):
        values = product[where, :] * scale
        direction = unit[where, :].astype(F32)
        back[where, :] = (
            (values - direction * sums(direction * values)) * factors[where, :1]
        ).astype(BF16)

    over_rows(rows, 32, image_chunk)
    norm_back[...] = dot(back[...], proj[...], LAST)
    token[...] = jnp.zeros_like(token)


def feature_body(features, gain, norm_back, before, feature_grad, token):
    rows, width = features.shape

    def feature_chunk(where):
        values = features[where, :].astype(F32)
        centred = values - sums(values) * (1.0 / width)
        deviation = lax.rsqrt(sums(centred * centred) * (1.0 / width) + 1e-06)
        xhat = centred * deviation
        scaled = norm_back[where, :] * gain[...]
        feature_grad[where, :] = (
            deviation
            * (scaled - sums(scaled) * (1.0 / width) - xhat * (sums(scaled * xhat) * (1.0 / width)))
        ).astype(BF16)

    over_rows(rows, 32, feature_chunk)
    token[...] = jnp.zeros_like(token)


def text_body(
    scale, text, weights_near, weights_far, unit_near, unit_far, before, text_grad, token, product,
):
    rows = text_grad.shape[0]
    scale = scale[0]
    product[...] = dot(weights_near[:rows, :], unit_near[...]) + dot(weights_far[:rows, :], unit_far[...])

    def text_chunk(where):
        values = product[where, :] * scale
        own = text[where, :].astype(F32)
        own_inverse = lax.rsqrt(sums(own * own) + 1e-06)
        direction = own * own_inverse
        text_grad[where, :] = (
            (values - direction * sums(direction * values)) * own_inverse
        ).astype(BF16)

    over_rows(rows, 32, text_chunk)
    token[...] = jnp.zeros_like(token)


def one_sum_body(place, before, keep, come, total):
    total[...] = (keep[place].astype(F32) + come[...].astype(F32)).astype(BF16)


def far_sum_body(before, two_on, three_on, total):
    total[...] = two_on[...].astype(F32) + three_on[...].astype(F32)


def others_sum_body(far, next_one, total):
    total[...] = far[...] + next_one[...].astype(F32)


def last_sum_body(others, keep, come, next_one, two_on, three_on, total, ordered, own):
    own[...] = (keep[0].astype(F32) + come[...].astype(F32)).astype(BF16)
    parts = (own, next_one, two_on, three_on)
    total[...] = (own[...].astype(F32) + others[...]).astype(BF16)
    count, full = total.shape
    z = lax.axis_index("rep") // 2
    for step, part in enumerate(parts):
        ordered[z ^ step] = part[count - BAND :, full - LANES :].astype(F32)
    value = ordered[0]
    for at in range(1, len(parts)):
        value = value + ordered[at]
    total[count - BAND :, full - LANES :] = value.astype(BF16)


def finish_body(members, before, *refs):
    packets, (proj_grad, gain_gradient, ordered) = refs[:members], refs[members:]
    count, full = packets[0].shape
    rows, width = proj_grad.shape
    rest = width // members - full
    per_band = full // rest
    for k in range(members):
        member = lax.axis_index("loop") ^ k
        proj_grad[:, pl.ds(pl.multiple_of(member * full, LANES), full)] = packets[k][:rows, :].astype(F32)
        ordered[member] = packets[k][rows:, :].astype(F32)
    tails = []
    for index in range(rows // BAND):
        at, lane = (index // per_band) * BAND, (index % per_band) * rest
        tails.append(
            jnp.concatenate([ordered[member][at : at + BAND, lane : lane + rest] for member in range(members)], axis=1)
        )
    proj_grad[:, members * full :] = jnp.concatenate(tails, axis=0)
    value = ordered[0][count - rows - BAND :, full - LANES :]
    for member in range(1, members):
        value = value + ordered[member][count - rows - BAND :, full - LANES :]
    for at in range(width // LANES):
        gain_gradient[at * LANES : (at + 1) * LANES] = value[at]


def local_four(features, text, proj, gain, scale, bias):
    members = lax.axis_size("loop")
    groups = lax.axis_size("rep")
    rows, width = features.shape[0], features.shape[2]
    near, every = 2 * rows, 4 * rows
    columns = width // members
    full = columns // LANES * LANES
    each = width // groups
    bands = -(-(each // BAND) // (full // (columns - full)))
    packet = (each + bands * BAND, full)


    f0, t0 = features[:, 0, :], text[:, 0, :]
    f2 = send(f0, "loop", lambda p: p ^ 2)
    f1 = send(f0, "loop", lambda p: p ^ 1)

    wide, half = ((near, width), BF16), ((rows, width), BF16)
    square, part, turned = ((near, near), BF16), ((near, columns), BF16), ((width, near), BF16)

    line, mine = ((1, near), F32), ((columns, near), BF16)
    kept = ((width, width), BF16)
    f0_kept, proj_kept, t0_kept, gain_row, normed_near, unit_near, factors, text_own, token = call(
        near_body,
        [half, kept, half, ((1, width), F32), wide, wide, ((near, LANES), F32), half, TOKEN],
        [((near, width), F32)],
        smem=2,
        hbm=3,
        limit=46,
        flops=2 * near * width * width,
        moved=8 * near * width,
    )(scale, bias, f0, proj, t0, f1, gain)

    t2 = send(text_own, "loop", lambda p: p ^ 2)
    t1 = send(text_own, "loop", lambda p: p ^ 1)
    head = rows // 6 * 5
    f3_head, f3_tail = call(split_body, [((head, width), BF16), ((rows - head, width), BF16)], moved=1000)(f2, token)
    f3_head = send(f3_head, "loop", lambda p: p ^ 1)
    f3_tail = send(f3_tail, "loop", lambda p: p ^ 1)

    (
        text_near, turned_near, flat_near, unit_turned_near, inverse_near, text_columns_near, weights_near, totals_near, proj_columns,
        token,
    ) = call(
        near_pairs_body,
        [wide, turned, turned, mine, line, part, square, line, ((width, columns), BF16), TOKEN],
        [((near, near), F32)],
        smem=2,
        flops=1000,
        moved=1000,
    )(scale, bias, normed_near, unit_near, factors, text_own, t1, proj_kept, token)

    back_kind = ((columns, near), F32)
    (
        turned_far, unit_far, flat_far, unit_turned_far, inverse_far, weights_far, totals_far, early_near, early_far,
        token,
    ) = call(
        far_body,
        [turned, wide, turned, mine, line, square, line, back_kind, back_kind, TOKEN],
        [wide, ((near, width), F32), ((near, near), F32), ((near, LANES), F32)],
        smem=2,
        flops=1000,
        moved=1000,
    )(
        scale, bias, f2, f3_head, f3_tail, proj_kept, gain_row, text_near, text_columns_near, weights_near,
    )

    text_grad, token = call(
        text_body,
        [half, TOKEN],
        [((rows, width), F32)],
        smem=1,
        flops=1000,
        moved=1000,
    )(scale, t0_kept, weights_near, weights_far, unit_near, unit_far, token)

    t2_after, token = lax.optimization_barrier((t2, token))
    t3 = send(t2_after, "loop", lambda p: p ^ 1)

    narrow = ((rows, every), BF16)
    weights_third, back_near, back_far, totals = call(
        third_body,
        [narrow, back_kind, back_kind, ((1, every), F32)],
        [((rows, columns), BF16), ((rows, every), F32)],
        smem=2,
        flops=2 * near * width * width,
        moved=8 * near * width,
    )(
        scale, bias, t2, flat_near, flat_far, totals_near, totals_far, early_near, early_far, token,
    )

    outs = call(
        functools.partial(partial_body, members, groups),
        [(packet, BF16)] * 4 + [((4,) + packet, BF16), narrow],
        [((rows, columns), BF16), ((rows, every), F32), ((groups,) + packet, BF16)],
        smem=2,
        flops=4 * near * width * width,
        moved=16 * near * width,
    )(
        scale, bias, t3, flat_near, flat_far, totals, back_near, back_far, unit_turned_near, unit_turned_far,
        inverse_near, inverse_far, turned_near, turned_far, proj_columns, gain_row,
    )
    across_three, across_two, across_next, across_own, keep, weights_fourth = outs
    come_two = send(across_two, "rep", lambda p: p ^ 1)
    come_three = send(across_three, "rep", lambda p: p ^ 1)
    come_next = send(across_next, "rep", lambda p: p ^ 1)
    come_own = send(across_own, "rep", lambda p: p ^ 1)
    (two_sum,) = call(functools.partial(one_sum_body, 2), [(packet, BF16)], flops=1000, moved=1000)(
        keep, keep, come_two
    )
    two_on = send(two_sum, "rep", lambda p: p ^ 4)
    (three_sum,) = call(functools.partial(one_sum_body, 3), [(packet, BF16)], flops=1000, moved=1000)(
        two_sum, keep, come_three
    )
    three_on = send(three_sum, "rep", lambda p: p ^ 6)
    (next_sum,) = call(functools.partial(one_sum_body, 1), [(packet, BF16)], flops=1000, moved=1000)(
        three_sum, keep, come_next
    )
    next_one = send(next_sum, "rep", lambda p: p ^ 2)
    norm_back, token = call(
        image_body,
        [((rows, width), F32), TOKEN],
        [half, ((rows, width), F32)],
        smem=1,
        flops=1000,
        moved=1000,
    )(
        scale, proj_kept, text_near, t2, t3, weights_near, weights_third, weights_fourth,
        unit_near, factors, next_sum,
    )
    (far_sum,) = call(far_sum_body, [(packet, F32)], moved=1000)(token, two_on, three_on)
    (others,) = call(others_sum_body, [(packet, F32)], moved=1000)(far_sum, next_one)
    (reduced,) = call(last_sum_body, [(packet, BF16)], [((4, BAND, LANES), F32), (packet, BF16)], moved=1000)(
        others, keep, come_own, next_one, two_on, three_on
    )
    far_block = send(reduced, "loop", lambda p: p ^ 2)
    near_block = send(reduced, "loop", lambda p: p ^ 1)
    feature_grad, token = call(feature_body, [half, TOKEN], moved=12 * near * width)(
        f0_kept, gain_row, norm_back, reduced
    )
    far_block, token = lax.optimization_barrier((far_block, token))
    blocks = [reduced, near_block, far_block, send(far_block, "loop", lambda p: p ^ 1)]

    proj_grad, gain_gradient = call(
        functools.partial(finish_body, members),
        [((each, width), F32), ((width,), F32)],
        [((members, bands * BAND, full), F32)],
        moved=8 * each * width,
    )(token, *blocks)
    return feature_grad[:, None, :], text_grad[:, None, :], proj_grad, gain_gradient


def four_fits(mesh, rows_shape):
    members, groups = mesh.shape["loop"], mesh.shape["rep"]
    rows, width = rows_shape[0] // members, rows_shape[2]
    if members != 4 or groups != 8 or width % (members * groups) or width % LANES:
        return False
    columns, each = width // members, width // groups
    full = columns // LANES * LANES
    rest = columns - full
    if rest == 0 or full < LANES or full % rest or each % BAND or rows % 64 or width // LANES > BAND:
        return False
    chunks = each // BAND
    used = (chunks - 1) % (full // rest) + 1
    return used * rest <= full - LANES


def solution(mesh):
    def run(features, text, proj, gain, scale, bias):
        body = local_four if four_fits(mesh, features.shape) else local_any_size
        return jax.shard_map(
            body,
            mesh=mesh,
            in_specs=(P("loop", "rep", None), P("loop", "rep", None), P(), P(), P(), P()),
            out_specs=(P("loop", "rep", None), P("loop", "rep", None), P("rep", None), P()),
            check_vma=False,
        )(features, text, proj, gain, scale, bias)

    return run
```

```python
import functools

import jax
import jax.numpy as jnp
from jax import lax
from jax.experimental import pallas as pl
from jax.experimental.pallas import tpu as pltpu
from jax.sharding import PartitionSpec as P

F32 = jnp.float32
BF16 = jnp.bfloat16
LAST = (((1,), (1,)), ((), ()))
FIRST = (((0,), (0,)), ((), ()))


def dot(a, b, dims=(((1,), (0,)), ((), ()))):
    return lax.dot_general(a, b, dims, preferred_element_type=F32)


def unit_rows(values):
    inverse = lax.rsqrt(jnp.sum(values * values, axis=-1, keepdims=True) + 1e-06)
    return values * inverse, inverse


def standardize(rows):
    values = rows.astype(F32)
    centred = values - jnp.mean(values, axis=-1, keepdims=True)
    inverse = lax.rsqrt(jnp.mean(centred * centred, axis=-1, keepdims=True) + 1e-06)
    return centred * inverse, inverse


def send(value, axis, target):
    count = lax.axis_size(axis)
    return lax.ppermute(value, axis, [(p, target(p)) for p in range(count)])


def gather_group(value, count):
    mine = [value]
    for step in range(1, count // 2):
        mine.append(send(value, "loop", lambda p: (p + 2 * step) % count))
    mates = [send(block, "loop", lambda p: p ^ 1) for block in mine]
    return mine + mates


def local_any_size(features, text, proj, gain, scale, bias):
    n = lax.axis_size("loop")
    m = lax.axis_size("rep")
    me = lax.axis_index("loop")
    half = n // 2
    rows, width = features.shape[0], features.shape[2]
    columns = proj.shape[1] // n
    group_rows = rows * n
    logit_scale, logit_bias = scale[0], bias[0]

    own_features = features[:, 0, :]
    own_text = text[:, 0, :]
    text_blocks = gather_group(own_text, n)
    feature_blocks = gather_group(own_features, n)

    xhat, deviation = standardize(own_features)
    normed = (xhat * gain).astype(BF16)
    img_dir, img_inv = unit_rows(dot(normed, proj))
    img_unit = img_dir.astype(BF16)

    txt_dir, txt_inv = unit_rows(own_text.astype(F32))
    own_txt_unit = txt_dir.astype(BF16)
    txt_unit = jnp.concatenate(
        [own_txt_unit] + [unit_rows(block.astype(F32))[0].astype(BF16) for block in text_blocks[1:]]
    )
    row_ids = lax.broadcasted_iota(jnp.int32, (rows, group_rows), 0)
    column_ids = lax.broadcasted_iota(jnp.int32, (rows, group_rows), 1)
    diagonal = (row_ids == column_ids).astype(F32)

    def weights(left, right):
        logits = logit_scale * dot(left, right, LAST) + logit_bias
        return (jax.nn.sigmoid(logits) - diagonal).astype(BF16)

    img_back = logit_scale * dot(weights(img_unit, txt_unit), txt_unit)
    proj_back = (
        (img_back - img_dir * jnp.sum(img_dir * img_back, axis=-1, keepdims=True)) * img_inv
    ).astype(BF16)

    blocks = jnp.transpose(proj_back.reshape(rows, n, columns), (1, 0, 2))
    blocks = lax.all_to_all(blocks, "loop", 0, 0, tiled=True)
    back_columns = blocks.reshape(group_rows, columns)

    norm_back = dot(proj_back, proj, LAST)
    scaled = norm_back * gain
    feature_grad = (
        deviation
        * (
            scaled
            - jnp.mean(scaled, axis=-1, keepdims=True)
            - xhat * jnp.mean(scaled * xhat, axis=-1, keepdims=True)
        )
    ).astype(BF16)
    gain_term = jnp.sum(norm_back * xhat, axis=0) * (1.0 / group_rows)

    other_normed = [(standardize(block)[0] * gain).astype(BF16) for block in feature_blocks[1:]]
    relative = jnp.stack([normed] + other_normed)
    member = jnp.arange(n)
    same_core = (member % 2) == (me % 2)
    chips_back = ((me // 2 - member // 2) % half)
    position = jnp.where(same_core, chips_back, half + chips_back)
    group_normed = relative[position].reshape(group_rows, width)

    partial = (dot(group_normed, back_columns, FIRST) * (1.0 / group_rows)).astype(BF16)
    pieces = lax.all_to_all(partial.reshape(m, width // m, columns), "rep", 0, 0, tiled=True)
    reduced = jnp.sum(pieces.astype(F32), axis=0).astype(BF16)
    gains = lax.all_gather(gain_term, "rep")
    gain_sum = jnp.sum(gains, axis=0)
    proj_rows = lax.all_gather(reduced, "loop")
    proj_grad = jnp.transpose(proj_rows, (1, 0, 2)).reshape(width // m, n * columns).astype(F32)
    gain_gradient = jnp.sum(lax.all_gather(gain_sum, "loop"), axis=0)

    group_unit = jnp.concatenate(
        [img_unit] + [unit_rows(dot(block, proj))[0].astype(BF16) for block in other_normed]
    )
    text_weights = weights(own_txt_unit, group_unit)
    txt_back = logit_scale * dot(text_weights, group_unit)
    text_grad = (
        (txt_back - txt_dir * jnp.sum(txt_dir * txt_back, axis=-1, keepdims=True)) * txt_inv
    ).astype(BF16)
    return feature_grad[:, None, :], text_grad[:, None, :], proj_grad, gain_gradient


VMEM = pl.BlockSpec(memory_space=pltpu.VMEM)
SMEM = pl.BlockSpec(memory_space=pltpu.SMEM)
HBM = pl.BlockSpec(memory_space=pltpu.HBM)
LANES = 128
BAND = 16
TOKEN = ((8, LANES), F32)


def call(body, outs, scratch=(), smem=0, hbm=0, limit=24, flops=0, moved=0):
    def run(*operands):
        specs = [SMEM] * smem + [HBM] * hbm + [VMEM] * (len(operands) - smem - hbm)
        return pl.pallas_call(
            body,
            out_shape=[jax.ShapeDtypeStruct(shape, kind) for shape, kind in outs],
            in_specs=specs,
            out_specs=[VMEM] * len(outs),
            scratch_shapes=[pltpu.VMEM(shape, kind) for shape, kind in scratch]
            + [pltpu.SemaphoreType.DMA((hbm,))] * bool(hbm),
            compiler_params=pltpu.CompilerParams(vmem_limit_bytes=limit * 2**20),
            cost_estimate=pl.CostEstimate(flops=flops, bytes_accessed=moved, transcendentals=0),
        )(*operands)

    return run


def over_rows(count, step, body):
    def turn(index, _):
        body(pl.ds(pl.multiple_of(index * step, step), step))
        return 0

    lax.fori_loop(0, count // step, turn, 0, unroll=min(4, count // step))


def sums(values):
    return jnp.sum(values, axis=-1, keepdims=True)


def normalize_into(source, gain, target, at):
    rows, width = source.shape

    def chunk(where):
        values = source[where, :].astype(F32)
        centred = values - sums(values) * (1.0 / width)
        inverse = lax.rsqrt(sums(centred * centred) * (1.0 / width) + 1e-06)
        target[pl.ds(at + where.start, where.size), :] = (centred * inverse * gain[...]).astype(BF16)

    over_rows(rows, 32, chunk)


def unit_into(source, target, at, inverses=None):
    rows = source.shape[0]

    def chunk(where):
        values = source[where, :].astype(F32)
        inverse = lax.rsqrt(sums(values * values) + 1e-06)
        place = pl.ds(at + where.start, where.size)
        target[place, :] = (values * inverse).astype(BF16)
        if inverses is not None:
            inverses[place, :] = jnp.broadcast_to(inverse, (where.size, LANES))

    over_rows(rows, 32, chunk)


def weigh(dots, scale, bias, diagonal, weights):
    texts, images = dots.shape

    def chunk(index, total):
        where = pl.ds(pl.multiple_of(index * BAND, BAND), BAND)
        product = dots[where, :]
        weight = jnp.tanh((0.5 * scale) * product + 0.5 * bias)
        offset = 0.5
        if diagonal is not None:
            text = index * BAND + diagonal + lax.broadcasted_iota(jnp.int32, product.shape, 0)
            image = lax.broadcasted_iota(jnp.int32, product.shape, 1)
            offset = jnp.where(text == image, -0.5, 0.5)
        weight = (0.5 * weight + offset).astype(BF16)
        weights[where, :] = weight
        both = weight.astype(F32) * product
        return total + both[:8, :] + both[8:, :]

    total = lax.fori_loop(0, texts // BAND, chunk, jnp.zeros((8, images), F32), unroll=12)
    return jnp.sum(total, axis=0, keepdims=True)


def take_columns(source, target):
    members = source.shape[1] // target.shape[1]
    full = target.shape[1] // LANES * LANES
    rest = target.shape[1] - full
    target[:, :full] = source[:, pl.ds(pl.multiple_of(lax.axis_index("loop") * full, LANES), full)]
    for member in range(members):

        @pl.when(lax.axis_index("loop") == member)
        def _():
            target[:, full:] = source[:, members * full + member * rest : members * full + (member + 1) * rest]


def near_body(
    scale, bias, f0_far, proj_far, t0_far, f1, gain_line,
    f0, proj, t0, gain, normed, unit, factors, text_unit, token, projected, semaphores,
):
    rows = f0.shape[0]
    copies = [
        pltpu.make_async_copy(source, target, semaphores.at[at])
        for at, (source, target) in enumerate(((f0_far, f0), (proj_far, proj), (t0_far, t0)))
    ]
    for copy in copies:
        copy.start()
    for at in range(0, gain.shape[1], LANES):
        gain[:, at : at + LANES] = gain_line[at : at + LANES].reshape(1, LANES)
    normalize_into(f1, gain, normed, rows)
    copies[0].wait()
    normalize_into(f0, gain, normed, 0)
    copies[1].wait()
    projected[...] = dot(normed[...], proj[...])
    copies[2].wait()
    unit_into(t0, text_unit, 0)
    unit_into(projected, unit, 0, factors)
    token[...] = jnp.zeros_like(token)


def near_pairs_body(
    scale, bias, normed, unit, factors, text_own, t1, proj, before,
    text_unit, normed_turned, turned, unit_turned, inverse, text_columns, weights, totals, proj_columns, token, dots,
):
    token[...] = jnp.zeros_like(token)
    rows = t1.shape[0]
    text_unit[:rows, :] = text_own[...]
    text_unit[rows:, :] = t1[...]
    dots[...] = dot(text_unit[...], unit[...], LAST)
    totals[...] = weigh(dots, scale[0], bias[0], 0, weights)
    take_columns(text_unit, text_columns)
    take_columns(proj, proj_columns)
    turn_own(unit, factors, turned, unit_turned, inverse)
    normed_turned[...] = normed[...].T


def turn_own(unit, factors, turned, unit_turned, inverse):
    columns = unit_turned.shape[0]
    full = columns // LANES * LANES
    rest = columns - full
    turned[...] = unit[...].T
    unit_turned[:full, :] = turned[pl.ds(pl.multiple_of(lax.axis_index("loop") * full, LANES), full), :]
    begin = turned.shape[0] // columns * full
    unit_turned[full:, :] = turned[pl.ds(pl.multiple_of(begin + lax.axis_index("loop") * rest, BAND), rest), :]
    inverse[...] = factors[...].T[:1, :]


def split_body(f2, before, head, tail):
    head[...] = f2[: head.shape[0], :]
    tail[...] = f2[head.shape[0] :, :]


def far_body(
    scale, bias, f2, f3_head, f3_tail, proj, gain, text_near, text_columns, weights_near,
    normed_turned, unit, turned, unit_turned, inverse, weights, totals, early_near, early_far, token,
    normed, projected, dots, factors,
):
    rows = f2.shape[0]
    normalize_into(f2, gain, normed, 0)
    normalize_into(f3_head, gain, normed, rows)
    normalize_into(f3_tail, gain, normed, rows + f3_head.shape[0])
    projected[...] = dot(normed[...], proj[...])
    unit_into(projected, unit, 0, factors)
    dots[...] = dot(text_near[...], unit[...], LAST)
    totals[...] = weigh(dots, scale[0], bias[0], None, weights)
    turn_own(unit, factors, turned, unit_turned, inverse)
    normed_turned[...] = normed[...].T
    early_near[...] = dot(text_columns[...], weights_near[...], FIRST)
    early_far[...] = dot(text_columns[...], weights[...], FIRST)
    token[...] = jnp.zeros_like(token)


def third_body(
    scale, bias, text_unit, flat_near, flat_far, totals_near, totals_far, early_near, early_far,
    before, weights, back_near, back_far, totals,
    text_columns, dots,
):
    rows = text_unit.shape[0]
    near = 2 * rows
    take_columns(text_unit, text_columns)
    dots[:, :near] = dot(text_unit[...], flat_near[...])
    dots[:, near:] = dot(text_unit[...], flat_far[...])
    added = weigh(dots, scale[0], bias[0], near, weights)
    totals[:, :near] = totals_near[...] + added[:, :near]
    totals[:, near:] = totals_far[...] + added[:, near:]
    added = dot(text_columns[...], weights[...], FIRST)
    back_near[...] = early_near[...] + added[:, :near]
    back_far[...] = early_far[...] + added[:, near:]


def pack_into(target, block, full):
    rows, columns = block.shape
    rest = columns - full
    target[:rows, :] = block[:, :full].astype(BF16)
    per_band = full // rest
    tail = block[:, full:]
    chunks = [tail[at : at + BAND, :] for at in range(0, rows, BAND)]
    for band in range(0, len(chunks), per_band):
        part = chunks[band : band + per_band]
        if len(part) < per_band:
            part.append(jnp.zeros((BAND, full - rest * len(part)), block.dtype))
        at = rows + (band // per_band) * BAND
        target[at : at + BAND, :] = jnp.concatenate(part, axis=1).astype(BF16)


def partial_body(
    members, groups, scale, bias, text_unit, flat_near, flat_far, totals, back_near, back_far, unit_turned_near,
    unit_turned_far, inverse_near, inverse_far, turned_near, turned_far, proj_columns, gain,
    across_three, across_two, across_next, across_own, keep, weights, text_columns, dots, packed,
):
    rows = text_unit.shape[0]
    near = 2 * rows
    every = members * rows
    width = text_unit.shape[1]
    columns = width // members
    count, full = packed.shape[1:]
    scale, bias = scale[0], bias[0]
    take_columns(text_unit, text_columns)
    dots[:, :near] = dot(text_unit[...], flat_near[...])
    dots[:, near:] = dot(text_unit[...], flat_far[...])
    total = totals[...] + weigh(dots, scale, bias, near + rows, weights)
    added = dot(text_columns[...], weights[...], FIRST)
    back = []
    for where, earlier, unit_turned, inverse in (
        (slice(0, near), back_near, unit_turned_near, inverse_near),
        (slice(near, every), back_far, unit_turned_far, inverse_far),
    ):
        whole = earlier[...] + added[:, where]
        part = (whole - unit_turned[...].astype(F32) * total[:, where]) * (inverse[...] * (scale * (1.0 / every)))
        back.append(part.astype(BF16))
    turned = jnp.concatenate([turned_near[...], turned_far[...]], axis=1)
    product = dot(turned, jnp.concatenate(back, axis=1), LAST)
    each = width // groups
    for group in range(groups):
        pack_into(packed.at[group], product[group * each : (group + 1) * each, :], full)

    terms = product * proj_columns[...].astype(F32)
    folded = jnp.concatenate([terms[:, full:], jnp.zeros((width, full + LANES - columns), F32)], axis=1)
    for at in range(0, full, LANES):
        folded = folded + terms[:, at : at + LANES]
    high = folded.astype(BF16)
    low = (folded - high.astype(F32)).astype(BF16)
    ones = jnp.ones((BAND, 2 * LANES), BF16)
    gain_row = dot(ones, jnp.concatenate([high, low], axis=1), LAST)[:1, :] / gain[...]
    pieces = [gain_row[:, at : at + LANES] for at in range(0, width, LANES)]
    pieces.append(jnp.zeros((BAND - len(pieces), LANES), F32))
    gain_tile = jnp.concatenate(pieces, axis=0).astype(BF16)
    for group in range(groups):
        packed[group, count - BAND :, full - LANES :] = gain_tile

    own = lax.axis_index("rep")
    across_three[...] = packed[own ^ 7]
    across_two[...] = packed[own ^ 5]
    across_next[...] = packed[own ^ 3]
    across_own[...] = packed[own ^ 1]
    for at in range(4):
        keep[at] = packed[own ^ (2 * at)]


def image_body(
    scale, proj, text_near, text_third, text_fourth, weights_near, weights_third, weights_fourth,
    unit, factors, before, norm_back, token, back, product,
):
    rows = back.shape[0]
    scale = scale[0]
    product[...] = (
        dot(weights_near[:, :rows], text_near[...], FIRST)
        + dot(weights_third[:, :rows], text_third[...], FIRST)
        + dot(weights_fourth[:, :rows], text_fourth[...], FIRST)
    )

    def image_chunk(where):
        values = product[where, :] * scale
        direction = unit[where, :].astype(F32)
        back[where, :] = (
            (values - direction * sums(direction * values)) * factors[where, :1]
        ).astype(BF16)

    over_rows(rows, 32, image_chunk)
    norm_back[...] = dot(back[...], proj[...], LAST)
    token[...] = jnp.zeros_like(token)


def feature_body(features, gain, norm_back, before, feature_grad, token):
    rows, width = features.shape

    def feature_chunk(where):
        values = features[where, :].astype(F32)
        centred = values - sums(values) * (1.0 / width)
        deviation = lax.rsqrt(sums(centred * centred) * (1.0 / width) + 1e-06)
        xhat = centred * deviation
        scaled = norm_back[where, :] * gain[...]
        feature_grad[where, :] = (
            deviation
            * (scaled - sums(scaled) * (1.0 / width) - xhat * (sums(scaled * xhat) * (1.0 / width)))
        ).astype(BF16)

    over_rows(rows, 32, feature_chunk)
    token[...] = jnp.zeros_like(token)


def text_body(
    scale, text, weights_near, weights_far, unit_near, unit_far, before, text_grad, token, product,
):
    rows = text_grad.shape[0]
    scale = scale[0]
    product[...] = dot(weights_near[:rows, :], unit_near[...]) + dot(weights_far[:rows, :], unit_far[...])

    def text_chunk(where):
        values = product[where, :] * scale
        own = text[where, :].astype(F32)
        own_inverse = lax.rsqrt(sums(own * own) + 1e-06)
        direction = own * own_inverse
        text_grad[where, :] = (
            (values - direction * sums(direction * values)) * own_inverse
        ).astype(BF16)

    over_rows(rows, 32, text_chunk)
    token[...] = jnp.zeros_like(token)


def one_sum_body(place, before, keep, come, total):
    total[...] = (keep[place].astype(F32) + come[...].astype(F32)).astype(BF16)


def far_sum_body(before, two_on, three_on, total):
    total[...] = two_on[...].astype(F32) + three_on[...].astype(F32)


def others_sum_body(far, next_one, total):
    total[...] = far[...] + next_one[...].astype(F32)


def last_sum_body(others, keep, come, next_one, two_on, three_on, total, ordered, own):
    own[...] = (keep[0].astype(F32) + come[...].astype(F32)).astype(BF16)
    parts = (own, next_one, two_on, three_on)
    total[...] = (own[...].astype(F32) + others[...]).astype(BF16)
    count, full = total.shape
    z = lax.axis_index("rep") // 2
    for step, part in enumerate(parts):
        ordered[z ^ step] = part[count - BAND :, full - LANES :].astype(F32)
    value = ordered[0]
    for at in range(1, len(parts)):
        value = value + ordered[at]
    total[count - BAND :, full - LANES :] = value.astype(BF16)


def finish_body(members, before, *refs):
    packets, (proj_grad, gain_gradient, ordered) = refs[:members], refs[members:]
    count, full = packets[0].shape
    rows, width = proj_grad.shape
    rest = width // members - full
    per_band = full // rest
    for k in range(members):
        member = lax.axis_index("loop") ^ k
        proj_grad[:, pl.ds(pl.multiple_of(member * full, LANES), full)] = packets[k][:rows, :].astype(F32)
        ordered[member] = packets[k][rows:, :].astype(F32)
    tails = []
    for index in range(rows // BAND):
        at, lane = (index // per_band) * BAND, (index % per_band) * rest
        tails.append(
            jnp.concatenate([ordered[member][at : at + BAND, lane : lane + rest] for member in range(members)], axis=1)
        )
    proj_grad[:, members * full :] = jnp.concatenate(tails, axis=0)
    value = ordered[0][count - rows - BAND :, full - LANES :]
    for member in range(1, members):
        value = value + ordered[member][count - rows - BAND :, full - LANES :]
    for at in range(width // LANES):
        gain_gradient[at * LANES : (at + 1) * LANES] = value[at]


def local_four(features, text, proj, gain, scale, bias):
    members = lax.axis_size("loop")
    groups = lax.axis_size("rep")
    rows, width = features.shape[0], features.shape[2]
    near, every = 2 * rows, 4 * rows
    columns = width // members
    full = columns // LANES * LANES
    each = width // groups
    bands = -(-(each // BAND) // (full // (columns - full)))
    packet = (each + bands * BAND, full)


    f0, t0 = features[:, 0, :], text[:, 0, :]
    f2 = send(f0, "loop", lambda p: p ^ 2)
    f1 = send(f0, "loop", lambda p: p ^ 1)

    wide, half = ((near, width), BF16), ((rows, width), BF16)
    square, part, turned = ((near, near), BF16), ((near, columns), BF16), ((width, near), BF16)

    line, mine = ((1, near), F32), ((columns, near), BF16)
    kept = ((width, width), BF16)
    f0_kept, proj_kept, t0_kept, gain_row, normed_near, unit_near, factors, text_own, token = call(
        near_body,
        [half, kept, half, ((1, width), F32), wide, wide, ((near, LANES), F32), half, TOKEN],
        [((near, width), F32)],
        smem=2,
        hbm=3,
        limit=46,
        flops=2 * near * width * width,
        moved=8 * near * width,
    )(scale, bias, f0, proj, t0, f1, gain)

    t2 = send(text_own, "loop", lambda p: p ^ 2)
    t1 = send(text_own, "loop", lambda p: p ^ 1)
    head = rows // 6 * 5
    f3_head, f3_tail = call(split_body, [((head, width), BF16), ((rows - head, width), BF16)], moved=1000)(f2, token)
    f3_head = send(f3_head, "loop", lambda p: p ^ 1)
    f3_tail = send(f3_tail, "loop", lambda p: p ^ 1)

    (
        text_near, turned_near, flat_near, unit_turned_near, inverse_near, text_columns_near, weights_near, totals_near, proj_columns,
        token,
    ) = call(
        near_pairs_body,
        [wide, turned, turned, mine, line, part, square, line, ((width, columns), BF16), TOKEN],
        [((near, near), F32)],
        smem=2,
        flops=1000,
        moved=1000,
    )(scale, bias, normed_near, unit_near, factors, text_own, t1, proj_kept, token)

    back_kind = ((columns, near), F32)
    (
        turned_far, unit_far, flat_far, unit_turned_far, inverse_far, weights_far, totals_far, early_near, early_far,
        token,
    ) = call(
        far_body,
        [turned, wide, turned, mine, line, square, line, back_kind, back_kind, TOKEN],
        [wide, ((near, width), F32), ((near, near), F32), ((near, LANES), F32)],
        smem=2,
        flops=1000,
        moved=1000,
    )(
        scale, bias, f2, f3_head, f3_tail, proj_kept, gain_row, text_near, text_columns_near, weights_near,
    )

    text_grad, token = call(
        text_body,
        [half, TOKEN],
        [((rows, width), F32)],
        smem=1,
        flops=1000,
        moved=1000,
    )(scale, t0_kept, weights_near, weights_far, unit_near, unit_far, token)

    t2_after, token = lax.optimization_barrier((t2, token))
    t3 = send(t2_after, "loop", lambda p: p ^ 1)

    narrow = ((rows, every), BF16)
    weights_third, back_near, back_far, totals = call(
        third_body,
        [narrow, back_kind, back_kind, ((1, every), F32)],
        [((rows, columns), BF16), ((rows, every), F32)],
        smem=2,
        flops=2 * near * width * width,
        moved=8 * near * width,
    )(
        scale, bias, t2, flat_near, flat_far, totals_near, totals_far, early_near, early_far, token,
    )

    outs = call(
        functools.partial(partial_body, members, groups),
        [(packet, BF16)] * 4 + [((4,) + packet, BF16), narrow],
        [((rows, columns), BF16), ((rows, every), F32), ((groups,) + packet, BF16)],
        smem=2,
        flops=4 * near * width * width,
        moved=16 * near * width,
    )(
        scale, bias, t3, flat_near, flat_far, totals, back_near, back_far, unit_turned_near, unit_turned_far,
        inverse_near, inverse_far, turned_near, turned_far, proj_columns, gain_row,
    )
    across_three, across_two, across_next, across_own, keep, weights_fourth = outs
    come_two = send(across_two, "rep", lambda p: p ^ 1)
    come_three = send(across_three, "rep", lambda p: p ^ 1)
    come_next = send(across_next, "rep", lambda p: p ^ 1)
    come_own = send(across_own, "rep", lambda p: p ^ 1)
    (two_sum,) = call(functools.partial(one_sum_body, 2), [(packet, BF16)], flops=1000, moved=1000)(
        keep, keep, come_two
    )
    two_on = send(two_sum, "rep", lambda p: p ^ 4)
    (three_sum,) = call(functools.partial(one_sum_body, 3), [(packet, BF16)], flops=1000, moved=1000)(
        two_sum, keep, come_three
    )
    three_on = send(three_sum, "rep", lambda p: p ^ 6)
    (next_sum,) = call(functools.partial(one_sum_body, 1), [(packet, BF16)], flops=1000, moved=1000)(
        three_sum, keep, come_next
    )
    next_one = send(next_sum, "rep", lambda p: p ^ 2)
    norm_back, token = call(
        image_body,
        [((rows, width), F32), TOKEN],
        [half, ((rows, width), F32)],
        smem=1,
        flops=1000,
        moved=1000,
    )(
        scale, proj_kept, text_near, t2, t3, weights_near, weights_third, weights_fourth,
        unit_near, factors, next_sum,
    )
    (far_sum,) = call(far_sum_body, [(packet, F32)], moved=1000)(token, two_on, three_on)
    (others,) = call(others_sum_body, [(packet, F32)], moved=1000)(far_sum, next_one)
    (reduced,) = call(last_sum_body, [(packet, BF16)], [((4, BAND, LANES), F32), (packet, BF16)], moved=1000)(
        others, keep, come_own, next_one, two_on, three_on
    )
    far_block = send(reduced, "loop", lambda p: p ^ 2)
    near_block = send(reduced, "loop", lambda p: p ^ 1)
    feature_grad, token = call(feature_body, [half, TOKEN], moved=12 * near * width)(
        f0_kept, gain_row, norm_back, reduced
    )
    far_block, token = lax.optimization_barrier((far_block, token))
    blocks = [reduced, near_block, far_block, send(far_block, "loop", lambda p: p ^ 1)]

    proj_grad, gain_gradient = call(
        functools.partial(finish_body, members),
        [((each, width), F32), ((width,), F32)],
        [((members, bands * BAND, full), F32)],
        moved=8 * each * width,
    )(token, *blocks)
    return feature_grad[:, None, :], text_grad[:, None, :], proj_grad, gain_gradient


def four_fits(mesh, rows_shape):
    members, groups = mesh.shape["loop"], mesh.shape["rep"]
    rows, width = rows_shape[0] // members, rows_shape[2]
    if members != 4 or groups != 8 or width % (members * groups) or width % LANES:
        return False
    columns, each = width // members, width // groups
    full = columns // LANES * LANES
    rest = columns - full
    if rest == 0 or full < LANES or full % rest or each % BAND or rows % 64 or width // LANES > BAND:
        return False
    chunks = each // BAND
    used = (chunks - 1) % (full // rest) + 1
    return used * rest <= full - LANES


def solution(mesh):
    def run(features, text, proj, gain, scale, bias):
        body = local_four if four_fits(mesh, features.shape) else local_any_size
        return jax.shard_map(
            body,
            mesh=mesh,
            in_specs=(P("loop", "rep", None), P("loop", "rep", None), P(), P(), P(), P()),
            out_specs=(P("loop", "rep", None), P("loop", "rep", None), P("rep", None), P()),
            check_vma=False,
        )(features, text, proj, gain, scale, bias)

    return run
```
